32 devices in a mesh: grp: 2 (over y), exp: 16 (over z, x, core).
Axes of the slice: x: 2, y: 2, z: 4, core: 2. Of those that a mesh axis runs over, the one named last changes fastest.
Arguments:
- tokens: bfloat16 [4096, 2048], P(('grp', 'exp')), parts along dimension 0, may hold values from -6 to 6
- cotangent: bfloat16 [4096, 2048], P(('grp', 'exp')), parts along dimension 0, may hold values from -0.29882812 to 0.29882812
- routes: int32 [4096, 8], P(('grp', 'exp')), parts along dimension 0, may hold values from 0 to 15, all different within a row; in each aligned block of 128 rows (0 to 127, 128 to 255, ...) at most 80 rows name the same one
- combine: bfloat16 [4096, 8], P(('grp', 'exp')), parts along dimension 0, may hold values from 0.049804688 to 0.5
- doc_ids: int32 [4096], P(('grp', 'exp')), parts along dimension 0, may hold values from 0 to 3, never falling along the last dimension, each value on 1 to 1024 neighbouring positions
- w_gate: bfloat16 [16, 2048, 768], P('exp'), may hold values from -0.125 to 0.125
- w_up: bfloat16 [16, 2048, 768], P('exp'), may hold values from -0.125 to 0.125
- w_down: bfloat16 [16, 768, 2048], P('exp'), may hold values from -0.21875 to 0.21875
- proj_hidden: bfloat16 [16, 768, 64], P('exp'), may hold values from -0.21875 to 0.21875
- proj_output: bfloat16 [16, 2048, 64], P('exp'), may hold values from -6 to 6
Outputs:
- features: float32 [8, 16, 64, 64], P('grp', 'exp'), parts along dimension 0
- route_grad: float32 [4096, 8], P(('grp', 'exp')), parts along dimension 0
The draws below stay inside these ranges and needn't reach their ends.
There are 2 independent parts, one for each index of `grp`. The reference program is written for one: setup_inputs(seed, part) draws one part's arguments, and reference() takes and returns one part's arrays. A program takes and returns all parts, laid end to end along the dimension named above; an argument that names none is the same for every part. Nothing has to cross between parts.
Inputs may be any that keep to these rules, and one draw needn't show every extreme that they name: `routes`: among the 128 rows of one device no expert is named more than 80 times, a bound that some block reaches; a row names 8 different experts. `doc_ids`: document ids never fall along the tokens; each of the 4 documents holds 1 to 1024 tokens, one exactly 1024.
All inputs are finite; a program needn't handle non-finite values.
Results may differ from the reference program's by a relative error of at most 0.0051.
Values may be sent and summed in bfloat16 or wider, within the bound.
No kernel may reach another device: no remote copies, remote signals or barrier semaphores. Data moves between devices by JAX's collectives and lax.ppermute only.
A program may use at most 128 MiB of HBM per device.

```python
import math
import jax
import jax.numpy as jnp
import numpy as np
from jax import lax

D = 2048
FF = 768
RANK = 64
TOPK = 8
TOK_DEV = 128
EXPERTS = 16
TOKENS = 2048
CAP = 80
DOCS = 4
DOC_MOST = 1024
N_EXP = 16


def level_of(stream_key, dims, pieces, smallest, high):
    def one(position, blocks):
        heights = jax.random.uniform(jax.random.fold_in(jax.random.fold_in(stream_key, 6), position), (blocks,), jnp.float32, smallest / len(pieces), high / len(pieces))
        return jnp.repeat(jnp.exp(heights), dims[position] // blocks).reshape((-1,) + (1,) * (len(dims) - position - 1))

    gain = one(*pieces[0])
    for cut in pieces[1:]:
        gain = gain * one(*cut)
    return gain


def profile(amount, total, limit, skew):
    portions = [(1 << 20) // math.isqrt(standing ** skew) + 1 for standing in range(2, amount + 1)]
    surplus, given = total - limit - (amount - 1), [1] * (amount - 1)
    while surplus > 0:
        movable = [i for i in range(amount - 1) if given[i] < limit]
        pool, left = sum([portions[i] for i in movable]), surplus
        for i in movable:
            addition = min(limit - given[i], max(1, left * portions[i] // pool), surplus)
            given[i] = given[i] + addition
            surplus = surplus - addition
    return np.array([limit] + given)


def uneven(key, count, total, reach, slope):
    if count == 2:
        one = jax.random.randint(key, (), max(1, total - reach), min(reach, total - 1) + 1)
        return jnp.stack([one, total - one])
    sizes = jnp.asarray(profile(count, total, reach, slope), jnp.int32)
    couples = (count - 1) // 2
    source_of, receiver = sizes[1:1 + 2 * couples:2], sizes[2:2 + 2 * couples:2]
    slack = jnp.minimum(source_of - 1, reach - receiver)
    moved = jax.random.randint(jax.random.fold_in(key, 1), (couples,), 0, 1 << 20) % (slack + 1)
    sizes = sizes.at[1:1 + 2 * couples:2].set(source_of - moved).at[2:2 + 2 * couples:2].set(receiver + moved)
    return sizes[jax.random.permutation(jax.random.fold_in(key, 2), count)]


def routed_block(own_key, own, number, rows, amount, top, most, skew):
    sequence = jax.random.permutation(own_key, amount)
    crowded, common = load_shares(amount, rows * top, most, skew, True), load_shares(amount, rows * top, most, skew, False)
    places = jnp.arange(amount)

    def named(lengths, turn):
        used = int((lengths > 0).sum())
        fixed = max(1, used // 4)
        shifted = fixed + (places - fixed + turn * (used - fixed)) % max(1, amount - fixed)
        return jnp.zeros((amount,), jnp.int32).at[sequence[jnp.where(places < fixed, places, shifted)]].set(jnp.asarray(lengths, jnp.int32))

    lengths = jnp.where(number % 4 == 0, named(crowded, number // 4), named(common, number - number // 4 - 1))
    mixed = jax.random.permutation(jax.random.fold_in(own, 3), amount)
    source_of, receiver = mixed[0:amount // 2 * 2:2], mixed[1:amount // 2 * 2:2]
    margin = jnp.minimum(lengths[source_of] - 1, most - lengths[receiver]) // 2
    margin = jnp.where((source_of == sequence[0]) | (receiver == sequence[0]) | (lengths[receiver] == 0), 0, jnp.maximum(margin, 0))
    shifted = jax.random.randint(jax.random.fold_in(own, 4), (amount // 2,), 0, 1 << 20) % (margin + 1)
    lengths = lengths.at[source_of].add(-shifted).at[receiver].add(shifted)
    items = jnp.searchsorted(jnp.cumsum(lengths), jnp.arange(rows * top), side="right").astype(jnp.int32)
    listing = items.reshape(top, rows).T
    listing = listing[jax.random.permutation(jax.random.fold_in(own, 1), rows)]
    turn = jax.random.randint(jax.random.fold_in(own, 2), (rows, 1), 0, top)
    return jnp.take_along_axis(listing, (jnp.arange(top)[None, :] + turn) % top, axis=1)


def load_shares(count, total, reach, slope, full):
    portions = [(1 << 20) // math.isqrt(standing ** slope) + 1 for standing in range(1, count + 1)]
    largest = reach if full else min(reach, max(-(-total // count), total * portions[0] // sum(portions)))
    least = 1 if total - largest >= count - 1 else 0
    given, rest = [largest] + [least] * (count - 1), total - largest - least * (count - 1)
    while rest > 0:
        candidates = [i for i in range(1, count) if given[i] < largest] or [i for i in range(1, count) if given[i] < reach]
        pool, budget = sum([portions[i] for i in candidates]), rest
        for i in candidates:
            extra = min(reach - given[i], max(1, budget * portions[i] // pool), rest)
            given[i] = given[i] + extra
            rest = rest - extra
    return np.array(given)


def bell_draw(stream_key, shape, deviation, limit, pieces=(), held_as=jnp.bfloat16):
    result = jax.random.normal(stream_key, shape, jnp.float32) * deviation
    if len(pieces) > 0:
        result = level_of(stream_key, shape, pieces, -0.22, 0.18) * result
    return jnp.clip(result, min=-limit, max=limit).astype(held_as)


def setup_inputs(seed: int = 0, part: int = 0) -> dict:
    key_of = jax.random.split(jax.random.key(seed), 11)
    own_keys = jax.random.split(jax.random.fold_in(key_of[10], part), 11)
    tokens = bell_draw(own_keys[0], (TOKENS, D), 1.0, 6.0, ((0, 16),))
    cotangent = bell_draw(own_keys[1], (TOKENS, D), 0.05, 0.29882812, ((0, 16),))
    routes_keys = jax.random.split(jax.random.fold_in(own_keys[2], 1), TOKENS // TOK_DEV)
    routes_turns = jax.random.permutation(jax.random.fold_in(own_keys[2], 3), TOKENS // TOK_DEV)
    routes = jax.vmap(lambda own, number: routed_block(jax.random.fold_in(own_keys[2], 2), own, number, TOK_DEV, EXPERTS, TOPK, CAP, 2))(routes_keys, routes_turns).reshape((TOKENS, TOPK))
    combine = jnp.clip(jnp.exp(math.log(0.5) - 2.306499 * jax.random.uniform(own_keys[3], (TOKENS, TOPK), jnp.float32) ** level_of(own_keys[3], (TOKENS, TOPK), ((0, 16),), -0.2, 0.2)), 0.049804688, 0.5).astype(jnp.bfloat16)
    doc_ids = jnp.searchsorted(jnp.cumsum(uneven(own_keys[4], DOCS, TOKENS, DOC_MOST, 1)), jnp.arange(TOKENS), side="right").astype(jnp.int32)
    w_gate = bell_draw(key_of[5], (EXPERTS, D, FF), D ** -0.5, 0.125, ((0, 16),))
    w_up = bell_draw(key_of[6], (EXPERTS, D, FF), D ** -0.5, 0.125, ((0, 16),))
    w_down = bell_draw(key_of[7], (EXPERTS, FF, D), FF ** -0.5, 0.21875, ((0, 16),))
    proj_hidden = bell_draw(key_of[8], (EXPERTS, FF, RANK), FF ** -0.5, 0.21875, ((0, 16),))
    proj_output = bell_draw(key_of[9], (EXPERTS, D, RANK), 1.0, 6.0, ((0, 16),))
    return dict(tokens=tokens, cotangent=cotangent, routes=routes, combine=combine, doc_ids=doc_ids, w_gate=w_gate, w_up=w_up, w_down=w_down, proj_hidden=proj_hidden, proj_output=proj_output)


def reference(tokens, cotangent, routes, combine, doc_ids, w_gate, w_up, w_down, proj_hidden, proj_output):
    flat_routes = routes.reshape(-1).astype(jnp.int32)
    sorted_idx = jnp.argsort(flat_routes, stable=True).astype(jnp.int32)
    counts = jnp.bincount(flat_routes, length=EXPERTS).astype(jnp.int32)
    starts = (jnp.cumsum(counts) - counts).astype(jnp.int32)
    buffer_rows = N_EXP * CAP
    padded = jnp.concatenate([sorted_idx, jnp.zeros((buffer_rows,), jnp.int32)])
    flat_combine = combine.reshape(-1)

    def expert(expert_id):
        begin_at = starts[expert_id]
        entry_idx = lax.dynamic_slice(padded, (begin_at,), (buffer_rows,)).astype(jnp.int32)
        is_live = jnp.arange(buffer_rows, dtype=jnp.int32) < counts[expert_id]
        token_idx = entry_idx // TOPK
        tok_x = tokens[token_idx]
        tok_dy = cotangent[token_idx]
        tok_w = jnp.where(is_live, flat_combine[entry_idx].astype(jnp.float32), jnp.float32(0.0))
        tok_doc = jnp.where(is_live, doc_ids[token_idx], -1)
        gate_val = jnp.dot(tok_x, w_gate[expert_id], preferred_element_type=jnp.float32)
        up_val = jnp.dot(tok_x, w_up[expert_id], preferred_element_type=jnp.float32)
        hidden = (jax.nn.silu(gate_val) * up_val).astype(jnp.bfloat16)
        out_val = jnp.dot(hidden, w_down[expert_id], preferred_element_type=jnp.float32)
        slot_grad = jnp.sum(tok_dy.astype(jnp.float32) * out_val, axis=1)
        low_side = jnp.dot(hidden, proj_hidden[expert_id], preferred_element_type=jnp.float32).astype(jnp.bfloat16)
        proj_cot = jnp.dot(tok_dy, proj_output[expert_id], preferred_element_type=jnp.float32)
        high_side = (tok_w[:, None] * proj_cot).astype(jnp.bfloat16)
        onehot = (tok_doc[:, None] == jnp.arange(DOCS, dtype=jnp.int32)[None, :]).astype(jnp.bfloat16)
        spread = (onehot[:, :, None] * low_side[:, None, :]).reshape(buffer_rows, DOCS * RANK)
        feature = lax.dot_general(spread, high_side, (((0,), (0,)), ((), ())), preferred_element_type=jnp.float32)
        where_to = jnp.where(is_live, entry_idx, TOKENS * TOPK).astype(jnp.int32)
        return feature.reshape(DOCS, RANK, RANK), slot_grad, where_to

    feats, grads, where_to = lax.map(expert, jnp.arange(EXPERTS, dtype=jnp.int32))
    route_grad = jnp.zeros((TOKENS * TOPK,), jnp.float32).at[where_to.reshape(-1)].set(grads.reshape(-1), mode="drop")
    features = jnp.transpose(feats, (1, 0, 2, 3))
    return features, route_grad.reshape(TOKENS, TOPK)
```

```python
import jax
import jax.numpy as jnp
from jax import lax
from jax.sharding import PartitionSpec as P

DOC_TOK = 512


def swiglu(rows, w_gate, w_up):
    gate_val = jnp.dot(rows, w_gate, preferred_element_type=jnp.float32)
    up_val = jnp.dot(rows, w_up, preferred_element_type=jnp.float32)
    return (jax.nn.silu(gate_val) * up_val).astype(jnp.bfloat16)


def finish(hidden, rows_dy, rows_w, rows_doc, w_down, proj_hidden, proj_output, docs_count):
    out_val = jnp.dot(hidden, w_down, preferred_element_type=jnp.float32)
    grad = jnp.sum(rows_dy.astype(jnp.float32) * out_val, axis=-1)
    low_side = jnp.dot(hidden, proj_hidden, preferred_element_type=jnp.float32).astype(
        jnp.bfloat16
    )
    proj_cot = jnp.dot(rows_dy, proj_output, preferred_element_type=jnp.float32)
    high_side = (rows_w.astype(jnp.float32)[:, None] * proj_cot).astype(jnp.bfloat16)
    doc_table = jnp.arange(docs_count, dtype=jnp.int32).astype(jnp.bfloat16)
    onehot = (rows_doc[:, None] == doc_table).astype(jnp.bfloat16)
    spread = onehot[:, :, None] * low_side[:, None, :]
    spread = spread.reshape(spread.shape[0], -1)
    feature = lax.dot_general(
        spread, high_side, (((0,), (0,)), ((), ())), preferred_element_type=jnp.float32
    )
    return grad, feature.reshape(docs_count, low_side.shape[1], high_side.shape[1])


def pick_own(returned, routes):
    experts = returned.shape[0]
    table = jnp.arange(experts, dtype=jnp.int32)
    hit = routes[:, :, None] == table
    return jnp.sum(jnp.where(hit, returned.T[:, None, :], 0.0), axis=-1)


def by_gather(
    tokens, cotangent, routes, combine, doc_ids, w_gate, w_up, w_down, proj_hidden, proj_output
):
    tok_rows, chosen = routes.shape
    groups = lax.axis_size("exp")
    docs_count = max(2, tok_rows * groups // DOC_TOK)
    me = lax.axis_index("exp")
    table = jnp.arange(groups, dtype=jnp.int32)
    weight = jnp.sum(
        jnp.where(routes[None, :, :] == table[:, None, None], combine[None, :, :], 0), axis=-1
    ).astype(jnp.bfloat16)
    meta = jnp.concatenate([weight, doc_ids.astype(jnp.bfloat16)[None, :]], axis=0)
    all_meta = lax.all_gather(meta, "exp")
    all_x = lax.all_gather(tokens, "exp", tiled=True)
    all_dy = lax.all_gather(cotangent, "exp", tiled=True)
    all_w = lax.dynamic_index_in_dim(all_meta, me, axis=1, keepdims=False).reshape(-1)
    all_doc = all_meta[:, groups, :].reshape(-1)
    hidden = swiglu(all_x, w_gate[0], w_up[0])
    grad, feature = finish(
        hidden, all_dy, all_w, all_doc, w_down[0], proj_hidden[0], proj_output[0], docs_count
    )
    returned = lax.all_to_all(
        grad.reshape(groups, tok_rows), "exp", split_axis=0, concat_axis=0, tiled=True
    )
    return feature[:, None], pick_own(returned, routes)


def by_routing(
    tokens, cotangent, routes, combine, doc_ids, w_gate, w_up, w_down, proj_hidden, proj_output
):
    tok_rows, chosen = routes.shape
    local_count = w_gate.shape[0]
    groups = lax.axis_size("exp")
    experts = local_count * groups
    capacity = max(2, tok_rows * chosen * 5 // (4 * experts))
    docs_count = max(2, tok_rows * groups // DOC_TOK)
    entries = tok_rows * chosen
    width = tokens.shape[1]
    flat_routes = routes.reshape(-1)
    member = (flat_routes[:, None] == jnp.arange(experts, dtype=jnp.int32)[None, :]).astype(
        jnp.int32
    )
    slot_rank = jnp.sum((jnp.cumsum(member, axis=0) - 1) * member, axis=1)
    position = flat_routes * capacity + slot_rank
    source = (
        jnp.full((experts * capacity,), -1, jnp.int32)
        .at[position]
        .set(jnp.arange(entries, dtype=jnp.int32))
    )
    filled = source >= 0
    safe_source = jnp.maximum(source, 0)
    token_of = safe_source // chosen
    send_x = jnp.where(filled[:, None], tokens[token_of], 0)
    send_dy = jnp.where(filled[:, None], cotangent[token_of], 0)
    send_w = jnp.where(filled, combine.reshape(-1)[safe_source], 0)
    send_doc = jnp.where(filled, doc_ids[token_of], -1).astype(jnp.bfloat16)

    def exchange(array):
        array = array.reshape((groups, local_count, capacity) + array.shape[1:])
        return lax.all_to_all(array, "exp", split_axis=0, concat_axis=0, tiled=True)

    recv_x, recv_dy, recv_w, recv_doc = (
        exchange(send_x),
        exchange(send_dy),
        exchange(send_w),
        exchange(send_doc),
    )
    slots = groups * capacity
    grads, feats = [], []
    for e in range(local_count):
        hidden = swiglu(recv_x[:, e].reshape(slots, width), w_gate[e], w_up[e])
        grad, feature = finish(
            hidden,
            recv_dy[:, e].reshape(slots, width),
            recv_w[:, e].reshape(slots),
            recv_doc[:, e].reshape(slots),
            w_down[e],
            proj_hidden[e],
            proj_output[e],
            docs_count,
        )
        grads.append(grad.reshape(groups, capacity))
        feats.append(feature)
    slot_grad = jnp.stack(grads, axis=1)
    returned = lax.all_to_all(slot_grad, "exp", split_axis=0, concat_axis=0, tiled=True)
    route_grad = returned.reshape(-1)[position].reshape(tok_rows, chosen)
    return jnp.stack(feats, axis=1), route_grad


def on_device(tokens, cotangent, routes, combine, doc_ids, w_gate, *rest):
    tok_rows, chosen = routes.shape
    experts = w_gate.shape[0] * lax.axis_size("exp")
    dense = w_gate.shape[0] == 1 and 4 * chosen >= experts
    plan = by_gather if dense else by_routing
    return plan(tokens, cotangent, routes, combine, doc_ids, w_gate, *rest)


def solution(mesh):
    placed = (
        P(("grp", "exp"), None),
        P(("grp", "exp"), None),
        P(("grp", "exp"), None),
        P(("grp", "exp"), None),
        P(("grp", "exp")),
        P("exp", None, None),
        P("exp", None, None),
        P("exp", None, None),
        P("exp", None, None),
        P("exp", None, None),
    )
    return jax.shard_map(
        on_device,
        mesh=mesh,
        in_specs=placed,
        out_specs=(P("grp", "exp", None, None), P(("grp", "exp"), None)),
        check_vma=False,
    )
```

```python
import jax
import jax.numpy as jnp
import numpy as np
from jax import lax
from jax.sharding import PartitionSpec as P

DOC_TOK = 512


def swiglu(rows, w_gate, w_up):
    gate_val = jnp.dot(rows, w_gate, preferred_element_type=jnp.float32)
    up_val = jnp.dot(rows, w_up, preferred_element_type=jnp.float32)
    return (jax.nn.silu(gate_val) * up_val).astype(jnp.bfloat16)


def finish(hidden, rows_dy, rows_w, rows_doc, w_down, proj_hidden, proj_output, docs_count):
    out_val = jnp.dot(hidden, w_down, preferred_element_type=jnp.float32)
    grad = jnp.sum(rows_dy.astype(jnp.float32) * out_val, axis=-1)
    low_side = jnp.dot(hidden, proj_hidden, preferred_element_type=jnp.float32).astype(
        jnp.bfloat16
    )
    proj_cot = jnp.dot(rows_dy, proj_output, preferred_element_type=jnp.float32)
    high_side = (rows_w.astype(jnp.float32)[:, None] * proj_cot).astype(jnp.bfloat16)
    doc_table = jnp.arange(docs_count, dtype=jnp.int32).astype(jnp.bfloat16)
    onehot = (rows_doc[:, None] == doc_table).astype(jnp.bfloat16)
    spread = onehot[:, :, None] * low_side[:, None, :]
    spread = spread.reshape(spread.shape[0], -1)
    feature = lax.dot_general(
        spread, high_side, (((0,), (0,)), ((), ())), preferred_element_type=jnp.float32
    )
    return grad, feature.reshape(docs_count, low_side.shape[1], high_side.shape[1])


def pick_own(returned, routes):
    experts = returned.shape[0]
    table = jnp.arange(experts, dtype=jnp.int32)
    hit = routes[:, :, None] == table
    return jnp.sum(jnp.where(hit, returned.T[:, None, :], 0.0), axis=-1)


def by_ring(
    tokens, cotangent, routes, combine, doc_ids, w_gate, w_up, w_down, proj_hidden, proj_output
):
    tok_rows, chosen = routes.shape
    groups = lax.axis_size("exp")
    docs_count = max(2, tok_rows * groups // DOC_TOK)
    chips = groups // 2
    half = chips // 2
    ring = list(range(0, chips, 2)) + list(range(chips - 1, 0, -2))
    onward = []
    for place in range(chips):
        onward.append((2 * ring[place], 2 * ring[(place + 1) % chips]))
        onward.append((2 * ring[place] + 1, 2 * ring[place - 1] + 1))
    across = [(i, i ^ 1) for i in range(groups)]

    def hop(block):
        return lax.ppermute(block, "exp", onward)

    def swap(block):
        return lax.ppermute(block, "exp", across)

    orders = np.zeros((groups, groups), np.int32)
    for place in range(chips):
        for core in range(2):
            way = 1 - 2 * core

            def owner(steps, which):
                return 2 * ring[(place + steps) % chips] + which

            order = [owner(0, core), owner(0, 1 - core)]
            for step in range(1, half + 1):
                near, far = -step * way, step * way
                if step < half:
                    order += [owner(near, core), owner(near, 1 - core)]
                    order += [owner(far, 1 - core), owner(far, core)]
                else:
                    order += [owner(near, core), owner(far, 1 - core)]
            orders[owner(0, core)] = order
    me = lax.axis_index("exp")
    mine = lax.dynamic_index_in_dim(jnp.asarray(orders), me, axis=0, keepdims=False)
    owned = mine[:, None] == jnp.arange(groups, dtype=jnp.int32)

    table = jnp.arange(groups, dtype=jnp.int32)
    weight = jnp.sum(
        jnp.where(routes[None, :, :] == table[:, None, None], combine[None, :, :], 0), axis=-1
    ).astype(jnp.bfloat16)
    own_doc = jnp.broadcast_to(doc_ids.astype(jnp.bfloat16)[None, :], weight.shape)
    meta = lax.all_to_all(
        jnp.stack([weight, own_doc], axis=1), "exp", split_axis=0, concat_axis=0, tiled=True
    )
    meta = jnp.sum(
        jnp.where(owned[:, :, None, None], meta[None].astype(jnp.float32), 0.0), axis=1
    ).astype(jnp.bfloat16)

    sets = [[(tokens, cotangent)]]
    last = [(tokens, cotangent)]
    beside = tuple(swap(block) for block in last[0])
    sets[0].append(beside)
    last.append(beside)
    for step in range(1, half + 1):
        if step == half:
            last = last[:1]
        x_in = [hop(pair[0]) for pair in last]
        dy_in = [hop(pair[1]) for pair in last]
        last = list(zip(x_in, dy_in))
        sets.append(last + [(swap(pair[0]), swap(pair[1])) for pair in last])

    grads, feature, begin = [], 0.0, 0
    for blocks in sets:
        x = jnp.concatenate([pair[0] for pair in blocks], axis=0)
        dy = jnp.concatenate([pair[1] for pair in blocks], axis=0)
        part = meta[begin : begin + len(blocks)]
        begin += len(blocks)
        hidden = swiglu(x, w_gate[0], w_up[0])
        grad, term = finish(
            hidden,
            dy,
            part[:, 0].reshape(-1),
            part[:, 1].reshape(-1),
            w_down[0],
            proj_hidden[0],
            proj_output[0],
            docs_count,
        )
        grads.append(grad.reshape(len(blocks), tok_rows))
        feature = feature + term
    grads = jnp.concatenate(grads, axis=0)
    grads = jnp.sum(jnp.where(owned[:, :, None], grads[:, None, :], 0.0), axis=0)
    returned = lax.all_to_all(grads, "exp", split_axis=0, concat_axis=0, tiled=True)
    return feature[:, None], pick_own(returned, routes)


def by_routing(
    tokens, cotangent, routes, combine, doc_ids, w_gate, w_up, w_down, proj_hidden, proj_output
):
    tok_rows, chosen = routes.shape
    local_count = w_gate.shape[0]
    groups = lax.axis_size("exp")
    experts = local_count * groups
    capacity = max(2, tok_rows * chosen * 5 // (4 * experts))
    docs_count = max(2, tok_rows * groups // DOC_TOK)
    entries = tok_rows * chosen
    width = tokens.shape[1]
    flat_routes = routes.reshape(-1)
    member = (flat_routes[:, None] == jnp.arange(experts, dtype=jnp.int32)[None, :]).astype(
        jnp.int32
    )
    slot_rank = jnp.sum((jnp.cumsum(member, axis=0) - 1) * member, axis=1)
    position = flat_routes * capacity + slot_rank
    source = (
        jnp.full((experts * capacity,), -1, jnp.int32)
        .at[position]
        .set(jnp.arange(entries, dtype=jnp.int32))
    )
    filled = source >= 0
    safe_source = jnp.maximum(source, 0)
    token_of = safe_source // chosen
    send_x = jnp.where(filled[:, None], tokens[token_of], 0)
    send_dy = jnp.where(filled[:, None], cotangent[token_of], 0)
    send_w = jnp.where(filled, combine.reshape(-1)[safe_source], 0)
    send_doc = jnp.where(filled, doc_ids[token_of], -1).astype(jnp.bfloat16)

    def exchange(array):
        array = array.reshape((groups, local_count, capacity) + array.shape[1:])
        return lax.all_to_all(array, "exp", split_axis=0, concat_axis=0, tiled=True)

    recv_x, recv_dy, recv_w, recv_doc = (
        exchange(send_x),
        exchange(send_dy),
        exchange(send_w),
        exchange(send_doc),
    )
    slots = groups * capacity
    grads, feats = [], []
    for e in range(local_count):
        hidden = swiglu(recv_x[:, e].reshape(slots, width), w_gate[e], w_up[e])
        grad, feature = finish(
            hidden,
            recv_dy[:, e].reshape(slots, width),
            recv_w[:, e].reshape(slots),
            recv_doc[:, e].reshape(slots),
            w_down[e],
            proj_hidden[e],
            proj_output[e],
            docs_count,
        )
        grads.append(grad.reshape(groups, capacity))
        feats.append(feature)
    slot_grad = jnp.stack(grads, axis=1)
    returned = lax.all_to_all(slot_grad, "exp", split_axis=0, concat_axis=0, tiled=True)
    route_grad = returned.reshape(-1)[position].reshape(tok_rows, chosen)
    return jnp.stack(feats, axis=1), route_grad


def on_device(tokens, cotangent, routes, combine, doc_ids, w_gate, *rest):
    tok_rows, chosen = routes.shape
    experts = w_gate.shape[0] * lax.axis_size("exp")
    dense = w_gate.shape[0] == 1 and 4 * chosen >= experts and experts % 4 == 0
    plan = by_ring if dense else by_routing
    return plan(tokens, cotangent, routes, combine, doc_ids, w_gate, *rest)


def solution(mesh):
    placed = (
        P(("grp", "exp"), None),
        P(("grp", "exp"), None),
        P(("grp", "exp"), None),
        P(("grp", "exp"), None),
        P(("grp", "exp")),
        P("exp", None, None),
        P("exp", None, None),
        P("exp", None, None),
        P("exp", None, None),
        P("exp", None, None),
    )
    return jax.shard_map(
        on_device,
        mesh=mesh,
        in_specs=placed,
        out_specs=(P("grp", "exp", None, None), P(("grp", "exp"), None)),
        check_vma=False,
    )
```

```python
import jax
import jax.numpy as jnp
import numpy as np
from jax import lax
from jax.sharding import PartitionSpec as P

DOC_TOK = 512


def swiglu(rows, w_gate, w_up):
    gate_val = jnp.dot(rows, w_gate, preferred_element_type=jnp.float32)
    up_val = jnp.dot(rows, w_up, preferred_element_type=jnp.float32)
    return (jax.nn.silu(gate_val) * up_val).astype(jnp.bfloat16)


def finish(hidden, rows_dy, rows_w, rows_doc, w_down, proj_hidden, proj_output, docs_count):
    out_val = jnp.dot(hidden, w_down, preferred_element_type=jnp.float32)
    grad = jnp.sum(rows_dy.astype(jnp.float32) * out_val, axis=-1)
    low_side = jnp.dot(hidden, proj_hidden, preferred_element_type=jnp.float32).astype(
        jnp.bfloat16
    )
    proj_cot = jnp.dot(rows_dy, proj_output, preferred_element_type=jnp.float32)
    high_side = (rows_w.astype(jnp.float32)[:, None] * proj_cot).astype(jnp.bfloat16)
    doc_table = jnp.arange(docs_count, dtype=jnp.int32).astype(jnp.bfloat16)
    onehot = (rows_doc[:, None] == doc_table).astype(jnp.bfloat16)
    spread = onehot[:, :, None] * low_side[:, None, :]
    spread = spread.reshape(spread.shape[0], -1)
    feature = lax.dot_general(
        spread, high_side, (((0,), (0,)), ((), ())), preferred_element_type=jnp.float32
    )
    return grad, feature.reshape(docs_count, low_side.shape[1], high_side.shape[1])


def pick_own(returned, routes):
    experts = returned.shape[0]
    table = jnp.arange(experts, dtype=jnp.int32)
    hit = routes[:, :, None] == table
    return jnp.sum(jnp.where(hit, returned.T[:, None, :], 0.0), axis=-1)


def by_ring(
    tokens, cotangent, routes, combine, doc_ids, w_gate, w_up, w_down, proj_hidden, proj_output
):
    tok_rows, chosen = routes.shape
    groups = lax.axis_size("exp")
    docs_count = max(2, tok_rows * groups // DOC_TOK)
    chips = groups // 2
    half = chips // 2
    ring = list(range(0, chips, 2)) + list(range(chips - 1, 0, -2))
    onward = []
    for place in range(chips):
        onward.append((2 * ring[place], 2 * ring[(place + 1) % chips]))
        onward.append((2 * ring[place] + 1, 2 * ring[place - 1] + 1))
    across = [(i, i ^ 1) for i in range(groups)]

    def hop(block):
        return lax.ppermute(block, "exp", onward)

    def swap(block):
        return lax.ppermute(block, "exp", across)

    orders = np.zeros((groups, groups), np.int32)
    for place in range(chips):
        for core in range(2):
            way = 1 - 2 * core

            def owner(steps, which):
                return 2 * ring[(place + steps) % chips] + which

            order = [owner(0, core), owner(0, 1 - core)]
            for step in range(1, half + 1):
                near, far = -step * way, step * way
                if step < half:
                    order += [owner(near, core), owner(near, 1 - core)]
                    order += [owner(far, 1 - core), owner(far, core)]
                else:
                    order += [owner(near, core), owner(far, 1 - core)]
            orders[owner(0, core)] = order
    me = lax.axis_index("exp")
    mine = lax.dynamic_index_in_dim(jnp.asarray(orders), me, axis=0, keepdims=False)
    owned = mine[:, None] == jnp.arange(groups, dtype=jnp.int32)

    table = jnp.arange(groups, dtype=jnp.int32)
    weight = jnp.sum(
        jnp.where(routes[None, :, :] == table[:, None, None], combine[None, :, :], 0), axis=-1
    ).astype(jnp.bfloat16)
    own_doc = jnp.broadcast_to(doc_ids.astype(jnp.bfloat16)[None, :], weight.shape)
    meta = lax.all_to_all(
        jnp.stack([weight, own_doc], axis=1), "exp", split_axis=0, concat_axis=0, tiled=True
    )
    meta = jnp.sum(
        jnp.where(owned[:, :, None, None], meta[None].astype(jnp.float32), 0.0), axis=1
    ).astype(jnp.bfloat16)

    x, dy = tokens, cotangent
    x_beside, dy_beside = swap(x), swap(dy)
    sets = [(jnp.concatenate([x, x_beside]), jnp.concatenate([dy, dy_beside]))]
    x = jnp.concatenate([hop(x), hop(x_beside)])
    dy = jnp.concatenate([hop(dy), hop(dy_beside)])
    for step in range(1, half):
        sets += [(x, dy), (swap(x), swap(dy))]
        if step < half - 1:
            x, dy = hop(x), hop(dy)
    x, dy = hop(x[:tok_rows]), hop(dy[:tok_rows])
    sets.append((jnp.concatenate([x, swap(x)]), jnp.concatenate([dy, swap(dy)])))

    grads, feature = [], 0.0
    for begin, (x, dy) in enumerate(sets):
        part = meta[2 * begin : 2 * begin + 2]
        hidden = swiglu(x, w_gate[0], w_up[0])
        grad, term = finish(
            hidden,
            dy,
            part[:, 0].reshape(-1),
            part[:, 1].reshape(-1),
            w_down[0],
            proj_hidden[0],
            proj_output[0],
            docs_count,
        )
        grads.append(grad.reshape(2, tok_rows))
        feature = feature + term
    grads = jnp.concatenate(grads, axis=0)
    grads = jnp.sum(jnp.where(owned[:, :, None], grads[:, None, :], 0.0), axis=0)
    returned = lax.all_to_all(grads, "exp", split_axis=0, concat_axis=0, tiled=True)
    return feature[:, None], pick_own(returned, routes)


def by_routing(
    tokens, cotangent, routes, combine, doc_ids, w_gate, w_up, w_down, proj_hidden, proj_output
):
    tok_rows, chosen = routes.shape
    local_count = w_gate.shape[0]
    groups = lax.axis_size("exp")
    experts = local_count * groups
    capacity = max(2, tok_rows * chosen * 5 // (4 * experts))
    docs_count = max(2, tok_rows * groups // DOC_TOK)
    entries = tok_rows * chosen
    width = tokens.shape[1]
    flat_routes = routes.reshape(-1)
    member = (flat_routes[:, None] == jnp.arange(experts, dtype=jnp.int32)[None, :]).astype(
        jnp.int32
    )
    slot_rank = jnp.sum((jnp.cumsum(member, axis=0) - 1) * member, axis=1)
    position = flat_routes * capacity + slot_rank
    source = (
        jnp.full((experts * capacity,), -1, jnp.int32)
        .at[position]
        .set(jnp.arange(entries, dtype=jnp.int32))
    )
    filled = source >= 0
    safe_source = jnp.maximum(source, 0)
    token_of = safe_source // chosen
    send_x = jnp.where(filled[:, None], tokens[token_of], 0)
    send_dy = jnp.where(filled[:, None], cotangent[token_of], 0)
    send_w = jnp.where(filled, combine.reshape(-1)[safe_source], 0)
    send_doc = jnp.where(filled, doc_ids[token_of], -1).astype(jnp.bfloat16)

    def exchange(array):
        array = array.reshape((groups, local_count, capacity) + array.shape[1:])
        return lax.all_to_all(array, "exp", split_axis=0, concat_axis=0, tiled=True)

    recv_x, recv_dy, recv_w, recv_doc = (
        exchange(send_x),
        exchange(send_dy),
        exchange(send_w),
        exchange(send_doc),
    )
    slots = groups * capacity
    grads, feats = [], []
    for e in range(local_count):
        hidden = swiglu(recv_x[:, e].reshape(slots, width), w_gate[e], w_up[e])
        grad, feature = finish(
            hidden,
            recv_dy[:, e].reshape(slots, width),
            recv_w[:, e].reshape(slots),
            recv_doc[:, e].reshape(slots),
            w_down[e],
            proj_hidden[e],
            proj_output[e],
            docs_count,
        )
        grads.append(grad.reshape(groups, capacity))
        feats.append(feature)
    slot_grad = jnp.stack(grads, axis=1)
    returned = lax.all_to_all(slot_grad, "exp", split_axis=0, concat_axis=0, tiled=True)
    route_grad = returned.reshape(-1)[position].reshape(tok_rows, chosen)
    return jnp.stack(feats, axis=1), route_grad


def on_device(tokens, cotangent, routes, combine, doc_ids, w_gate, *rest):
    tok_rows, chosen = routes.shape
    experts = w_gate.shape[0] * lax.axis_size("exp")
    dense = w_gate.shape[0] == 1 and 4 * chosen >= experts and experts % 4 == 0
    plan = by_ring if dense else by_routing
    return plan(tokens, cotangent, routes, combine, doc_ids, w_gate, *rest)


def solution(mesh):
    placed = (
        P(("grp", "exp"), None),
        P(("grp", "exp"), None),
        P(("grp", "exp"), None),
        P(("grp", "exp"), None),
        P(("grp", "exp")),
        P("exp", None, None),
        P("exp", None, None),
        P("exp", None, None),
        P("exp", None, None),
        P("exp", None, None),
    )
    return jax.shard_map(
        on_device,
        mesh=mesh,
        in_specs=placed,
        out_specs=(P("grp", "exp", None, None), P(("grp", "exp"), None)),
        check_vma=False,
    )
```

```python
import functools

import jax
import jax.numpy as jnp
import numpy as np
from jax import lax
from jax.experimental import pallas as pl
from jax.experimental.pallas import tpu as pltpu
from jax.sharding import PartitionSpec as P

DOC_TOK = 512


def swiglu(rows, w_gate, w_up):
    gate_val = jnp.dot(rows, w_gate, preferred_element_type=jnp.float32)
    up_val = jnp.dot(rows, w_up, preferred_element_type=jnp.float32)
    return (jax.nn.silu(gate_val) * up_val).astype(jnp.bfloat16)


def finish(hidden, rows_dy, rows_w, rows_doc, w_down, proj_hidden, proj_output, docs_count):
    out_val = jnp.dot(hidden, w_down, preferred_element_type=jnp.float32)
    grad = jnp.sum(rows_dy.astype(jnp.float32) * out_val, axis=-1)
    low_side = jnp.dot(hidden, proj_hidden, preferred_element_type=jnp.float32).astype(
        jnp.bfloat16
    )
    proj_cot = jnp.dot(rows_dy, proj_output, preferred_element_type=jnp.float32)
    high_side = (rows_w.astype(jnp.float32)[:, None] * proj_cot).astype(jnp.bfloat16)
    doc_table = jnp.arange(docs_count, dtype=jnp.int32).astype(jnp.bfloat16)
    onehot = (rows_doc[:, None] == doc_table).astype(jnp.bfloat16)
    spread = onehot[:, :, None] * low_side[:, None, :]
    spread = spread.reshape(spread.shape[0], -1)
    feature = lax.dot_general(
        spread, high_side, (((0,), (0,)), ((), ())), preferred_element_type=jnp.float32
    )
    return grad, feature.reshape(docs_count, low_side.shape[1], high_side.shape[1])


def pick_own(returned, routes):
    experts = returned.shape[0]
    table = jnp.arange(experts, dtype=jnp.int32)
    hit = routes[:, :, None] == table
    return jnp.sum(jnp.where(hit, returned.T[:, None, :], 0.0), axis=-1)


def rows_kernel(blocks, begin, first, *refs):
    order, meta = refs[:2]
    x_in, dy_in = refs[2 : 2 + blocks], refs[2 + blocks : 2 + 2 * blocks]
    w_gate, w_up, w_down, low_proj, high_proj = refs[2 + 2 * blocks : 7 + 2 * blocks]
    grads, feat, x_all, dy_all, low_sum, grad_sum, sems = refs[-7:]
    tile = pl.program_id(0)
    rows = x_in[0].shape[0]
    across = (((1,), (1,)), ((), ()))

    @pl.when(tile == 0)
    def _():
        copies = []
        for i in range(blocks):
            place = pl.ds(i * rows, rows)
            copies.append(pltpu.make_async_copy(x_in[i], x_all.at[place], sems.at[2 * i]))
            copies.append(pltpu.make_async_copy(dy_in[i], dy_all.at[place], sems.at[2 * i + 1]))
        for copy in copies:
            copy.start()
        low_sum[...] = jnp.zeros_like(low_sum)
        grad_sum[...] = jnp.zeros_like(grad_sum)
        if first:
            grads[...] = jnp.zeros_like(grads)
            feat[...] = jnp.zeros_like(feat)
        else:
            grads_in, feat_in = refs[7 + 2 * blocks : 9 + 2 * blocks]
            grads[...] = grads_in[...]
            feat[...] = feat_in[...]
        for copy in copies:
            copy.wait()

    gate_val = jnp.dot(x_all[...], w_gate[...], preferred_element_type=jnp.float32)
    up_val = jnp.dot(x_all[...], w_up[...], preferred_element_type=jnp.float32)
    hidden = (jax.nn.silu(gate_val) * up_val).astype(jnp.bfloat16)
    back = lax.dot_general(dy_all[...], w_down[...], across, preferred_element_type=jnp.float32)
    terms = hidden.astype(jnp.float32) * back
    lanes = grad_sum.shape[1]
    for cut in range(0, terms.shape[1], lanes):
        grad_sum[...] += terms[:, cut : cut + lanes]
    low_sum[...] += lax.dot_general(
        hidden, low_proj[...], across, preferred_element_type=jnp.float32
    )

    @pl.when(tile == pl.num_programs(0) - 1)
    def _():
        proj_cot = lax.dot_general(
            dy_all[...], high_proj[...], across, preferred_element_type=jnp.float32
        )
        rank = proj_cot.shape[1]
        width = low_sum.shape[1]
        doc_of = lax.broadcasted_iota(jnp.int32, (rows, width), 1) // rank
        spread, high_side = [], []
        for i in range(blocks):
            place = slice(i * rows, (i + 1) * rows)
            owner = order[begin + i]
            facts = meta[pl.ds(owner, 1), :]
            weight = jnp.transpose(jnp.broadcast_to(facts[:, :rows], (rows, rows)))
            doc = jnp.transpose(jnp.broadcast_to(facts[:, rows:], (rows, rows)))
            doc = jnp.concatenate([doc] * (width // rows), axis=1).astype(jnp.int32)
            high_side.append((weight[:, :rank] * proj_cot[place]).astype(jnp.bfloat16))
            low_side = jnp.where(doc == doc_of, low_sum[place, :], 0.0)
            spread.append(low_side.astype(jnp.bfloat16))
            grads[pl.ds(owner, 1), :] = jnp.sum(
                jnp.transpose(grad_sum[place, :]), axis=0, keepdims=True
            )
        feat[...] += lax.dot_general(
            jnp.concatenate(spread, axis=0),
            jnp.concatenate(high_side, axis=0),
            (((0,), (0,)), ((), ())),
            preferred_element_type=jnp.float32,
        )


def work(begin, order, meta, x_in, dy_in, weights, sums, after):
    w_gate, w_up, w_down, low_proj, high_proj = weights
    blocks = len(x_in)
    rows, width = x_in[0].shape
    hidden = w_gate.shape[2]
    tile = 256 if hidden % 256 == 0 else hidden
    groups = order.shape[0]
    low_width, rank = low_proj.shape[0], high_proj.shape[0]
    anywhere = pl.BlockSpec(memory_space=pl.ANY)

    def whole(shape):
        return pl.BlockSpec(shape, lambda j: (0,) * len(shape))

    sum_shapes = ((groups, rows), (low_width, rank))
    call = pl.pallas_call(
        functools.partial(rows_kernel, blocks, begin, not sums),
        grid=(hidden // tile,),
        out_shape=[jax.ShapeDtypeStruct(shape, jnp.float32) for shape in sum_shapes],
        in_specs=[pl.BlockSpec(memory_space=pltpu.SMEM), whole(meta.shape)]
        + [anywhere] * (2 * blocks)
        + [
            pl.BlockSpec((None, width, tile), lambda j: (0, 0, j)),
            pl.BlockSpec((None, width, tile), lambda j: (0, 0, j)),
            pl.BlockSpec((None, tile, width), lambda j: (0, j, 0)),
            pl.BlockSpec((low_width, tile), lambda j: (0, j)),
            whole(high_proj.shape),
        ]
        + [whole(shape) for shape in sum_shapes[: len(sums)]]
        + [anywhere] * len(after),
        out_specs=[whole(shape) for shape in sum_shapes],
        scratch_shapes=[
            pltpu.VMEM((blocks * rows, width), jnp.bfloat16),
            pltpu.VMEM((blocks * rows, width), jnp.bfloat16),
            pltpu.VMEM((blocks * rows, low_width), jnp.float32),
            pltpu.VMEM((blocks * rows, 128), jnp.float32),
            pltpu.SemaphoreType.DMA((2 * blocks,)),
        ],
        compiler_params=pltpu.CompilerParams(vmem_limit_bytes=60 * 1024 * 1024),
        cost_estimate=pl.CostEstimate(
            flops=6 * blocks * rows * width * hidden,
            bytes_accessed=6 * width * hidden + 4 * blocks * rows * width,
            transcendentals=blocks * rows * hidden,
        ),
    )
    return call(order, meta, *x_in, *dy_in, *weights, *sums, *after)


def facts_kernel(routes, combine, doc_ids, after, out):
    groups, rows = out.shape[0], routes.shape[1]
    expert = lax.broadcasted_iota(jnp.int32, (groups, rows), 0)
    weight = jnp.zeros((groups, rows), jnp.float32)
    for k in range(routes.shape[0]):
        share = combine[k : k + 1, :].astype(jnp.float32)
        weight += jnp.where(routes[k : k + 1, :] == expert, share, 0.0)
    out[:, :rows] = weight.astype(out.dtype)
    doc = jnp.broadcast_to(doc_ids[...], (groups, rows)).astype(jnp.float32)
    out[:, rows:] = doc.astype(out.dtype)


def by_ring(
    tokens, cotangent, routes, combine, doc_ids, w_gate, w_up, w_down, proj_hidden, proj_output
):
    tok_rows, chosen = routes.shape
    groups = lax.axis_size("exp")
    docs_count = max(2, tok_rows * groups // DOC_TOK)
    chips = groups // 2
    half = chips // 2
    ring = list(range(0, chips, 2)) + list(range(chips - 1, 0, -2))
    onward = []
    for place in range(chips):
        onward.append((2 * ring[place], 2 * ring[(place + 1) % chips]))
        onward.append((2 * ring[place] + 1, 2 * ring[place - 1] + 1))
    across = [(i, i ^ 1) for i in range(groups)]

    def hop(block):
        return lax.ppermute(block, "exp", onward)

    def swap(block):
        return lax.ppermute(block, "exp", across)

    orders = np.zeros((groups, groups), np.int32)
    for place in range(chips):
        for core in range(2):
            way = 1 - 2 * core

            def owner(steps, which):
                return 2 * ring[(place + steps) % chips] + which

            order = [owner(0, core), owner(0, 1 - core)]
            for step in range(1, half + 1):
                near, far = -step * way, step * way
                order += [owner(near, core), owner(far, 1 - core)]
                if step < half:
                    order += [owner(near, 1 - core), owner(far, core)]
            orders[owner(0, core)] = order
    me = lax.axis_index("exp")
    order = lax.dynamic_index_in_dim(jnp.asarray(orders), me, axis=0, keepdims=False)

    own = (tokens, cotangent)
    beside = (swap(tokens), swap(cotangent))
    near = [(own, beside)]
    far = []
    for step in range(1, half + 1):
        pairs = near[-1] if step < half else near[-1][:1]
        arrived = tuple((hop(x), hop(dy)) for x, dy in pairs)
        near.append(arrived)
        far.append(tuple((swap(x), swap(dy)) for x, dy in arrived))

    facts = pl.pallas_call(
        facts_kernel,
        out_shape=jax.ShapeDtypeStruct((groups, 2 * tok_rows), jnp.bfloat16),
        in_specs=[pl.BlockSpec(memory_space=pltpu.VMEM)] * 3
        + [pl.BlockSpec(memory_space=pl.ANY)],
        out_specs=pl.BlockSpec(memory_space=pltpu.VMEM),
    )(routes.T, combine.T, doc_ids[None, :], beside[0])
    meta = lax.all_to_all(facts, "exp", split_axis=0, concat_axis=0, tiled=True)
    meta = meta.astype(jnp.float32)

    low_proj = jnp.concatenate([proj_hidden[0].T] * docs_count, axis=0)
    weights = (w_gate, w_up, w_down, low_proj, proj_output[0].T)
    jobs = [((own, beside), near[1][0][1])]
    for step in range(1, half + 1):
        for side in range(len(near[step])):
            if step == half:
                after = None
            elif side == 0:
                after = near[step][1][1]
            else:
                after = near[step + 1][0][1 if step + 1 < half else 0]
            jobs.append(((near[step][side], far[step - 1][side]), after))
    sums = []
    for i, (pair, after) in enumerate(jobs):
        sums = work(
            2 * i,
            order,
            meta,
            [block[0] for block in pair],
            [block[1] for block in pair],
            weights,
            sums,
            [] if after is None else [after],
        )
    grads, feature = sums
    returned = lax.all_to_all(grads, "exp", split_axis=0, concat_axis=0, tiled=True)
    rank = proj_output.shape[2]
    return feature.reshape(docs_count, 1, rank, rank), pick_own(returned, routes)


def by_routing(
    tokens, cotangent, routes, combine, doc_ids, w_gate, w_up, w_down, proj_hidden, proj_output
):
    tok_rows, chosen = routes.shape
    local_count = w_gate.shape[0]
    groups = lax.axis_size("exp")
    experts = local_count * groups
    capacity = max(2, tok_rows * chosen * 5 // (4 * experts))
    docs_count = max(2, tok_rows * groups // DOC_TOK)
    entries = tok_rows * chosen
    width = tokens.shape[1]
    flat_routes = routes.reshape(-1)
    member = (flat_routes[:, None] == jnp.arange(experts, dtype=jnp.int32)[None, :]).astype(
        jnp.int32
    )
    slot_rank = jnp.sum((jnp.cumsum(member, axis=0) - 1) * member, axis=1)
    position = flat_routes * capacity + slot_rank
    source = (
        jnp.full((experts * capacity,), -1, jnp.int32)
        .at[position]
        .set(jnp.arange(entries, dtype=jnp.int32))
    )
    filled = source >= 0
    safe_source = jnp.maximum(source, 0)
    token_of = safe_source // chosen
    send_x = jnp.where(filled[:, None], tokens[token_of], 0)
    send_dy = jnp.where(filled[:, None], cotangent[token_of], 0)
    send_w = jnp.where(filled, combine.reshape(-1)[safe_source], 0)
    send_doc = jnp.where(filled, doc_ids[token_of], -1).astype(jnp.bfloat16)

    def exchange(array):
        array = array.reshape((groups, local_count, capacity) + array.shape[1:])
        return lax.all_to_all(array, "exp", split_axis=0, concat_axis=0, tiled=True)

    recv_x, recv_dy, recv_w, recv_doc = (
        exchange(send_x),
        exchange(send_dy),
        exchange(send_w),
        exchange(send_doc),
    )
    slots = groups * capacity
    grads, feats = [], []
    for e in range(local_count):
        hidden = swiglu(recv_x[:, e].reshape(slots, width), w_gate[e], w_up[e])
        grad, feature = finish(
            hidden,
            recv_dy[:, e].reshape(slots, width),
            recv_w[:, e].reshape(slots),
            recv_doc[:, e].reshape(slots),
            w_down[e],
            proj_hidden[e],
            proj_output[e],
            docs_count,
        )
        grads.append(grad.reshape(groups, capacity))
        feats.append(feature)
    slot_grad = jnp.stack(grads, axis=1)
    returned = lax.all_to_all(slot_grad, "exp", split_axis=0, concat_axis=0, tiled=True)
    route_grad = returned.reshape(-1)[position].reshape(tok_rows, chosen)
    return jnp.stack(feats, axis=1), route_grad


def on_device(tokens, cotangent, routes, combine, doc_ids, w_gate, *rest):
    tok_rows, chosen = routes.shape
    experts = w_gate.shape[0] * lax.axis_size("exp")
    dense = w_gate.shape[0] == 1 and 4 * chosen >= experts and experts % 4 == 0
    plan = by_ring if dense else by_routing
    return plan(tokens, cotangent, routes, combine, doc_ids, w_gate, *rest)


def solution(mesh):
    placed = (
        P(("grp", "exp"), None),
        P(("grp", "exp"), None),
        P(("grp", "exp"), None),
        P(("grp", "exp"), None),
        P(("grp", "exp")),
        P("exp", None, None),
        P("exp", None, None),
        P("exp", None, None),
        P("exp", None, None),
        P("exp", None, None),
    )
    return jax.shard_map(
        on_device,
        mesh=mesh,
        in_specs=placed,
        out_specs=(P("grp", "exp", None, None), P(("grp", "exp"), None)),
        check_vma=False,
    )
```

```python
import functools

import jax
import jax.numpy as jnp
import numpy as np
from jax import lax
from jax.experimental import pallas as pl
from jax.experimental.pallas import tpu as pltpu
from jax.sharding import PartitionSpec as P

DOC_TOK = 512


def swiglu(rows, w_gate, w_up):
    gate_val = jnp.dot(rows, w_gate, preferred_element_type=jnp.float32)
    up_val = jnp.dot(rows, w_up, preferred_element_type=jnp.float32)
    return (jax.nn.silu(gate_val) * up_val).astype(jnp.bfloat16)


def finish(hidden, rows_dy, rows_w, rows_doc, w_down, proj_hidden, proj_output, docs_count):
    out_val = jnp.dot(hidden, w_down, preferred_element_type=jnp.float32)
    grad = jnp.sum(rows_dy.astype(jnp.float32) * out_val, axis=-1)
    low_side = jnp.dot(hidden, proj_hidden, preferred_element_type=jnp.float32).astype(
        jnp.bfloat16
    )
    proj_cot = jnp.dot(rows_dy, proj_output, preferred_element_type=jnp.float32)
    high_side = (rows_w.astype(jnp.float32)[:, None] * proj_cot).astype(jnp.bfloat16)
    doc_table = jnp.arange(docs_count, dtype=jnp.int32).astype(jnp.bfloat16)
    onehot = (rows_doc[:, None] == doc_table).astype(jnp.bfloat16)
    spread = onehot[:, :, None] * low_side[:, None, :]
    spread = spread.reshape(spread.shape[0], -1)
    feature = lax.dot_general(
        spread, high_side, (((0,), (0,)), ((), ())), preferred_element_type=jnp.float32
    )
    return grad, feature.reshape(docs_count, low_side.shape[1], high_side.shape[1])


def pick_own(returned, routes):
    experts = returned.shape[0]
    table = jnp.arange(experts, dtype=jnp.int32)
    hit = routes[:, :, None] == table
    return jnp.sum(jnp.where(hit, returned.T[:, None, :], 0.0), axis=-1)


def rows_kernel(blocks, first, *refs):
    order, facts = refs[:2]
    block_in = refs[2 : 2 + blocks]
    w_gate, w_up, w_down, low_proj, high_proj = refs[2 + blocks : 7 + blocks]
    grads, feat, x_all, dy_all, low_sum, grad_sum = refs[-6:]
    rows = block_in[0].shape[0] // 2
    across = (((1,), (1,)), ((), ()))
    for i in range(blocks):
        x_all[i * rows : (i + 1) * rows, :] = block_in[i][:rows, :]
        dy_all[i * rows : (i + 1) * rows, :] = block_in[i][rows:, :]
    low_sum[...] = jnp.zeros_like(low_sum)
    grad_sum[...] = jnp.zeros_like(grad_sum)
    units = w_gate.shape[2]
    tile = 256 if units % 256 == 0 else units
    lanes = grad_sum.shape[1]

    @pl.loop(0, units // tile)
    def _(j):
        part = pl.ds(pl.multiple_of(j * tile, tile), tile)
        gate_val = jnp.dot(x_all[...], w_gate[0, :, part], preferred_element_type=jnp.float32)
        up_val = jnp.dot(x_all[...], w_up[0, :, part], preferred_element_type=jnp.float32)
        hidden = (jax.nn.silu(gate_val) * up_val).astype(jnp.bfloat16)
        back = lax.dot_general(
            dy_all[...], w_down[0, part, :], across, preferred_element_type=jnp.float32
        )
        terms = hidden.astype(jnp.float32) * back
        for cut in range(0, tile, lanes):
            grad_sum[...] += terms[:, cut : cut + lanes]
        low_sum[...] += lax.dot_general(
            hidden, low_proj[:, part], across, preferred_element_type=jnp.float32
        )

    proj_cot = lax.dot_general(
        dy_all[...], high_proj[...], across, preferred_element_type=jnp.float32
    )
    rank = proj_cot.shape[1]
    width = low_sum.shape[1]
    doc_of = lax.broadcasted_iota(jnp.int32, (rows, width), 1) // rank
    if first:
        grads[...] = jnp.zeros_like(grads)
    else:
        grads_in, feat_in = refs[7 + blocks : 9 + blocks]
        grads[...] = grads_in[...]
    spread, high_side = [], []
    for i in range(blocks):
        place = slice(i * rows, (i + 1) * rows)
        owner = order[i]
        weight = jnp.transpose(jnp.broadcast_to(facts[owner, 0:1, :], (rows, rows)))
        doc = jnp.transpose(jnp.broadcast_to(facts[owner, 1:2, :], (rows, rows)))
        doc = jnp.concatenate([doc] * (width // rows), axis=1).astype(jnp.int32)
        high_side.append((weight[:, :rank] * proj_cot[place]).astype(jnp.bfloat16))
        low_side = jnp.where(doc == doc_of, low_sum[place, :], 0.0)
        spread.append(low_side.astype(jnp.bfloat16))
        grads[owner, :, :] = jnp.broadcast_to(
            jnp.sum(jnp.transpose(grad_sum[place, :]), axis=0, keepdims=True), (8, rows)
        )
    feature = lax.dot_general(
        jnp.concatenate(spread, axis=0),
        jnp.concatenate(high_side, axis=0),
        (((0,), (0,)), ((), ())),
        preferred_element_type=jnp.float32,
    )
    feat[...] = feature if first else feat_in[...] + feature


def work(order, facts, block_in, weights, sums):
    units = weights[0].shape[2]
    low_width, rank = weights[3].shape[0], weights[4].shape[0]
    blocks = len(block_in)
    rows, width = block_in[0].shape[0] // 2, block_in[0].shape[1]
    inside = pl.BlockSpec(memory_space=pltpu.VMEM)
    call = pl.pallas_call(
        functools.partial(rows_kernel, blocks, not sums),
        out_shape=[
            jax.ShapeDtypeStruct(facts.shape, jnp.float32),
            jax.ShapeDtypeStruct((low_width, rank), jnp.float32),
        ],
        in_specs=[pl.BlockSpec(memory_space=pltpu.SMEM)]
        + [inside] * (1 + blocks + len(weights) + len(sums)),
        out_specs=[inside] * 2,
        scratch_shapes=[
            pltpu.VMEM((blocks * rows, width), jnp.bfloat16),
            pltpu.VMEM((blocks * rows, width), jnp.bfloat16),
            pltpu.VMEM((blocks * rows, low_width), jnp.float32),
            pltpu.VMEM((blocks * rows, 128), jnp.float32),
        ],
        compiler_params=pltpu.CompilerParams(vmem_limit_bytes=16 * 1024 * 1024),
        cost_estimate=pl.CostEstimate(
            flops=6 * blocks * rows * width * units,
            bytes_accessed=4 * blocks * rows * width,
            transcendentals=blocks * rows * units,
        ),
    )
    return call(order, facts, *block_in, *weights, *sums)


def facts_kernel(routes, combine, doc_ids, out):
    groups, lines, rows = out.shape
    expert = lax.broadcasted_iota(jnp.int32, (groups, rows), 0)
    weight = jnp.zeros((groups, rows), jnp.float32)
    for k in range(routes.shape[0]):
        share = combine[k : k + 1, :].astype(jnp.float32)
        weight += jnp.where(routes[k : k + 1, :] == expert, share, 0.0)
    line = lax.broadcasted_iota(jnp.int32, (lines, rows), 0)
    doc = doc_ids[...].astype(jnp.float32)
    for e in range(groups):
        out[e] = jnp.where(line == 0, weight[e : e + 1, :], doc)


def stack_kernel(top, bottom, out, sems):
    rows = top.shape[0]
    copies = [
        pltpu.make_async_copy(top, out.at[:rows], sems.at[0]),
        pltpu.make_async_copy(bottom, out.at[rows:], sems.at[1]),
    ]
    for copy in copies:
        copy.start()
    for copy in copies:
        copy.wait()


def by_ring(
    tokens, cotangent, routes, combine, doc_ids, w_gate, w_up, w_down, proj_hidden, proj_output
):
    tok_rows, chosen = routes.shape
    groups = lax.axis_size("exp")
    docs_count = max(2, tok_rows * groups // DOC_TOK)
    chips = groups // 2
    half = chips // 2
    ring = list(range(0, chips, 2)) + list(range(chips - 1, 0, -2))
    onward = []
    for place in range(chips):
        onward.append((2 * ring[place], 2 * ring[(place + 1) % chips]))
        onward.append((2 * ring[place] + 1, 2 * ring[place - 1] + 1))
    across = [(i, i ^ 1) for i in range(groups)]

    def hop(block):
        return lax.ppermute(block, "exp", onward)

    def swap(block):
        return lax.ppermute(block, "exp", across)

    orders = np.zeros((groups, groups), np.int32)
    for place in range(chips):
        for core in range(2):
            way = 1 - 2 * core

            def owner(steps, which):
                return 2 * ring[(place + steps) % chips] + which

            order = [owner(0, core), owner(0, 1 - core)]
            for step in range(1, half + 1):
                near, far = -step * way, step * way
                order += [owner(near, core), owner(far, 1 - core)]
                if step < half:
                    order += [owner(near, 1 - core), owner(far, core)]
            orders[owner(0, core)] = order
    me = lax.axis_index("exp")
    order = lax.dynamic_index_in_dim(jnp.asarray(orders), me, axis=0, keepdims=False)

    rows, width = tokens.shape
    own = pl.pallas_call(
        stack_kernel,
        out_shape=jax.ShapeDtypeStruct((2 * rows, width), tokens.dtype),
        in_specs=[pl.BlockSpec(memory_space=pl.ANY)] * 2,
        out_specs=pl.BlockSpec(memory_space=pltpu.VMEM),
        scratch_shapes=[pltpu.SemaphoreType.DMA((2,))],
    )(tokens, cotangent)
    beside = swap(own)

    facts = pl.pallas_call(
        facts_kernel,
        out_shape=jax.ShapeDtypeStruct((groups, 8, rows), jnp.float32),
        in_specs=[pl.BlockSpec(memory_space=pltpu.VMEM)] * 3,
        out_specs=pl.BlockSpec(memory_space=pltpu.VMEM),
    )(routes.T, combine.T, doc_ids[None, :])
    facts = lax.all_to_all(facts, "exp", split_axis=0, concat_axis=0, tiled=True)

    low_proj = jnp.concatenate([proj_hidden[0].T] * docs_count, axis=0)
    weights = (w_gate, w_up, w_down, low_proj, proj_output[0].T)
    sums, done = [], 0
    jobs = [(own, beside)]

    def behind(block):
        nonlocal sums, done
        job = jobs.pop(0)
        sums = work(order[done : done + len(job)], facts, job, weights, sums)
        done += len(job)
        if block is None:
            return None
        sums, block = lax.optimization_barrier((sums, block))
        return block

    near, other = own, beside
    for step in range(1, half + 1):
        near = hop(near)
        if step > 1:
            near = behind(near)
        jobs.append((near, swap(near)))
        if step < half:
            other = behind(hop(other))
            jobs.append((other, swap(other)))
    while jobs:
        behind(None)
    grads, feature = sums
    returned = lax.all_to_all(grads, "exp", split_axis=0, concat_axis=0, tiled=True)
    rank = proj_output.shape[2]
    return feature.reshape(docs_count, 1, rank, rank), pick_own(returned[:, 0, :], routes)


def by_routing(
    tokens, cotangent, routes, combine, doc_ids, w_gate, w_up, w_down, proj_hidden, proj_output
):
    tok_rows, chosen = routes.shape
    local_count = w_gate.shape[0]
    groups = lax.axis_size("exp")
    experts = local_count * groups
    capacity = max(2, tok_rows * chosen * 5 // (4 * experts))
    docs_count = max(2, tok_rows * groups // DOC_TOK)
    entries = tok_rows * chosen
    width = tokens.shape[1]
    flat_routes = routes.reshape(-1)
    member = (flat_routes[:, None] == jnp.arange(experts, dtype=jnp.int32)[None, :]).astype(
        jnp.int32
    )
    slot_rank = jnp.sum((jnp.cumsum(member, axis=0) - 1) * member, axis=1)
    position = flat_routes * capacity + slot_rank
    source = (
        jnp.full((experts * capacity,), -1, jnp.int32)
        .at[position]
        .set(jnp.arange(entries, dtype=jnp.int32))
    )
    filled = source >= 0
    safe_source = jnp.maximum(source, 0)
    token_of = safe_source // chosen
    send_x = jnp.where(filled[:, None], tokens[token_of], 0)
    send_dy = jnp.where(filled[:, None], cotangent[token_of], 0)
    send_w = jnp.where(filled, combine.reshape(-1)[safe_source], 0)
    send_doc = jnp.where(filled, doc_ids[token_of], -1).astype(jnp.bfloat16)

    def exchange(array):
        array = array.reshape((groups, local_count, capacity) + array.shape[1:])
        return lax.all_to_all(array, "exp", split_axis=0, concat_axis=0, tiled=True)

    recv_x, recv_dy, recv_w, recv_doc = (
        exchange(send_x),
        exchange(send_dy),
        exchange(send_w),
        exchange(send_doc),
    )
    slots = groups * capacity
    grads, feats = [], []
    for e in range(local_count):
        hidden = swiglu(recv_x[:, e].reshape(slots, width), w_gate[e], w_up[e])
        grad, feature = finish(
            hidden,
            recv_dy[:, e].reshape(slots, width),
            recv_w[:, e].reshape(slots),
            recv_doc[:, e].reshape(slots),
            w_down[e],
            proj_hidden[e],
            proj_output[e],
            docs_count,
        )
        grads.append(grad.reshape(groups, capacity))
        feats.append(feature)
    slot_grad = jnp.stack(grads, axis=1)
    returned = lax.all_to_all(slot_grad, "exp", split_axis=0, concat_axis=0, tiled=True)
    route_grad = returned.reshape(-1)[position].reshape(tok_rows, chosen)
    return jnp.stack(feats, axis=1), route_grad


def on_device(tokens, cotangent, routes, combine, doc_ids, w_gate, *rest):
    tok_rows, chosen = routes.shape
    experts = w_gate.shape[0] * lax.axis_size("exp")
    dense = w_gate.shape[0] == 1 and 4 * chosen >= experts and experts % 4 == 0
    plan = by_ring if dense else by_routing
    return plan(tokens, cotangent, routes, combine, doc_ids, w_gate, *rest)


def solution(mesh):
    placed = (
        P(("grp", "exp"), None),
        P(("grp", "exp"), None),
        P(("grp", "exp"), None),
        P(("grp", "exp"), None),
        P(("grp", "exp")),
        P("exp", None, None),
        P("exp", None, None),
        P("exp", None, None),
        P("exp", None, None),
        P("exp", None, None),
    )
    return jax.shard_map(
        on_device,
        mesh=mesh,
        in_specs=placed,
        out_specs=(P("grp", "exp", None, None), P(("grp", "exp"), None)),
        check_vma=False,
    )
```

```python
import functools

import jax
import jax.numpy as jnp
import numpy as np
from jax import lax
from jax.experimental import pallas as pl
from jax.experimental.pallas import tpu as pltpu
from jax.sharding import PartitionSpec as P

DOC_TOK = 512


def swiglu(rows, w_gate, w_up):
    gate_val = jnp.dot(rows, w_gate, preferred_element_type=jnp.float32)
    up_val = jnp.dot(rows, w_up, preferred_element_type=jnp.float32)
    return (jax.nn.silu(gate_val) * up_val).astype(jnp.bfloat16)


def finish(hidden, rows_dy, rows_w, rows_doc, w_down, proj_hidden, proj_output, docs_count):
    out_val = jnp.dot(hidden, w_down, preferred_element_type=jnp.float32)
    grad = jnp.sum(rows_dy.astype(jnp.float32) * out_val, axis=-1)
    low_side = jnp.dot(hidden, proj_hidden, preferred_element_type=jnp.float32).astype(
        jnp.bfloat16
    )
    proj_cot = jnp.dot(rows_dy, proj_output, preferred_element_type=jnp.float32)
    high_side = (rows_w.astype(jnp.float32)[:, None] * proj_cot).astype(jnp.bfloat16)
    doc_table = jnp.arange(docs_count, dtype=jnp.int32).astype(jnp.bfloat16)
    onehot = (rows_doc[:, None] == doc_table).astype(jnp.bfloat16)
    spread = onehot[:, :, None] * low_side[:, None, :]
    spread = spread.reshape(spread.shape[0], -1)
    feature = lax.dot_general(
        spread, high_side, (((0,), (0,)), ((), ())), preferred_element_type=jnp.float32
    )
    return grad, feature.reshape(docs_count, low_side.shape[1], high_side.shape[1])


def rows_kernel(blocks, *refs):
    order, sheet_in = refs[:2]
    block_in = refs[2 : 2 + blocks]
    w_gate, w_up, w_down, low_proj, high_proj = refs[2 + blocks : 7 + blocks]
    sheet, low_side, proj_cot, x_all, dy_all, low_sum, grad_sum = refs[-7:]
    rows = block_in[0].shape[0] // 2
    across = (((1,), (1,)), ((), ()))
    for i in range(blocks):
        x_all[i * rows : (i + 1) * rows, :] = block_in[i][:rows, :]
        dy_all[i * rows : (i + 1) * rows, :] = block_in[i][rows:, :]
    low_sum[...] = jnp.zeros_like(low_sum)
    grad_sum[...] = jnp.zeros_like(grad_sum)
    units = w_gate.shape[1]
    tile = 256 if units % 256 == 0 else units
    lanes = grad_sum.shape[1]

    @pl.loop(0, units // tile)
    def _(j):
        part = pl.ds(pl.multiple_of(j * tile, tile), tile)
        gate_val = jnp.dot(x_all[...], w_gate[:, part], preferred_element_type=jnp.float32)
        up_val = jnp.dot(x_all[...], w_up[:, part], preferred_element_type=jnp.float32)
        hidden = (jax.nn.silu(gate_val) * up_val).astype(jnp.bfloat16)
        back = lax.dot_general(
            dy_all[...], w_down[part, :], across, preferred_element_type=jnp.float32
        )
        terms = hidden.astype(jnp.float32) * back
        for cut in range(0, tile, lanes):
            grad_sum[...] += terms[:, cut : cut + lanes]
        low_sum[...] += lax.dot_general(
            low_proj[:, part], hidden, across, preferred_element_type=jnp.float32
        )

    low_side[...] = low_sum[...].astype(low_side.dtype)
    proj_cot[...] = lax.dot_general(
        high_proj[...], dy_all[...], across, preferred_element_type=jnp.float32
    )
    sheet[...] = sheet_in[...]
    for i in range(blocks):
        total = jnp.sum(
            jnp.transpose(grad_sum[i * rows : (i + 1) * rows, :]), axis=0, keepdims=True
        )
        sheet[order[i], 0:1, :] = total


def work(order, sheet, block_in, weights):
    units = weights[0].shape[1]
    low_width, rank = weights[3].shape[0], weights[4].shape[0]
    blocks = len(block_in)
    rows, width = block_in[0].shape[0] // 2, block_in[0].shape[1]
    inside = pl.BlockSpec(memory_space=pltpu.VMEM)
    call = pl.pallas_call(
        functools.partial(rows_kernel, blocks),
        out_shape=[
            jax.ShapeDtypeStruct(sheet.shape, jnp.float32),
            jax.ShapeDtypeStruct((low_width, blocks * rows), jnp.bfloat16),
            jax.ShapeDtypeStruct((rank, blocks * rows), jnp.float32),
        ],
        in_specs=[pl.BlockSpec(memory_space=pltpu.SMEM)]
        + [inside] * (1 + blocks + len(weights)),
        out_specs=[inside] * 3,
        scratch_shapes=[
            pltpu.VMEM((blocks * rows, width), jnp.bfloat16),
            pltpu.VMEM((blocks * rows, width), jnp.bfloat16),
            pltpu.VMEM((low_width, blocks * rows), jnp.float32),
            pltpu.VMEM((blocks * rows, 128), jnp.float32),
        ],
        compiler_params=pltpu.CompilerParams(vmem_limit_bytes=16 * 1024 * 1024),
        cost_estimate=pl.CostEstimate(
            flops=6 * blocks * rows * width * units,
            bytes_accessed=4 * blocks * rows * width,
            transcendentals=blocks * rows * units,
        ),
    )
    return call(order, sheet, *block_in, *weights)


def outcome_kernel(pieces, order, returned, routes, *refs):
    low_in, proj_in = refs[:pieces], refs[pieces : 2 * pieces]
    feat, route_grad = refs[-2:]
    rows = returned.shape[2]
    width, rank = low_in[0].shape[0], proj_in[0].shape[0]
    doc_of = lax.broadcasted_iota(jnp.int32, (width, rows), 0) // rank
    total = jnp.zeros(feat.shape, jnp.float32)
    done = 0
    for low_side, proj_cot in zip(low_in, proj_in):
        spread, high_side = [], []
        for i in range(low_side.shape[1] // rows):
            place = slice(i * rows, (i + 1) * rows)
            owner = order[done]
            done += 1
            weight = returned[owner, 1:2, :]
            doc = returned[owner, 2:3, :].astype(jnp.int32)
            high_side.append((weight * proj_cot[:, place]).astype(jnp.bfloat16))
            low = low_side[:, place].astype(jnp.float32)
            spread.append(jnp.where(doc == doc_of, low, 0.0).astype(jnp.bfloat16))
        total += lax.dot_general(
            jnp.concatenate(spread, axis=1),
            jnp.concatenate(high_side, axis=1),
            (((1,), (1,)), ((), ())),
            preferred_element_type=jnp.float32,
        )
    feat[...] = total
    picked = jnp.zeros(route_grad.shape, jnp.float32)
    for e in range(returned.shape[0]):
        picked = jnp.where(routes[...] == e, returned[e, 0:1, :], picked)
    route_grad[...] = picked


def load_kernel(repeat, *refs):
    ins, outs, sems = refs[:5], refs[5:10], refs[10]
    rank = ins[3].shape[0]
    copies = [(src, dst) for i, (src, dst) in enumerate(zip(ins, outs)) if i != 3]
    for i in range(repeat):
        copies.append((ins[3], outs[3].at[i * rank : (i + 1) * rank]))
    copies = [
        pltpu.make_async_copy(src, dst, sems.at[i]) for i, (src, dst) in enumerate(copies)
    ]
    for copy in copies:
        copy.start()
    for copy in copies:
        copy.wait()


def facts_kernel(routes, combine, doc_ids, out):
    groups, lines, rows = out.shape
    expert = lax.broadcasted_iota(jnp.int32, (groups, rows), 0)
    weight = jnp.zeros((groups, rows), jnp.float32)
    for k in range(routes.shape[0]):
        share = combine[k : k + 1, :].astype(jnp.float32)
        weight += jnp.where(routes[k : k + 1, :] == expert, share, 0.0)
    line = lax.broadcasted_iota(jnp.int32, (lines, rows), 0)
    doc = doc_ids[...].astype(jnp.float32)
    for e in range(groups):
        out[e] = jnp.where(line == 1, weight[e : e + 1, :], doc)


def stack_kernel(top, bottom, out, sems):
    rows = top.shape[0]
    copies = [
        pltpu.make_async_copy(top, out.at[:rows], sems.at[0]),
        pltpu.make_async_copy(bottom, out.at[rows:], sems.at[1]),
    ]
    for copy in copies:
        copy.start()
    for copy in copies:
        copy.wait()


def by_ring(
    tokens, cotangent, routes, combine, doc_ids, w_gate, w_up, w_down, proj_hidden, proj_output
):
    tok_rows, chosen = routes.shape
    groups = lax.axis_size("exp")
    docs_count = max(2, tok_rows * groups // DOC_TOK)
    chips = groups // 2
    half = chips // 2
    ring = list(range(0, chips, 2)) + list(range(chips - 1, 0, -2))
    onward = []
    for place in range(chips):
        onward.append((2 * ring[place], 2 * ring[(place + 1) % chips]))
        onward.append((2 * ring[place] + 1, 2 * ring[place - 1] + 1))
    across = [(i, i ^ 1) for i in range(groups)]

    def hop(block):
        return lax.ppermute(block, "exp", onward)

    def swap(block):
        return lax.ppermute(block, "exp", across)

    orders = np.zeros((groups, groups), np.int32)
    for place in range(chips):
        for core in range(2):
            way = 1 - 2 * core

            def owner(steps, which):
                return 2 * ring[(place + steps) % chips] + which

            order = [owner(0, core), owner(0, 1 - core)]
            for step in range(1, half + 1):
                near, far = -step * way, step * way
                order += [owner(near, core), owner(far, 1 - core)]
                if step < half:
                    order += [owner(near, 1 - core), owner(far, core)]
            orders[owner(0, core)] = order
    me = lax.axis_index("exp")
    order = lax.dynamic_index_in_dim(jnp.asarray(orders), me, axis=0, keepdims=False)

    rows, width = tokens.shape
    own = pl.pallas_call(
        stack_kernel,
        out_shape=jax.ShapeDtypeStruct((2 * rows, width), tokens.dtype),
        in_specs=[pl.BlockSpec(memory_space=pltpu.HBM)] * 2,
        out_specs=pl.BlockSpec(memory_space=pltpu.VMEM),
        scratch_shapes=[pltpu.SemaphoreType.DMA((2,))],
    )(tokens, cotangent)
    beside = swap(own)

    sheet = pl.pallas_call(
        facts_kernel,
        out_shape=jax.ShapeDtypeStruct((groups, 8, rows), jnp.float32),
        in_specs=[pl.BlockSpec(memory_space=pltpu.VMEM)] * 3,
        out_specs=pl.BlockSpec(memory_space=pltpu.VMEM),
    )(routes.T, combine.T, doc_ids[None, :])
    inside = pl.BlockSpec(memory_space=pltpu.VMEM)
    given = (w_gate[0], w_up[0], w_down[0], proj_hidden[0].T, proj_output[0].T)
    shapes = [w.shape for w in given]
    shapes[3] = (docs_count * shapes[3][0], shapes[3][1])
    weights = pl.pallas_call(
        functools.partial(load_kernel, docs_count),
        out_shape=[jax.ShapeDtypeStruct(shape, w_gate.dtype) for shape in shapes],
        in_specs=[pl.BlockSpec(memory_space=pltpu.HBM)] * 5,
        out_specs=[inside] * 5,
        scratch_shapes=[pltpu.SemaphoreType.DMA((4 + docs_count,))],
    )(*given)
    lows, projs, done = [], [], 0
    jobs = [(own, beside)]

    def behind(block):
        nonlocal sheet, done
        job = jobs.pop(0)
        sheet, low_side, proj_cot = work(order[done : done + len(job)], sheet, job, weights)
        lows.append(low_side)
        projs.append(proj_cot)
        done += len(job)
        if block is not None:
            sheet, block = lax.optimization_barrier((sheet, block))
        return block

    near, other = own, beside
    for step in range(1, half + 1):
        near = hop(near)
        if step > 1:
            near = behind(near)
        jobs.append((near, swap(near)))
        if step < half:
            other = behind(hop(other))
            jobs.append((other, swap(other)))
    while jobs:
        behind(None)
    returned = lax.all_to_all(sheet, "exp", split_axis=0, concat_axis=0, tiled=True)
    rank = proj_output.shape[2]
    feature, route_grad = pl.pallas_call(
        functools.partial(outcome_kernel, len(lows)),
        out_shape=[
            jax.ShapeDtypeStruct((docs_count * rank, rank), jnp.float32),
            jax.ShapeDtypeStruct((chosen, tok_rows), jnp.float32),
        ],
        in_specs=[pl.BlockSpec(memory_space=pltpu.SMEM)] + [inside] * (2 + 2 * len(lows)),
        out_specs=[inside] * 2,
        compiler_params=pltpu.CompilerParams(vmem_limit_bytes=16 * 1024 * 1024),
    )(order, returned, routes.T, *lows, *projs)
    return feature.reshape(docs_count, 1, rank, rank), route_grad.T


def by_routing(
    tokens, cotangent, routes, combine, doc_ids, w_gate, w_up, w_down, proj_hidden, proj_output
):
    tok_rows, chosen = routes.shape
    local_count = w_gate.shape[0]
    groups = lax.axis_size("exp")
    experts = local_count * groups
    capacity = max(2, tok_rows * chosen * 5 // (4 * experts))
    docs_count = max(2, tok_rows * groups // DOC_TOK)
    entries = tok_rows * chosen
    width = tokens.shape[1]
    flat_routes = routes.reshape(-1)
    member = (flat_routes[:, None] == jnp.arange(experts, dtype=jnp.int32)[None, :]).astype(
        jnp.int32
    )
    slot_rank = jnp.sum((jnp.cumsum(member, axis=0) - 1) * member, axis=1)
    position = flat_routes * capacity + slot_rank
    source = (
        jnp.full((experts * capacity,), -1, jnp.int32)
        .at[position]
        .set(jnp.arange(entries, dtype=jnp.int32))
    )
    filled = source >= 0
    safe_source = jnp.maximum(source, 0)
    token_of = safe_source // chosen
    send_x = jnp.where(filled[:, None], tokens[token_of], 0)
    send_dy = jnp.where(filled[:, None], cotangent[token_of], 0)
    send_w = jnp.where(filled, combine.reshape(-1)[safe_source], 0)
    send_doc = jnp.where(filled, doc_ids[token_of], -1).astype(jnp.bfloat16)

    def exchange(array):
        array = array.reshape((groups, local_count, capacity) + array.shape[1:])
        return lax.all_to_all(array, "exp", split_axis=0, concat_axis=0, tiled=True)

    recv_x, recv_dy, recv_w, recv_doc = (
        exchange(send_x),
        exchange(send_dy),
        exchange(send_w),
        exchange(send_doc),
    )
    slots = groups * capacity
    grads, feats = [], []
    for e in range(local_count):
        hidden = swiglu(recv_x[:, e].reshape(slots, width), w_gate[e], w_up[e])
        grad, feature = finish(
            hidden,
            recv_dy[:, e].reshape(slots, width),
            recv_w[:, e].reshape(slots),
            recv_doc[:, e].reshape(slots),
            w_down[e],
            proj_hidden[e],
            proj_output[e],
            docs_count,
        )
        grads.append(grad.reshape(groups, capacity))
        feats.append(feature)
    slot_grad = jnp.stack(grads, axis=1)
    returned = lax.all_to_all(slot_grad, "exp", split_axis=0, concat_axis=0, tiled=True)
    route_grad = returned.reshape(-1)[position].reshape(tok_rows, chosen)
    return jnp.stack(feats, axis=1), route_grad


def on_device(tokens, cotangent, routes, combine, doc_ids, w_gate, *rest):
    tok_rows, chosen = routes.shape
    experts = w_gate.shape[0] * lax.axis_size("exp")
    dense = w_gate.shape[0] == 1 and 4 * chosen >= experts and experts % 4 == 0
    plan = by_ring if dense else by_routing
    return plan(tokens, cotangent, routes, combine, doc_ids, w_gate, *rest)


def solution(mesh):
    placed = (
        P(("grp", "exp"), None),
        P(("grp", "exp"), None),
        P(("grp", "exp"), None),
        P(("grp", "exp"), None),
        P(("grp", "exp")),
        P("exp", None, None),
        P("exp", None, None),
        P("exp", None, None),
        P("exp", None, None),
        P("exp", None, None),
    )
    return jax.shard_map(
        on_device,
        mesh=mesh,
        in_specs=placed,
        out_specs=(P("grp", "exp", None, None), P(("grp", "exp"), None)),
        check_vma=False,
    )
```

```python
import functools

import jax
import jax.numpy as jnp
import numpy as np
from jax import lax
from jax.experimental import pallas as pl
from jax.experimental.pallas import tpu as pltpu
from jax.sharding import PartitionSpec as P

DOC_TOK = 512
LOAD_MIB = 40


def swiglu(rows, w_gate, w_up):
    gate_val = jnp.dot(rows, w_gate, preferred_element_type=jnp.float32)
    up_val = jnp.dot(rows, w_up, preferred_element_type=jnp.float32)
    return (jax.nn.silu(gate_val) * up_val).astype(jnp.bfloat16)


def finish(hidden, rows_dy, rows_w, rows_doc, w_down, proj_hidden, proj_output, docs_count):
    out_val = jnp.dot(hidden, w_down, preferred_element_type=jnp.float32)
    grad = jnp.sum(rows_dy.astype(jnp.float32) * out_val, axis=-1)
    low_side = jnp.dot(hidden, proj_hidden, preferred_element_type=jnp.float32).astype(
        jnp.bfloat16
    )
    proj_cot = jnp.dot(rows_dy, proj_output, preferred_element_type=jnp.float32)
    high_side = (rows_w.astype(jnp.float32)[:, None] * proj_cot).astype(jnp.bfloat16)
    doc_table = jnp.arange(docs_count, dtype=jnp.int32).astype(jnp.bfloat16)
    onehot = (rows_doc[:, None] == doc_table).astype(jnp.bfloat16)
    spread = onehot[:, :, None] * low_side[:, None, :]
    spread = spread.reshape(spread.shape[0], -1)
    feature = lax.dot_general(
        spread, high_side, (((0,), (0,)), ((), ())), preferred_element_type=jnp.float32
    )
    return grad, feature.reshape(docs_count, low_side.shape[1], high_side.shape[1])


def rows_kernel(blocks, load, *refs):
    order, sheet_in = refs[:2]
    block_in = refs[2 : 2 + blocks]
    given = refs[2 + blocks : 7 + blocks]
    sheet, low_side, proj_cot = refs[7 + blocks : 10 + blocks]
    x_all, dy_all, low_sum, grad_sum = refs[-5:-1] if load else refs[-4:]
    w_gate, w_up, w_down, low_proj, high_proj = refs[10 + blocks : 15 + blocks] if load else given
    rows = block_in[0].shape[0] // 2
    across = (((1,), (1,)), ((), ()))
    units = w_gate.shape[1]
    tile = 256 if units % 256 == 0 else units
    tiles = units // tile
    lanes = grad_sum.shape[1]
    copies = []
    if load:
        rank = given[3].shape[0]
        for j in range(tiles):
            part = pl.ds(j * tile, tile)
            copies.append((given[0].at[:, part], w_gate.at[:, part]))
            copies.append((given[1].at[:, part], w_up.at[:, part]))
            copies.append((given[2].at[part, :], w_down.at[part, :]))
        for i in range(low_proj.shape[0] // rank):
            copies.append((given[3], low_proj.at[pl.ds(i * rank, rank), :]))
        copies.append((given[4], high_proj))
        copies = [
            pltpu.make_async_copy(src, dst, refs[-1].at[i]) for i, (src, dst) in enumerate(copies)
        ]
        for copy in copies[3 * tiles :] + copies[: 3 * tiles]:
            copy.start()
    for i in range(blocks):
        x_all[i * rows : (i + 1) * rows, :] = block_in[i][:rows, :]
        dy_all[i * rows : (i + 1) * rows, :] = block_in[i][rows:, :]
    low_sum[...] = jnp.zeros_like(low_sum)
    grad_sum[...] = jnp.zeros_like(grad_sum)

    def one_tile(j):
        part = pl.ds(j * tile, tile)
        gate_val = jnp.dot(x_all[...], w_gate[:, part], preferred_element_type=jnp.float32)
        up_val = jnp.dot(x_all[...], w_up[:, part], preferred_element_type=jnp.float32)
        hidden = (jax.nn.silu(gate_val) * up_val).astype(jnp.bfloat16)
        back = lax.dot_general(
            dy_all[...], w_down[part, :], across, preferred_element_type=jnp.float32
        )
        terms = hidden.astype(jnp.float32) * back
        for cut in range(0, tile, lanes):
            grad_sum[...] += terms[:, cut : cut + lanes]
        low_sum[...] += lax.dot_general(
            low_proj[:, part], hidden, across, preferred_element_type=jnp.float32
        )

    for copy in copies[3 * tiles :]:
        copy.wait()
    for j in range(tiles):
        for copy in copies[3 * j : 3 * j + 3] if load else []:
            copy.wait()
        one_tile(j)

    low_side[...] = low_sum[...].astype(low_side.dtype)
    proj_cot[...] = lax.dot_general(
        high_proj[...], dy_all[...], across, preferred_element_type=jnp.float32
    )
    own_lines = sheet.shape[0] == blocks
    if not own_lines:
        sheet[...] = sheet_in[...]
    for i in range(blocks):
        total = jnp.sum(
            jnp.transpose(grad_sum[i * rows : (i + 1) * rows, :]), axis=0, keepdims=True
        )
        if own_lines:
            sheet[i] = jnp.broadcast_to(total, sheet.shape[1:])
        else:
            sheet[order[i], 0:1, :] = total


def work(order, sheet, block_in, weights, load=0, apart=False):
    width, units = weights[0].shape
    low_width, rank = weights[3].shape[0] * max(load, 1), weights[4].shape[0]
    blocks = len(block_in)
    rows = block_in[0].shape[0] // 2
    inside = pl.BlockSpec(memory_space=pltpu.VMEM)
    loaded = []
    if load:
        shapes = [w.shape for w in weights]
        shapes[3] = (low_width, units)
        loaded = [jax.ShapeDtypeStruct(shape, weights[0].dtype) for shape in shapes]
    tiles = units // 256 if units % 256 == 0 else 1
    lines = (blocks if apart else sheet.shape[0],) + sheet.shape[1:]
    call = pl.pallas_call(
        functools.partial(rows_kernel, blocks, load > 0),
        out_shape=[
            jax.ShapeDtypeStruct(lines, jnp.float32),
            jax.ShapeDtypeStruct((low_width, blocks * rows), jnp.bfloat16),
            jax.ShapeDtypeStruct((rank, blocks * rows), jnp.float32),
        ]
        + loaded,
        in_specs=[pl.BlockSpec(memory_space=pltpu.SMEM)]
        + [inside] * (1 + blocks)
        + [pl.BlockSpec(memory_space=pl.ANY) if load else inside] * len(weights),
        out_specs=[inside] * (3 + len(loaded)),
        scratch_shapes=[
            pltpu.VMEM((blocks * rows, width), jnp.bfloat16),
            pltpu.VMEM((blocks * rows, width), jnp.bfloat16),
            pltpu.VMEM((low_width, blocks * rows), jnp.float32),
            pltpu.VMEM((blocks * rows, 128), jnp.float32),
        ]
        + ([pltpu.SemaphoreType.DMA((3 * tiles + load + 1,))] if load else []),
        compiler_params=pltpu.CompilerParams(
            vmem_limit_bytes=(LOAD_MIB if load else 16) * 1024 * 1024
        ),
        cost_estimate=pl.CostEstimate(
            flops=6 * blocks * rows * width * units,
            bytes_accessed=4 * blocks * rows * width,
            transcendentals=blocks * rows * units,
        ),
    )
    return call(order, sheet, *block_in, *weights)


def outcome_kernel(pieces, order, source, returned, routes, *refs):
    low_in, proj_in = refs[:pieces], refs[pieces : 2 * pieces]
    late = refs[2 * pieces : -2]
    feat, route_grad = refs[-2:]
    rows = returned.shape[2]
    width, rank = low_in[0].shape[0], proj_in[0].shape[0]
    doc_of = lax.broadcasted_iota(jnp.int32, (width, rows), 0) // rank
    total = jnp.zeros(feat.shape, jnp.float32)
    done = 0
    for low_side, proj_cot in zip(low_in, proj_in):
        spread, high_side = [], []
        for i in range(low_side.shape[1] // rows):
            place = slice(i * rows, (i + 1) * rows)
            owner = order[done]
            done += 1
            weight = returned[owner, 1:2, :]
            doc = returned[owner, 2:3, :].astype(jnp.int32)
            high_side.append((weight * proj_cot[:, place]).astype(jnp.bfloat16))
            low = low_side[:, place].astype(jnp.float32)
            spread.append(jnp.where(doc == doc_of, low, 0.0).astype(jnp.bfloat16))
        total += lax.dot_general(
            jnp.concatenate(spread, axis=1),
            jnp.concatenate(high_side, axis=1),
            (((1,), (1,)), ((), ())),
            preferred_element_type=jnp.float32,
        )
    feat[...] = total
    picked = jnp.zeros(route_grad.shape, jnp.float32)
    for e in range(returned.shape[0]):
        picked = jnp.where(routes[...] == e, returned[e, 0:1, :], picked)
    for i in range(len(late)):
        sender = source[source.shape[0] - len(late) + i]
        picked = jnp.where(routes[...] == sender, late[i][0, 0:1, :], picked)
    route_grad[...] = picked


def facts_kernel(routes, combine, doc_ids, out):
    groups, lines, rows = out.shape
    expert = lax.broadcasted_iota(jnp.int32, (groups, rows), 0)
    weight = jnp.zeros((groups, rows), jnp.float32)
    for k in range(routes.shape[0]):
        share = combine[k : k + 1, :].astype(jnp.float32)
        weight += jnp.where(routes[k : k + 1, :] == expert, share, 0.0)
    line = lax.broadcasted_iota(jnp.int32, (lines, rows), 0)
    doc = doc_ids[...].astype(jnp.float32)
    for e in range(groups):
        out[e] = jnp.where(line == 1, weight[e : e + 1, :], doc)


def stack_kernel(top, bottom, out, sems):
    rows = top.shape[0]
    copies = [
        pltpu.make_async_copy(top, out.at[:rows], sems.at[0]),
        pltpu.make_async_copy(bottom, out.at[rows:], sems.at[1]),
    ]
    for copy in copies:
        copy.start()
    for copy in copies:
        copy.wait()


def by_ring(
    tokens, cotangent, routes, combine, doc_ids, w_gate, w_up, w_down, proj_hidden, proj_output
):
    tok_rows, chosen = routes.shape
    groups = lax.axis_size("exp")
    docs_count = max(2, tok_rows * groups // DOC_TOK)
    chips = groups // 2
    half = chips // 2
    ring = list(range(0, chips, 2)) + list(range(chips - 1, 0, -2))
    onward = []
    for place in range(chips):
        onward.append((2 * ring[place], 2 * ring[(place + 1) % chips]))
        onward.append((2 * ring[place] + 1, 2 * ring[place - 1] + 1))
    across = [(i, i ^ 1) for i in range(groups)]

    def hop(block):
        return lax.ppermute(block, "exp", onward)

    def swap(block):
        return lax.ppermute(block, "exp", across)

    arrivals = [(c, step) for step in range(1, half + 1) for c in ("ab" if step < half else "a")]
    jobs = [[("a", 0, False), ("a", 0, True)]]
    for i, (c, step) in enumerate(arrivals):
        job = [(c, step, False)]
        if i > 0:
            job.append(arrivals[i - 1] + (True,))
        if i == 1:
            job.append(arrivals[0] + (False,))
        if i != 0:
            jobs.append(job)
    jobs.append([arrivals[-1] + (True,)])
    blocks_of = [block for job in jobs for block in job]

    orders = np.zeros((groups, 2 * groups), np.int32)
    for place in range(chips):
        for core in range(2):
            me = 2 * ring[place] + core
            for i, (c, step, handed) in enumerate(blocks_of):
                first = core if (c == "a") != handed else 1 - core
                way = (1 if core == 1 else -1) * (-1 if handed else 1)
                owner = 2 * ring[(place + way * step) % chips] + first
                orders[me, i] = owner
                orders[owner, groups + i] = me
    mine = lax.dynamic_index_in_dim(
        jnp.asarray(orders), lax.axis_index("exp"), axis=0, keepdims=False
    )
    order, source = mine[:groups], mine[groups:]

    rows, width = tokens.shape
    own = pl.pallas_call(
        stack_kernel,
        out_shape=jax.ShapeDtypeStruct((2 * rows, width), tokens.dtype),
        in_specs=[pl.BlockSpec(memory_space=pltpu.HBM)] * 2,
        out_specs=pl.BlockSpec(memory_space=pltpu.VMEM),
        scratch_shapes=[pltpu.SemaphoreType.DMA((2,))],
    )(tokens, cotangent)
    beside = swap(own)

    sheet = pl.pallas_call(
        facts_kernel,
        out_shape=jax.ShapeDtypeStruct((groups, 8, rows), jnp.float32),
        in_specs=[pl.BlockSpec(memory_space=pltpu.VMEM)] * 3,
        out_specs=pl.BlockSpec(memory_space=pltpu.VMEM),
    )(routes.T, combine.T, doc_ids[None, :])
    inside = pl.BlockSpec(memory_space=pltpu.VMEM)
    given = (w_gate[0], w_up[0], w_down[0], proj_hidden[0].T, proj_output[0].T)
    weights = None
    lows, projs, done = [], [], 0
    held = {("a", 0, False): own, ("a", 0, True): beside}

    def take(apart=False):
        nonlocal sheet, weights, done
        job = jobs.pop(0)
        share, blocks = order[done : done + len(job)], [held[name] for name in job]
        if weights is None:
            lines, low_side, proj_cot, *weights = work(
                share, sheet, blocks, given, load=docs_count
            )
        else:
            lines, low_side, proj_cot = work(share, sheet, blocks, weights, apart=apart)
        lows.append(low_side)
        projs.append(proj_cot)
        done += len(job)
        if not apart:
            sheet = lines
            return low_side
        for i in range(len(job)):
            spot = done - len(job) + i
            back = [(d, int(orders[d, spot])) for d in range(groups)]
            late.append(lax.ppermute(lines[i : i + 1], "exp", back))
        return low_side

    def tie(one, other):
        return lax.optimization_barrier((one, other))

    late = []
    chain = {"a": own, "b": beside}
    for i, (c, step) in enumerate(arrivals):
        block = hop(chain[c])
        if i != 1:
            lows[-1:], block = tie([take(apart=i == len(arrivals) - 1)], block)
        if i == len(arrivals) - 1:
            returned, block = tie(returned, block)
        chain[c] = held[(c, step, False)] = block
        held[(c, step, True)] = swap(block)
        if i == len(arrivals) - 2:
            returned = lax.all_to_all(sheet, "exp", split_axis=0, concat_axis=0, tiled=True)
    while jobs:
        take(apart=True)
    rank = proj_output.shape[2]
    feature, route_grad = pl.pallas_call(
        functools.partial(outcome_kernel, len(lows)),
        out_shape=[
            jax.ShapeDtypeStruct((docs_count * rank, rank), jnp.float32),
            jax.ShapeDtypeStruct((chosen, tok_rows), jnp.float32),
        ],
        in_specs=[pl.BlockSpec(memory_space=pltpu.SMEM)] * 2
        + [inside] * (2 + 2 * len(lows) + len(late)),
        out_specs=[inside] * 2,
        compiler_params=pltpu.CompilerParams(vmem_limit_bytes=16 * 1024 * 1024),
    )(order, source, returned, routes.T, *lows, *projs, *late)
    return feature.reshape(docs_count, 1, rank, rank), route_grad.T


def by_routing(
    tokens, cotangent, routes, combine, doc_ids, w_gate, w_up, w_down, proj_hidden, proj_output
):
    tok_rows, chosen = routes.shape
    local_count = w_gate.shape[0]
    groups = lax.axis_size("exp")
    experts = local_count * groups
    capacity = max(2, tok_rows * chosen * 5 // (4 * experts))
    docs_count = max(2, tok_rows * groups // DOC_TOK)
    entries = tok_rows * chosen
    width = tokens.shape[1]
    flat_routes = routes.reshape(-1)
    member = (flat_routes[:, None] == jnp.arange(experts, dtype=jnp.int32)[None, :]).astype(
        jnp.int32
    )
    slot_rank = jnp.sum((jnp.cumsum(member, axis=0) - 1) * member, axis=1)
    position = flat_routes * capacity + slot_rank
    source = (
        jnp.full((experts * capacity,), -1, jnp.int32)
        .at[position]
        .set(jnp.arange(entries, dtype=jnp.int32))
    )
    filled = source >= 0
    safe_source = jnp.maximum(source, 0)
    token_of = safe_source // chosen
    send_x = jnp.where(filled[:, None], tokens[token_of], 0)
    send_dy = jnp.where(filled[:, None], cotangent[token_of], 0)
    send_w = jnp.where(filled, combine.reshape(-1)[safe_source], 0)
    send_doc = jnp.where(filled, doc_ids[token_of], -1).astype(jnp.bfloat16)

    def exchange(array):
        array = array.reshape((groups, local_count, capacity) + array.shape[1:])
        return lax.all_to_all(array, "exp", split_axis=0, concat_axis=0, tiled=True)

    recv_x, recv_dy, recv_w, recv_doc = (
        exchange(send_x),
        exchange(send_dy),
        exchange(send_w),
        exchange(send_doc),
    )
    slots = groups * capacity
    grads, feats = [], []
    for e in range(local_count):
        hidden = swiglu(recv_x[:, e].reshape(slots, width), w_gate[e], w_up[e])
        grad, feature = finish(
            hidden,
            recv_dy[:, e].reshape(slots, width),
            recv_w[:, e].reshape(slots),
            recv_doc[:, e].reshape(slots),
            w_down[e],
            proj_hidden[e],
            proj_output[e],
            docs_count,
        )
        grads.append(grad.reshape(groups, capacity))
        feats.append(feature)
    slot_grad = jnp.stack(grads, axis=1)
    returned = lax.all_to_all(slot_grad, "exp", split_axis=0, concat_axis=0, tiled=True)
    route_grad = returned.reshape(-1)[position].reshape(tok_rows, chosen)
    return jnp.stack(feats, axis=1), route_grad


def on_device(tokens, cotangent, routes, combine, doc_ids, w_gate, *rest):
    tok_rows, chosen = routes.shape
    experts = w_gate.shape[0] * lax.axis_size("exp")
    dense = w_gate.shape[0] == 1 and 4 * chosen >= experts and experts >= 8 and experts % 4 == 0
    plan = by_ring if dense else by_routing
    return plan(tokens, cotangent, routes, combine, doc_ids, w_gate, *rest)


def solution(mesh):
    placed = (
        P(("grp", "exp"), None),
        P(("grp", "exp"), None),
        P(("grp", "exp"), None),
        P(("grp", "exp"), None),
        P(("grp", "exp")),
        P("exp", None, None),
        P("exp", None, None),
        P("exp", None, None),
        P("exp", None, None),
        P("exp", None, None),
    )
    return jax.shard_map(
        on_device,
        mesh=mesh,
        in_specs=placed,
        out_specs=(P("grp", "exp", None, None), P(("grp", "exp"), None)),
        check_vma=False,
    )
```

```python
import functools

import jax
import jax.numpy as jnp
from jax import lax
from jax.experimental import pallas as pl
from jax.experimental.pallas import tpu as pltpu
from jax.sharding import PartitionSpec as P

DOC_TOK = 512
LOAD_MIB = 40


def swiglu(rows, w_gate, w_up):
    gate_val = jnp.dot(rows, w_gate, preferred_element_type=jnp.float32)
    up_val = jnp.dot(rows, w_up, preferred_element_type=jnp.float32)
    return (jax.nn.silu(gate_val) * up_val).astype(jnp.bfloat16)


def finish(hidden, rows_dy, rows_w, rows_doc, w_down, proj_hidden, proj_output, docs_count):
    out_val = jnp.dot(hidden, w_down, preferred_element_type=jnp.float32)
    grad = jnp.sum(rows_dy.astype(jnp.float32) * out_val, axis=-1)
    low_side = jnp.dot(hidden, proj_hidden, preferred_element_type=jnp.float32).astype(
        jnp.bfloat16
    )
    proj_cot = jnp.dot(rows_dy, proj_output, preferred_element_type=jnp.float32)
    high_side = (rows_w.astype(jnp.float32)[:, None] * proj_cot).astype(jnp.bfloat16)
    doc_table = jnp.arange(docs_count, dtype=jnp.int32).astype(jnp.bfloat16)
    onehot = (rows_doc[:, None] == doc_table).astype(jnp.bfloat16)
    spread = onehot[:, :, None] * low_side[:, None, :]
    spread = spread.reshape(spread.shape[0], -1)
    feature = lax.dot_general(
        spread, high_side, (((0,), (0,)), ((), ())), preferred_element_type=jnp.float32
    )
    return grad, feature.reshape(docs_count, low_side.shape[1], high_side.shape[1])


def block_owner(name, chips):
    chain, step, handed = name
    me = lax.axis_index("exp")
    core, chip = lax.rem(me, 2), lax.div(me, 2)
    turn = chips // 2
    place = jnp.where(lax.rem(chip, 2) == 0, lax.div(chip, 2), chips - 1 - lax.div(chip, 2))
    way = 2 * core - 1
    place = place + (-way if handed else way) * step
    place = lax.rem(place + chips, chips)
    chip = jnp.where(place < turn, 2 * place, 2 * (chips - 1 - place) + 1)
    return 2 * chip + (core if (chain == "a") != handed else 1 - core)


def rows_kernel(names, load, *refs):
    blocks = len(names)
    sheet_in, block_in = refs[0], refs[1 : 1 + blocks]
    given = refs[1 + blocks : 6 + blocks]
    sheet, low_side, proj_cot = refs[6 + blocks : 9 + blocks]
    x_all, dy_all, low_sum, grad_sum = refs[-5:-1] if load else refs[-4:]
    w_gate, w_up, w_down, low_proj, high_proj = refs[9 + blocks : 14 + blocks] if load else given
    rows = block_in[0].shape[0] // 2
    across = (((1,), (1,)), ((), ()))
    units = w_gate.shape[1]
    tile = 256 if units % 256 == 0 else units
    tiles = units // tile
    lanes = grad_sum.shape[1]
    copies = []
    if load:
        rank = given[3].shape[0]
        for j in range(tiles):
            part = pl.ds(j * tile, tile)
            copies.append((given[0].at[:, part], w_gate.at[:, part]))
            copies.append((given[1].at[:, part], w_up.at[:, part]))
            copies.append((given[2].at[part, :], w_down.at[part, :]))
        for i in range(low_proj.shape[0] // rank):
            copies.append((given[3], low_proj.at[pl.ds(i * rank, rank), :]))
        copies.append((given[4], high_proj))
        copies = [
            pltpu.make_async_copy(src, dst, refs[-1].at[i]) for i, (src, dst) in enumerate(copies)
        ]
        for copy in copies[3 * tiles :] + copies[: 3 * tiles]:
            copy.start()
    for i in range(blocks):
        x_all[i * rows : (i + 1) * rows, :] = block_in[i][:rows, :]
        dy_all[i * rows : (i + 1) * rows, :] = block_in[i][rows:, :]
    low_sum[...] = jnp.zeros_like(low_sum)
    grad_sum[...] = jnp.zeros_like(grad_sum)

    def one_tile(j):
        part = pl.ds(j * tile, tile)
        gate_val = jnp.dot(x_all[...], w_gate[:, part], preferred_element_type=jnp.float32)
        up_val = jnp.dot(x_all[...], w_up[:, part], preferred_element_type=jnp.float32)
        hidden = (jax.nn.silu(gate_val) * up_val).astype(jnp.bfloat16)
        back = lax.dot_general(
            dy_all[...], w_down[part, :], across, preferred_element_type=jnp.float32
        )
        terms = hidden.astype(jnp.float32) * back
        for cut in range(0, tile, lanes):
            grad_sum[...] += terms[:, cut : cut + lanes]
        low_sum[...] += lax.dot_general(
            low_proj[:, part], hidden, across, preferred_element_type=jnp.float32
        )

    for copy in copies[3 * tiles :]:
        copy.wait()
    for j in range(tiles):
        for copy in copies[3 * j : 3 * j + 3] if load else []:
            copy.wait()
        one_tile(j)

    low_side[...] = low_sum[...].astype(low_side.dtype)
    proj_cot[...] = lax.dot_general(
        high_proj[...], dy_all[...], across, preferred_element_type=jnp.float32
    )
    sheet[...] = sheet_in[...]
    for i in range(blocks):
        total = jnp.sum(
            jnp.transpose(grad_sum[i * rows : (i + 1) * rows, :]), axis=0, keepdims=True
        )
        sheet[block_owner(names[i], sheet.shape[0] // 2), 0:1, :] = total


def work(names, sheet, block_in, weights, load=0):
    width, units = weights[0].shape
    low_width, rank = weights[3].shape[0] * max(load, 1), weights[4].shape[0]
    blocks = len(block_in)
    rows = block_in[0].shape[0] // 2
    inside = pl.BlockSpec(memory_space=pltpu.VMEM)
    loaded = []
    if load:
        shapes = [w.shape for w in weights]
        shapes[3] = (low_width, units)
        loaded = [jax.ShapeDtypeStruct(shape, weights[0].dtype) for shape in shapes]
    tiles = units // 256 if units % 256 == 0 else 1
    call = pl.pallas_call(
        functools.partial(rows_kernel, names, load > 0),
        out_shape=[
            jax.ShapeDtypeStruct(sheet.shape, jnp.float32),
            jax.ShapeDtypeStruct((low_width, blocks * rows), jnp.bfloat16),
            jax.ShapeDtypeStruct((rank, blocks * rows), jnp.float32),
        ]
        + loaded,
        in_specs=[inside] * (1 + blocks)
        + [pl.BlockSpec(memory_space=pl.ANY) if load else inside] * len(weights),
        out_specs=[inside] * (3 + len(loaded)),
        scratch_shapes=[
            pltpu.VMEM((blocks * rows, width), jnp.bfloat16),
            pltpu.VMEM((blocks * rows, width), jnp.bfloat16),
            pltpu.VMEM((low_width, blocks * rows), jnp.float32),
            pltpu.VMEM((blocks * rows, 128), jnp.float32),
        ]
        + ([pltpu.SemaphoreType.DMA((3 * tiles + load + 1,))] if load else []),
        compiler_params=pltpu.CompilerParams(
            vmem_limit_bytes=(LOAD_MIB if load else 16) * 1024 * 1024
        ),
        cost_estimate=pl.CostEstimate(
            flops=6 * blocks * rows * width * units,
            bytes_accessed=4 * blocks * rows * width,
            transcendentals=blocks * rows * units,
        ),
    )
    return call(sheet, *block_in, *weights)


def outcome_kernel(jobs, returned, routes, *refs):
    low_in, proj_in = refs[: len(jobs)], refs[len(jobs) : 2 * len(jobs)]
    feat, route_grad = refs[-2:]
    rows = returned.shape[2]
    width, rank = low_in[0].shape[0], proj_in[0].shape[0]
    doc_of = lax.broadcasted_iota(jnp.int32, (width, rows), 0) // rank
    total = jnp.zeros(feat.shape, jnp.float32)
    for names, low_side, proj_cot in zip(jobs, low_in, proj_in):
        spread, high_side = [], []
        for i, name in enumerate(names):
            place = slice(i * rows, (i + 1) * rows)
            owner = block_owner(name, returned.shape[0] // 2)
            weight = returned[owner, 1:2, :]
            doc = returned[owner, 2:3, :].astype(jnp.int32)
            high_side.append((weight * proj_cot[:, place]).astype(jnp.bfloat16))
            low = low_side[:, place].astype(jnp.float32)
            spread.append(jnp.where(doc == doc_of, low, 0.0).astype(jnp.bfloat16))
        total += lax.dot_general(
            jnp.concatenate(spread, axis=1),
            jnp.concatenate(high_side, axis=1),
            (((1,), (1,)), ((), ())),
            preferred_element_type=jnp.float32,
        )
    feat[...] = total
    picked = jnp.zeros(route_grad.shape, jnp.float32)
    for e in range(returned.shape[0]):
        picked = jnp.where(routes[...] == e, returned[e, 0:1, :], picked)
    route_grad[...] = picked


def facts_kernel(routes, combine, doc_ids, out):
    groups, lines, rows = out.shape
    expert = lax.broadcasted_iota(jnp.int32, (groups, rows), 0)
    weight = jnp.zeros((groups, rows), jnp.float32)
    for k in range(routes.shape[0]):
        share = combine[k : k + 1, :].astype(jnp.float32)
        weight += jnp.where(routes[k : k + 1, :] == expert, share, 0.0)
    line = lax.broadcasted_iota(jnp.int32, (lines, rows), 0)
    doc = doc_ids[...].astype(jnp.float32)
    for e in range(groups):
        out[e] = jnp.where(line == 1, weight[e : e + 1, :], doc)


def stack_kernel(top, bottom, out, sems):
    rows = top.shape[0]
    copies = [
        pltpu.make_async_copy(top, out.at[:rows], sems.at[0]),
        pltpu.make_async_copy(bottom, out.at[rows:], sems.at[1]),
    ]
    for copy in copies:
        copy.start()
    for copy in copies:
        copy.wait()


def by_ring(
    tokens, cotangent, routes, combine, doc_ids, w_gate, w_up, w_down, proj_hidden, proj_output
):
    tok_rows, chosen = routes.shape
    groups = lax.axis_size("exp")
    docs_count = max(2, tok_rows * groups // DOC_TOK)
    chips = groups // 2
    half = chips // 2
    ring = list(range(0, chips, 2)) + list(range(chips - 1, 0, -2))
    onward = []
    for place in range(chips):
        onward.append((2 * ring[place], 2 * ring[(place + 1) % chips]))
        onward.append((2 * ring[place] + 1, 2 * ring[place - 1] + 1))
    across = [(i, i ^ 1) for i in range(groups)]

    def hop(block):
        return lax.ppermute(block, "exp", onward)

    def swap(block):
        return lax.ppermute(block, "exp", across)

    arrivals = [(c, step) for step in range(1, half + 1) for c in ("ab" if step < half else "a")]
    jobs = [(("a", 0, False), ("a", 0, True))]
    for i, (c, step) in enumerate(arrivals):
        job = ((c, step, False),)
        if i > 0:
            job += (arrivals[i - 1] + (True,),)
        if i == 1:
            job += (arrivals[0] + (False,),)
        if i != 0:
            jobs.append(job)
    jobs.append((arrivals[-1] + (True,),))

    rows, width = tokens.shape
    own = pl.pallas_call(
        stack_kernel,
        out_shape=jax.ShapeDtypeStruct((2 * rows, width), tokens.dtype),
        in_specs=[pl.BlockSpec(memory_space=pltpu.HBM)] * 2,
        out_specs=pl.BlockSpec(memory_space=pltpu.VMEM),
        scratch_shapes=[pltpu.SemaphoreType.DMA((2,))],
    )(tokens, cotangent)
    beside = swap(own)

    sheet = pl.pallas_call(
        facts_kernel,
        out_shape=jax.ShapeDtypeStruct((groups, 8, rows), jnp.float32),
        in_specs=[pl.BlockSpec(memory_space=pltpu.VMEM)] * 3,
        out_specs=pl.BlockSpec(memory_space=pltpu.VMEM),
        compiler_params=pltpu.CompilerParams(vmem_limit_bytes=8 * 1024 * 1024),
    )(routes.T, combine.T, doc_ids[None, :])
    inside = pl.BlockSpec(memory_space=pltpu.VMEM)
    given = (w_gate[0], w_up[0], w_down[0], proj_hidden[0].T, proj_output[0].T)
    weights = None
    lows, projs = [], []
    held = {("a", 0, False): own, ("a", 0, True): beside}
    todo = list(jobs)

    def take():
        nonlocal sheet, weights
        names = todo.pop(0)
        blocks = [held[name] for name in names]
        if weights is None:
            sheet, low_side, proj_cot, *weights = work(
                names, sheet, blocks, given, load=docs_count
            )
        else:
            sheet, low_side, proj_cot = work(names, sheet, blocks, weights)
        lows.append(low_side)
        projs.append(proj_cot)

    chain = {"a": own, "b": beside}
    for i, (c, step) in enumerate(arrivals):
        block = hop(chain[c])
        if i != 1:
            take()
            sheet, block = lax.optimization_barrier((sheet, block))
        chain[c] = held[(c, step, False)] = block
        held[(c, step, True)] = swap(block)
    while todo:
        take()
    returned = lax.all_to_all(sheet, "exp", split_axis=0, concat_axis=0, tiled=True)
    rank = proj_output.shape[2]
    feature, route_grad = pl.pallas_call(
        functools.partial(outcome_kernel, jobs),
        out_shape=[
            jax.ShapeDtypeStruct((docs_count * rank, rank), jnp.float32),
            jax.ShapeDtypeStruct((chosen, tok_rows), jnp.float32),
        ],
        in_specs=[inside] * (2 + 2 * len(lows)),
        out_specs=[inside] * 2,
        compiler_params=pltpu.CompilerParams(vmem_limit_bytes=16 * 1024 * 1024),
    )(returned, routes.T, *lows, *projs)
    return feature.reshape(docs_count, 1, rank, rank), route_grad.T


def by_routing(
    tokens, cotangent, routes, combine, doc_ids, w_gate, w_up, w_down, proj_hidden, proj_output
):
    tok_rows, chosen = routes.shape
    local_count = w_gate.shape[0]
    groups = lax.axis_size("exp")
    experts = local_count * groups
    capacity = max(2, tok_rows * chosen * 5 // (4 * experts))
    docs_count = max(2, tok_rows * groups // DOC_TOK)
    entries = tok_rows * chosen
    width = tokens.shape[1]
    flat_routes = routes.reshape(-1)
    member = (flat_routes[:, None] == jnp.arange(experts, dtype=jnp.int32)[None, :]).astype(
        jnp.int32
    )
    slot_rank = jnp.sum((jnp.cumsum(member, axis=0) - 1) * member, axis=1)
    position = flat_routes * capacity + slot_rank
    source = (
        jnp.full((experts * capacity,), -1, jnp.int32)
        .at[position]
        .set(jnp.arange(entries, dtype=jnp.int32))
    )
    filled = source >= 0
    safe_source = jnp.maximum(source, 0)
    token_of = safe_source // chosen
    send_x = jnp.where(filled[:, None], tokens[token_of], 0)
    send_dy = jnp.where(filled[:, None], cotangent[token_of], 0)
    send_w = jnp.where(filled, combine.reshape(-1)[safe_source], 0)
    send_doc = jnp.where(filled, doc_ids[token_of], -1).astype(jnp.bfloat16)

    def exchange(array):
        array = array.reshape((groups, local_count, capacity) + array.shape[1:])
        return lax.all_to_all(array, "exp", split_axis=0, concat_axis=0, tiled=True)

    recv_x, recv_dy, recv_w, recv_doc = (
        exchange(send_x),
        exchange(send_dy),
        exchange(send_w),
        exchange(send_doc),
    )
    slots = groups * capacity
    grads, feats = [], []
    for e in range(local_count):
        hidden = swiglu(recv_x[:, e].reshape(slots, width), w_gate[e], w_up[e])
        grad, feature = finish(
            hidden,
            recv_dy[:, e].reshape(slots, width),
            recv_w[:, e].reshape(slots),
            recv_doc[:, e].reshape(slots),
            w_down[e],
            proj_hidden[e],
            proj_output[e],
            docs_count,
        )
        grads.append(grad.reshape(groups, capacity))
        feats.append(feature)
    slot_grad = jnp.stack(grads, axis=1)
    returned = lax.all_to_all(slot_grad, "exp", split_axis=0, concat_axis=0, tiled=True)
    route_grad = returned.reshape(-1)[position].reshape(tok_rows, chosen)
    return jnp.stack(feats, axis=1), route_grad


def on_device(tokens, cotangent, routes, combine, doc_ids, w_gate, *rest):
    tok_rows, chosen = routes.shape
    experts = w_gate.shape[0] * lax.axis_size("exp")
    dense = w_gate.shape[0] == 1 and 4 * chosen >= experts and experts >= 8 and experts % 4 == 0
    plan = by_ring if dense else by_routing
    return plan(tokens, cotangent, routes, combine, doc_ids, w_gate, *rest)


def solution(mesh):
    placed = (
        P(("grp", "exp"), None),
        P(("grp", "exp"), None),
        P(("grp", "exp"), None),
        P(("grp", "exp"), None),
        P(("grp", "exp")),
        P("exp", None, None),
        P("exp", None, None),
        P("exp", None, None),
        P("exp", None, None),
        P("exp", None, None),
    )
    return jax.shard_map(
        on_device,
        mesh=mesh,
        in_specs=placed,
        out_specs=(P("grp", "exp", None, None), P(("grp", "exp"), None)),
        check_vma=False,
    )
```

```python
import functools

import jax
import jax.numpy as jnp
from jax import lax
from jax.experimental import pallas as pl
from jax.experimental.pallas import tpu as pltpu
from jax.sharding import PartitionSpec as P

DOC_TOK = 512
LOAD_MIB = 40


def swiglu(rows, w_gate, w_up):
    gate_val = jnp.dot(rows, w_gate, preferred_element_type=jnp.float32)
    up_val = jnp.dot(rows, w_up, preferred_element_type=jnp.float32)
    return (jax.nn.silu(gate_val) * up_val).astype(jnp.bfloat16)


def finish(hidden, rows_dy, rows_w, rows_doc, w_down, proj_hidden, proj_output, docs_count):
    out_val = jnp.dot(hidden, w_down, preferred_element_type=jnp.float32)
    grad = jnp.sum(rows_dy.astype(jnp.float32) * out_val, axis=-1)
    low_side = jnp.dot(hidden, proj_hidden, preferred_element_type=jnp.float32).astype(
        jnp.bfloat16
    )
    proj_cot = jnp.dot(rows_dy, proj_output, preferred_element_type=jnp.float32)
    high_side = (rows_w.astype(jnp.float32)[:, None] * proj_cot).astype(jnp.bfloat16)
    doc_table = jnp.arange(docs_count, dtype=jnp.int32).astype(jnp.bfloat16)
    onehot = (rows_doc[:, None] == doc_table).astype(jnp.bfloat16)
    spread = onehot[:, :, None] * low_side[:, None, :]
    spread = spread.reshape(spread.shape[0], -1)
    feature = lax.dot_general(
        spread, high_side, (((0,), (0,)), ((), ())), preferred_element_type=jnp.float32
    )
    return grad, feature.reshape(docs_count, low_side.shape[1], high_side.shape[1])


def block_owner(name, chips):
    chain, step, handed = name
    me = lax.axis_index("exp")
    core, chip = lax.rem(me, 2), lax.div(me, 2)
    turn = chips // 2
    place = jnp.where(lax.rem(chip, 2) == 0, lax.div(chip, 2), chips - 1 - lax.div(chip, 2))
    way = 2 * core - 1
    place = place + (-way if handed else way) * step
    place = lax.rem(place + chips, chips)
    chip = jnp.where(place < turn, 2 * place, 2 * (chips - 1 - place) + 1)
    return 2 * chip + (core if (chain == "a") != handed else 1 - core)


def rows_kernel(names, load, *refs):
    blocks = len(names)
    apart = refs[1:3] if load else ()
    refs = refs[:1] + refs[3:] if load else refs
    whole = blocks - 1 if load else blocks
    sheet_in, block_in = refs[0], refs[1 : 1 + whole]
    given = refs[1 + whole : 6 + whole]
    sheet, low_side, proj_cot = refs[6 + whole : 9 + whole]
    x_all, dy_all, low_sum, grad_sum = refs[-5:-1] if load else refs[-4:]
    w_gate, w_up, w_down, low_proj, high_proj = refs[9 + whole : 14 + whole] if load else given
    rows = x_all.shape[0] // blocks
    across = (((1,), (1,)), ((), ()))
    units = w_gate.shape[1]
    tile = 256 if units % 256 == 0 else units
    tiles = units // tile
    lanes = grad_sum.shape[1]
    copies = []
    if load:
        rank = given[3].shape[0]
        for j in range(tiles):
            part = pl.ds(j * tile, tile)
            copies.append((given[0].at[:, part], w_gate.at[:, part]))
            copies.append((given[1].at[:, part], w_up.at[:, part]))
            copies.append((given[2].at[part, :], w_down.at[part, :]))
        for i in range(low_proj.shape[0] // rank):
            copies.append((given[3], low_proj.at[pl.ds(i * rank, rank), :]))
        copies.append((given[4], high_proj))
        copies.append((apart[0], x_all.at[:rows]))
        copies.append((apart[1], dy_all.at[:rows]))
        copies = [
            pltpu.make_async_copy(src, dst, refs[-1].at[i]) for i, (src, dst) in enumerate(copies)
        ]
        for copy in copies[3 * tiles :] + copies[: 3 * tiles]:
            copy.start()
    for i, block in enumerate(block_in):
        place = slice((blocks - whole + i) * rows, (blocks - whole + i + 1) * rows)
        x_all[place, :] = block[:rows, :]
        dy_all[place, :] = block[rows:, :]
    low_sum[...] = jnp.zeros_like(low_sum)
    grad_sum[...] = jnp.zeros_like(grad_sum)

    def one_tile(j):
        part = pl.ds(j * tile, tile)
        gate_val = jnp.dot(x_all[...], w_gate[:, part], preferred_element_type=jnp.float32)
        up_val = jnp.dot(x_all[...], w_up[:, part], preferred_element_type=jnp.float32)
        hidden = (jax.nn.silu(gate_val) * up_val).astype(jnp.bfloat16)
        back = lax.dot_general(
            dy_all[...], w_down[part, :], across, preferred_element_type=jnp.float32
        )
        terms = hidden.astype(jnp.float32) * back
        for cut in range(0, tile, lanes):
            grad_sum[...] += terms[:, cut : cut + lanes]
        low_sum[...] += lax.dot_general(
            low_proj[:, part], hidden, across, preferred_element_type=jnp.float32
        )

    for copy in copies[3 * tiles :]:
        copy.wait()
    for j in range(tiles):
        for copy in copies[3 * j : 3 * j + 3] if load else []:
            copy.wait()
        one_tile(j)

    low_side[...] = low_sum[...].astype(low_side.dtype)
    proj_cot[...] = lax.dot_general(
        high_proj[...], dy_all[...], across, preferred_element_type=jnp.float32
    )
    sheet[...] = sheet_in[...]
    for i in range(blocks):
        total = jnp.sum(
            jnp.transpose(grad_sum[i * rows : (i + 1) * rows, :]), axis=0, keepdims=True
        )
        sheet[block_owner(names[i], sheet.shape[0] // 2), 0:1, :] = total


def work(names, sheet, block_in, weights, apart=(), load=0):
    width, units = weights[0].shape
    low_width, rank = weights[3].shape[0] * max(load, 1), weights[4].shape[0]
    blocks = len(names)
    rows = block_in[0].shape[0] // 2
    inside = pl.BlockSpec(memory_space=pltpu.VMEM)
    loaded = []
    if load:
        shapes = [w.shape for w in weights]
        shapes[3] = (low_width, units)
        loaded = [jax.ShapeDtypeStruct(shape, weights[0].dtype) for shape in shapes]
    tiles = units // 256 if units % 256 == 0 else 1
    call = pl.pallas_call(
        functools.partial(rows_kernel, names, load > 0),
        out_shape=[
            jax.ShapeDtypeStruct(sheet.shape, jnp.float32),
            jax.ShapeDtypeStruct((low_width, blocks * rows), jnp.bfloat16),
            jax.ShapeDtypeStruct((rank, blocks * rows), jnp.float32),
        ]
        + loaded,
        in_specs=[inside]
        + [pl.BlockSpec(memory_space=pl.ANY)] * len(apart)
        + [inside] * len(block_in)
        + [pl.BlockSpec(memory_space=pl.ANY) if load else inside] * len(weights),
        out_specs=[inside] * (3 + len(loaded)),
        scratch_shapes=[
            pltpu.VMEM((blocks * rows, width), jnp.bfloat16),
            pltpu.VMEM((blocks * rows, width), jnp.bfloat16),
            pltpu.VMEM((low_width, blocks * rows), jnp.float32),
            pltpu.VMEM((blocks * rows, 128), jnp.float32),
        ]
        + ([pltpu.SemaphoreType.DMA((3 * tiles + load + 3,))] if load else []),
        compiler_params=pltpu.CompilerParams(
            vmem_limit_bytes=(LOAD_MIB if load else 16) * 1024 * 1024
        ),
        cost_estimate=pl.CostEstimate(
            flops=6 * blocks * rows * width * units,
            bytes_accessed=4 * blocks * rows * width,
            transcendentals=blocks * rows * units,
        ),
    )
    return call(sheet, *apart, *block_in, *weights)


def outcome_kernel(jobs, returned, routes, *refs):
    low_in, proj_in = refs[: len(jobs)], refs[len(jobs) : 2 * len(jobs)]
    feat, route_grad = refs[-2:]
    rows = returned.shape[2]
    width, rank = low_in[0].shape[0], proj_in[0].shape[0]
    doc_of = lax.broadcasted_iota(jnp.int32, (width, rows), 0) // rank
    total = jnp.zeros(feat.shape, jnp.float32)
    for names, low_side, proj_cot in zip(jobs, low_in, proj_in):
        spread, high_side = [], []
        for i, name in enumerate(names):
            place = slice(i * rows, (i + 1) * rows)
            owner = block_owner(name, returned.shape[0] // 2)
            weight = returned[owner, 1:2, :]
            doc = returned[owner, 2:3, :].astype(jnp.int32)
            high_side.append((weight * proj_cot[:, place]).astype(jnp.bfloat16))
            low = low_side[:, place].astype(jnp.float32)
            spread.append(jnp.where(doc == doc_of, low, 0.0).astype(jnp.bfloat16))
        total += lax.dot_general(
            jnp.concatenate(spread, axis=1),
            jnp.concatenate(high_side, axis=1),
            (((1,), (1,)), ((), ())),
            preferred_element_type=jnp.float32,
        )
    feat[...] = total
    picked = jnp.zeros(route_grad.shape, jnp.float32)
    for e in range(returned.shape[0]):
        picked = jnp.where(routes[...] == e, returned[e, 0:1, :], picked)
    route_grad[...] = picked


def facts_kernel(routes, combine, doc_ids, out):
    groups, lines, rows = out.shape
    expert = lax.broadcasted_iota(jnp.int32, (groups, rows), 0)
    weight = jnp.zeros((groups, rows), jnp.float32)
    for k in range(routes.shape[0]):
        share = combine[k : k + 1, :].astype(jnp.float32)
        weight += jnp.where(routes[k : k + 1, :] == expert, share, 0.0)
    line = lax.broadcasted_iota(jnp.int32, (lines, rows), 0)
    doc = doc_ids[...].astype(jnp.float32)
    for e in range(groups):
        out[e] = jnp.where(line == 1, weight[e : e + 1, :], doc)


def stack_kernel(top, bottom, out):
    rows = top.shape[0]
    out[:rows, :] = top[...]
    out[rows:, :] = bottom[...]


def stack(top, bottom):
    inside = pl.BlockSpec(memory_space=pltpu.VMEM)
    return pl.pallas_call(
        stack_kernel,
        out_shape=jax.ShapeDtypeStruct((2 * top.shape[0], top.shape[1]), top.dtype),
        in_specs=[inside] * 2,
        out_specs=inside,
        compiler_params=pltpu.CompilerParams(vmem_limit_bytes=8 * 1024 * 1024),
    )(top, bottom)


def by_ring(
    tokens, cotangent, routes, combine, doc_ids, w_gate, w_up, w_down, proj_hidden, proj_output
):
    tok_rows, chosen = routes.shape
    groups = lax.axis_size("exp")
    docs_count = max(2, tok_rows * groups // DOC_TOK)
    chips = groups // 2
    half = chips // 2
    ring = list(range(0, chips, 2)) + list(range(chips - 1, 0, -2))
    onward = []
    for place in range(chips):
        onward.append((2 * ring[place], 2 * ring[(place + 1) % chips]))
        onward.append((2 * ring[place] + 1, 2 * ring[place - 1] + 1))
    across = [(i, i ^ 1) for i in range(groups)]

    def hop(block):
        return lax.ppermute(block, "exp", onward)

    def swap(block):
        return lax.ppermute(block, "exp", across)

    arrivals = [(c, step) for step in range(1, half + 1) for c in ("ab" if step < half else "a")]
    jobs = [(("a", 0, False), ("a", 0, True))]
    for i, (c, step) in enumerate(arrivals):
        job = ((c, step, False),)
        if i > 0:
            job += (arrivals[i - 1] + (True,),)
        if i == 1:
            job += (arrivals[0] + (False,),)
        if i != 0:
            jobs.append(job)
    jobs.append((arrivals[-1] + (True,),))

    sheet = pl.pallas_call(
        facts_kernel,
        out_shape=jax.ShapeDtypeStruct((groups, 8, tok_rows), jnp.float32),
        in_specs=[pl.BlockSpec(memory_space=pltpu.VMEM)] * 3,
        out_specs=pl.BlockSpec(memory_space=pltpu.VMEM),
        compiler_params=pltpu.CompilerParams(vmem_limit_bytes=8 * 1024 * 1024),
    )(routes.T, combine.T, doc_ids[None, :])
    x, dy = hop(tokens), hop(cotangent)
    x, *own = lax.optimization_barrier((x, tokens, cotangent))
    first = (x, dy)
    beside = stack(swap(own[0]), swap(own[1]))

    inside = pl.BlockSpec(memory_space=pltpu.VMEM)
    given = (w_gate[0], w_up[0], w_down[0], proj_hidden[0].T, proj_output[0].T)
    weights = None
    lows, projs = [], []
    held = {("a", 0, True): beside}
    todo = list(jobs)

    def take():
        nonlocal sheet, weights
        names = todo.pop(0)
        blocks = [held[name] for name in names if name in held]
        if weights is None:
            sheet, low_side, proj_cot, *weights = work(
                names, sheet, blocks, given, apart=(tokens, cotangent), load=docs_count
            )
        else:
            sheet, low_side, proj_cot = work(names, sheet, blocks, weights)
        lows.append(low_side)
        projs.append(proj_cot)

    chain = {"b": beside}
    for i, (c, step) in enumerate(arrivals):
        block = hop(chain[c]) if i > 0 else first
        if i != 1:
            take()
            sheet, block = lax.optimization_barrier((sheet, block))
        if i == 0:
            block = stack(*block)
        chain[c] = held[(c, step, False)] = block
        held[(c, step, True)] = swap(block)
    while todo:
        take()
    returned = lax.all_to_all(sheet, "exp", split_axis=0, concat_axis=0, tiled=True)
    rank = proj_output.shape[2]
    feature, route_grad = pl.pallas_call(
        functools.partial(outcome_kernel, jobs),
        out_shape=[
            jax.ShapeDtypeStruct((docs_count * rank, rank), jnp.float32),
            jax.ShapeDtypeStruct((chosen, tok_rows), jnp.float32),
        ],
        in_specs=[inside] * (2 + 2 * len(lows)),
        out_specs=[inside] * 2,
        compiler_params=pltpu.CompilerParams(vmem_limit_bytes=16 * 1024 * 1024),
    )(returned, routes.T, *lows, *projs)
    return feature.reshape(docs_count, 1, rank, rank), route_grad.T


def by_routing(
    tokens, cotangent, routes, combine, doc_ids, w_gate, w_up, w_down, proj_hidden, proj_output
):
    tok_rows, chosen = routes.shape
    local_count = w_gate.shape[0]
    groups = lax.axis_size("exp")
    experts = local_count * groups
    capacity = max(2, tok_rows * chosen * 5 // (4 * experts))
    docs_count = max(2, tok_rows * groups // DOC_TOK)
    entries = tok_rows * chosen
    width = tokens.shape[1]
    flat_routes = routes.reshape(-1)
    member = (flat_routes[:, None] == jnp.arange(experts, dtype=jnp.int32)[None, :]).astype(
        jnp.int32
    )
    slot_rank = jnp.sum((jnp.cumsum(member, axis=0) - 1) * member, axis=1)
    position = flat_routes * capacity + slot_rank
    source = (
        jnp.full((experts * capacity,), -1, jnp.int32)
        .at[position]
        .set(jnp.arange(entries, dtype=jnp.int32))
    )
    filled = source >= 0
    safe_source = jnp.maximum(source, 0)
    token_of = safe_source // chosen
    send_x = jnp.where(filled[:, None], tokens[token_of], 0)
    send_dy = jnp.where(filled[:, None], cotangent[token_of], 0)
    send_w = jnp.where(filled, combine.reshape(-1)[safe_source], 0)
    send_doc = jnp.where(filled, doc_ids[token_of], -1).astype(jnp.bfloat16)

    def exchange(array):
        array = array.reshape((groups, local_count, capacity) + array.shape[1:])
        return lax.all_to_all(array, "exp", split_axis=0, concat_axis=0, tiled=True)

    recv_x, recv_dy, recv_w, recv_doc = (
        exchange(send_x),
        exchange(send_dy),
        exchange(send_w),
        exchange(send_doc),
    )
    slots = groups * capacity
    grads, feats = [], []
    for e in range(local_count):
        hidden = swiglu(recv_x[:, e].reshape(slots, width), w_gate[e], w_up[e])
        grad, feature = finish(
            hidden,
            recv_dy[:, e].reshape(slots, width),
            recv_w[:, e].reshape(slots),
            recv_doc[:, e].reshape(slots),
            w_down[e],
            proj_hidden[e],
            proj_output[e],
            docs_count,
        )
        grads.append(grad.reshape(groups, capacity))
        feats.append(feature)
    slot_grad = jnp.stack(grads, axis=1)
    returned = lax.all_to_all(slot_grad, "exp", split_axis=0, concat_axis=0, tiled=True)
    route_grad = returned.reshape(-1)[position].reshape(tok_rows, chosen)
    return jnp.stack(feats, axis=1), route_grad


def on_device(tokens, cotangent, routes, combine, doc_ids, w_gate, *rest):
    tok_rows, chosen = routes.shape
    experts = w_gate.shape[0] * lax.axis_size("exp")
    dense = w_gate.shape[0] == 1 and 4 * chosen >= experts and experts >= 8 and experts % 4 == 0
    plan = by_ring if dense else by_routing
    return plan(tokens, cotangent, routes, combine, doc_ids, w_gate, *rest)


def solution(mesh):
    placed = (
        P(("grp", "exp"), None),
        P(("grp", "exp"), None),
        P(("grp", "exp"), None),
        P(("grp", "exp"), None),
        P(("grp", "exp")),
        P("exp", None, None),
        P("exp", None, None),
        P("exp", None, None),
        P("exp", None, None),
        P("exp", None, None),
    )
    return jax.shard_map(
        on_device,
        mesh=mesh,
        in_specs=placed,
        out_specs=(P("grp", "exp", None, None), P(("grp", "exp"), None)),
        check_vma=False,
    )
```

```python
import functools

import jax
import jax.numpy as jnp
from jax import lax
from jax.experimental import pallas as pl
from jax.experimental.pallas import tpu as pltpu
from jax.sharding import PartitionSpec as P

DOC_TOK = 512
LOAD_MIB = 40


def swiglu(rows, w_gate, w_up):
    gate_val = jnp.dot(rows, w_gate, preferred_element_type=jnp.float32)
    up_val = jnp.dot(rows, w_up, preferred_element_type=jnp.float32)
    return (jax.nn.silu(gate_val) * up_val).astype(jnp.bfloat16)


def finish(hidden, rows_dy, rows_w, rows_doc, w_down, proj_hidden, proj_output, docs_count):
    out_val = jnp.dot(hidden, w_down, preferred_element_type=jnp.float32)
    grad = jnp.sum(rows_dy.astype(jnp.float32) * out_val, axis=-1)
    low_side = jnp.dot(hidden, proj_hidden, preferred_element_type=jnp.float32).astype(
        jnp.bfloat16
    )
    proj_cot = jnp.dot(rows_dy, proj_output, preferred_element_type=jnp.float32)
    high_side = (rows_w.astype(jnp.float32)[:, None] * proj_cot).astype(jnp.bfloat16)
    doc_table = jnp.arange(docs_count, dtype=jnp.int32).astype(jnp.bfloat16)
    onehot = (rows_doc[:, None] == doc_table).astype(jnp.bfloat16)
    spread = onehot[:, :, None] * low_side[:, None, :]
    spread = spread.reshape(spread.shape[0], -1)
    feature = lax.dot_general(
        spread, high_side, (((0,), (0,)), ((), ())), preferred_element_type=jnp.float32
    )
    return grad, feature.reshape(docs_count, low_side.shape[1], high_side.shape[1])


def block_owner(name, chips):
    chain, step, handed = name
    me = lax.axis_index("exp")
    core, chip = lax.rem(me, 2), lax.div(me, 2)
    turn = chips // 2
    place = jnp.where(lax.rem(chip, 2) == 0, lax.div(chip, 2), chips - 1 - lax.div(chip, 2))
    way = 2 * core - 1
    place = place + (-way if handed else way) * step
    place = lax.rem(place + chips, chips)
    chip = jnp.where(place < turn, 2 * place, 2 * (chips - 1 - place) + 1)
    return 2 * chip + (core if (chain == "a") != handed else 1 - core)


def rows_kernel(names, load, parted, late, *refs):
    blocks = len(names)
    refs = list(refs)

    def some(count):
        taken = refs[:count]
        del refs[:count]
        return taken

    sheet_in = None if late else some(1)[0]
    apart, block_in = some(2 if parted else 0), some(blocks - parted)
    whole = len(block_in)
    given = some(5)
    sheets = some(blocks if late else 1)
    low_side, proj_cot = some(2)
    loaded = some(5 if load else 0)
    x_all, dy_all, low_sum, grad_sum = some(4)
    w_gate, w_up, w_down, low_proj, high_proj = loaded if load else given
    rows = x_all.shape[0] // blocks
    across = (((1,), (1,)), ((), ()))
    units = w_gate.shape[1]
    tile = 256 if units % 256 == 0 else units
    tiles = units // tile
    lanes = grad_sum.shape[1]
    copies = []
    if load:
        rank = given[3].shape[0]
        for j in range(tiles):
            part = pl.ds(j * tile, tile)
            copies.append((given[0].at[:, part], w_gate.at[:, part]))
            copies.append((given[1].at[:, part], w_up.at[:, part]))
            copies.append((given[2].at[part, :], w_down.at[part, :]))
        for i in range(low_proj.shape[0] // rank):
            copies.append((given[3], low_proj.at[pl.ds(i * rank, rank), :]))
        copies.append((given[4], high_proj))
        if parted:
            copies.append((apart[0], x_all.at[:rows]))
            copies.append((apart[1], dy_all.at[:rows]))
        copies = [
            pltpu.make_async_copy(src, dst, refs[0].at[i]) for i, (src, dst) in enumerate(copies)
        ]
        for copy in copies[3 * tiles :] + copies[: 3 * tiles]:
            copy.start()
    for i, block in enumerate(block_in):
        place = slice((blocks - whole + i) * rows, (blocks - whole + i + 1) * rows)
        x_all[place, :] = block[:rows, :]
        dy_all[place, :] = block[rows:, :]
    low_sum[...] = jnp.zeros_like(low_sum)
    grad_sum[...] = jnp.zeros_like(grad_sum)

    def one_tile(j):
        part = pl.ds(j * tile, tile)
        gate_val = jnp.dot(x_all[...], w_gate[:, part], preferred_element_type=jnp.float32)
        up_val = jnp.dot(x_all[...], w_up[:, part], preferred_element_type=jnp.float32)
        hidden = (jax.nn.silu(gate_val) * up_val).astype(jnp.bfloat16)
        back = lax.dot_general(
            dy_all[...], w_down[part, :], across, preferred_element_type=jnp.float32
        )
        terms = hidden.astype(jnp.float32) * back
        for cut in range(0, tile, lanes):
            grad_sum[...] += terms[:, cut : cut + lanes]
        low_sum[...] += lax.dot_general(
            low_proj[:, part], hidden, across, preferred_element_type=jnp.float32
        )

    for copy in copies[3 * tiles :]:
        copy.wait()
    for j in range(tiles):
        for copy in copies[3 * j : 3 * j + 3] if load else []:
            copy.wait()
        one_tile(j)

    low_side[...] = low_sum[...].astype(low_side.dtype)
    proj_cot[...] = lax.dot_general(
        high_proj[...], dy_all[...], across, preferred_element_type=jnp.float32
    )
    if not late:
        sheets[0][...] = sheet_in[...]
    for i in range(blocks):
        total = jnp.sum(
            jnp.transpose(grad_sum[i * rows : (i + 1) * rows, :]), axis=0, keepdims=True
        )
        if late:
            sheets[i][...] = jnp.broadcast_to(total, sheets[i].shape)
        else:
            owner = block_owner(names[i], sheets[0].shape[0] // 2)
            sheets[0][owner, 0:1, :] = total


def work(names, sheet, block_in, weights, apart=(), load=0):
    width, units = weights[0].shape
    low_width, rank = weights[3].shape[0] * max(load, 1), weights[4].shape[0]
    blocks = len(names)
    rows = block_in[0].shape[0] // 2
    inside = pl.BlockSpec(memory_space=pltpu.VMEM)
    loaded = []
    if load:
        shapes = [w.shape for w in weights]
        shapes[3] = (low_width, units)
        loaded = [jax.ShapeDtypeStruct(shape, weights[0].dtype) for shape in shapes]
    tiles = units // 256 if units % 256 == 0 else 1
    sheets = [(8, rows)] * blocks if sheet is None else [sheet.shape]
    sheet = [] if sheet is None else [sheet]
    call = pl.pallas_call(
        functools.partial(rows_kernel, names, load > 0, len(apart) > 0, not sheet),
        out_shape=[jax.ShapeDtypeStruct(shape, jnp.float32) for shape in sheets]
        + [
            jax.ShapeDtypeStruct((low_width, blocks * rows), jnp.bfloat16),
            jax.ShapeDtypeStruct((rank, blocks * rows), jnp.float32),
        ]
        + loaded,
        in_specs=[inside] * len(sheet)
        + [pl.BlockSpec(memory_space=pl.ANY)] * len(apart)
        + [inside] * len(block_in)
        + [pl.BlockSpec(memory_space=pl.ANY) if load else inside] * len(weights),
        out_specs=[inside] * (len(sheets) + 2 + len(loaded)),
        scratch_shapes=[
            pltpu.VMEM((blocks * rows, width), jnp.bfloat16),
            pltpu.VMEM((blocks * rows, width), jnp.bfloat16),
            pltpu.VMEM((low_width, blocks * rows), jnp.float32),
            pltpu.VMEM((blocks * rows, 128), jnp.float32),
        ]
        + ([pltpu.SemaphoreType.DMA((3 * tiles + load + 1 + len(apart),))] if load else []),
        compiler_params=pltpu.CompilerParams(
            vmem_limit_bytes=(LOAD_MIB if load else 16) * 1024 * 1024
        ),
        cost_estimate=pl.CostEstimate(
            flops=6 * blocks * rows * width * units,
            bytes_accessed=4 * blocks * rows * width,
            transcendentals=blocks * rows * units,
        ),
    )
    results = call(*sheet, *apart, *block_in, *weights)
    cut = len(sheets)
    return results[:cut], results[cut], results[cut + 1], results[cut + 2 :]


def outcome_kernel(jobs, senders, returned, routes, *refs):
    low_in, proj_in = refs[: len(jobs)], refs[len(jobs) : 2 * len(jobs)]
    late = refs[2 * len(jobs) : -2]
    feat, route_grad = refs[-2:]
    rows = returned.shape[2]
    width, rank = low_in[0].shape[0], proj_in[0].shape[0]
    doc_of = lax.broadcasted_iota(jnp.int32, (width, rows), 0) // rank
    total = jnp.zeros(feat.shape, jnp.float32)
    for names, low_side, proj_cot in zip(jobs, low_in, proj_in):
        spread, high_side = [], []
        for i, name in enumerate(names):
            place = slice(i * rows, (i + 1) * rows)
            owner = block_owner(name, returned.shape[0] // 2)
            weight = returned[owner, 1:2, :]
            doc = returned[owner, 2:3, :].astype(jnp.int32)
            high_side.append((weight * proj_cot[:, place]).astype(jnp.bfloat16))
            low = low_side[:, place].astype(jnp.float32)
            spread.append(jnp.where(doc == doc_of, low, 0.0).astype(jnp.bfloat16))
        total += lax.dot_general(
            jnp.concatenate(spread, axis=1),
            jnp.concatenate(high_side, axis=1),
            (((1,), (1,)), ((), ())),
            preferred_element_type=jnp.float32,
        )
    feat[...] = total
    picked = jnp.zeros(route_grad.shape, jnp.float32)
    for e in range(returned.shape[0]):
        picked = jnp.where(routes[...] == e, returned[e, 0:1, :], picked)
    for name, lines in zip(senders, late):
        sender = block_owner(name, returned.shape[0] // 2)
        picked = jnp.where(routes[...] == sender, lines[0:1, :], picked)
    route_grad[...] = picked


def facts_kernel(routes, combine, doc_ids, out):
    groups, lines, rows = out.shape
    expert = lax.broadcasted_iota(jnp.int32, (groups, rows), 0)
    weight = jnp.zeros((groups, rows), jnp.float32)
    for k in range(routes.shape[0]):
        share = combine[k : k + 1, :].astype(jnp.float32)
        weight += jnp.where(routes[k : k + 1, :] == expert, share, 0.0)
    line = lax.broadcasted_iota(jnp.int32, (lines, rows), 0)
    doc = doc_ids[...].astype(jnp.float32)
    for e in range(groups):
        out[e] = jnp.where(line == 1, weight[e : e + 1, :], doc)


def stack_kernel(top, bottom, out):
    rows = top.shape[0]
    out[:rows, :] = top[...]
    out[rows:, :] = bottom[...]


def stack(top, bottom):
    inside = pl.BlockSpec(memory_space=pltpu.VMEM)
    return pl.pallas_call(
        stack_kernel,
        out_shape=jax.ShapeDtypeStruct((2 * top.shape[0], top.shape[1]), top.dtype),
        in_specs=[inside] * 2,
        out_specs=inside,
        compiler_params=pltpu.CompilerParams(vmem_limit_bytes=8 * 1024 * 1024),
    )(top, bottom)


def by_ring(
    tokens, cotangent, routes, combine, doc_ids, w_gate, w_up, w_down, proj_hidden, proj_output
):
    tok_rows, chosen = routes.shape
    groups = lax.axis_size("exp")
    docs_count = max(2, tok_rows * groups // DOC_TOK)
    chips = groups // 2
    half = chips // 2
    ring = list(range(0, chips, 2)) + list(range(chips - 1, 0, -2))
    onward = []
    for place in range(chips):
        onward.append((2 * ring[place], 2 * ring[(place + 1) % chips]))
        onward.append((2 * ring[place] + 1, 2 * ring[place - 1] + 1))
    across = [(i, i ^ 1) for i in range(groups)]

    def hop(block):
        return lax.ppermute(block, "exp", onward)

    def swap(block):
        return lax.ppermute(block, "exp", across)

    arrivals = [(c, step) for step in range(1, half + 1) for c in ("ab" if step < half else "a")]
    jobs = [(("a", 0, False), ("a", 0, True))]
    for i, (c, step) in enumerate(arrivals):
        job = ((c, step, False),)
        if i > 0:
            job += (arrivals[i - 1] + (True,),)
        if i == 1:
            job += (arrivals[0] + (False,),)
        if i != 0:
            jobs.append(job)
    jobs.append((arrivals[-1] + (True,),))

    sheet = pl.pallas_call(
        facts_kernel,
        out_shape=jax.ShapeDtypeStruct((groups, 8, tok_rows), jnp.float32),
        in_specs=[pl.BlockSpec(memory_space=pltpu.VMEM)] * 3,
        out_specs=pl.BlockSpec(memory_space=pltpu.VMEM),
        compiler_params=pltpu.CompilerParams(vmem_limit_bytes=8 * 1024 * 1024),
    )(routes.T, combine.T, doc_ids[None, :])
    first = (hop(tokens), hop(cotangent))
    beside = stack(swap(tokens), swap(cotangent))

    inside = pl.BlockSpec(memory_space=pltpu.VMEM)
    given = (w_gate[0], w_up[0], w_down[0], proj_hidden[0].T, proj_output[0].T)
    weights = None
    lows, projs, late, senders = [], [], [], []
    held = {("a", 0, True): beside}
    todo = list(jobs)

    def back(name):
        chain, step, handed = name
        pairs = []
        for place in range(chips):
            for core in range(2):
                way = (2 * core - 1) * (-1 if handed else 1)
                owner = 2 * ring[(place + way * step) % chips]
                owner += core if (chain == "a") != handed else 1 - core
                pairs.append((2 * ring[place] + core, owner))
        if 0 < step < half and (chain == "a") != handed:
            return pairs, ("b" if chain == "a" else "a", step, not handed)
        return pairs, name

    def take(direct=False, load=False):
        nonlocal sheet, weights
        names = todo.pop(0)
        blocks = [held[name] for name in names if name in held]
        apart = () if len(blocks) == len(names) else (tokens, cotangent)
        sheets, low_side, proj_cot, loaded = work(
            names,
            None if direct else sheet,
            blocks,
            given if load else weights,
            apart=apart,
            load=docs_count if load else 0,
        )
        weights = loaded if load else weights
        lows.append(low_side)
        projs.append(proj_cot)
        if not direct:
            (sheet,) = sheets
            return
        for name, lines in zip(names, sheets):
            pairs, sender = back(name)
            late.append(lax.ppermute(lines, "exp", pairs))
            senders.append(sender)

    chain = {"b": beside}
    end = len(arrivals) - 1
    for i, (c, step) in enumerate(arrivals):
        block = hop(chain[c]) if i > 0 else first
        if i != 1:
            take(direct=i == end, load=i in (0, end))
            lows[-1:], block = lax.optimization_barrier((lows[-1:], block))
        if i == 0:
            block = stack(*block)
        if i == end - 1:
            returned = lax.all_to_all(sheet, "exp", split_axis=0, concat_axis=0, tiled=True)
            returned, block = lax.optimization_barrier((returned, block))
        chain[c] = held[(c, step, False)] = block
        held[(c, step, True)] = swap(block)
    while todo:
        take(direct=True)
    rank = proj_output.shape[2]
    feature, route_grad = pl.pallas_call(
        functools.partial(outcome_kernel, jobs, senders),
        out_shape=[
            jax.ShapeDtypeStruct((docs_count * rank, rank), jnp.float32),
            jax.ShapeDtypeStruct((chosen, tok_rows), jnp.float32),
        ],
        in_specs=[inside] * (2 + 2 * len(lows) + len(late)),
        out_specs=[inside] * 2,
        compiler_params=pltpu.CompilerParams(vmem_limit_bytes=16 * 1024 * 1024),
    )(returned, routes.T, *lows, *projs, *late)
    return feature.reshape(docs_count, 1, rank, rank), route_grad.T


def by_routing(
    tokens, cotangent, routes, combine, doc_ids, w_gate, w_up, w_down, proj_hidden, proj_output
):
    tok_rows, chosen = routes.shape
    local_count = w_gate.shape[0]
    groups = lax.axis_size("exp")
    experts = local_count * groups
    capacity = max(2, tok_rows * chosen * 5 // (4 * experts))
    docs_count = max(2, tok_rows * groups // DOC_TOK)
    entries = tok_rows * chosen
    width = tokens.shape[1]
    flat_routes = routes.reshape(-1)
    member = (flat_routes[:, None] == jnp.arange(experts, dtype=jnp.int32)[None, :]).astype(
        jnp.int32
    )
    slot_rank = jnp.sum((jnp.cumsum(member, axis=0) - 1) * member, axis=1)
    position = flat_routes * capacity + slot_rank
    source = (
        jnp.full((experts * capacity,), -1, jnp.int32)
        .at[position]
        .set(jnp.arange(entries, dtype=jnp.int32))
    )
    filled = source >= 0
    safe_source = jnp.maximum(source, 0)
    token_of = safe_source // chosen
    send_x = jnp.where(filled[:, None], tokens[token_of], 0)
    send_dy = jnp.where(filled[:, None], cotangent[token_of], 0)
    send_w = jnp.where(filled, combine.reshape(-1)[safe_source], 0)
    send_doc = jnp.where(filled, doc_ids[token_of], -1).astype(jnp.bfloat16)

    def exchange(array):
        array = array.reshape((groups, local_count, capacity) + array.shape[1:])
        return lax.all_to_all(array, "exp", split_axis=0, concat_axis=0, tiled=True)

    recv_x, recv_dy, recv_w, recv_doc = (
        exchange(send_x),
        exchange(send_dy),
        exchange(send_w),
        exchange(send_doc),
    )
    slots = groups * capacity
    grads, feats = [], []
    for e in range(local_count):
        hidden = swiglu(recv_x[:, e].reshape(slots, width), w_gate[e], w_up[e])
        grad, feature = finish(
            hidden,
            recv_dy[:, e].reshape(slots, width),
            recv_w[:, e].reshape(slots),
            recv_doc[:, e].reshape(slots),
            w_down[e],
            proj_hidden[e],
            proj_output[e],
            docs_count,
        )
        grads.append(grad.reshape(groups, capacity))
        feats.append(feature)
    slot_grad = jnp.stack(grads, axis=1)
    returned = lax.all_to_all(slot_grad, "exp", split_axis=0, concat_axis=0, tiled=True)
    route_grad = returned.reshape(-1)[position].reshape(tok_rows, chosen)
    return jnp.stack(feats, axis=1), route_grad


def on_device(tokens, cotangent, routes, combine, doc_ids, w_gate, *rest):
    tok_rows, chosen = routes.shape
    experts = w_gate.shape[0] * lax.axis_size("exp")
    dense = w_gate.shape[0] == 1 and 4 * chosen >= experts and experts >= 8 and experts % 4 == 0
    plan = by_ring if dense else by_routing
    return plan(tokens, cotangent, routes, combine, doc_ids, w_gate, *rest)


def solution(mesh):
    placed = (
        P(("grp", "exp"), None),
        P(("grp", "exp"), None),
        P(("grp", "exp"), None),
        P(("grp", "exp"), None),
        P(("grp", "exp")),
        P("exp", None, None),
        P("exp", None, None),
        P("exp", None, None),
        P("exp", None, None),
        P("exp", None, None),
    )
    return jax.shard_map(
        on_device,
        mesh=mesh,
        in_specs=placed,
        out_specs=(P("grp", "exp", None, None), P(("grp", "exp"), None)),
        check_vma=False,
    )
```

```python
import functools

import jax
import jax.numpy as jnp
from jax import lax
from jax.experimental import pallas as pl
from jax.experimental.pallas import tpu as pltpu
from jax.sharding import PartitionSpec as P

DOC_TOK = 512
LOAD_MIB = 40


def swiglu(rows, w_gate, w_up):
    gate_val = jnp.dot(rows, w_gate, preferred_element_type=jnp.float32)
    up_val = jnp.dot(rows, w_up, preferred_element_type=jnp.float32)
    return (jax.nn.silu(gate_val) * up_val).astype(jnp.bfloat16)


def finish(hidden, rows_dy, rows_w, rows_doc, w_down, proj_hidden, proj_output, docs_count):
    out_val = jnp.dot(hidden, w_down, preferred_element_type=jnp.float32)
    grad = jnp.sum(rows_dy.astype(jnp.float32) * out_val, axis=-1)
    low_side = jnp.dot(hidden, proj_hidden, preferred_element_type=jnp.float32).astype(
        jnp.bfloat16
    )
    proj_cot = jnp.dot(rows_dy, proj_output, preferred_element_type=jnp.float32)
    high_side = (rows_w.astype(jnp.float32)[:, None] * proj_cot).astype(jnp.bfloat16)
    doc_table = jnp.arange(docs_count, dtype=jnp.int32).astype(jnp.bfloat16)
    onehot = (rows_doc[:, None] == doc_table).astype(jnp.bfloat16)
    spread = onehot[:, :, None] * low_side[:, None, :]
    spread = spread.reshape(spread.shape[0], -1)
    feature = lax.dot_general(
        spread, high_side, (((0,), (0,)), ((), ())), preferred_element_type=jnp.float32
    )
    return grad, feature.reshape(docs_count, low_side.shape[1], high_side.shape[1])


def block_owner(name, chips):
    chain, step, handed = name
    me = lax.axis_index("exp")
    core, chip = lax.rem(me, 2), lax.div(me, 2)
    turn = chips // 2
    place = jnp.where(lax.rem(chip, 2) == 0, lax.div(chip, 2), chips - 1 - lax.div(chip, 2))
    way = 2 * core - 1
    place = place + (-way if handed else way) * step
    place = lax.rem(place + chips, chips)
    chip = jnp.where(place < turn, 2 * place, 2 * (chips - 1 - place) + 1)
    return 2 * chip + (core if (chain == "a") != handed else 1 - core)


def rows_kernel(names, load, *refs):
    blocks = len(names)
    apart = refs[1:3] if load else ()
    refs = refs[:1] + refs[3:] if load else refs
    whole = blocks - 1 if load else blocks
    sheet_in, block_in = refs[0], refs[1 : 1 + whole]
    given = refs[1 + whole : 6 + whole]
    sheet, low_side, proj_cot = refs[6 + whole : 9 + whole]
    x_all, dy_all, low_sum, grad_sum = refs[-5:-1] if load else refs[-4:]
    w_gate, w_up, w_down, low_proj, high_proj = refs[9 + whole : 14 + whole] if load else given
    rows = x_all.shape[0] // blocks
    across = (((1,), (1,)), ((), ()))
    units = w_gate.shape[1]
    tile = 256 if units % 256 == 0 else units
    tiles = units // tile
    lanes = grad_sum.shape[1]
    copies = []
    if load:
        rank = given[3].shape[0]
        for j in range(tiles):
            part = pl.ds(j * tile, tile)
            copies.append((given[0].at[:, part], w_gate.at[:, part]))
            copies.append((given[1].at[:, part], w_up.at[:, part]))
            copies.append((given[2].at[part, :], w_down.at[part, :]))
        for i in range(low_proj.shape[0] // rank):
            copies.append((given[3], low_proj.at[pl.ds(i * rank, rank), :]))
        copies.append((given[4], high_proj))
        copies.append((apart[0], x_all.at[:rows]))
        copies.append((apart[1], dy_all.at[:rows]))
        copies = [
            pltpu.make_async_copy(src, dst, refs[-1].at[i]) for i, (src, dst) in enumerate(copies)
        ]
        for copy in copies[3 * tiles :] + copies[: 3 * tiles]:
            copy.start()
    for i, block in enumerate(block_in):
        place = slice((blocks - whole + i) * rows, (blocks - whole + i + 1) * rows)
        x_all[place, :] = block[:rows, :]
        dy_all[place, :] = block[rows:, :]
    low_sum[...] = jnp.zeros_like(low_sum)
    grad_sum[...] = jnp.zeros_like(grad_sum)

    def one_tile(j):
        part = pl.ds(j * tile, tile)
        gate_val = jnp.dot(x_all[...], w_gate[:, part], preferred_element_type=jnp.float32)
        up_val = jnp.dot(x_all[...], w_up[:, part], preferred_element_type=jnp.float32)
        hidden = (jax.nn.silu(gate_val) * up_val).astype(jnp.bfloat16)
        back = lax.dot_general(
            dy_all[...], w_down[part, :], across, preferred_element_type=jnp.float32
        )
        terms = hidden.astype(jnp.float32) * back
        for cut in range(0, tile, lanes):
            grad_sum[...] += terms[:, cut : cut + lanes]
        low_sum[...] += lax.dot_general(
            low_proj[:, part], hidden, across, preferred_element_type=jnp.float32
        )

    for copy in copies[3 * tiles :]:
        copy.wait()
    for j in range(tiles):
        for copy in copies[3 * j : 3 * j + 3] if load else []:
            copy.wait()
        one_tile(j)

    low_side[...] = low_sum[...].astype(low_side.dtype)
    proj_cot[...] = lax.dot_general(
        high_proj[...], dy_all[...], across, preferred_element_type=jnp.float32
    )
    sheet[...] = sheet_in[...]
    for i in range(blocks):
        total = jnp.sum(
            jnp.transpose(grad_sum[i * rows : (i + 1) * rows, :]), axis=0, keepdims=True
        )
        sheet[block_owner(names[i], sheet.shape[0] // 2), 0:1, :] = total


def work(names, sheet, block_in, weights, apart=(), load=0):
    width, units = weights[0].shape
    low_width, rank = weights[3].shape[0] * max(load, 1), weights[4].shape[0]
    blocks = len(names)
    rows = block_in[0].shape[0] // 2
    inside = pl.BlockSpec(memory_space=pltpu.VMEM)
    loaded = []
    if load:
        shapes = [w.shape for w in weights]
        shapes[3] = (low_width, units)
        loaded = [jax.ShapeDtypeStruct(shape, weights[0].dtype) for shape in shapes]
    tiles = units // 256 if units % 256 == 0 else 1
    call = pl.pallas_call(
        functools.partial(rows_kernel, names, load > 0),
        out_shape=[
            jax.ShapeDtypeStruct(sheet.shape, jnp.float32),
            jax.ShapeDtypeStruct((low_width, blocks * rows), jnp.bfloat16),
            jax.ShapeDtypeStruct((rank, blocks * rows), jnp.float32),
        ]
        + loaded,
        in_specs=[inside]
        + [pl.BlockSpec(memory_space=pl.ANY)] * len(apart)
        + [inside] * len(block_in)
        + [pl.BlockSpec(memory_space=pl.ANY) if load else inside] * len(weights),
        out_specs=[inside] * (3 + len(loaded)),
        scratch_shapes=[
            pltpu.VMEM((blocks * rows, width), jnp.bfloat16),
            pltpu.VMEM((blocks * rows, width), jnp.bfloat16),
            pltpu.VMEM((low_width, blocks * rows), jnp.float32),
            pltpu.VMEM((blocks * rows, 128), jnp.float32),
        ]
        + ([pltpu.SemaphoreType.DMA((3 * tiles + load + 3,))] if load else []),
        compiler_params=pltpu.CompilerParams(
            vmem_limit_bytes=(LOAD_MIB if load else 16) * 1024 * 1024
        ),
        cost_estimate=pl.CostEstimate(
            flops=6 * blocks * rows * width * units,
            bytes_accessed=4 * blocks * rows * width,
            transcendentals=blocks * rows * units,
        ),
    )
    return call(sheet, *apart, *block_in, *weights)


def outcome_kernel(jobs, returned, routes, *refs):
    low_in, proj_in = refs[: len(jobs)], refs[len(jobs) : 2 * len(jobs)]
    feat, route_grad = refs[-2:]
    rows = returned.shape[2]
    width, rank = low_in[0].shape[0], proj_in[0].shape[0]
    doc_of = lax.broadcasted_iota(jnp.int32, (width, rows), 0) // rank
    total = jnp.zeros(feat.shape, jnp.float32)
    for names, low_side, proj_cot in zip(jobs, low_in, proj_in):
        spread, high_side = [], []
        for i, name in enumerate(names):
            place = slice(i * rows, (i + 1) * rows)
            owner = block_owner(name, returned.shape[0] // 2)
            weight = returned[owner, 1:2, :]
            doc = returned[owner, 2:3, :].astype(jnp.int32)
            high_side.append((weight * proj_cot[:, place]).astype(jnp.bfloat16))
            low = low_side[:, place].astype(jnp.float32)
            spread.append(jnp.where(doc == doc_of, low, 0.0).astype(jnp.bfloat16))
        total += lax.dot_general(
            jnp.concatenate(spread, axis=1),
            jnp.concatenate(high_side, axis=1),
            (((1,), (1,)), ((), ())),
            preferred_element_type=jnp.float32,
        )
    feat[...] = total
    picked = jnp.zeros(route_grad.shape, jnp.float32)
    for e in range(returned.shape[0]):
        picked = jnp.where(routes[...] == e, returned[e, 0:1, :], picked)
    route_grad[...] = picked


def facts_kernel(routes, combine, doc_ids, out):
    groups, lines, rows = out.shape
    expert = lax.broadcasted_iota(jnp.int32, (groups, rows), 0)
    weight = jnp.zeros((groups, rows), jnp.float32)
    for k in range(routes.shape[0]):
        share = combine[k : k + 1, :].astype(jnp.float32)
        weight += jnp.where(routes[k : k + 1, :] == expert, share, 0.0)
    line = lax.broadcasted_iota(jnp.int32, (lines, rows), 0)
    doc = doc_ids[...].astype(jnp.float32)
    for e in range(groups):
        out[e] = jnp.where(line == 1, weight[e : e + 1, :], doc)


def stack_kernel(top, bottom, out):
    rows = top.shape[0]
    out[:rows, :] = top[...]
    out[rows:, :] = bottom[...]


def stack(top, bottom):
    inside = pl.BlockSpec(memory_space=pltpu.VMEM)
    return pl.pallas_call(
        stack_kernel,
        out_shape=jax.ShapeDtypeStruct((2 * top.shape[0], top.shape[1]), top.dtype),
        in_specs=[inside] * 2,
        out_specs=inside,
        compiler_params=pltpu.CompilerParams(vmem_limit_bytes=8 * 1024 * 1024),
    )(top, bottom)


def by_ring(
    tokens, cotangent, routes, combine, doc_ids, w_gate, w_up, w_down, proj_hidden, proj_output
):
    tok_rows, chosen = routes.shape
    groups = lax.axis_size("exp")
    docs_count = max(2, tok_rows * groups // DOC_TOK)
    chips = groups // 2
    half = chips // 2
    ring = list(range(0, chips, 2)) + list(range(chips - 1, 0, -2))
    onward = []
    for place in range(chips):
        onward.append((2 * ring[place], 2 * ring[(place + 1) % chips]))
        onward.append((2 * ring[place] + 1, 2 * ring[place - 1] + 1))
    across = [(i, i ^ 1) for i in range(groups)]

    def hop(block):
        return lax.ppermute(block, "exp", onward)

    def swap(block):
        return lax.ppermute(block, "exp", across)

    arrivals = [(c, step) for step in range(1, half + 1) for c in ("ab" if step < half else "a")]
    jobs = [(("a", 0, False), ("a", 0, True))]
    for i, (c, step) in enumerate(arrivals):
        job = ((c, step, False),)
        if i > 0:
            job += (arrivals[i - 1] + (True,),)
        if i == 1:
            job += (arrivals[0] + (False,),)
        if i != 0:
            jobs.append(job)
    jobs.append((arrivals[-1] + (True,),))

    sheet = pl.pallas_call(
        facts_kernel,
        out_shape=jax.ShapeDtypeStruct((groups, 8, tok_rows), jnp.float32),
        in_specs=[pl.BlockSpec(memory_space=pltpu.VMEM)] * 3,
        out_specs=pl.BlockSpec(memory_space=pltpu.VMEM),
        compiler_params=pltpu.CompilerParams(vmem_limit_bytes=8 * 1024 * 1024),
    )(routes.T, combine.T, doc_ids[None, :])
    first = (hop(tokens), hop(cotangent))
    beside = stack(swap(tokens), swap(cotangent))

    inside = pl.BlockSpec(memory_space=pltpu.VMEM)
    given = (w_gate[0], w_up[0], w_down[0], proj_hidden[0].T, proj_output[0].T)
    weights = None
    lows, projs = [], []
    held = {("a", 0, True): beside}
    todo = list(jobs)

    def take():
        nonlocal sheet, weights
        names = todo.pop(0)
        blocks = [held[name] for name in names if name in held]
        if weights is None:
            sheet, low_side, proj_cot, *weights = work(
                names, sheet, blocks, given, apart=(tokens, cotangent), load=docs_count
            )
        else:
            sheet, low_side, proj_cot = work(names, sheet, blocks, weights)
        lows.append(low_side)
        projs.append(proj_cot)

    chain = {"b": beside}
    for i, (c, step) in enumerate(arrivals):
        block = hop(chain[c]) if i > 0 else first
        if i != 1:
            take()
            sheet, block = lax.optimization_barrier((sheet, block))
        if i == 0:
            block = stack(*block)
        chain[c] = held[(c, step, False)] = block
        held[(c, step, True)] = swap(block)
    while todo:
        take()
    returned = lax.all_to_all(sheet, "exp", split_axis=0, concat_axis=0, tiled=True)
    rank = proj_output.shape[2]
    feature, route_grad = pl.pallas_call(
        functools.partial(outcome_kernel, jobs),
        out_shape=[
            jax.ShapeDtypeStruct((docs_count * rank, rank), jnp.float32),
            jax.ShapeDtypeStruct((chosen, tok_rows), jnp.float32),
        ],
        in_specs=[inside] * (2 + 2 * len(lows)),
        out_specs=[inside] * 2,
        compiler_params=pltpu.CompilerParams(vmem_limit_bytes=16 * 1024 * 1024),
    )(returned, routes.T, *lows, *projs)
    return feature.reshape(docs_count, 1, rank, rank), route_grad.T


def by_routing(
    tokens, cotangent, routes, combine, doc_ids, w_gate, w_up, w_down, proj_hidden, proj_output
):
    tok_rows, chosen = routes.shape
    local_count = w_gate.shape[0]
    groups = lax.axis_size("exp")
    experts = local_count * groups
    capacity = max(2, tok_rows * chosen * 5 // (4 * experts))
    docs_count = max(2, tok_rows * groups // DOC_TOK)
    entries = tok_rows * chosen
    width = tokens.shape[1]
    flat_routes = routes.reshape(-1)
    member = (flat_routes[:, None] == jnp.arange(experts, dtype=jnp.int32)[None, :]).astype(
        jnp.int32
    )
    slot_rank = jnp.sum((jnp.cumsum(member, axis=0) - 1) * member, axis=1)
    position = flat_routes * capacity + slot_rank
    source = (
        jnp.full((experts * capacity,), -1, jnp.int32)
        .at[position]
        .set(jnp.arange(entries, dtype=jnp.int32))
    )
    filled = source >= 0
    safe_source = jnp.maximum(source, 0)
    token_of = safe_source // chosen
    send_x = jnp.where(filled[:, None], tokens[token_of], 0)
    send_dy = jnp.where(filled[:, None], cotangent[token_of], 0)
    send_w = jnp.where(filled, combine.reshape(-1)[safe_source], 0)
    send_doc = jnp.where(filled, doc_ids[token_of], -1).astype(jnp.bfloat16)

    def exchange(array):
        array = array.reshape((groups, local_count, capacity) + array.shape[1:])
        return lax.all_to_all(array, "exp", split_axis=0, concat_axis=0, tiled=True)

    recv_x, recv_dy, recv_w, recv_doc = (
        exchange(send_x),
        exchange(send_dy),
        exchange(send_w),
        exchange(send_doc),
    )
    slots = groups * capacity
    grads, feats = [], []
    for e in range(local_count):
        hidden = swiglu(recv_x[:, e].reshape(slots, width), w_gate[e], w_up[e])
        grad, feature = finish(
            hidden,
            recv_dy[:, e].reshape(slots, width),
            recv_w[:, e].reshape(slots),
            recv_doc[:, e].reshape(slots),
            w_down[e],
            proj_hidden[e],
            proj_output[e],
            docs_count,
        )
        grads.append(grad.reshape(groups, capacity))
        feats.append(feature)
    slot_grad = jnp.stack(grads, axis=1)
    returned = lax.all_to_all(slot_grad, "exp", split_axis=0, concat_axis=0, tiled=True)
    route_grad = returned.reshape(-1)[position].reshape(tok_rows, chosen)
    return jnp.stack(feats, axis=1), route_grad


def on_device(tokens, cotangent, routes, combine, doc_ids, w_gate, *rest):
    tok_rows, chosen = routes.shape
    experts = w_gate.shape[0] * lax.axis_size("exp")
    dense = w_gate.shape[0] == 1 and 4 * chosen >= experts and experts >= 8 and experts % 4 == 0
    plan = by_ring if dense else by_routing
    return plan(tokens, cotangent, routes, combine, doc_ids, w_gate, *rest)


def solution(mesh):
    placed = (
        P(("grp", "exp"), None),
        P(("grp", "exp"), None),
        P(("grp", "exp"), None),
        P(("grp", "exp"), None),
        P(("grp", "exp")),
        P("exp", None, None),
        P("exp", None, None),
        P("exp", None, None),
        P("exp", None, None),
        P("exp", None, None),
    )
    return jax.shard_map(
        on_device,
        mesh=mesh,
        in_specs=placed,
        out_specs=(P("grp", "exp", None, None), P(("grp", "exp"), None)),
        check_vma=False,
    )
```

```python
import functools

import jax
import jax.numpy as jnp
from jax import lax
from jax.experimental import pallas as pl
from jax.experimental.pallas import tpu as pltpu
from jax.sharding import PartitionSpec as P

DOC_TOK = 512
LOAD_MIB = 40


def swiglu(rows, w_gate, w_up):
    gate_val = jnp.dot(rows, w_gate, preferred_element_type=jnp.float32)
    up_val = jnp.dot(rows, w_up, preferred_element_type=jnp.float32)
    return (jax.nn.silu(gate_val) * up_val).astype(jnp.bfloat16)


def finish(hidden, rows_dy, rows_w, rows_doc, w_down, proj_hidden, proj_output, docs_count):
    out_val = jnp.dot(hidden, w_down, preferred_element_type=jnp.float32)
    grad = jnp.sum(rows_dy.astype(jnp.float32) * out_val, axis=-1)
    low_side = jnp.dot(hidden, proj_hidden, preferred_element_type=jnp.float32).astype(
        jnp.bfloat16
    )
    proj_cot = jnp.dot(rows_dy, proj_output, preferred_element_type=jnp.float32)
    high_side = (rows_w.astype(jnp.float32)[:, None] * proj_cot).astype(jnp.bfloat16)
    doc_table = jnp.arange(docs_count, dtype=jnp.int32).astype(jnp.bfloat16)
    onehot = (rows_doc[:, None] == doc_table).astype(jnp.bfloat16)
    spread = onehot[:, :, None] * low_side[:, None, :]
    spread = spread.reshape(spread.shape[0], -1)
    feature = lax.dot_general(
        spread, high_side, (((0,), (0,)), ((), ())), preferred_element_type=jnp.float32
    )
    return grad, feature.reshape(docs_count, low_side.shape[1], high_side.shape[1])


def block_owner(name, chips):
    chain, step, handed = name
    me = lax.axis_index("exp")
    core, chip = lax.rem(me, 2), lax.div(me, 2)
    turn = chips // 2
    place = jnp.where(lax.rem(chip, 2) == 0, lax.div(chip, 2), chips - 1 - lax.div(chip, 2))
    way = 2 * core - 1
    place = place + (-way if handed else way) * step
    place = lax.rem(place + chips, chips)
    chip = jnp.where(place < turn, 2 * place, 2 * (chips - 1 - place) + 1)
    return 2 * chip + (core if (chain == "a") != handed else 1 - core)


def rows_kernel(names, load, *refs):
    blocks = len(names)
    apart = refs[1:3] if load else ()
    refs = refs[:1] + refs[3:] if load else refs
    whole = blocks - 1 if load else blocks
    sheet_in, block_in = refs[0], refs[1 : 1 + whole]
    given = refs[1 + whole : 6 + whole]
    sheet, low_side, proj_cot = refs[6 + whole : 9 + whole]
    x_all, dy_all, low_sum, grad_sum = refs[-5:-1] if load else refs[-4:]
    w_gate, w_up, w_down, low_proj, high_proj = refs[9 + whole : 14 + whole] if load else given
    rows = x_all.shape[0] // blocks
    across = (((1,), (1,)), ((), ()))
    units = w_gate.shape[1]
    tile = 256 if units % 256 == 0 else units
    tiles = units // tile
    lanes = grad_sum.shape[1]
    copies = []
    if load:
        rank = given[3].shape[0]
        for j in range(tiles):
            part = pl.ds(j * tile, tile)
            copies.append((given[0].at[:, part], w_gate.at[:, part]))
            copies.append((given[1].at[:, part], w_up.at[:, part]))
            copies.append((given[2].at[part, :], w_down.at[part, :]))
        for i in range(low_proj.shape[0] // rank):
            copies.append((given[3], low_proj.at[pl.ds(i * rank, rank), :]))
        copies.append((given[4], high_proj))
        copies.append((apart[0], x_all.at[:rows]))
        copies.append((apart[1], dy_all.at[:rows]))
        copies = [
            pltpu.make_async_copy(src, dst, refs[-1].at[i]) for i, (src, dst) in enumerate(copies)
        ]
        for copy in copies[3 * tiles :] + copies[: 3 * tiles]:
            copy.start()
    for i, block in enumerate(block_in):
        place = slice((blocks - whole + i) * rows, (blocks - whole + i + 1) * rows)
        x_all[place, :] = block[:rows, :]
        dy_all[place, :] = block[rows:, :]
    low_sum[...] = jnp.zeros_like(low_sum)
    grad_sum[...] = jnp.zeros_like(grad_sum)

    def one_tile(j):
        part = pl.ds(j * tile, tile)
        gate_val = jnp.dot(x_all[...], w_gate[:, part], preferred_element_type=jnp.float32)
        up_val = jnp.dot(x_all[...], w_up[:, part], preferred_element_type=jnp.float32)
        hidden = (jax.nn.silu(gate_val) * up_val).astype(jnp.bfloat16)
        back = lax.dot_general(
            dy_all[...], w_down[part, :], across, preferred_element_type=jnp.float32
        )
        terms = hidden.astype(jnp.float32) * back
        for cut in range(0, tile, lanes):
            grad_sum[...] += terms[:, cut : cut + lanes]
        low_sum[...] += lax.dot_general(
            low_proj[:, part], hidden, across, preferred_element_type=jnp.float32
        )

    for copy in copies[3 * tiles :]:
        copy.wait()
    for j in range(tiles):
        for copy in copies[3 * j : 3 * j + 3] if load else []:
            copy.wait()
        one_tile(j)

    low_side[...] = low_sum[...].astype(low_side.dtype)
    proj_cot[...] = lax.dot_general(
        high_proj[...], dy_all[...], across, preferred_element_type=jnp.float32
    )
    sheet[...] = sheet_in[...]
    for i in range(blocks):
        total = jnp.sum(
            jnp.transpose(grad_sum[i * rows : (i + 1) * rows, :]), axis=0, keepdims=True
        )
        sheet[block_owner(names[i], sheet.shape[0] // 2), 0:1, :] = total


def work(names, sheet, block_in, weights, apart=(), load=0):
    width, units = weights[0].shape
    low_width, rank = weights[3].shape[0] * max(load, 1), weights[4].shape[0]
    blocks = len(names)
    rows = block_in[0].shape[0] // 2
    inside = pl.BlockSpec(memory_space=pltpu.VMEM)
    loaded = []
    if load:
        shapes = [w.shape for w in weights]
        shapes[3] = (low_width, units)
        loaded = [jax.ShapeDtypeStruct(shape, weights[0].dtype) for shape in shapes]
    tiles = units // 256 if units % 256 == 0 else 1
    call = pl.pallas_call(
        functools.partial(rows_kernel, names, load > 0),
        out_shape=[
            jax.ShapeDtypeStruct(sheet.shape, jnp.float32),
            jax.ShapeDtypeStruct((low_width, blocks * rows), jnp.bfloat16),
            jax.ShapeDtypeStruct((rank, blocks * rows), jnp.float32),
        ]
        + loaded,
        in_specs=[inside]
        + [pl.BlockSpec(memory_space=pl.ANY)] * len(apart)
        + [inside] * len(block_in)
        + [pl.BlockSpec(memory_space=pl.ANY) if load else inside] * len(weights),
        out_specs=[inside] * (3 + len(loaded)),
        scratch_shapes=[
            pltpu.VMEM((blocks * rows, width), jnp.bfloat16),
            pltpu.VMEM((blocks * rows, width), jnp.bfloat16),
            pltpu.VMEM((low_width, blocks * rows), jnp.float32),
            pltpu.VMEM((blocks * rows, 128), jnp.float32),
        ]
        + ([pltpu.SemaphoreType.DMA((3 * tiles + load + 3,))] if load else []),
        compiler_params=pltpu.CompilerParams(
            vmem_limit_bytes=(LOAD_MIB if load else 16) * 1024 * 1024
        ),
        cost_estimate=pl.CostEstimate(
            flops=6 * blocks * rows * width * units,
            bytes_accessed=4 * blocks * rows * width,
            transcendentals=blocks * rows * units,
        ),
    )
    return call(sheet, *apart, *block_in, *weights)


def front_kernel(*refs):
    blocks = len(refs) - 7
    x_in = refs[:blocks]
    w_gate, w_up, low_proj, hidden, low_side, x_all, low_sum = refs[blocks:]
    rows = x_in[0].shape[0]
    for i in range(blocks):
        x_all[i * rows : (i + 1) * rows, :] = x_in[i][...]
    units = w_gate.shape[1]
    tile = 256 if units % 256 == 0 else units
    for cut in range(0, units, tile):
        part = pl.ds(cut, tile)
        gate_val = jnp.dot(x_all[...], w_gate[:, part], preferred_element_type=jnp.float32)
        up_val = jnp.dot(x_all[...], w_up[:, part], preferred_element_type=jnp.float32)
        piece = (jax.nn.silu(gate_val) * up_val).astype(jnp.bfloat16)
        hidden[:, part] = piece
        low = lax.dot_general(
            low_proj[:, part],
            piece,
            (((1,), (1,)), ((), ())),
            preferred_element_type=jnp.float32,
        )
        low_sum[...] = low if cut == 0 else low_sum[...] + low
    low_side[...] = low_sum[...].astype(low_side.dtype)


def front(x_in, weights):
    w_gate, w_up, _, low_proj, _ = weights
    rows, width = len(x_in) * x_in[0].shape[0], x_in[0].shape[1]
    units = w_gate.shape[1]
    inside = pl.BlockSpec(memory_space=pltpu.VMEM)
    return pl.pallas_call(
        front_kernel,
        out_shape=[
            jax.ShapeDtypeStruct((rows, units), jnp.bfloat16),
            jax.ShapeDtypeStruct((low_proj.shape[0], rows), jnp.bfloat16),
        ],
        in_specs=[inside] * (len(x_in) + 3),
        out_specs=[inside] * 2,
        scratch_shapes=[
            pltpu.VMEM((rows, width), jnp.bfloat16),
            pltpu.VMEM((low_proj.shape[0], rows), jnp.float32),
        ],
        compiler_params=pltpu.CompilerParams(vmem_limit_bytes=16 * 1024 * 1024),
        cost_estimate=pl.CostEstimate(
            flops=4 * rows * width * units,
            bytes_accessed=2 * rows * width,
            transcendentals=rows * units,
        ),
    )(*x_in, w_gate, w_up, low_proj)


def back_kernel(names, *refs):
    blocks = len(names)
    sheet_in, dy_in = refs[0], refs[1 : 1 + blocks]
    hidden, w_down, high_proj, sheet, proj_cot, dy_all, grad_sum = refs[1 + blocks :]
    rows = dy_in[0].shape[0]
    across = (((1,), (1,)), ((), ()))
    for i in range(blocks):
        dy_all[i * rows : (i + 1) * rows, :] = dy_in[i][...]
    units, lanes = hidden.shape[1], grad_sum.shape[1]
    tile = 256 if units % 256 == 0 else units
    for cut in range(0, units, tile):
        part = pl.ds(cut, tile)
        back = lax.dot_general(
            dy_all[...], w_down[part, :], across, preferred_element_type=jnp.float32
        )
        terms = hidden[:, part].astype(jnp.float32) * back
        total = terms[:, :lanes]
        for spot in range(lanes, tile, lanes):
            total += terms[:, spot : spot + lanes]
        grad_sum[...] = total if cut == 0 else grad_sum[...] + total
    proj_cot[...] = lax.dot_general(
        high_proj[...], dy_all[...], across, preferred_element_type=jnp.float32
    )
    sheet[...] = sheet_in[...]
    for i in range(blocks):
        total = jnp.sum(
            jnp.transpose(grad_sum[i * rows : (i + 1) * rows, :]), axis=0, keepdims=True
        )
        sheet[block_owner(names[i], sheet.shape[0] // 2), 0:1, :] = total


def finish_late(names, sheet, dy_in, hidden, weights):
    _, _, w_down, _, high_proj = weights
    rows, width = len(dy_in) * dy_in[0].shape[0], dy_in[0].shape[1]
    units = hidden.shape[1]
    inside = pl.BlockSpec(memory_space=pltpu.VMEM)
    return pl.pallas_call(
        functools.partial(back_kernel, names),
        out_shape=[
            jax.ShapeDtypeStruct(sheet.shape, jnp.float32),
            jax.ShapeDtypeStruct((high_proj.shape[0], rows), jnp.float32),
        ],
        in_specs=[inside] * (len(dy_in) + 4),
        out_specs=[inside] * 2,
        scratch_shapes=[
            pltpu.VMEM((rows, width), jnp.bfloat16),
            pltpu.VMEM((rows, 128), jnp.float32),
        ],
        compiler_params=pltpu.CompilerParams(vmem_limit_bytes=16 * 1024 * 1024),
        cost_estimate=pl.CostEstimate(
            flops=2 * rows * width * units,
            bytes_accessed=2 * rows * width,
            transcendentals=0,
        ),
    )(sheet, *dy_in, hidden, w_down, high_proj)


def outcome_kernel(jobs, returned, routes, *refs):
    low_in, proj_in = refs[: len(jobs)], refs[len(jobs) : 2 * len(jobs)]
    feat, route_grad = refs[-2:]
    rows = returned.shape[2]
    width, rank = low_in[0].shape[0], proj_in[0].shape[0]
    doc_of = lax.broadcasted_iota(jnp.int32, (width, rows), 0) // rank
    total = jnp.zeros(feat.shape, jnp.float32)
    for names, low_side, proj_cot in zip(jobs, low_in, proj_in):
        spread, high_side = [], []
        for i, name in enumerate(names):
            place = slice(i * rows, (i + 1) * rows)
            owner = block_owner(name, returned.shape[0] // 2)
            weight = returned[owner, 1:2, :]
            doc = returned[owner, 2:3, :].astype(jnp.int32)
            high_side.append((weight * proj_cot[:, place]).astype(jnp.bfloat16))
            low = low_side[:, place].astype(jnp.float32)
            spread.append(jnp.where(doc == doc_of, low, 0.0).astype(jnp.bfloat16))
        total += lax.dot_general(
            jnp.concatenate(spread, axis=1),
            jnp.concatenate(high_side, axis=1),
            (((1,), (1,)), ((), ())),
            preferred_element_type=jnp.float32,
        )
    feat[...] = total
    picked = jnp.zeros(route_grad.shape, jnp.float32)
    for e in range(returned.shape[0]):
        picked = jnp.where(routes[...] == e, returned[e, 0:1, :], picked)
    route_grad[...] = picked


def facts_kernel(routes, combine, doc_ids, out):
    groups, lines, rows = out.shape
    expert = lax.broadcasted_iota(jnp.int32, (groups, rows), 0)
    weight = jnp.zeros((groups, rows), jnp.float32)
    for k in range(routes.shape[0]):
        share = combine[k : k + 1, :].astype(jnp.float32)
        weight += jnp.where(routes[k : k + 1, :] == expert, share, 0.0)
    line = lax.broadcasted_iota(jnp.int32, (lines, rows), 0)
    doc = doc_ids[...].astype(jnp.float32)
    for e in range(groups):
        out[e] = jnp.where(line == 1, weight[e : e + 1, :], doc)


def stack_kernel(top, bottom, out):
    rows = top.shape[0]
    out[:rows, :] = top[...]
    out[rows:, :] = bottom[...]


def stack(top, bottom):
    inside = pl.BlockSpec(memory_space=pltpu.VMEM)
    return pl.pallas_call(
        stack_kernel,
        out_shape=jax.ShapeDtypeStruct((2 * top.shape[0], top.shape[1]), top.dtype),
        in_specs=[inside] * 2,
        out_specs=inside,
        compiler_params=pltpu.CompilerParams(vmem_limit_bytes=8 * 1024 * 1024),
    )(top, bottom)


def split_kernel(cuts, block, *parts):
    for (begin, count), part in zip(cuts, parts):
        part[...] = block[begin : begin + count, :]


def split(block, cuts):
    inside = pl.BlockSpec(memory_space=pltpu.VMEM)
    return pl.pallas_call(
        functools.partial(split_kernel, cuts),
        out_shape=[
            jax.ShapeDtypeStruct((count, block.shape[1]), block.dtype) for _, count in cuts
        ],
        in_specs=[inside],
        out_specs=[inside] * len(cuts),
        compiler_params=pltpu.CompilerParams(vmem_limit_bytes=8 * 1024 * 1024),
    )(block)


def by_ring(
    tokens, cotangent, routes, combine, doc_ids, w_gate, w_up, w_down, proj_hidden, proj_output
):
    tok_rows, chosen = routes.shape
    groups = lax.axis_size("exp")
    docs_count = max(2, tok_rows * groups // DOC_TOK)
    chips = groups // 2
    half = chips // 2
    ring = list(range(0, chips, 2)) + list(range(chips - 1, 0, -2))
    onward = []
    for place in range(chips):
        onward.append((2 * ring[place], 2 * ring[(place + 1) % chips]))
        onward.append((2 * ring[place] + 1, 2 * ring[place - 1] + 1))
    across = [(i, i ^ 1) for i in range(groups)]

    def hop(block):
        return lax.ppermute(block, "exp", onward)

    def swap(block):
        return lax.ppermute(block, "exp", across)

    arrivals = [(c, step) for step in range(1, half + 1) for c in ("ab" if step < half else "a")]
    jobs = [(("a", 0, False), ("a", 0, True))]
    for i, (c, step) in enumerate(arrivals):
        job = ((c, step, False),)
        if i > 0:
            job += (arrivals[i - 1] + (True,),)
        if i == 1:
            job += (arrivals[0] + (False,),)
        if i == len(arrivals) - 1:
            jobs += [job[1:], (job[0], (c, step, True))]
        elif i != 0:
            jobs.append(job)

    sheet = pl.pallas_call(
        facts_kernel,
        out_shape=jax.ShapeDtypeStruct((groups, 8, tok_rows), jnp.float32),
        in_specs=[pl.BlockSpec(memory_space=pltpu.VMEM)] * 3,
        out_specs=pl.BlockSpec(memory_space=pltpu.VMEM),
        compiler_params=pltpu.CompilerParams(vmem_limit_bytes=8 * 1024 * 1024),
    )(routes.T, combine.T, doc_ids[None, :])
    first = (hop(tokens), hop(cotangent))
    beside = stack(swap(tokens), swap(cotangent))

    inside = pl.BlockSpec(memory_space=pltpu.VMEM)
    given = (w_gate[0], w_up[0], w_down[0], proj_hidden[0].T, proj_output[0].T)
    weights = None
    lows, projs = [], []
    held = {("a", 0, True): beside}
    todo = list(jobs)

    def take():
        nonlocal sheet, weights
        names = todo.pop(0)
        blocks = [held[name] for name in names if name in held]
        if weights is None:
            sheet, low_side, proj_cot, *weights = work(
                names, sheet, blocks, given, apart=(tokens, cotangent), load=docs_count
            )
        else:
            sheet, low_side, proj_cot = work(names, sheet, blocks, weights)
        lows.append(low_side)
        projs.append(proj_cot)

    chain = {"b": beside}
    for i, (c, step) in enumerate(arrivals[:-1]):
        block = hop(chain[c]) if i > 0 else first
        if i != 1:
            take()
            sheet, block = lax.optimization_barrier((sheet, block))
        if i == 0:
            block = stack(*block)
        chain[c] = held[(c, step, False)] = block
        held[(c, step, True)] = swap(block)
    cut = tok_rows // 2
    *x, dy = split(chain["a"], ((0, cut), (cut, cut), (tok_rows, tok_rows)))
    dy, _ = lax.optimization_barrier((dy, chain["b"]))
    x, dy = [hop(part) for part in x], hop(dy)
    take()
    sheet, x = lax.optimization_barrier((sheet, x))
    hidden, low_side = front(x + [swap(part) for part in x], weights)
    hidden, dy = lax.optimization_barrier((hidden, dy))
    dy_beside = swap(dy)
    take()
    sheet, proj_cot = finish_late(todo.pop(0), sheet, [dy, dy_beside], hidden, weights)
    lows.append(low_side)
    projs.append(proj_cot)
    returned = lax.all_to_all(sheet, "exp", split_axis=0, concat_axis=0, tiled=True)
    rank = proj_output.shape[2]
    feature, route_grad = pl.pallas_call(
        functools.partial(outcome_kernel, jobs),
        out_shape=[
            jax.ShapeDtypeStruct((docs_count * rank, rank), jnp.float32),
            jax.ShapeDtypeStruct((chosen, tok_rows), jnp.float32),
        ],
        in_specs=[inside] * (2 + 2 * len(lows)),
        out_specs=[inside] * 2,
        compiler_params=pltpu.CompilerParams(vmem_limit_bytes=16 * 1024 * 1024),
    )(returned, routes.T, *lows, *projs)
    return feature.reshape(docs_count, 1, rank, rank), route_grad.T


def by_routing(
    tokens, cotangent, routes, combine, doc_ids, w_gate, w_up, w_down, proj_hidden, proj_output
):
    tok_rows, chosen = routes.shape
    local_count = w_gate.shape[0]
    groups = lax.axis_size("exp")
    experts = local_count * groups
    capacity = max(2, tok_rows * chosen * 5 // (4 * experts))
    docs_count = max(2, tok_rows * groups // DOC_TOK)
    entries = tok_rows * chosen
    width = tokens.shape[1]
    flat_routes = routes.reshape(-1)
    member = (flat_routes[:, None] == jnp.arange(experts, dtype=jnp.int32)[None, :]).astype(
        jnp.int32
    )
    slot_rank = jnp.sum((jnp.cumsum(member, axis=0) - 1) * member, axis=1)
    position = flat_routes * capacity + slot_rank
    source = (
        jnp.full((experts * capacity,), -1, jnp.int32)
        .at[position]
        .set(jnp.arange(entries, dtype=jnp.int32))
    )
    filled = source >= 0
    safe_source = jnp.maximum(source, 0)
    token_of = safe_source // chosen
    send_x = jnp.where(filled[:, None], tokens[token_of], 0)
    send_dy = jnp.where(filled[:, None], cotangent[token_of], 0)
    send_w = jnp.where(filled, combine.reshape(-1)[safe_source], 0)
    send_doc = jnp.where(filled, doc_ids[token_of], -1).astype(jnp.bfloat16)

    def exchange(array):
        array = array.reshape((groups, local_count, capacity) + array.shape[1:])
        return lax.all_to_all(array, "exp", split_axis=0, concat_axis=0, tiled=True)

    recv_x, recv_dy, recv_w, recv_doc = (
        exchange(send_x),
        exchange(send_dy),
        exchange(send_w),
        exchange(send_doc),
    )
    slots = groups * capacity
    grads, feats = [], []
    for e in range(local_count):
        hidden = swiglu(recv_x[:, e].reshape(slots, width), w_gate[e], w_up[e])
        grad, feature = finish(
            hidden,
            recv_dy[:, e].reshape(slots, width),
            recv_w[:, e].reshape(slots),
            recv_doc[:, e].reshape(slots),
            w_down[e],
            proj_hidden[e],
            proj_output[e],
            docs_count,
        )
        grads.append(grad.reshape(groups, capacity))
        feats.append(feature)
    slot_grad = jnp.stack(grads, axis=1)
    returned = lax.all_to_all(slot_grad, "exp", split_axis=0, concat_axis=0, tiled=True)
    route_grad = returned.reshape(-1)[position].reshape(tok_rows, chosen)
    return jnp.stack(feats, axis=1), route_grad


def on_device(tokens, cotangent, routes, combine, doc_ids, w_gate, *rest):
    tok_rows, chosen = routes.shape
    experts = w_gate.shape[0] * lax.axis_size("exp")
    dense = w_gate.shape[0] == 1 and 4 * chosen >= experts and experts >= 8 and experts % 4 == 0
    plan = by_ring if dense else by_routing
    return plan(tokens, cotangent, routes, combine, doc_ids, w_gate, *rest)


def solution(mesh):
    placed = (
        P(("grp", "exp"), None),
        P(("grp", "exp"), None),
        P(("grp", "exp"), None),
        P(("grp", "exp"), None),
        P(("grp", "exp")),
        P("exp", None, None),
        P("exp", None, None),
        P("exp", None, None),
        P("exp", None, None),
        P("exp", None, None),
    )
    return jax.shard_map(
        on_device,
        mesh=mesh,
        in_specs=placed,
        out_specs=(P("grp", "exp", None, None), P(("grp", "exp"), None)),
        check_vma=False,
    )
```

```python
import functools

import jax
import jax.numpy as jnp
from jax import lax
from jax.experimental import pallas as pl
from jax.experimental.pallas import tpu as pltpu
from jax.sharding import PartitionSpec as P

DOC_TOK = 512
LOAD_MIB = 40


def swiglu(rows, w_gate, w_up):
    gate_val = jnp.dot(rows, w_gate, preferred_element_type=jnp.float32)
    up_val = jnp.dot(rows, w_up, preferred_element_type=jnp.float32)
    return (jax.nn.silu(gate_val) * up_val).astype(jnp.bfloat16)


def finish(hidden, rows_dy, rows_w, rows_doc, w_down, proj_hidden, proj_output, docs_count):
    out_val = jnp.dot(hidden, w_down, preferred_element_type=jnp.float32)
    grad = jnp.sum(rows_dy.astype(jnp.float32) * out_val, axis=-1)
    low_side = jnp.dot(hidden, proj_hidden, preferred_element_type=jnp.float32).astype(
        jnp.bfloat16
    )
    proj_cot = jnp.dot(rows_dy, proj_output, preferred_element_type=jnp.float32)
    high_side = (rows_w.astype(jnp.float32)[:, None] * proj_cot).astype(jnp.bfloat16)
    doc_table = jnp.arange(docs_count, dtype=jnp.int32).astype(jnp.bfloat16)
    onehot = (rows_doc[:, None] == doc_table).astype(jnp.bfloat16)
    spread = onehot[:, :, None] * low_side[:, None, :]
    spread = spread.reshape(spread.shape[0], -1)
    feature = lax.dot_general(
        spread, high_side, (((0,), (0,)), ((), ())), preferred_element_type=jnp.float32
    )
    return grad, feature.reshape(docs_count, low_side.shape[1], high_side.shape[1])


def block_owner(name, chips):
    chain, step, handed = name
    me = lax.axis_index("exp")
    core, chip = lax.rem(me, 2), lax.div(me, 2)
    turn = chips // 2
    place = jnp.where(lax.rem(chip, 2) == 0, lax.div(chip, 2), chips - 1 - lax.div(chip, 2))
    way = 2 * core - 1
    place = place + (-way if handed else way) * step
    place = lax.rem(place + chips, chips)
    chip = jnp.where(place < turn, 2 * place, 2 * (chips - 1 - place) + 1)
    return 2 * chip + (core if (chain == "a") != handed else 1 - core)


def rows_kernel(names, load, *refs):
    blocks = len(names)
    apart = refs[1:3] if load else ()
    refs = refs[:1] + refs[3:] if load else refs
    whole = blocks - 1 if load else blocks
    sheet_in, block_in = refs[0], refs[1 : 1 + whole]
    given = refs[1 + whole : 6 + whole]
    sheet, low_side, proj_cot = refs[6 + whole : 9 + whole]
    x_all, dy_all, low_sum, grad_sum = refs[-5:-1] if load else refs[-4:]
    w_gate, w_up, w_down, low_proj, high_proj = refs[9 + whole : 14 + whole] if load else given
    rows = x_all.shape[0] // blocks
    across = (((1,), (1,)), ((), ()))
    units = w_gate.shape[1]
    tile = 256 if units % 256 == 0 else units
    tiles = units // tile
    lanes = grad_sum.shape[1]
    copies = []
    if load:
        rank = given[3].shape[0]
        for j in range(tiles):
            part = pl.ds(j * tile, tile)
            copies.append((given[0].at[:, part], w_gate.at[:, part]))
            copies.append((given[1].at[:, part], w_up.at[:, part]))
            copies.append((given[2].at[part, :], w_down.at[part, :]))
        for i in range(low_proj.shape[0] // rank):
            copies.append((given[3], low_proj.at[pl.ds(i * rank, rank), :]))
        copies.append((given[4], high_proj))
        copies.append((apart[0], x_all.at[:rows]))
        copies.append((apart[1], dy_all.at[:rows]))
        copies = [
            pltpu.make_async_copy(src, dst, refs[-1].at[i]) for i, (src, dst) in enumerate(copies)
        ]
        for copy in copies[3 * tiles :] + copies[: 3 * tiles]:
            copy.start()
    if blocks == 1:
        x_all, dy_all = block_in[0].at[:rows, :], block_in[0].at[rows:, :]
    for i, block in enumerate(block_in if blocks > 1 else ()):
        place = slice((blocks - whole + i) * rows, (blocks - whole + i + 1) * rows)
        x_all[place, :] = block[:rows, :]
        dy_all[place, :] = block[rows:, :]

    def one_tile(j):
        part = pl.ds(j * tile, tile)
        gate_val = jnp.dot(x_all[...], w_gate[:, part], preferred_element_type=jnp.float32)
        up_val = jnp.dot(x_all[...], w_up[:, part], preferred_element_type=jnp.float32)
        hidden = (jax.nn.silu(gate_val) * up_val).astype(jnp.bfloat16)
        back = lax.dot_general(
            dy_all[...], w_down[part, :], across, preferred_element_type=jnp.float32
        )
        terms = hidden.astype(jnp.float32) * back
        total = terms[:, :lanes]
        for cut in range(lanes, tile, lanes):
            total += terms[:, cut : cut + lanes]
        grad_sum[...] = total if j == 0 else grad_sum[...] + total
        low = lax.dot_general(
            low_proj[:, part], hidden, across, preferred_element_type=jnp.float32
        )
        low_sum[...] = low if j == 0 else low_sum[...] + low

    for copy in copies[3 * tiles :]:
        copy.wait()
    for j in range(tiles):
        for copy in copies[3 * j : 3 * j + 3] if load else []:
            copy.wait()
        one_tile(j)

    low_side[...] = low_sum[...].astype(low_side.dtype)
    proj_cot[...] = lax.dot_general(
        high_proj[...], dy_all[...], across, preferred_element_type=jnp.float32
    )
    sheet[...] = sheet_in[...]
    for i in range(blocks):
        total = jnp.sum(
            jnp.transpose(grad_sum[i * rows : (i + 1) * rows, :]), axis=0, keepdims=True
        )
        sheet[block_owner(names[i], sheet.shape[0] // 2), 0:1, :] = total


def work(names, sheet, block_in, weights, apart=(), load=0):
    width, units = weights[0].shape
    low_width, rank = weights[3].shape[0] * max(load, 1), weights[4].shape[0]
    blocks = len(names)
    rows = block_in[0].shape[0] // 2
    inside = pl.BlockSpec(memory_space=pltpu.VMEM)
    loaded = []
    if load:
        shapes = [w.shape for w in weights]
        shapes[3] = (low_width, units)
        loaded = [jax.ShapeDtypeStruct(shape, weights[0].dtype) for shape in shapes]
    tiles = units // 256 if units % 256 == 0 else 1
    call = pl.pallas_call(
        functools.partial(rows_kernel, names, load > 0),
        out_shape=[
            jax.ShapeDtypeStruct(sheet.shape, jnp.float32),
            jax.ShapeDtypeStruct((low_width, blocks * rows), jnp.bfloat16),
            jax.ShapeDtypeStruct((rank, blocks * rows), jnp.float32),
        ]
        + loaded,
        in_specs=[inside]
        + [pl.BlockSpec(memory_space=pl.ANY)] * len(apart)
        + [inside] * len(block_in)
        + [pl.BlockSpec(memory_space=pl.ANY) if load else inside] * len(weights),
        out_specs=[inside] * (3 + len(loaded)),
        scratch_shapes=[
            pltpu.VMEM((blocks * rows, width), jnp.bfloat16),
            pltpu.VMEM((blocks * rows, width), jnp.bfloat16),
            pltpu.VMEM((low_width, blocks * rows), jnp.float32),
            pltpu.VMEM((blocks * rows, 128), jnp.float32),
        ]
        + ([pltpu.SemaphoreType.DMA((3 * tiles + load + 3,))] if load else []),
        compiler_params=pltpu.CompilerParams(
            vmem_limit_bytes=(LOAD_MIB if load else 16) * 1024 * 1024
        ),
        cost_estimate=pl.CostEstimate(
            flops=6 * blocks * rows * width * units,
            bytes_accessed=4 * blocks * rows * width,
            transcendentals=blocks * rows * units,
        ),
    )
    return call(sheet, *apart, *block_in, *weights)


def front_kernel(*refs):
    blocks = len(refs) - 7
    x_in = refs[:blocks]
    w_gate, w_up, low_proj, hidden, low_side, x_all, low_sum = refs[blocks:]
    rows = x_in[0].shape[0]
    for i in range(blocks):
        x_all[i * rows : (i + 1) * rows, :] = x_in[i][...]
    units = w_gate.shape[1]
    tile = 256 if units % 256 == 0 else units
    for cut in range(0, units, tile):
        part = pl.ds(cut, tile)
        gate_val = jnp.dot(x_all[...], w_gate[:, part], preferred_element_type=jnp.float32)
        up_val = jnp.dot(x_all[...], w_up[:, part], preferred_element_type=jnp.float32)
        piece = (jax.nn.silu(gate_val) * up_val).astype(jnp.bfloat16)
        hidden[:, part] = piece
        low = lax.dot_general(
            low_proj[:, part],
            piece,
            (((1,), (1,)), ((), ())),
            preferred_element_type=jnp.float32,
        )
        low_sum[...] = low if cut == 0 else low_sum[...] + low
    low_side[...] = low_sum[...].astype(low_side.dtype)


def front(x_in, weights):
    w_gate, w_up, _, low_proj, _ = weights
    rows, width = len(x_in) * x_in[0].shape[0], x_in[0].shape[1]
    units = w_gate.shape[1]
    inside = pl.BlockSpec(memory_space=pltpu.VMEM)
    return pl.pallas_call(
        front_kernel,
        out_shape=[
            jax.ShapeDtypeStruct((rows, units), jnp.bfloat16),
            jax.ShapeDtypeStruct((low_proj.shape[0], rows), jnp.bfloat16),
        ],
        in_specs=[inside] * (len(x_in) + 3),
        out_specs=[inside] * 2,
        scratch_shapes=[
            pltpu.VMEM((rows, width), jnp.bfloat16),
            pltpu.VMEM((low_proj.shape[0], rows), jnp.float32),
        ],
        compiler_params=pltpu.CompilerParams(vmem_limit_bytes=16 * 1024 * 1024),
        cost_estimate=pl.CostEstimate(
            flops=4 * rows * width * units,
            bytes_accessed=2 * rows * width,
            transcendentals=rows * units,
        ),
    )(*x_in, w_gate, w_up, low_proj)


def back_kernel(names, *refs):
    blocks = len(names)
    sheet_in, dy_in = refs[0], refs[1 : 1 + blocks]
    hidden, w_down, high_proj, sheet, proj_cot, dy_all, grad_sum = refs[1 + blocks :]
    rows = dy_in[0].shape[0]
    across = (((1,), (1,)), ((), ()))
    for i in range(blocks):
        dy_all[i * rows : (i + 1) * rows, :] = dy_in[i][...]
    units, lanes = hidden.shape[1], grad_sum.shape[1]
    tile = 256 if units % 256 == 0 else units
    for cut in range(0, units, tile):
        part = pl.ds(cut, tile)
        back = lax.dot_general(
            dy_all[...], w_down[part, :], across, preferred_element_type=jnp.float32
        )
        terms = hidden[:, part].astype(jnp.float32) * back
        total = terms[:, :lanes]
        for spot in range(lanes, tile, lanes):
            total += terms[:, spot : spot + lanes]
        grad_sum[...] = total if cut == 0 else grad_sum[...] + total
    proj_cot[...] = lax.dot_general(
        high_proj[...], dy_all[...], across, preferred_element_type=jnp.float32
    )
    sheet[...] = sheet_in[...]
    for i in range(blocks):
        total = jnp.sum(
            jnp.transpose(grad_sum[i * rows : (i + 1) * rows, :]), axis=0, keepdims=True
        )
        sheet[block_owner(names[i], sheet.shape[0] // 2), 0:1, :] = total


def finish_late(names, sheet, dy_in, hidden, weights):
    _, _, w_down, _, high_proj = weights
    rows, width = len(dy_in) * dy_in[0].shape[0], dy_in[0].shape[1]
    units = hidden.shape[1]
    inside = pl.BlockSpec(memory_space=pltpu.VMEM)
    return pl.pallas_call(
        functools.partial(back_kernel, names),
        out_shape=[
            jax.ShapeDtypeStruct(sheet.shape, jnp.float32),
            jax.ShapeDtypeStruct((high_proj.shape[0], rows), jnp.float32),
        ],
        in_specs=[inside] * (len(dy_in) + 4),
        out_specs=[inside] * 2,
        scratch_shapes=[
            pltpu.VMEM((rows, width), jnp.bfloat16),
            pltpu.VMEM((rows, 128), jnp.float32),
        ],
        compiler_params=pltpu.CompilerParams(vmem_limit_bytes=16 * 1024 * 1024),
        cost_estimate=pl.CostEstimate(
            flops=2 * rows * width * units,
            bytes_accessed=2 * rows * width,
            transcendentals=0,
        ),
    )(sheet, *dy_in, hidden, w_down, high_proj)


def outcome_kernel(jobs, returned, routes, *refs):
    low_in, proj_in = refs[: len(jobs)], refs[len(jobs) : 2 * len(jobs)]
    feat, route_grad = refs[-2:]
    rows = returned.shape[2]
    width, rank = low_in[0].shape[0], proj_in[0].shape[0]
    doc_of = lax.broadcasted_iota(jnp.int32, (width, rows), 0) // rank
    spread, high_side = [], []
    for names, low_side, proj_cot in zip(jobs, low_in, proj_in):
        for i, name in enumerate(names):
            place = slice(i * rows, (i + 1) * rows)
            owner = block_owner(name, returned.shape[0] // 2)
            weight = returned[owner, 1:2, :]
            doc = returned[owner, 2:3, :].astype(jnp.int32)
            high_side.append((weight * proj_cot[:, place]).astype(jnp.bfloat16))
            low = low_side[:, place].astype(jnp.float32)
            spread.append(jnp.where(doc == doc_of, low, 0.0).astype(jnp.bfloat16))
    feat[...] = lax.dot_general(
        jnp.concatenate(spread, axis=1),
        jnp.concatenate(high_side, axis=1),
        (((1,), (1,)), ((), ())),
        preferred_element_type=jnp.float32,
    )
    picked = jnp.zeros(route_grad.shape, jnp.float32)
    for e in range(returned.shape[0]):
        picked = jnp.where(routes[...] == e, returned[e, 0:1, :], picked)
    route_grad[...] = picked


def facts_kernel(routes, combine, doc_ids, out):
    groups, lines, rows = out.shape
    expert = lax.broadcasted_iota(jnp.int32, (groups, rows), 0)
    weight = jnp.zeros((groups, rows), jnp.float32)
    for k in range(routes.shape[0]):
        share = combine[k : k + 1, :].astype(jnp.float32)
        weight += jnp.where(routes[k : k + 1, :] == expert, share, 0.0)
    line = lax.broadcasted_iota(jnp.int32, (lines, rows), 0)
    doc = doc_ids[...].astype(jnp.float32)
    for e in range(groups):
        out[e] = jnp.where(line == 1, weight[e : e + 1, :], doc)


def stack_kernel(top, bottom, out):
    rows = top.shape[0]
    out[:rows, :] = top[...]
    out[rows:, :] = bottom[...]


def stack(top, bottom):
    inside = pl.BlockSpec(memory_space=pltpu.VMEM)
    return pl.pallas_call(
        stack_kernel,
        out_shape=jax.ShapeDtypeStruct((2 * top.shape[0], top.shape[1]), top.dtype),
        in_specs=[inside] * 2,
        out_specs=inside,
        compiler_params=pltpu.CompilerParams(vmem_limit_bytes=8 * 1024 * 1024),
    )(top, bottom)


def split_kernel(cuts, block, *parts):
    for (begin, count), part in zip(cuts, parts):
        part[...] = block[begin : begin + count, :]


def split(block, cuts):
    inside = pl.BlockSpec(memory_space=pltpu.VMEM)
    return pl.pallas_call(
        functools.partial(split_kernel, cuts),
        out_shape=[
            jax.ShapeDtypeStruct((count, block.shape[1]), block.dtype) for _, count in cuts
        ],
        in_specs=[inside],
        out_specs=[inside] * len(cuts),
        compiler_params=pltpu.CompilerParams(vmem_limit_bytes=8 * 1024 * 1024),
    )(block)


def by_ring(
    tokens, cotangent, routes, combine, doc_ids, w_gate, w_up, w_down, proj_hidden, proj_output
):
    tok_rows, chosen = routes.shape
    groups = lax.axis_size("exp")
    docs_count = max(2, tok_rows * groups // DOC_TOK)
    chips = groups // 2
    half = chips // 2
    ring = list(range(0, chips, 2)) + list(range(chips - 1, 0, -2))
    onward = []
    for place in range(chips):
        onward.append((2 * ring[place], 2 * ring[(place + 1) % chips]))
        onward.append((2 * ring[place] + 1, 2 * ring[place - 1] + 1))
    across = [(i, i ^ 1) for i in range(groups)]

    def hop(block):
        return lax.ppermute(block, "exp", onward)

    def swap(block):
        return lax.ppermute(block, "exp", across)

    arrivals = [(c, step) for step in range(1, half + 1) for c in ("ab" if step < half else "a")]
    jobs = [(("a", 0, False), ("a", 0, True))]
    for i, (c, step) in enumerate(arrivals):
        job = ((c, step, False),)
        if i > 0:
            job += (arrivals[i - 1] + (True,),)
        if i == 1:
            job += (arrivals[0] + (False,),)
        if i == len(arrivals) - 1:
            jobs += [job[1:], (job[0], (c, step, True))]
        elif i != 0:
            jobs.append(job)

    sheet = pl.pallas_call(
        facts_kernel,
        out_shape=jax.ShapeDtypeStruct((groups, 4, tok_rows), jnp.float32),
        in_specs=[pl.BlockSpec(memory_space=pltpu.VMEM)] * 3,
        out_specs=pl.BlockSpec(memory_space=pltpu.VMEM),
        compiler_params=pltpu.CompilerParams(vmem_limit_bytes=8 * 1024 * 1024),
    )(routes.T, combine.T, doc_ids[None, :])
    first = (hop(tokens), hop(cotangent))
    beside = stack(swap(tokens), swap(cotangent))

    inside = pl.BlockSpec(memory_space=pltpu.VMEM)
    given = (w_gate[0], w_up[0], w_down[0], proj_hidden[0].T, proj_output[0].T)
    weights = None
    lows, projs = [], []
    held = {("a", 0, True): beside}
    todo = list(jobs)

    def take():
        nonlocal sheet, weights
        names = todo.pop(0)
        blocks = [held[name] for name in names if name in held]
        if weights is None:
            sheet, low_side, proj_cot, *weights = work(
                names, sheet, blocks, given, apart=(tokens, cotangent), load=docs_count
            )
        else:
            sheet, low_side, proj_cot = work(names, sheet, blocks, weights)
        lows.append(low_side)
        projs.append(proj_cot)

    chain = {"b": beside}
    for i, (c, step) in enumerate(arrivals[:-1]):
        block = hop(chain[c]) if i > 0 else first
        if i != 1:
            take()
            sheet, block = lax.optimization_barrier((sheet, block))
        if i == 0:
            block = stack(*block)
        chain[c] = held[(c, step, False)] = block
        held[(c, step, True)] = swap(block)
    cut = tok_rows // 2
    *x, dy = split(chain["a"], ((0, cut), (cut, cut), (tok_rows, tok_rows)))
    dy, _ = lax.optimization_barrier((dy, chain["b"]))
    x, dy = [hop(part) for part in x], hop(dy)
    take()
    sheet, x = lax.optimization_barrier((sheet, x))
    hidden, low_side = front(x + [swap(part) for part in x], weights)
    hidden, dy = lax.optimization_barrier((hidden, dy))
    dy_beside = swap(dy)
    take()
    sheet, proj_cot = finish_late(todo.pop(0), sheet, [dy, dy_beside], hidden, weights)
    lows.append(low_side)
    projs.append(proj_cot)
    returned = lax.all_to_all(sheet, "exp", split_axis=0, concat_axis=0, tiled=True)
    rank = proj_output.shape[2]
    feature, route_grad = pl.pallas_call(
        functools.partial(outcome_kernel, jobs),
        out_shape=[
            jax.ShapeDtypeStruct((docs_count * rank, rank), jnp.float32),
            jax.ShapeDtypeStruct((chosen, tok_rows), jnp.float32),
        ],
        in_specs=[inside] * (2 + 2 * len(lows)),
        out_specs=[inside] * 2,
        compiler_params=pltpu.CompilerParams(vmem_limit_bytes=16 * 1024 * 1024),
    )(returned, routes.T, *lows, *projs)
    return feature.reshape(docs_count, 1, rank, rank), route_grad.T


def by_routing(
    tokens, cotangent, routes, combine, doc_ids, w_gate, w_up, w_down, proj_hidden, proj_output
):
    tok_rows, chosen = routes.shape
    local_count = w_gate.shape[0]
    groups = lax.axis_size("exp")
    experts = local_count * groups
    capacity = max(2, tok_rows * chosen * 5 // (4 * experts))
    docs_count = max(2, tok_rows * groups // DOC_TOK)
    entries = tok_rows * chosen
    width = tokens.shape[1]
    flat_routes = routes.reshape(-1)
    member = (flat_routes[:, None] == jnp.arange(experts, dtype=jnp.int32)[None, :]).astype(
        jnp.int32
    )
    slot_rank = jnp.sum((jnp.cumsum(member, axis=0) - 1) * member, axis=1)
    position = flat_routes * capacity + slot_rank
    source = (
        jnp.full((experts * capacity,), -1, jnp.int32)
        .at[position]
        .set(jnp.arange(entries, dtype=jnp.int32))
    )
    filled = source >= 0
    safe_source = jnp.maximum(source, 0)
    token_of = safe_source // chosen
    send_x = jnp.where(filled[:, None], tokens[token_of], 0)
    send_dy = jnp.where(filled[:, None], cotangent[token_of], 0)
    send_w = jnp.where(filled, combine.reshape(-1)[safe_source], 0)
    send_doc = jnp.where(filled, doc_ids[token_of], -1).astype(jnp.bfloat16)

    def exchange(array):
        array = array.reshape((groups, local_count, capacity) + array.shape[1:])
        return lax.all_to_all(array, "exp", split_axis=0, concat_axis=0, tiled=True)

    recv_x, recv_dy, recv_w, recv_doc = (
        exchange(send_x),
        exchange(send_dy),
        exchange(send_w),
        exchange(send_doc),
    )
    slots = groups * capacity
    grads, feats = [], []
    for e in range(local_count):
        hidden = swiglu(recv_x[:, e].reshape(slots, width), w_gate[e], w_up[e])
        grad, feature = finish(
            hidden,
            recv_dy[:, e].reshape(slots, width),
            recv_w[:, e].reshape(slots),
            recv_doc[:, e].reshape(slots),
            w_down[e],
            proj_hidden[e],
            proj_output[e],
            docs_count,
        )
        grads.append(grad.reshape(groups, capacity))
        feats.append(feature)
    slot_grad = jnp.stack(grads, axis=1)
    returned = lax.all_to_all(slot_grad, "exp", split_axis=0, concat_axis=0, tiled=True)
    route_grad = returned.reshape(-1)[position].reshape(tok_rows, chosen)
    return jnp.stack(feats, axis=1), route_grad


def on_device(tokens, cotangent, routes, combine, doc_ids, w_gate, *rest):
    tok_rows, chosen = routes.shape
    experts = w_gate.shape[0] * lax.axis_size("exp")
    dense = w_gate.shape[0] == 1 and 4 * chosen >= experts and experts >= 8 and experts % 4 == 0
    plan = by_ring if dense else by_routing
    return plan(tokens, cotangent, routes, combine, doc_ids, w_gate, *rest)


def solution(mesh):
    placed = (
        P(("grp", "exp"), None),
        P(("grp", "exp"), None),
        P(("grp", "exp"), None),
        P(("grp", "exp"), None),
        P(("grp", "exp")),
        P("exp", None, None),
        P("exp", None, None),
        P("exp", None, None),
        P("exp", None, None),
        P("exp", None, None),
    )
    return jax.shard_map(
        on_device,
        mesh=mesh,
        in_specs=placed,
        out_specs=(P("grp", "exp", None, None), P(("grp", "exp"), None)),
        check_vma=False,
    )
```

```python
import functools

import jax
import jax.numpy as jnp
from jax import lax
from jax.experimental import pallas as pl
from jax.experimental.pallas import tpu as pltpu
from jax.sharding import PartitionSpec as P

DOC_TOK = 512
LOAD_MIB = 40
PAIR_MIB = 38


def swiglu(rows, w_gate, w_up):
    gate_val = jnp.dot(rows, w_gate, preferred_element_type=jnp.float32)
    up_val = jnp.dot(rows, w_up, preferred_element_type=jnp.float32)
    return (jax.nn.silu(gate_val) * up_val).astype(jnp.bfloat16)


def finish(hidden, rows_dy, rows_w, rows_doc, w_down, proj_hidden, proj_output, docs_count):
    out_val = jnp.dot(hidden, w_down, preferred_element_type=jnp.float32)
    grad = jnp.sum(rows_dy.astype(jnp.float32) * out_val, axis=-1)
    low_side = jnp.dot(hidden, proj_hidden, preferred_element_type=jnp.float32).astype(
        jnp.bfloat16
    )
    proj_cot = jnp.dot(rows_dy, proj_output, preferred_element_type=jnp.float32)
    high_side = (rows_w.astype(jnp.float32)[:, None] * proj_cot).astype(jnp.bfloat16)
    doc_table = jnp.arange(docs_count, dtype=jnp.int32).astype(jnp.bfloat16)
    onehot = (rows_doc[:, None] == doc_table).astype(jnp.bfloat16)
    spread = onehot[:, :, None] * low_side[:, None, :]
    spread = spread.reshape(spread.shape[0], -1)
    feature = lax.dot_general(
        spread, high_side, (((0,), (0,)), ((), ())), preferred_element_type=jnp.float32
    )
    return grad, feature.reshape(docs_count, low_side.shape[1], high_side.shape[1])


def block_owner(name, chips):
    chain, step, handed = name
    me = lax.axis_index("exp")
    core, chip = lax.rem(me, 2), lax.div(me, 2)
    turn = chips // 2
    place = jnp.where(lax.rem(chip, 2) == 0, lax.div(chip, 2), chips - 1 - lax.div(chip, 2))
    way = 2 * core - 1
    place = place + (-way if handed else way) * step
    place = lax.rem(place + chips, chips)
    chip = jnp.where(place < turn, 2 * place, 2 * (chips - 1 - place) + 1)
    return 2 * chip + (core if (chain == "a") != handed else 1 - core)


def rows_kernel(names, load, *refs):
    blocks = len(names)
    apart = refs[1:3] if load else ()
    refs = refs[:1] + refs[3:] if load else refs
    whole = blocks - 1 if load else blocks
    sheet_in, block_in = refs[0], refs[1 : 1 + whole]
    given = refs[1 + whole : 6 + whole]
    sheet, low_side, proj_cot = refs[6 + whole : 9 + whole]
    x_all, dy_all, low_sum, grad_sum = refs[-5:-1] if load else refs[-4:]
    w_gate, w_up, w_down, low_proj, high_proj = refs[9 + whole : 14 + whole] if load else given
    rows = x_all.shape[0] // blocks
    across = (((1,), (1,)), ((), ()))
    units = w_gate.shape[1]
    tile = 256 if units % 256 == 0 else units
    tiles = units // tile
    lanes = grad_sum.shape[1]
    copies = []
    if load:
        rank = given[3].shape[0]
        for j in range(tiles):
            part = pl.ds(j * tile, tile)
            copies.append((given[0].at[:, part], w_gate.at[:, part]))
            copies.append((given[1].at[:, part], w_up.at[:, part]))
            copies.append((given[2].at[part, :], w_down.at[part, :]))
        for i in range(low_proj.shape[0] // rank):
            copies.append((given[3], low_proj.at[pl.ds(i * rank, rank), :]))
        copies.append((given[4], high_proj))
        copies.append((apart[0], x_all.at[:rows]))
        copies.append((apart[1], dy_all.at[:rows]))
        copies = [
            pltpu.make_async_copy(src, dst, refs[-1].at[i]) for i, (src, dst) in enumerate(copies)
        ]
        for copy in copies[3 * tiles :] + copies[: 3 * tiles]:
            copy.start()
    if blocks == 1:
        x_all, dy_all = block_in[0].at[:rows, :], block_in[0].at[rows:, :]
    for i, block in enumerate(block_in if blocks > 1 else ()):
        place = slice((blocks - whole + i) * rows, (blocks - whole + i + 1) * rows)
        x_all[place, :] = block[:rows, :]
        dy_all[place, :] = block[rows:, :]
    low_sum[...] = jnp.zeros_like(low_sum)
    grad_sum[...] = jnp.zeros_like(grad_sum)

    def one_tile(j):
        part = pl.ds(j * tile, tile)
        gate_val = jnp.dot(x_all[...], w_gate[:, part], preferred_element_type=jnp.float32)
        up_val = jnp.dot(x_all[...], w_up[:, part], preferred_element_type=jnp.float32)
        hidden = (jax.nn.silu(gate_val) * up_val).astype(jnp.bfloat16)
        back = lax.dot_general(
            dy_all[...], w_down[part, :], across, preferred_element_type=jnp.float32
        )
        terms = hidden.astype(jnp.float32) * back
        for cut in range(0, tile, lanes):
            grad_sum[...] += terms[:, cut : cut + lanes]
        low_sum[...] += lax.dot_general(
            low_proj[:, part], hidden, across, preferred_element_type=jnp.float32
        )

    for copy in copies[3 * tiles :]:
        copy.wait()
    for j in range(tiles):
        for copy in copies[3 * j : 3 * j + 3] if load else []:
            copy.wait()
        one_tile(j)

    low_side[...] = low_sum[...].astype(low_side.dtype)
    proj_cot[...] = lax.dot_general(
        high_proj[...], dy_all[...], across, preferred_element_type=jnp.float32
    )
    sheet[...] = sheet_in[...]
    for i in range(blocks):
        total = jnp.sum(
            jnp.transpose(grad_sum[i * rows : (i + 1) * rows, :]), axis=0, keepdims=True
        )
        sheet[block_owner(names[i], sheet.shape[0] // 2), 0:1, :] = total


def work(names, sheet, block_in, weights, apart=(), load=0):
    width, units = weights[0].shape
    low_width, rank = weights[3].shape[0] * max(load, 1), weights[4].shape[0]
    blocks = len(names)
    rows = block_in[0].shape[0] // 2
    inside = pl.BlockSpec(memory_space=pltpu.VMEM)
    loaded = []
    if load:
        shapes = [w.shape for w in weights]
        shapes[3] = (low_width, units)
        loaded = [jax.ShapeDtypeStruct(shape, weights[0].dtype) for shape in shapes]
    tiles = units // 256 if units % 256 == 0 else 1
    call = pl.pallas_call(
        functools.partial(rows_kernel, names, load > 0),
        out_shape=[
            jax.ShapeDtypeStruct(sheet.shape, jnp.float32),
            jax.ShapeDtypeStruct((low_width, blocks * rows), jnp.bfloat16),
            jax.ShapeDtypeStruct((rank, blocks * rows), jnp.float32),
        ]
        + loaded,
        in_specs=[inside]
        + [pl.BlockSpec(memory_space=pl.ANY)] * len(apart)
        + [inside] * len(block_in)
        + [pl.BlockSpec(memory_space=pl.ANY) if load else inside] * len(weights),
        out_specs=[inside] * (3 + len(loaded)),
        scratch_shapes=[
            pltpu.VMEM((blocks * rows, width), jnp.bfloat16),
            pltpu.VMEM((blocks * rows, width), jnp.bfloat16),
            pltpu.VMEM((low_width, blocks * rows), jnp.float32),
            pltpu.VMEM((blocks * rows, 128), jnp.float32),
        ]
        + ([pltpu.SemaphoreType.DMA((3 * tiles + load + 3,))] if load else []),
        compiler_params=pltpu.CompilerParams(
            vmem_limit_bytes=(LOAD_MIB if load else 16) * 1024 * 1024
        ),
        cost_estimate=pl.CostEstimate(
            flops=6 * blocks * rows * width * units,
            bytes_accessed=4 * blocks * rows * width,
            transcendentals=blocks * rows * units,
        ),
    )
    return call(sheet, *apart, *block_in, *weights)


def front_part(x, weights):
    w_gate, w_up, _, low_proj, _ = weights
    across = (((1,), (1,)), ((), ()))
    units = w_gate.shape[1]
    tile = 256 if units % 256 == 0 else units
    pieces, low = [], 0.0
    for cut in range(0, units, tile):
        part = pl.ds(cut, tile)
        gate_val = jnp.dot(x[...], w_gate[:, part], preferred_element_type=jnp.float32)
        up_val = jnp.dot(x[...], w_up[:, part], preferred_element_type=jnp.float32)
        pieces.append((jax.nn.silu(gate_val) * up_val).astype(jnp.bfloat16))
        low += lax.dot_general(
            low_proj[:, part], pieces[-1], across, preferred_element_type=jnp.float32
        )
    return pieces, low


def back_part(dy, pieces, weights):
    _, _, w_down, _, high_proj = weights
    across = (((1,), (1,)), ((), ()))
    total, cut = 0.0, 0
    for piece in pieces:
        part = pl.ds(cut, piece.shape[1])
        cut += piece.shape[1]
        back = lax.dot_general(
            dy[...], w_down[part, :], across, preferred_element_type=jnp.float32
        )
        terms = piece.astype(jnp.float32) * back
        for spot in range(0, terms.shape[1], 128):
            total += terms[:, spot : spot + 128]
    proj = lax.dot_general(
        high_proj[...], dy[...], across, preferred_element_type=jnp.float32
    )
    return jnp.sum(jnp.transpose(total), axis=0, keepdims=True), proj


def other_kernel(name, block, *refs):
    weights, sheet_in, sheet, out = refs[:5], *refs[5:]
    rows = block.shape[0] // 2
    pieces, low = front_part(block.at[:rows, :], weights)
    line, proj = back_part(block.at[rows:, :], pieces, weights)
    sheet[...] = sheet_in[...]
    sheet[block_owner(name, sheet.shape[0] // 2), 3:4, :] = line
    out[: low.shape[0], :] = low
    out[low.shape[0] :, :] = proj


def front_kernel(x, *refs):
    hidden, low_side, hidden_other, low_other = refs[10:]
    for weights, units, low in (
        (refs[:5], hidden, low_side),
        (refs[5:10], hidden_other, low_other),
    ):
        pieces, value = front_part(x, weights)
        low[...] = value.astype(low.dtype)
        for i, piece in enumerate(pieces):
            width = piece.shape[1]
            units[:, i * width : (i + 1) * width] = piece


def back_kernel(name, dy, hidden, hidden_other, low_other, before, *refs):
    sheet_in, sheet, proj_cot, other = refs[10:]
    sheet[...] = sheet_in[...]
    owner = block_owner(name, sheet.shape[0] // 2)
    rank = proj_cot.shape[0]
    other[0] = before[...]
    other[1, :rank, :] = low_other[...]
    for which, units in enumerate((hidden, hidden_other)):
        width = units.shape[1]
        tile = 256 if width % 256 == 0 else width
        pieces = [units[:, cut : cut + tile] for cut in range(0, width, tile)]
        line, proj = back_part(dy, pieces, refs[5 * which : 5 * which + 5])
        sheet[owner, 3 * which : 3 * which + 1, :] = line
        if which:
            other[1, rank:, :] = proj
        else:
            proj_cot[...] = proj


def on_core(kernel, args, out_shape, flops=0):
    inside = pl.BlockSpec(memory_space=pltpu.VMEM)
    return pl.pallas_call(
        kernel,
        out_shape=out_shape,
        in_specs=[inside] * len(args),
        out_specs=[inside] * len(out_shape),
        compiler_params=pltpu.CompilerParams(vmem_limit_bytes=16 * 1024 * 1024),
        cost_estimate=pl.CostEstimate(flops=flops, bytes_accessed=2**20, transcendentals=0),
    )(*args)


def outcome_kernel(jobs, late, returned, routes, handed, *refs):
    low_in, proj_in = refs[: len(jobs)], refs[len(jobs) : 2 * len(jobs)]
    feat, route_grad = refs[-2:]
    rows = returned.shape[2]
    width, rank = low_in[0].shape[0], proj_in[0].shape[0]
    doc_of = lax.broadcasted_iota(jnp.int32, (width, rows), 0) // rank
    total = jnp.zeros(feat.shape, jnp.float32)
    for names, low_side, proj_cot in zip(jobs, low_in, proj_in):
        spread, high_side = [], []
        for i, name in enumerate(names):
            place = slice(i * rows, (i + 1) * rows)
            owner = block_owner(name, returned.shape[0] // 2)
            weight = returned[owner, 1:2, :]
            doc = returned[owner, 2:3, :].astype(jnp.int32)
            high_side.append((weight * proj_cot[:, place]).astype(jnp.bfloat16))
            low = low_side[:, place].astype(jnp.float32)
            spread.append(jnp.where(doc == doc_of, low, 0.0).astype(jnp.bfloat16))
        total += lax.dot_general(
            jnp.concatenate(spread, axis=1),
            jnp.concatenate(high_side, axis=1),
            (((1,), (1,)), ((), ())),
            preferred_element_type=jnp.float32,
        )
    spread, high_side = [], []
    for i, (chain, step, _) in enumerate(late):
        owner = block_owner((chain, step, True), returned.shape[0] // 2)
        weight = returned[owner, 1:2, :]
        doc = returned[owner, 2:3, :].astype(jnp.int32)
        high_side.append((weight * handed[i, rank:, :]).astype(jnp.bfloat16))
        low = handed[i, :rank, :].astype(jnp.bfloat16).astype(jnp.float32)
        parts = [jnp.where(doc == d, low, 0.0) for d in range(width // rank)]
        spread.append(jnp.concatenate(parts, axis=0).astype(jnp.bfloat16))
    total += lax.dot_general(
        jnp.concatenate(spread, axis=1),
        jnp.concatenate(high_side, axis=1),
        (((1,), (1,)), ((), ())),
        preferred_element_type=jnp.float32,
    )
    feat[...] = total
    picked = jnp.zeros(route_grad.shape, jnp.float32)
    for e in range(returned.shape[0]):
        picked = jnp.where(routes[...] == e, returned[e, 0:1, :], picked)
    for name in late:
        sender = block_owner(name, returned.shape[0] // 2)
        other = sender + 1 - 2 * lax.rem(sender, 2)
        picked = jnp.where(routes[...] == other, returned[sender, 3:4, :], picked)
    route_grad[...] = picked


def facts_kernel(routes, combine, doc_ids, out):
    groups, lines, rows = out.shape
    expert = lax.broadcasted_iota(jnp.int32, (groups, rows), 0)
    weight = jnp.zeros((groups, rows), jnp.float32)
    for k in range(routes.shape[0]):
        share = combine[k : k + 1, :].astype(jnp.float32)
        weight += jnp.where(routes[k : k + 1, :] == expert, share, 0.0)
    line = lax.broadcasted_iota(jnp.int32, (lines, rows), 0)
    doc = doc_ids[...].astype(jnp.float32)
    for e in range(groups):
        out[e] = jnp.where(line == 1, weight[e : e + 1, :], doc)


def stack_kernel(top, bottom, out):
    rows = top.shape[0]
    out[:rows, :] = top[...]
    out[rows:, :] = bottom[...]


def stack(top, bottom):
    inside = pl.BlockSpec(memory_space=pltpu.VMEM)
    return pl.pallas_call(
        stack_kernel,
        out_shape=jax.ShapeDtypeStruct((2 * top.shape[0], top.shape[1]), top.dtype),
        in_specs=[inside] * 2,
        out_specs=inside,
        compiler_params=pltpu.CompilerParams(vmem_limit_bytes=8 * 1024 * 1024),
    )(top, bottom)


def split_kernel(block, top, bottom):
    rows = top.shape[0]
    top[...] = block[:rows, :]
    bottom[...] = block[rows:, :]


def split(block):
    half = jax.ShapeDtypeStruct((block.shape[0] // 2, block.shape[1]), block.dtype)
    return on_core(split_kernel, (block,), [half] * 2)


def load_kernel(*refs):
    ins, outs, sems = refs[:5], refs[5:10], refs[10]
    other = 1 - lax.rem(lax.axis_index("exp"), 2)
    copies = [
        pltpu.make_async_copy(src.at[other], dst, sems.at[i])
        for i, (src, dst) in enumerate(zip(ins, outs))
    ]
    for copy in copies:
        copy.start()
    for copy in copies:
        copy.wait()


def load_other(pairs):
    return pl.pallas_call(
        load_kernel,
        out_shape=[jax.ShapeDtypeStruct(w.shape[1:], w.dtype) for w in pairs],
        in_specs=[pl.BlockSpec(memory_space=pl.ANY)] * len(pairs),
        out_specs=[pl.BlockSpec(memory_space=pltpu.VMEM)] * len(pairs),
        scratch_shapes=[pltpu.SemaphoreType.DMA((len(pairs),))],
        compiler_params=pltpu.CompilerParams(vmem_limit_bytes=PAIR_MIB * 1024 * 1024),
    )(*pairs)


def by_ring(
    tokens, cotangent, routes, combine, doc_ids, w_gate, w_up, w_down, proj_hidden, proj_output
):
    tok_rows, chosen = routes.shape
    groups = lax.axis_size("exp")
    docs_count = max(2, tok_rows * groups // DOC_TOK)
    chips = groups // 2
    half = chips // 2
    ring = list(range(0, chips, 2)) + list(range(chips - 1, 0, -2))
    onward = []
    for place in range(chips):
        onward.append((2 * ring[place], 2 * ring[(place + 1) % chips]))
        onward.append((2 * ring[place] + 1, 2 * ring[place - 1] + 1))
    across = [(i, i ^ 1) for i in range(groups)]

    def hop(block):
        return lax.ppermute(block, "exp", onward)

    def swap(block):
        return lax.ppermute(block, "exp", across)

    arrivals = [(c, step) for step in range(1, half + 1) for c in ("ab" if step < half else "a")]
    jobs = [(("a", 0, False), ("a", 0, True))]
    for i, (c, step) in enumerate(arrivals):
        job = ((c, step, False),)
        if i > 0:
            job += (arrivals[i - 1] + (True,),)
        if i == 1:
            job += (arrivals[0] + (False,),)
        if i == len(arrivals) - 1:
            jobs.append(job[:1])
        elif i == len(arrivals) - 2:
            jobs += [job[:1], job[1:]]
        elif i != 0:
            jobs.append(job)

    sheet = pl.pallas_call(
        facts_kernel,
        out_shape=jax.ShapeDtypeStruct((groups, 4, tok_rows), jnp.float32),
        in_specs=[pl.BlockSpec(memory_space=pltpu.VMEM)] * 3,
        out_specs=pl.BlockSpec(memory_space=pltpu.VMEM),
        compiler_params=pltpu.CompilerParams(vmem_limit_bytes=8 * 1024 * 1024),
    )(routes.T, combine.T, doc_ids[None, :])
    first = (hop(tokens), hop(cotangent))
    beside = stack(swap(tokens), swap(cotangent))

    inside = pl.BlockSpec(memory_space=pltpu.VMEM)
    given = (w_gate[0], w_up[0], w_down[0], proj_hidden[0].T, proj_output[0].T)
    weights = None
    lows, projs = [], []
    held = {("a", 0, True): beside}
    todo = list(jobs)

    def take():
        nonlocal sheet, weights
        names = todo.pop(0)
        blocks = [held[name] for name in names if name in held]
        if weights is None:
            sheet, low_side, proj_cot, *weights = work(
                names, sheet, blocks, given, apart=(tokens, cotangent), load=docs_count
            )
        else:
            sheet, low_side, proj_cot = work(names, sheet, blocks, weights)
        lows.append(low_side)
        projs.append(proj_cot)

    chain = {"b": beside}
    pairs = [[i, i + 1] for i in range(0, groups, 2)]
    gathered = [
        lax.all_gather(w, "exp", axis_index_groups=pairs, axis=0) for w in given
    ]
    for i, (c, step) in enumerate(arrivals[:-1]):
        block = hop(chain[c]) if i > 0 else first
        if i != 1:
            take()
            sheet, block = lax.optimization_barrier((sheet, block))
        if i == len(arrivals) - 3:
            sheet, gathered = lax.optimization_barrier((sheet, gathered))
            others = load_other(gathered)
            others, block = lax.optimization_barrier((others, block))
        if i == 0:
            block = stack(*block)
        chain[c] = held[(c, step, False)] = block
        if i < len(arrivals) - 2:
            held[(c, step, True)] = swap(block)
    x, dy = split(chain["a"])
    late = (arrivals[-2] + (False,), arrivals[-1] + (False,))
    dy, block = lax.optimization_barrier((dy, chain["b"]))
    held[late[0]] = block
    x, dy = hop(x), hop(dy)
    take()
    rank, units = proj_output.shape[2], w_gate.shape[2]
    flops = 2 * tok_rows * tokens.shape[1] * units
    lines = jax.ShapeDtypeStruct((2 * rank, tok_rows), jnp.float32)
    sheet_shape = jax.ShapeDtypeStruct(sheet.shape, jnp.float32)
    sheet, before = on_core(
        functools.partial(other_kernel, late[0]),
        (block, *others, sheet),
        [sheet_shape, lines],
        flops=3 * flops,
    )
    sheet, x = lax.optimization_barrier((sheet, x))
    hidden = jax.ShapeDtypeStruct((tok_rows, units), jnp.bfloat16)
    hidden, low_side, hidden_other, low_other = on_core(
        front_kernel,
        (x, *weights, *others),
        [
            hidden,
            jax.ShapeDtypeStruct((docs_count * rank, tok_rows), jnp.bfloat16),
            hidden,
            jax.ShapeDtypeStruct((rank, tok_rows), jnp.float32),
        ],
        flops=4 * flops,
    )
    take()
    sheet, dy = lax.optimization_barrier((sheet, dy))
    sheet, proj_cot, other = on_core(
        functools.partial(back_kernel, late[1]),
        (dy, hidden, hidden_other, low_other, before, *weights, *others, sheet),
        [
            sheet_shape,
            jax.ShapeDtypeStruct((rank, tok_rows), jnp.float32),
            jax.ShapeDtypeStruct((2,) + lines.shape, jnp.float32),
        ],
        flops=2 * flops,
    )
    lows.append(low_side)
    projs.append(proj_cot)
    handed = swap(other)
    returned = lax.all_to_all(sheet, "exp", split_axis=0, concat_axis=0, tiled=True)
    feature, route_grad = pl.pallas_call(
        functools.partial(outcome_kernel, jobs, late),
        out_shape=[
            jax.ShapeDtypeStruct((docs_count * rank, rank), jnp.float32),
            jax.ShapeDtypeStruct((chosen, tok_rows), jnp.float32),
        ],
        in_specs=[inside] * (3 + 2 * len(lows)),
        out_specs=[inside] * 2,
        compiler_params=pltpu.CompilerParams(vmem_limit_bytes=16 * 1024 * 1024),
    )(returned, routes.T, handed, *lows, *projs)
    return feature.reshape(docs_count, 1, rank, rank), route_grad.T


def by_routing(
    tokens, cotangent, routes, combine, doc_ids, w_gate, w_up, w_down, proj_hidden, proj_output
):
    tok_rows, chosen = routes.shape
    local_count = w_gate.shape[0]
    groups = lax.axis_size("exp")
    experts = local_count * groups
    capacity = max(2, tok_rows * chosen * 5 // (4 * experts))
    docs_count = max(2, tok_rows * groups // DOC_TOK)
    entries = tok_rows * chosen
    width = tokens.shape[1]
    flat_routes = routes.reshape(-1)
    member = (flat_routes[:, None] == jnp.arange(experts, dtype=jnp.int32)[None, :]).astype(
        jnp.int32
    )
    slot_rank = jnp.sum((jnp.cumsum(member, axis=0) - 1) * member, axis=1)
    position = flat_routes * capacity + slot_rank
    source = (
        jnp.full((experts * capacity,), -1, jnp.int32)
        .at[position]
        .set(jnp.arange(entries, dtype=jnp.int32))
    )
    filled = source >= 0
    safe_source = jnp.maximum(source, 0)
    token_of = safe_source // chosen
    send_x = jnp.where(filled[:, None], tokens[token_of], 0)
    send_dy = jnp.where(filled[:, None], cotangent[token_of], 0)
    send_w = jnp.where(filled, combine.reshape(-1)[safe_source], 0)
    send_doc = jnp.where(filled, doc_ids[token_of], -1).astype(jnp.bfloat16)

    def exchange(array):
        array = array.reshape((groups, local_count, capacity) + array.shape[1:])
        return lax.all_to_all(array, "exp", split_axis=0, concat_axis=0, tiled=True)

    recv_x, recv_dy, recv_w, recv_doc = (
        exchange(send_x),
        exchange(send_dy),
        exchange(send_w),
        exchange(send_doc),
    )
    slots = groups * capacity
    grads, feats = [], []
    for e in range(local_count):
        hidden = swiglu(recv_x[:, e].reshape(slots, width), w_gate[e], w_up[e])
        grad, feature = finish(
            hidden,
            recv_dy[:, e].reshape(slots, width),
            recv_w[:, e].reshape(slots),
            recv_doc[:, e].reshape(slots),
            w_down[e],
            proj_hidden[e],
            proj_output[e],
            docs_count,
        )
        grads.append(grad.reshape(groups, capacity))
        feats.append(feature)
    slot_grad = jnp.stack(grads, axis=1)
    returned = lax.all_to_all(slot_grad, "exp", split_axis=0, concat_axis=0, tiled=True)
    route_grad = returned.reshape(-1)[position].reshape(tok_rows, chosen)
    return jnp.stack(feats, axis=1), route_grad


def on_device(tokens, cotangent, routes, combine, doc_ids, w_gate, *rest):
    tok_rows, chosen = routes.shape
    experts = w_gate.shape[0] * lax.axis_size("exp")
    dense = w_gate.shape[0] == 1 and 4 * chosen >= experts and experts >= 8 and experts % 4 == 0
    plan = by_ring if dense else by_routing
    return plan(tokens, cotangent, routes, combine, doc_ids, w_gate, *rest)


def solution(mesh):
    placed = (
        P(("grp", "exp"), None),
        P(("grp", "exp"), None),
        P(("grp", "exp"), None),
        P(("grp", "exp"), None),
        P(("grp", "exp")),
        P("exp", None, None),
        P("exp", None, None),
        P("exp", None, None),
        P("exp", None, None),
        P("exp", None, None),
    )
    return jax.shard_map(
        on_device,
        mesh=mesh,
        in_specs=placed,
        out_specs=(P("grp", "exp", None, None), P(("grp", "exp"), None)),
        check_vma=False,
    )
```

```python
import functools

import jax
import jax.numpy as jnp
from jax import lax
from jax.experimental import pallas as pl
from jax.experimental.pallas import tpu as pltpu
from jax.sharding import PartitionSpec as P

DOC_TOK = 512
LOAD_MIB = 40


def swiglu(rows, w_gate, w_up):
    gate_val = jnp.dot(rows, w_gate, preferred_element_type=jnp.float32)
    up_val = jnp.dot(rows, w_up, preferred_element_type=jnp.float32)
    return (jax.nn.silu(gate_val) * up_val).astype(jnp.bfloat16)


def finish(hidden, rows_dy, rows_w, rows_doc, w_down, proj_hidden, proj_output, docs_count):
    out_val = jnp.dot(hidden, w_down, preferred_element_type=jnp.float32)
    grad = jnp.sum(rows_dy.astype(jnp.float32) * out_val, axis=-1)
    low_side = jnp.dot(hidden, proj_hidden, preferred_element_type=jnp.float32).astype(
        jnp.bfloat16
    )
    proj_cot = jnp.dot(rows_dy, proj_output, preferred_element_type=jnp.float32)
    high_side = (rows_w.astype(jnp.float32)[:, None] * proj_cot).astype(jnp.bfloat16)
    doc_table = jnp.arange(docs_count, dtype=jnp.int32).astype(jnp.bfloat16)
    onehot = (rows_doc[:, None] == doc_table).astype(jnp.bfloat16)
    spread = onehot[:, :, None] * low_side[:, None, :]
    spread = spread.reshape(spread.shape[0], -1)
    feature = lax.dot_general(
        spread, high_side, (((0,), (0,)), ((), ())), preferred_element_type=jnp.float32
    )
    return grad, feature.reshape(docs_count, low_side.shape[1], high_side.shape[1])


def block_owner(name, chips):
    chain, step, handed = name
    me = lax.axis_index("exp")
    core, chip = lax.rem(me, 2), lax.div(me, 2)
    turn = chips // 2
    place = jnp.where(lax.rem(chip, 2) == 0, lax.div(chip, 2), chips - 1 - lax.div(chip, 2))
    way = 2 * core - 1
    place = place + (-way if handed else way) * step
    place = lax.rem(place + chips, chips)
    chip = jnp.where(place < turn, 2 * place, 2 * (chips - 1 - place) + 1)
    return 2 * chip + (core if (chain == "a") != handed else 1 - core)


def rows_kernel(names, load, *refs):
    blocks = len(names)
    apart = refs[1:3] if load else ()
    refs = refs[:1] + refs[3:] if load else refs
    whole = blocks - 1 if load else blocks
    sheet_in, block_in = refs[0], refs[1 : 1 + whole]
    given = refs[1 + whole : 6 + whole]
    sheet, low_side, proj_cot = refs[6 + whole : 9 + whole]
    x_all, dy_all, low_sum, grad_sum = refs[-5:-1] if load else refs[-4:]
    w_gate, w_up, w_down, low_proj, high_proj = refs[9 + whole : 14 + whole] if load else given
    rows = x_all.shape[0] // blocks
    across = (((1,), (1,)), ((), ()))
    units = w_gate.shape[1]
    tile = 256 if units % 256 == 0 else units
    tiles = units // tile
    lanes = grad_sum.shape[1]
    copies = []
    if load:
        rank = given[3].shape[0]
        for j in range(tiles):
            part = pl.ds(j * tile, tile)
            copies.append((given[0].at[:, part], w_gate.at[:, part]))
            copies.append((given[1].at[:, part], w_up.at[:, part]))
            copies.append((given[2].at[part, :], w_down.at[part, :]))
        for i in range(low_proj.shape[0] // rank):
            copies.append((given[3], low_proj.at[pl.ds(i * rank, rank), :]))
        copies.append((given[4], high_proj))
        copies.append((apart[0], x_all.at[:rows]))
        copies.append((apart[1], dy_all.at[:rows]))
        copies = [
            pltpu.make_async_copy(src, dst, refs[-1].at[i]) for i, (src, dst) in enumerate(copies)
        ]
        for copy in copies[3 * tiles :] + copies[: 3 * tiles]:
            copy.start()
    if blocks == 1:
        x_all, dy_all = block_in[0].at[:rows, :], block_in[0].at[rows:, :]
    for i, block in enumerate(block_in if blocks > 1 else ()):
        place = slice((blocks - whole + i) * rows, (blocks - whole + i + 1) * rows)
        x_all[place, :] = block[:rows, :]
        dy_all[place, :] = block[rows:, :]

    def one_tile(j):
        part = pl.ds(j * tile, tile)
        gate_val = jnp.dot(x_all[...], w_gate[:, part], preferred_element_type=jnp.float32)
        up_val = jnp.dot(x_all[...], w_up[:, part], preferred_element_type=jnp.float32)
        hidden = (jax.nn.silu(gate_val) * up_val).astype(jnp.bfloat16)
        back = lax.dot_general(
            dy_all[...], w_down[part, :], across, preferred_element_type=jnp.float32
        )
        terms = hidden.astype(jnp.float32) * back
        total = terms[:, :lanes]
        for cut in range(lanes, tile, lanes):
            total += terms[:, cut : cut + lanes]
        grad_sum[...] = total if j == 0 else grad_sum[...] + total
        low = lax.dot_general(
            low_proj[:, part], hidden, across, preferred_element_type=jnp.float32
        )
        low_sum[...] = low if j == 0 else low_sum[...] + low

    for copy in copies[3 * tiles :]:
        copy.wait()
    for j in range(tiles):
        for copy in copies[3 * j : 3 * j + 3] if load else []:
            copy.wait()
        one_tile(j)

    low_side[...] = low_sum[...].astype(low_side.dtype)
    proj_cot[...] = lax.dot_general(
        high_proj[...], dy_all[...], across, preferred_element_type=jnp.float32
    )
    sheet[...] = sheet_in[...]
    for i in range(blocks):
        total = jnp.sum(
            jnp.transpose(grad_sum[i * rows : (i + 1) * rows, :]), axis=0, keepdims=True
        )
        sheet[block_owner(names[i], sheet.shape[0] // 2), 0:1, :] = total


def work(names, sheet, block_in, weights, apart=(), load=0):
    width, units = weights[0].shape
    low_width, rank = weights[3].shape[0] * max(load, 1), weights[4].shape[0]
    blocks = len(names)
    rows = block_in[0].shape[0] // 2
    inside = pl.BlockSpec(memory_space=pltpu.VMEM)
    loaded = []
    if load:
        shapes = [w.shape for w in weights]
        shapes[3] = (low_width, units)
        loaded = [jax.ShapeDtypeStruct(shape, weights[0].dtype) for shape in shapes]
    tiles = units // 256 if units % 256 == 0 else 1
    call = pl.pallas_call(
        functools.partial(rows_kernel, names, load > 0),
        out_shape=[
            jax.ShapeDtypeStruct(sheet.shape, jnp.float32),
            jax.ShapeDtypeStruct((low_width, blocks * rows), jnp.bfloat16),
            jax.ShapeDtypeStruct((rank, blocks * rows), jnp.float32),
        ]
        + loaded,
        in_specs=[inside]
        + [pl.BlockSpec(memory_space=pl.ANY)] * len(apart)
        + [inside] * len(block_in)
        + [pl.BlockSpec(memory_space=pl.ANY) if load else inside] * len(weights),
        out_specs=[inside] * (3 + len(loaded)),
        scratch_shapes=[
            pltpu.VMEM((blocks * rows, width), jnp.bfloat16),
            pltpu.VMEM((blocks * rows, width), jnp.bfloat16),
            pltpu.VMEM((low_width, blocks * rows), jnp.float32),
            pltpu.VMEM((blocks * rows, 128), jnp.float32),
        ]
        + ([pltpu.SemaphoreType.DMA((3 * tiles + load + 3,))] if load else []),
        compiler_params=pltpu.CompilerParams(
            vmem_limit_bytes=(LOAD_MIB if load else 16) * 1024 * 1024
        ),
        cost_estimate=pl.CostEstimate(
            flops=6 * blocks * rows * width * units,
            bytes_accessed=4 * blocks * rows * width,
            transcendentals=blocks * rows * units,
        ),
    )
    return call(sheet, *apart, *block_in, *weights)


def front_kernel(*refs):
    blocks = len(refs) - 8
    x_in = refs[:blocks]
    w_gate, w_up, low_proj, hidden, low_first, low_last, x_all, low_sum = refs[blocks:]
    begin = 0
    for x in x_in:
        x_all[begin : begin + x.shape[0], :] = x[...]
        begin += x.shape[0]
    units = w_gate.shape[1]
    tile = 256 if units % 256 == 0 else units
    for cut in range(0, units, tile):
        part = pl.ds(cut, tile)
        gate_val = jnp.dot(x_all[...], w_gate[:, part], preferred_element_type=jnp.float32)
        up_val = jnp.dot(x_all[...], w_up[:, part], preferred_element_type=jnp.float32)
        piece = (jax.nn.silu(gate_val) * up_val).astype(jnp.bfloat16)
        hidden[:, part] = piece
        low = lax.dot_general(
            low_proj[:, part],
            piece,
            (((1,), (1,)), ((), ())),
            preferred_element_type=jnp.float32,
        )
        low_sum[...] = low if cut == 0 else low_sum[...] + low
    cut = low_first.shape[1]
    low_first[...] = low_sum[:, :cut].astype(low_first.dtype)
    low_last[...] = low_sum[:, cut:].astype(low_last.dtype)


def front(x_in, weights, last):
    w_gate, w_up, _, low_proj, _ = weights
    rows, width = sum(x.shape[0] for x in x_in), x_in[0].shape[1]
    units = w_gate.shape[1]
    inside = pl.BlockSpec(memory_space=pltpu.VMEM)
    return pl.pallas_call(
        front_kernel,
        out_shape=[
            jax.ShapeDtypeStruct((rows, units), jnp.bfloat16),
            jax.ShapeDtypeStruct((low_proj.shape[0], rows - last), jnp.bfloat16),
            jax.ShapeDtypeStruct((low_proj.shape[0], last), jnp.bfloat16),
        ],
        in_specs=[inside] * (len(x_in) + 3),
        out_specs=[inside] * 3,
        scratch_shapes=[
            pltpu.VMEM((rows, width), jnp.bfloat16),
            pltpu.VMEM((low_proj.shape[0], rows), jnp.float32),
        ],
        compiler_params=pltpu.CompilerParams(vmem_limit_bytes=16 * 1024 * 1024),
        cost_estimate=pl.CostEstimate(
            flops=4 * rows * width * units,
            bytes_accessed=2 * rows * width,
            transcendentals=rows * units,
        ),
    )(*x_in, w_gate, w_up, low_proj)


def back_kernel(names, begin, *refs):
    blocks = len(names)
    sheet_in, dy_in = refs[0], refs[1 : 1 + blocks]
    hidden, w_down, high_proj, sheet, proj_cot, dy_all, grad_sum = refs[1 + blocks :]
    rows = dy_in[0].shape[0]
    across = (((1,), (1,)), ((), ()))
    for i in range(blocks):
        dy_all[i * rows : (i + 1) * rows, :] = dy_in[i][...]
    units, lanes = hidden.shape[1], grad_sum.shape[1]
    tile = 256 if units % 256 == 0 else units
    for cut in range(0, units, tile):
        part = pl.ds(cut, tile)
        back = lax.dot_general(
            dy_all[...], w_down[part, :], across, preferred_element_type=jnp.float32
        )
        terms = hidden[begin : begin + blocks * rows, part].astype(jnp.float32) * back
        total = terms[:, :lanes]
        for spot in range(lanes, tile, lanes):
            total += terms[:, spot : spot + lanes]
        grad_sum[...] = total if cut == 0 else grad_sum[...] + total
    proj_cot[...] = lax.dot_general(
        high_proj[...], dy_all[...], across, preferred_element_type=jnp.float32
    )
    sheet[...] = sheet_in[...]
    for i in range(blocks):
        total = jnp.sum(
            jnp.transpose(grad_sum[i * rows : (i + 1) * rows, :]), axis=0, keepdims=True
        )
        sheet[block_owner(names[i], sheet.shape[0] // 2), 0:1, :] = total


def finish_late(names, sheet, dy_in, hidden, begin, weights):
    _, _, w_down, _, high_proj = weights
    rows, width = len(dy_in) * dy_in[0].shape[0], dy_in[0].shape[1]
    units = hidden.shape[1]
    inside = pl.BlockSpec(memory_space=pltpu.VMEM)
    return pl.pallas_call(
        functools.partial(back_kernel, names, begin),
        out_shape=[
            jax.ShapeDtypeStruct(sheet.shape, jnp.float32),
            jax.ShapeDtypeStruct((high_proj.shape[0], rows), jnp.float32),
        ],
        in_specs=[inside] * (len(dy_in) + 4),
        out_specs=[inside] * 2,
        scratch_shapes=[
            pltpu.VMEM((rows, width), jnp.bfloat16),
            pltpu.VMEM((rows, 128), jnp.float32),
        ],
        compiler_params=pltpu.CompilerParams(vmem_limit_bytes=16 * 1024 * 1024),
        cost_estimate=pl.CostEstimate(
            flops=2 * rows * width * units,
            bytes_accessed=2 * rows * width,
            transcendentals=0,
        ),
    )(sheet, *dy_in, hidden, w_down, high_proj)


def outcome_kernel(jobs, returned, routes, *refs):
    low_in, proj_in = refs[: len(jobs)], refs[len(jobs) : 2 * len(jobs)]
    feat, route_grad = refs[-2:]
    rows = returned.shape[2]
    width, rank = low_in[0].shape[0], proj_in[0].shape[0]
    doc_of = lax.broadcasted_iota(jnp.int32, (width, rows), 0) // rank
    spread, high_side = [], []
    for names, low_side, proj_cot in zip(jobs, low_in, proj_in):
        for i, name in enumerate(names):
            place = slice(i * rows, (i + 1) * rows)
            owner = block_owner(name, returned.shape[0] // 2)
            weight = returned[owner, 1:2, :]
            doc = returned[owner, 2:3, :].astype(jnp.int32)
            high_side.append((weight * proj_cot[:, place]).astype(jnp.bfloat16))
            low = low_side[:, place].astype(jnp.float32)
            spread.append(jnp.where(doc == doc_of, low, 0.0).astype(jnp.bfloat16))
    feat[...] = lax.dot_general(
        jnp.concatenate(spread, axis=1),
        jnp.concatenate(high_side, axis=1),
        (((1,), (1,)), ((), ())),
        preferred_element_type=jnp.float32,
    )
    picked = jnp.zeros(route_grad.shape, jnp.float32)
    for e in range(returned.shape[0]):
        picked = jnp.where(routes[...] == e, returned[e, 0:1, :], picked)
    route_grad[...] = picked


def facts_kernel(routes, combine, doc_ids, out):
    groups, lines, rows = out.shape
    expert = lax.broadcasted_iota(jnp.int32, (groups, rows), 0)
    weight = jnp.zeros((groups, rows), jnp.float32)
    for k in range(routes.shape[0]):
        share = combine[k : k + 1, :].astype(jnp.float32)
        weight += jnp.where(routes[k : k + 1, :] == expert, share, 0.0)
    line = lax.broadcasted_iota(jnp.int32, (lines, rows), 0)
    doc = doc_ids[...].astype(jnp.float32)
    for e in range(groups):
        out[e] = jnp.where(line == 1, weight[e : e + 1, :], doc)


def stack_kernel(top, bottom, out):
    rows = top.shape[0]
    out[:rows, :] = top[...]
    out[rows:, :] = bottom[...]


def stack(top, bottom):
    inside = pl.BlockSpec(memory_space=pltpu.VMEM)
    return pl.pallas_call(
        stack_kernel,
        out_shape=jax.ShapeDtypeStruct((2 * top.shape[0], top.shape[1]), top.dtype),
        in_specs=[inside] * 2,
        out_specs=inside,
        compiler_params=pltpu.CompilerParams(vmem_limit_bytes=8 * 1024 * 1024),
    )(top, bottom)


def split_kernel(cuts, block, *parts):
    for (begin, count), part in zip(cuts, parts):
        part[...] = block[begin : begin + count, :]


def split(block, cuts):
    inside = pl.BlockSpec(memory_space=pltpu.VMEM)
    return pl.pallas_call(
        functools.partial(split_kernel, cuts),
        out_shape=[
            jax.ShapeDtypeStruct((count, block.shape[1]), block.dtype) for _, count in cuts
        ],
        in_specs=[inside],
        out_specs=[inside] * len(cuts),
        compiler_params=pltpu.CompilerParams(vmem_limit_bytes=8 * 1024 * 1024),
    )(block)


def by_ring(
    tokens, cotangent, routes, combine, doc_ids, w_gate, w_up, w_down, proj_hidden, proj_output
):
    tok_rows, chosen = routes.shape
    groups = lax.axis_size("exp")
    docs_count = max(2, tok_rows * groups // DOC_TOK)
    chips = groups // 2
    half = chips // 2
    ring = list(range(0, chips, 2)) + list(range(chips - 1, 0, -2))
    onward = []
    for place in range(chips):
        onward.append((2 * ring[place], 2 * ring[(place + 1) % chips]))
        onward.append((2 * ring[place] + 1, 2 * ring[place - 1] + 1))
    across = [(i, i ^ 1) for i in range(groups)]

    def hop(block):
        return lax.ppermute(block, "exp", onward)

    def swap(block):
        return lax.ppermute(block, "exp", across)

    arrivals = [(c, step) for step in range(1, half + 1) for c in ("ab" if step < half else "a")]
    jobs = [(("a", 0, False), ("a", 0, True))]
    for i, (c, step) in enumerate(arrivals):
        job = ((c, step, False),)
        if i > 0:
            job += (arrivals[i - 1] + (True,),)
        if i == 1:
            job += (arrivals[0] + (False,),)
        if i == len(arrivals) - 1:
            jobs += [(job[1], job[0]), ((c, step, True),)]
        elif i != 0:
            jobs.append(job)

    sheet = pl.pallas_call(
        facts_kernel,
        out_shape=jax.ShapeDtypeStruct((groups, 4, tok_rows), jnp.float32),
        in_specs=[pl.BlockSpec(memory_space=pltpu.VMEM)] * 3,
        out_specs=pl.BlockSpec(memory_space=pltpu.VMEM),
        compiler_params=pltpu.CompilerParams(vmem_limit_bytes=8 * 1024 * 1024),
    )(routes.T, combine.T, doc_ids[None, :])
    first = (hop(tokens), hop(cotangent))
    beside = stack(swap(tokens), swap(cotangent))

    inside = pl.BlockSpec(memory_space=pltpu.VMEM)
    given = (w_gate[0], w_up[0], w_down[0], proj_hidden[0].T, proj_output[0].T)
    weights = None
    lows, projs = [], []
    held = {("a", 0, True): beside}
    todo = list(jobs)

    def take():
        nonlocal sheet, weights
        names = todo.pop(0)
        blocks = [held[name] for name in names if name in held]
        if weights is None:
            sheet, low_side, proj_cot, *weights = work(
                names, sheet, blocks, given, apart=(tokens, cotangent), load=docs_count
            )
        else:
            sheet, low_side, proj_cot = work(names, sheet, blocks, weights)
        lows.append(low_side)
        projs.append(proj_cot)

    chain = {"b": beside}
    for i, (c, step) in enumerate(arrivals[:-1]):
        block = hop(chain[c]) if i > 0 else first
        if i != 1:
            take()
            sheet, block = lax.optimization_barrier((sheet, block))
        if i == 0:
            block = stack(*block)
        chain[c] = held[(c, step, False)] = block
        if i < len(arrivals) - 2:
            held[(c, step, True)] = swap(block)
    cut = tok_rows // 2
    cuts = ((0, cut), (cut, cut), (tok_rows, tok_rows))
    *x, dy = split(chain["a"], cuts)
    dy, _ = lax.optimization_barrier((dy, chain["b"]))
    x, dy = [hop(part) for part in x], hop(dy)
    *x_before, dy_before = split(chain["b"], ((0, tok_rows), (tok_rows, tok_rows)))
    x_before, dy_before = [swap(part) for part in x_before], swap(dy_before)
    take()
    sheet, x = lax.optimization_barrier((sheet, x))
    hidden, low_first, low_last = front(
        x_before + x + [swap(part) for part in x], weights, tok_rows
    )
    hidden, dy = lax.optimization_barrier((hidden, dy))
    dy_beside = swap(dy)
    sheet, proj_cot = finish_late(todo.pop(0), sheet, [dy_before, dy], hidden, 0, weights)
    lows.append(low_first)
    projs.append(proj_cot)
    sheet, proj_cot = finish_late(
        todo.pop(0), sheet, [dy_beside], hidden, 2 * tok_rows, weights
    )
    lows.append(low_last)
    projs.append(proj_cot)
    returned = lax.all_to_all(sheet, "exp", split_axis=0, concat_axis=0, tiled=True)
    rank = proj_output.shape[2]
    feature, route_grad = pl.pallas_call(
        functools.partial(outcome_kernel, jobs),
        out_shape=[
            jax.ShapeDtypeStruct((docs_count * rank, rank), jnp.float32),
            jax.ShapeDtypeStruct((chosen, tok_rows), jnp.float32),
        ],
        in_specs=[inside] * (2 + 2 * len(lows)),
        out_specs=[inside] * 2,
        compiler_params=pltpu.CompilerParams(vmem_limit_bytes=16 * 1024 * 1024),
    )(returned, routes.T, *lows, *projs)
    return feature.reshape(docs_count, 1, rank, rank), route_grad.T


def by_routing(
    tokens, cotangent, routes, combine, doc_ids, w_gate, w_up, w_down, proj_hidden, proj_output
):
    tok_rows, chosen = routes.shape
    local_count = w_gate.shape[0]
    groups = lax.axis_size("exp")
    experts = local_count * groups
    capacity = max(2, tok_rows * chosen * 5 // (4 * experts))
    docs_count = max(2, tok_rows * groups // DOC_TOK)
    entries = tok_rows * chosen
    width = tokens.shape[1]
    flat_routes = routes.reshape(-1)
    member = (flat_routes[:, None] == jnp.arange(experts, dtype=jnp.int32)[None, :]).astype(
        jnp.int32
    )
    slot_rank = jnp.sum((jnp.cumsum(member, axis=0) - 1) * member, axis=1)
    position = flat_routes * capacity + slot_rank
    source = (
        jnp.full((experts * capacity,), -1, jnp.int32)
        .at[position]
        .set(jnp.arange(entries, dtype=jnp.int32))
    )
    filled = source >= 0
    safe_source = jnp.maximum(source, 0)
    token_of = safe_source // chosen
    send_x = jnp.where(filled[:, None], tokens[token_of], 0)
    send_dy = jnp.where(filled[:, None], cotangent[token_of], 0)
    send_w = jnp.where(filled, combine.reshape(-1)[safe_source], 0)
    send_doc = jnp.where(filled, doc_ids[token_of], -1).astype(jnp.bfloat16)

    def exchange(array):
        array = array.reshape((groups, local_count, capacity) + array.shape[1:])
        return lax.all_to_all(array, "exp", split_axis=0, concat_axis=0, tiled=True)

    recv_x, recv_dy, recv_w, recv_doc = (
        exchange(send_x),
        exchange(send_dy),
        exchange(send_w),
        exchange(send_doc),
    )
    slots = groups * capacity
    grads, feats = [], []
    for e in range(local_count):
        hidden = swiglu(recv_x[:, e].reshape(slots, width), w_gate[e], w_up[e])
        grad, feature = finish(
            hidden,
            recv_dy[:, e].reshape(slots, width),
            recv_w[:, e].reshape(slots),
            recv_doc[:, e].reshape(slots),
            w_down[e],
            proj_hidden[e],
            proj_output[e],
            docs_count,
        )
        grads.append(grad.reshape(groups, capacity))
        feats.append(feature)
    slot_grad = jnp.stack(grads, axis=1)
    returned = lax.all_to_all(slot_grad, "exp", split_axis=0, concat_axis=0, tiled=True)
    route_grad = returned.reshape(-1)[position].reshape(tok_rows, chosen)
    return jnp.stack(feats, axis=1), route_grad


def on_device(tokens, cotangent, routes, combine, doc_ids, w_gate, *rest):
    tok_rows, chosen = routes.shape
    experts = w_gate.shape[0] * lax.axis_size("exp")
    dense = w_gate.shape[0] == 1 and 4 * chosen >= experts and experts >= 8 and experts % 4 == 0
    plan = by_ring if dense else by_routing
    return plan(tokens, cotangent, routes, combine, doc_ids, w_gate, *rest)


def solution(mesh):
    placed = (
        P(("grp", "exp"), None),
        P(("grp", "exp"), None),
        P(("grp", "exp"), None),
        P(("grp", "exp"), None),
        P(("grp", "exp")),
        P("exp", None, None),
        P("exp", None, None),
        P("exp", None, None),
        P("exp", None, None),
        P("exp", None, None),
    )
    return jax.shard_map(
        on_device,
        mesh=mesh,
        in_specs=placed,
        out_specs=(P("grp", "exp", None, None), P(("grp", "exp"), None)),
        check_vma=False,
    )
```

```python
import functools

import jax
import jax.numpy as jnp
from jax import lax
from jax.experimental import pallas as pl
from jax.experimental.pallas import tpu as pltpu
from jax.sharding import PartitionSpec as P

DOC_TOK = 512
LOAD_MIB = 40


def swiglu(rows, w_gate, w_up):
    gate_val = jnp.dot(rows, w_gate, preferred_element_type=jnp.float32)
    up_val = jnp.dot(rows, w_up, preferred_element_type=jnp.float32)
    return (jax.nn.silu(gate_val) * up_val).astype(jnp.bfloat16)


def finish(hidden, rows_dy, rows_w, rows_doc, w_down, proj_hidden, proj_output, docs_count):
    out_val = jnp.dot(hidden, w_down, preferred_element_type=jnp.float32)
    grad = jnp.sum(rows_dy.astype(jnp.float32) * out_val, axis=-1)
    low_side = jnp.dot(hidden, proj_hidden, preferred_element_type=jnp.float32).astype(
        jnp.bfloat16
    )
    proj_cot = jnp.dot(rows_dy, proj_output, preferred_element_type=jnp.float32)
    high_side = (rows_w.astype(jnp.float32)[:, None] * proj_cot).astype(jnp.bfloat16)
    doc_table = jnp.arange(docs_count, dtype=jnp.int32).astype(jnp.bfloat16)
    onehot = (rows_doc[:, None] == doc_table).astype(jnp.bfloat16)
    spread = onehot[:, :, None] * low_side[:, None, :]
    spread = spread.reshape(spread.shape[0], -1)
    feature = lax.dot_general(
        spread, high_side, (((0,), (0,)), ((), ())), preferred_element_type=jnp.float32
    )
    return grad, feature.reshape(docs_count, low_side.shape[1], high_side.shape[1])


def block_owner(name, chips):
    chain, step, handed = name
    me = lax.axis_index("exp")
    core, chip = lax.rem(me, 2), lax.div(me, 2)
    turn = chips // 2
    place = jnp.where(lax.rem(chip, 2) == 0, lax.div(chip, 2), chips - 1 - lax.div(chip, 2))
    way = 2 * core - 1
    place = place + (-way if handed else way) * step
    place = lax.rem(place + chips, chips)
    chip = jnp.where(place < turn, 2 * place, 2 * (chips - 1 - place) + 1)
    return 2 * chip + (core if (chain == "a") != handed else 1 - core)


def rows_kernel(names, load, *refs):
    blocks = len(names)
    apart = refs[1:3] if load else ()
    refs = refs[:1] + refs[3:] if load else refs
    whole = blocks - 1 if load else blocks
    sheet_in, block_in = refs[0], refs[1 : 1 + whole]
    given = refs[1 + whole : 6 + whole]
    sheet, low_side, proj_cot = refs[6 + whole : 9 + whole]
    x_all, dy_all, low_sum, grad_sum = refs[-5:-1] if load else refs[-4:]
    w_gate, w_up, w_down, low_proj, high_proj = refs[9 + whole : 14 + whole] if load else given
    rows = x_all.shape[0] // blocks
    across = (((1,), (1,)), ((), ()))
    units = w_gate.shape[1]
    tile = 256 if units % 256 == 0 else units
    tiles = units // tile
    lanes = grad_sum.shape[1]
    copies = []
    if load:
        rank = given[3].shape[0]
        for j in range(tiles):
            part = pl.ds(j * tile, tile)
            copies.append((given[0].at[:, part], w_gate.at[:, part]))
            copies.append((given[1].at[:, part], w_up.at[:, part]))
            copies.append((given[2].at[part, :], w_down.at[part, :]))
        for i in range(low_proj.shape[0] // rank):
            copies.append((given[3], low_proj.at[pl.ds(i * rank, rank), :]))
        copies.append((given[4], high_proj))
        copies.append((apart[0], x_all.at[:rows]))
        copies.append((apart[1], dy_all.at[:rows]))
        copies = [
            pltpu.make_async_copy(src, dst, refs[-1].at[i]) for i, (src, dst) in enumerate(copies)
        ]
        for copy in copies[3 * tiles :] + copies[: 3 * tiles]:
            copy.start()
    if blocks == 1:
        x_all, dy_all = block_in[0].at[:rows, :], block_in[0].at[rows:, :]
    for i, block in enumerate(block_in if blocks > 1 else ()):
        place = slice((blocks - whole + i) * rows, (blocks - whole + i + 1) * rows)
        x_all[place, :] = block[:rows, :]
        dy_all[place, :] = block[rows:, :]

    def one_tile(j):
        part = pl.ds(j * tile, tile)
        gate_val = jnp.dot(x_all[...], w_gate[:, part], preferred_element_type=jnp.float32)
        up_val = jnp.dot(x_all[...], w_up[:, part], preferred_element_type=jnp.float32)
        hidden = (jax.nn.silu(gate_val) * up_val).astype(jnp.bfloat16)
        back = lax.dot_general(
            dy_all[...], w_down[part, :], across, preferred_element_type=jnp.float32
        )
        terms = hidden.astype(jnp.float32) * back
        total = terms[:, :lanes]
        for cut in range(lanes, tile, lanes):
            total += terms[:, cut : cut + lanes]
        grad_sum[...] = total if j == 0 else grad_sum[...] + total
        low = lax.dot_general(
            low_proj[:, part], hidden, across, preferred_element_type=jnp.float32
        )
        low_sum[...] = low if j == 0 else low_sum[...] + low

    for copy in copies[3 * tiles :]:
        copy.wait()
    for j in range(tiles):
        for copy in copies[3 * j : 3 * j + 3] if load else []:
            copy.wait()
        one_tile(j)

    low_side[...] = low_sum[...].astype(low_side.dtype)
    proj_cot[...] = lax.dot_general(
        high_proj[...], dy_all[...], across, preferred_element_type=jnp.float32
    )
    sheet[...] = sheet_in[...]
    for i in range(blocks):
        total = jnp.sum(
            jnp.transpose(grad_sum[i * rows : (i + 1) * rows, :]), axis=0, keepdims=True
        )
        sheet[block_owner(names[i], sheet.shape[0] // 2), 0:1, :] = total


def work(names, sheet, block_in, weights, apart=(), load=0):
    width, units = weights[0].shape
    low_width, rank = weights[3].shape[0] * max(load, 1), weights[4].shape[0]
    blocks = len(names)
    rows = block_in[0].shape[0] // 2
    inside = pl.BlockSpec(memory_space=pltpu.VMEM)
    loaded = []
    if load:
        shapes = [w.shape for w in weights]
        shapes[3] = (low_width, units)
        loaded = [jax.ShapeDtypeStruct(shape, weights[0].dtype) for shape in shapes]
    tiles = units // 256 if units % 256 == 0 else 1
    call = pl.pallas_call(
        functools.partial(rows_kernel, names, load > 0),
        out_shape=[
            jax.ShapeDtypeStruct(sheet.shape, jnp.float32),
            jax.ShapeDtypeStruct((low_width, blocks * rows), jnp.bfloat16),
            jax.ShapeDtypeStruct((rank, blocks * rows), jnp.float32),
        ]
        + loaded,
        in_specs=[inside]
        + [pl.BlockSpec(memory_space=pl.ANY)] * len(apart)
        + [inside] * len(block_in)
        + [pl.BlockSpec(memory_space=pl.ANY) if load else inside] * len(weights),
        out_specs=[inside] * (3 + len(loaded)),
        scratch_shapes=[
            pltpu.VMEM((blocks * rows, width), jnp.bfloat16),
            pltpu.VMEM((blocks * rows, width), jnp.bfloat16),
            pltpu.VMEM((low_width, blocks * rows), jnp.float32),
            pltpu.VMEM((blocks * rows, 128), jnp.float32),
        ]
        + ([pltpu.SemaphoreType.DMA((3 * tiles + load + 3,))] if load else []),
        compiler_params=pltpu.CompilerParams(
            vmem_limit_bytes=(LOAD_MIB if load else 16) * 1024 * 1024
        ),
        cost_estimate=pl.CostEstimate(
            flops=6 * blocks * rows * width * units,
            bytes_accessed=4 * blocks * rows * width,
            transcendentals=blocks * rows * units,
        ),
    )
    return call(sheet, *apart, *block_in, *weights)


def front_kernel(*refs):
    blocks = len(refs) - 8
    x_in = refs[:blocks]
    w_gate, w_up, low_proj, hidden, low_first, low_last, x_all, low_sum = refs[blocks:]
    begin = 0
    for x in x_in:
        x_all[begin : begin + x.shape[0], :] = x[...]
        begin += x.shape[0]
    units = w_gate.shape[1]
    tile = 256 if units % 256 == 0 else units
    for cut in range(0, units, tile):
        part = pl.ds(cut, tile)
        gate_val = jnp.dot(x_all[...], w_gate[:, part], preferred_element_type=jnp.float32)
        up_val = jnp.dot(x_all[...], w_up[:, part], preferred_element_type=jnp.float32)
        piece = (jax.nn.silu(gate_val) * up_val).astype(jnp.bfloat16)
        hidden[:, part] = piece
        low = lax.dot_general(
            low_proj[:, part],
            piece,
            (((1,), (1,)), ((), ())),
            preferred_element_type=jnp.float32,
        )
        low_sum[...] = low if cut == 0 else low_sum[...] + low
    cut = low_first.shape[1]
    low_first[...] = low_sum[:, :cut].astype(low_first.dtype)
    low_last[...] = low_sum[:, cut:].astype(low_last.dtype)


def front(x_in, weights, last):
    w_gate, w_up, _, low_proj, _ = weights
    rows, width = sum(x.shape[0] for x in x_in), x_in[0].shape[1]
    units = w_gate.shape[1]
    inside = pl.BlockSpec(memory_space=pltpu.VMEM)
    return pl.pallas_call(
        front_kernel,
        out_shape=[
            jax.ShapeDtypeStruct((rows, units), jnp.bfloat16),
            jax.ShapeDtypeStruct((low_proj.shape[0], rows - last), jnp.bfloat16),
            jax.ShapeDtypeStruct((low_proj.shape[0], last), jnp.bfloat16),
        ],
        in_specs=[inside] * (len(x_in) + 3),
        out_specs=[inside] * 3,
        scratch_shapes=[
            pltpu.VMEM((rows, width), jnp.bfloat16),
            pltpu.VMEM((low_proj.shape[0], rows), jnp.float32),
        ],
        compiler_params=pltpu.CompilerParams(vmem_limit_bytes=16 * 1024 * 1024),
        cost_estimate=pl.CostEstimate(
            flops=4 * rows * width * units,
            bytes_accessed=2 * rows * width,
            transcendentals=rows * units,
        ),
    )(*x_in, w_gate, w_up, low_proj)


def fold(product):
    total = product[:, :128]
    for spot in range(128, product.shape[1], 128):
        total += product[:, spot : spot + 128]
    return total


def enter(sheet, name, total):
    sheet[block_owner(name, sheet.shape[0] // 2), 0:1, :] = jnp.sum(
        jnp.transpose(total), axis=0, keepdims=True
    )


def out_kernel(names, *refs):
    blocks = len(names)
    sheet_in, dy_in = refs[0], refs[1 : 1 + blocks]
    hidden, w_down, high_proj, sheet, proj_cot, rest = refs[1 + blocks :]
    rows = dy_in[0].shape[0]
    across = (((1,), (1,)), ((), ()))
    width = w_down.shape[1]
    tile = 512 if width % 512 == 0 else width
    totals = [0.0] * blocks
    for cut in range(0, width, tile):
        part = pl.ds(cut, tile)
        out_val = jnp.dot(hidden[...], w_down[:, part], preferred_element_type=jnp.float32)
        for i in range(blocks):
            dy = dy_in[i][:, part].astype(jnp.float32)
            totals[i] += fold(dy * out_val[i * rows : (i + 1) * rows, :])
        rest[:, part] = out_val[blocks * rows :, :]
    sheet[...] = sheet_in[...]
    for i in range(blocks):
        enter(sheet, names[i], totals[i])
        proj_cot[:, i * rows : (i + 1) * rows] = lax.dot_general(
            high_proj[...], dy_in[i][...], across, preferred_element_type=jnp.float32
        )


def last_kernel(name, sheet_in, dy, out_val, high_proj, sheet, proj_cot):
    width = dy.shape[1]
    tile = 512 if width % 512 == 0 else width
    total = 0.0
    for cut in range(0, width, tile):
        part = pl.ds(cut, tile)
        total += fold(dy[:, part].astype(jnp.float32) * out_val[:, part])
    sheet[...] = sheet_in[...]
    enter(sheet, name, total)
    proj_cot[...] = lax.dot_general(
        high_proj[...], dy[...], (((1,), (1,)), ((), ())), preferred_element_type=jnp.float32
    )


def on_core(kernel, args, out_shape, flops=0):
    inside = pl.BlockSpec(memory_space=pltpu.VMEM)
    return pl.pallas_call(
        kernel,
        out_shape=[jax.ShapeDtypeStruct(shape, jnp.float32) for shape in out_shape],
        in_specs=[inside] * len(args),
        out_specs=[inside] * len(out_shape),
        compiler_params=pltpu.CompilerParams(vmem_limit_bytes=16 * 1024 * 1024),
        cost_estimate=pl.CostEstimate(flops=flops, bytes_accessed=2**20, transcendentals=0),
    )(*args)


def outcome_kernel(jobs, returned, routes, *refs):
    low_in, proj_in = refs[: len(jobs)], refs[len(jobs) : 2 * len(jobs)]
    feat, route_grad = refs[-2:]
    rows = returned.shape[2]
    width, rank = low_in[0].shape[0], proj_in[0].shape[0]
    doc_of = lax.broadcasted_iota(jnp.int32, (width, rows), 0) // rank
    spread, high_side = [], []
    for names, low_side, proj_cot in zip(jobs, low_in, proj_in):
        for i, name in enumerate(names):
            place = slice(i * rows, (i + 1) * rows)
            owner = block_owner(name, returned.shape[0] // 2)
            weight = returned[owner, 1:2, :]
            doc = returned[owner, 2:3, :].astype(jnp.int32)
            high_side.append((weight * proj_cot[:, place]).astype(jnp.bfloat16))
            low = low_side[:, place].astype(jnp.float32)
            spread.append(jnp.where(doc == doc_of, low, 0.0).astype(jnp.bfloat16))
    feat[...] = lax.dot_general(
        jnp.concatenate(spread, axis=1),
        jnp.concatenate(high_side, axis=1),
        (((1,), (1,)), ((), ())),
        preferred_element_type=jnp.float32,
    )
    picked = jnp.zeros(route_grad.shape, jnp.float32)
    for e in range(returned.shape[0]):
        picked = jnp.where(routes[...] == e, returned[e, 0:1, :], picked)
    route_grad[...] = picked


def facts_kernel(routes, combine, doc_ids, out):
    groups, lines, rows = out.shape
    expert = lax.broadcasted_iota(jnp.int32, (groups, rows), 0)
    weight = jnp.zeros((groups, rows), jnp.float32)
    for k in range(routes.shape[0]):
        share = combine[k : k + 1, :].astype(jnp.float32)
        weight += jnp.where(routes[k : k + 1, :] == expert, share, 0.0)
    line = lax.broadcasted_iota(jnp.int32, (lines, rows), 0)
    doc = doc_ids[...].astype(jnp.float32)
    for e in range(groups):
        out[e] = jnp.where(line == 1, weight[e : e + 1, :], doc)


def stack_kernel(top, bottom, out):
    rows = top.shape[0]
    out[:rows, :] = top[...]
    out[rows:, :] = bottom[...]


def stack(top, bottom):
    inside = pl.BlockSpec(memory_space=pltpu.VMEM)
    return pl.pallas_call(
        stack_kernel,
        out_shape=jax.ShapeDtypeStruct((2 * top.shape[0], top.shape[1]), top.dtype),
        in_specs=[inside] * 2,
        out_specs=inside,
        compiler_params=pltpu.CompilerParams(vmem_limit_bytes=8 * 1024 * 1024),
    )(top, bottom)


def split_kernel(cuts, block, *parts):
    for (begin, count), part in zip(cuts, parts):
        part[...] = block[begin : begin + count, :]


def split(block, cuts):
    inside = pl.BlockSpec(memory_space=pltpu.VMEM)
    return pl.pallas_call(
        functools.partial(split_kernel, cuts),
        out_shape=[
            jax.ShapeDtypeStruct((count, block.shape[1]), block.dtype) for _, count in cuts
        ],
        in_specs=[inside],
        out_specs=[inside] * len(cuts),
        compiler_params=pltpu.CompilerParams(vmem_limit_bytes=8 * 1024 * 1024),
    )(block)


def by_ring(
    tokens, cotangent, routes, combine, doc_ids, w_gate, w_up, w_down, proj_hidden, proj_output
):
    tok_rows, chosen = routes.shape
    groups = lax.axis_size("exp")
    docs_count = max(2, tok_rows * groups // DOC_TOK)
    chips = groups // 2
    half = chips // 2
    ring = list(range(0, chips, 2)) + list(range(chips - 1, 0, -2))
    onward = []
    for place in range(chips):
        onward.append((2 * ring[place], 2 * ring[(place + 1) % chips]))
        onward.append((2 * ring[place] + 1, 2 * ring[place - 1] + 1))
    across = [(i, i ^ 1) for i in range(groups)]

    def hop(block):
        return lax.ppermute(block, "exp", onward)

    def swap(block):
        return lax.ppermute(block, "exp", across)

    arrivals = [(c, step) for step in range(1, half + 1) for c in ("ab" if step < half else "a")]
    jobs = [(("a", 0, False), ("a", 0, True))]
    for i, (c, step) in enumerate(arrivals):
        job = ((c, step, False),)
        if i > 0:
            job += (arrivals[i - 1] + (True,),)
        if i == 1:
            job += (arrivals[0] + (False,),)
        if i == len(arrivals) - 1:
            jobs += [(job[1], job[0]), ((c, step, True),)]
        elif i != 0:
            jobs.append(job)

    sheet = pl.pallas_call(
        facts_kernel,
        out_shape=jax.ShapeDtypeStruct((groups, 4, tok_rows), jnp.float32),
        in_specs=[pl.BlockSpec(memory_space=pltpu.VMEM)] * 3,
        out_specs=pl.BlockSpec(memory_space=pltpu.VMEM),
        compiler_params=pltpu.CompilerParams(vmem_limit_bytes=8 * 1024 * 1024),
    )(routes.T, combine.T, doc_ids[None, :])
    first = (hop(tokens), hop(cotangent))
    beside = stack(swap(tokens), swap(cotangent))

    inside = pl.BlockSpec(memory_space=pltpu.VMEM)
    given = (w_gate[0], w_up[0], w_down[0], proj_hidden[0].T, proj_output[0].T)
    weights = None
    lows, projs = [], []
    held = {("a", 0, True): beside}
    todo = list(jobs)

    def take():
        nonlocal sheet, weights
        names = todo.pop(0)
        blocks = [held[name] for name in names if name in held]
        if weights is None:
            sheet, low_side, proj_cot, *weights = work(
                names, sheet, blocks, given, apart=(tokens, cotangent), load=docs_count
            )
        else:
            sheet, low_side, proj_cot = work(names, sheet, blocks, weights)
        lows.append(low_side)
        projs.append(proj_cot)

    chain = {"b": beside}
    for i, (c, step) in enumerate(arrivals[:-1]):
        block = hop(chain[c]) if i > 0 else first
        if i != 1:
            take()
            sheet, block = lax.optimization_barrier((sheet, block))
        if i == 0:
            block = stack(*block)
        chain[c] = held[(c, step, False)] = block
        if i < len(arrivals) - 2:
            held[(c, step, True)] = swap(block)
    cut = tok_rows // 2
    cuts = ((0, cut), (cut, cut), (tok_rows, tok_rows))
    *x, dy = split(chain["a"], cuts)
    dy, _ = lax.optimization_barrier((dy, chain["b"]))
    x, dy = [hop(part) for part in x], hop(dy)
    *x_before, dy_before = split(chain["b"], ((0, tok_rows), (tok_rows, tok_rows)))
    x_before, dy_before = [swap(part) for part in x_before], swap(dy_before)
    take()
    sheet, x = lax.optimization_barrier((sheet, x))
    hidden, low_first, low_last = front(
        x_before + x + [swap(part) for part in x], weights, tok_rows
    )
    hidden, dy = lax.optimization_barrier((hidden, dy))
    dy_beside = swap(dy)
    rank = proj_output.shape[2]
    sheet, proj_cot, out_val = on_core(
        functools.partial(out_kernel, todo.pop(0)),
        (sheet, dy_before, dy, hidden, weights[2], weights[4]),
        [sheet.shape, (rank, 2 * tok_rows), tokens.shape],
        flops=6 * tok_rows * hidden.shape[1] * tokens.shape[1],
    )
    lows.append(low_first)
    projs.append(proj_cot)
    ((name,),) = todo
    sheet, proj_cot = on_core(
        functools.partial(last_kernel, name),
        (sheet, dy_beside, out_val, weights[4]),
        [sheet.shape, (rank, tok_rows)],
    )
    lows.append(low_last)
    projs.append(proj_cot)
    returned = lax.all_to_all(sheet, "exp", split_axis=0, concat_axis=0, tiled=True)
    feature, route_grad = pl.pallas_call(
        functools.partial(outcome_kernel, jobs),
        out_shape=[
            jax.ShapeDtypeStruct((docs_count * rank, rank), jnp.float32),
            jax.ShapeDtypeStruct((chosen, tok_rows), jnp.float32),
        ],
        in_specs=[inside] * (2 + 2 * len(lows)),
        out_specs=[inside] * 2,
        compiler_params=pltpu.CompilerParams(vmem_limit_bytes=16 * 1024 * 1024),
    )(returned, routes.T, *lows, *projs)
    return feature.reshape(docs_count, 1, rank, rank), route_grad.T


def by_routing(
    tokens, cotangent, routes, combine, doc_ids, w_gate, w_up, w_down, proj_hidden, proj_output
):
    tok_rows, chosen = routes.shape
    local_count = w_gate.shape[0]
    groups = lax.axis_size("exp")
    experts = local_count * groups
    capacity = max(2, tok_rows * chosen * 5 // (4 * experts))
    docs_count = max(2, tok_rows * groups // DOC_TOK)
    entries = tok_rows * chosen
    width = tokens.shape[1]
    flat_routes = routes.reshape(-1)
    member = (flat_routes[:, None] == jnp.arange(experts, dtype=jnp.int32)[None, :]).astype(
        jnp.int32
    )
    slot_rank = jnp.sum((jnp.cumsum(member, axis=0) - 1) * member, axis=1)
    position = flat_routes * capacity + slot_rank
    source = (
        jnp.full((experts * capacity,), -1, jnp.int32)
        .at[position]
        .set(jnp.arange(entries, dtype=jnp.int32))
    )
    filled = source >= 0
    safe_source = jnp.maximum(source, 0)
    token_of = safe_source // chosen
    send_x = jnp.where(filled[:, None], tokens[token_of], 0)
    send_dy = jnp.where(filled[:, None], cotangent[token_of], 0)
    send_w = jnp.where(filled, combine.reshape(-1)[safe_source], 0)
    send_doc = jnp.where(filled, doc_ids[token_of], -1).astype(jnp.bfloat16)

    def exchange(array):
        array = array.reshape((groups, local_count, capacity) + array.shape[1:])
        return lax.all_to_all(array, "exp", split_axis=0, concat_axis=0, tiled=True)

    recv_x, recv_dy, recv_w, recv_doc = (
        exchange(send_x),
        exchange(send_dy),
        exchange(send_w),
        exchange(send_doc),
    )
    slots = groups * capacity
    grads, feats = [], []
    for e in range(local_count):
        hidden = swiglu(recv_x[:, e].reshape(slots, width), w_gate[e], w_up[e])
        grad, feature = finish(
            hidden,
            recv_dy[:, e].reshape(slots, width),
            recv_w[:, e].reshape(slots),
            recv_doc[:, e].reshape(slots),
            w_down[e],
            proj_hidden[e],
            proj_output[e],
            docs_count,
        )
        grads.append(grad.reshape(groups, capacity))
        feats.append(feature)
    slot_grad = jnp.stack(grads, axis=1)
    returned = lax.all_to_all(slot_grad, "exp", split_axis=0, concat_axis=0, tiled=True)
    route_grad = returned.reshape(-1)[position].reshape(tok_rows, chosen)
    return jnp.stack(feats, axis=1), route_grad


def on_device(tokens, cotangent, routes, combine, doc_ids, w_gate, *rest):
    tok_rows, chosen = routes.shape
    experts = w_gate.shape[0] * lax.axis_size("exp")
    dense = w_gate.shape[0] == 1 and 4 * chosen >= experts and experts >= 8 and experts % 4 == 0
    plan = by_ring if dense else by_routing
    return plan(tokens, cotangent, routes, combine, doc_ids, w_gate, *rest)


def solution(mesh):
    placed = (
        P(("grp", "exp"), None),
        P(("grp", "exp"), None),
        P(("grp", "exp"), None),
        P(("grp", "exp"), None),
        P(("grp", "exp")),
        P("exp", None, None),
        P("exp", None, None),
        P("exp", None, None),
        P("exp", None, None),
        P("exp", None, None),
    )
    return jax.shard_map(
        on_device,
        mesh=mesh,
        in_specs=placed,
        out_specs=(P("grp", "exp", None, None), P(("grp", "exp"), None)),
        check_vma=False,
    )
```

```python
import functools

import jax
import jax.numpy as jnp
from jax import lax
from jax.experimental import pallas as pl
from jax.experimental.pallas import tpu as pltpu
from jax.sharding import PartitionSpec as P

DOC_TOK = 512
LOAD_MIB = 40


def swiglu(rows, w_gate, w_up):
    gate_val = jnp.dot(rows, w_gate, preferred_element_type=jnp.float32)
    up_val = jnp.dot(rows, w_up, preferred_element_type=jnp.float32)
    return (jax.nn.silu(gate_val) * up_val).astype(jnp.bfloat16)


def finish(hidden, rows_dy, rows_w, rows_doc, w_down, proj_hidden, proj_output, docs_count):
    out_val = jnp.dot(hidden, w_down, preferred_element_type=jnp.float32)
    grad = jnp.sum(rows_dy.astype(jnp.float32) * out_val, axis=-1)
    low_side = jnp.dot(hidden, proj_hidden, preferred_element_type=jnp.float32).astype(
        jnp.bfloat16
    )
    proj_cot = jnp.dot(rows_dy, proj_output, preferred_element_type=jnp.float32)
    high_side = (rows_w.astype(jnp.float32)[:, None] * proj_cot).astype(jnp.bfloat16)
    doc_table = jnp.arange(docs_count, dtype=jnp.int32).astype(jnp.bfloat16)
    onehot = (rows_doc[:, None] == doc_table).astype(jnp.bfloat16)
    spread = onehot[:, :, None] * low_side[:, None, :]
    spread = spread.reshape(spread.shape[0], -1)
    feature = lax.dot_general(
        spread, high_side, (((0,), (0,)), ((), ())), preferred_element_type=jnp.float32
    )
    return grad, feature.reshape(docs_count, low_side.shape[1], high_side.shape[1])


def block_owner(name, chips):
    chain, step, handed = name
    me = lax.axis_index("exp")
    core, chip = lax.rem(me, 2), lax.div(me, 2)
    turn = chips // 2
    place = jnp.where(lax.rem(chip, 2) == 0, lax.div(chip, 2), chips - 1 - lax.div(chip, 2))
    way = 2 * core - 1
    place = place + (-way if handed else way) * step
    place = lax.rem(place + chips, chips)
    chip = jnp.where(place < turn, 2 * place, 2 * (chips - 1 - place) + 1)
    return 2 * chip + (core if (chain == "a") != handed else 1 - core)


def rows_kernel(names, load, *refs):
    blocks = len(names)
    apart = refs[1:3] if load else ()
    refs = refs[:1] + refs[3:] if load else refs
    whole = blocks - 1 if load else blocks
    sheet_in, block_in = refs[0], refs[1 : 1 + whole]
    given = refs[1 + whole : 6 + whole]
    sheet, low_side, proj_cot = refs[6 + whole : 9 + whole]
    x_all, dy_all, low_sum, grad_sum = refs[-5:-1] if load else refs[-4:]
    w_gate, w_up, w_down, low_proj, high_proj = refs[9 + whole : 14 + whole] if load else given
    rows = x_all.shape[0] // blocks
    across = (((1,), (1,)), ((), ()))
    units = w_gate.shape[1]
    tile = 256 if units % 256 == 0 else units
    tiles = units // tile
    lanes = grad_sum.shape[1]
    copies = []
    if load:
        rank = given[3].shape[0]
        for j in range(tiles):
            part = pl.ds(j * tile, tile)
            copies.append((given[0].at[:, part], w_gate.at[:, part]))
            copies.append((given[1].at[:, part], w_up.at[:, part]))
            copies.append((given[2].at[part, :], w_down.at[part, :]))
        for i in range(low_proj.shape[0] // rank):
            copies.append((given[3], low_proj.at[pl.ds(i * rank, rank), :]))
        copies.append((given[4], high_proj))
        copies.append((apart[0], x_all.at[:rows]))
        copies.append((apart[1], dy_all.at[:rows]))
        copies = [
            pltpu.make_async_copy(src, dst, refs[-1].at[i]) for i, (src, dst) in enumerate(copies)
        ]
        for copy in copies[3 * tiles :] + copies[: 3 * tiles]:
            copy.start()
    if blocks == 1:
        x_all, dy_all = block_in[0].at[:rows, :], block_in[0].at[rows:, :]
    for i, block in enumerate(block_in if blocks > 1 else ()):
        place = slice((blocks - whole + i) * rows, (blocks - whole + i + 1) * rows)
        x_all[place, :] = block[:rows, :]
        dy_all[place, :] = block[rows:, :]

    def one_tile(j):
        part = pl.ds(j * tile, tile)
        gate_val = jnp.dot(x_all[...], w_gate[:, part], preferred_element_type=jnp.float32)
        up_val = jnp.dot(x_all[...], w_up[:, part], preferred_element_type=jnp.float32)
        hidden = (jax.nn.silu(gate_val) * up_val).astype(jnp.bfloat16)
        back = lax.dot_general(
            dy_all[...], w_down[part, :], across, preferred_element_type=jnp.float32
        )
        terms = hidden.astype(jnp.float32) * back
        total = terms[:, :lanes]
        for cut in range(lanes, tile, lanes):
            total += terms[:, cut : cut + lanes]
        grad_sum[...] = total if j == 0 else grad_sum[...] + total
        low = lax.dot_general(
            low_proj[:, part], hidden, across, preferred_element_type=jnp.float32
        )
        low_sum[...] = low if j == 0 else low_sum[...] + low

    for copy in copies[3 * tiles :]:
        copy.wait()
    for j in range(tiles):
        for copy in copies[3 * j : 3 * j + 3] if load else []:
            copy.wait()
        one_tile(j)

    low_side[...] = low_sum[...].astype(low_side.dtype)
    proj_cot[...] = lax.dot_general(
        high_proj[...], dy_all[...], across, preferred_element_type=jnp.float32
    )
    sheet[...] = sheet_in[...]
    for i in range(blocks):
        total = jnp.sum(
            jnp.transpose(grad_sum[i * rows : (i + 1) * rows, :]), axis=0, keepdims=True
        )
        sheet[block_owner(names[i], sheet.shape[0] // 2), 0:1, :] = total


def work(names, sheet, block_in, weights, apart=(), load=0):
    width, units = weights[0].shape
    low_width, rank = weights[3].shape[0] * max(load, 1), weights[4].shape[0]
    blocks = len(names)
    rows = block_in[0].shape[0] // 2
    inside = pl.BlockSpec(memory_space=pltpu.VMEM)
    loaded = []
    if load:
        shapes = [w.shape for w in weights]
        shapes[3] = (low_width, units)
        loaded = [jax.ShapeDtypeStruct(shape, weights[0].dtype) for shape in shapes]
    tiles = units // 256 if units % 256 == 0 else 1
    call = pl.pallas_call(
        functools.partial(rows_kernel, names, load > 0),
        out_shape=[
            jax.ShapeDtypeStruct(sheet.shape, jnp.float32),
            jax.ShapeDtypeStruct((low_width, blocks * rows), jnp.bfloat16),
            jax.ShapeDtypeStruct((rank, blocks * rows), jnp.float32),
        ]
        + loaded,
        in_specs=[inside]
        + [pl.BlockSpec(memory_space=pl.ANY)] * len(apart)
        + [inside] * len(block_in)
        + [pl.BlockSpec(memory_space=pl.ANY) if load else inside] * len(weights),
        out_specs=[inside] * (3 + len(loaded)),
        scratch_shapes=[
            pltpu.VMEM((blocks * rows, width), jnp.bfloat16),
            pltpu.VMEM((blocks * rows, width), jnp.bfloat16),
            pltpu.VMEM((low_width, blocks * rows), jnp.float32),
            pltpu.VMEM((blocks * rows, 128), jnp.float32),
        ]
        + ([pltpu.SemaphoreType.DMA((3 * tiles + load + 3,))] if load else []),
        compiler_params=pltpu.CompilerParams(
            vmem_limit_bytes=(LOAD_MIB if load else 16) * 1024 * 1024
        ),
        cost_estimate=pl.CostEstimate(
            flops=6 * blocks * rows * width * units,
            bytes_accessed=4 * blocks * rows * width,
            transcendentals=blocks * rows * units,
        ),
    )
    return call(sheet, *apart, *block_in, *weights)


def front_kernel(*refs):
    blocks = len(refs) - 8
    x_in = refs[:blocks]
    w_gate, w_up, low_proj, hidden, low_first, low_last, x_all, low_sum = refs[blocks:]
    begin = 0
    for x in x_in:
        x_all[begin : begin + x.shape[0], :] = x[...]
        begin += x.shape[0]
    units = w_gate.shape[1]
    tile = 256 if units % 256 == 0 else units
    for cut in range(0, units, tile):
        part = pl.ds(cut, tile)
        gate_val = jnp.dot(x_all[...], w_gate[:, part], preferred_element_type=jnp.float32)
        up_val = jnp.dot(x_all[...], w_up[:, part], preferred_element_type=jnp.float32)
        piece = (jax.nn.silu(gate_val) * up_val).astype(jnp.bfloat16)
        hidden[:, part] = piece
        low = lax.dot_general(
            low_proj[:, part],
            piece,
            (((1,), (1,)), ((), ())),
            preferred_element_type=jnp.float32,
        )
        low_sum[...] = low if cut == 0 else low_sum[...] + low
    cut = low_first.shape[1]
    low_first[...] = low_sum[:, :cut].astype(low_first.dtype)
    low_last[...] = low_sum[:, cut:].astype(low_last.dtype)


def front(x_in, weights, last):
    w_gate, w_up, _, low_proj, _ = weights
    rows, width = sum(x.shape[0] for x in x_in), x_in[0].shape[1]
    units = w_gate.shape[1]
    inside = pl.BlockSpec(memory_space=pltpu.VMEM)
    return pl.pallas_call(
        front_kernel,
        out_shape=[
            jax.ShapeDtypeStruct((rows, units), jnp.bfloat16),
            jax.ShapeDtypeStruct((low_proj.shape[0], rows - last), jnp.bfloat16),
            jax.ShapeDtypeStruct((low_proj.shape[0], last), jnp.bfloat16),
        ],
        in_specs=[inside] * (len(x_in) + 3),
        out_specs=[inside] * 3,
        scratch_shapes=[
            pltpu.VMEM((rows, width), jnp.bfloat16),
            pltpu.VMEM((low_proj.shape[0], rows), jnp.float32),
        ],
        compiler_params=pltpu.CompilerParams(vmem_limit_bytes=16 * 1024 * 1024),
        cost_estimate=pl.CostEstimate(
            flops=4 * rows * width * units,
            bytes_accessed=2 * rows * width,
            transcendentals=rows * units,
        ),
    )(*x_in, w_gate, w_up, low_proj)


def fold(product):
    total = product[:, :128]
    for spot in range(128, product.shape[1], 128):
        total += product[:, spot : spot + 128]
    return total


def enter(sheet, name, total):
    sheet[block_owner(name, sheet.shape[0] // 2), 0:1, :] = jnp.sum(
        jnp.transpose(total), axis=0, keepdims=True
    )


def out_kernel(names, *refs):
    blocks = len(names)
    sheet_in, dy_in = refs[0], refs[1 : 1 + blocks]
    hidden, w_down, high_proj, sheet, proj_cot, rest = refs[1 + blocks :]
    rows = dy_in[0].shape[0]
    across = (((1,), (1,)), ((), ()))
    width = w_down.shape[1]
    tile = 512 if width % 512 == 0 else width
    totals = [0.0] * blocks
    for cut in range(0, width, tile):
        part = pl.ds(cut, tile)
        out_val = jnp.dot(hidden[...], w_down[:, part], preferred_element_type=jnp.float32)
        for i in range(blocks):
            dy = dy_in[i][:, part].astype(jnp.float32)
            totals[i] += fold(dy * out_val[i * rows : (i + 1) * rows, :])
        rest[:, part] = out_val[blocks * rows :, :]
    sheet[...] = sheet_in[...]
    for i in range(blocks):
        enter(sheet, names[i], totals[i])
        proj_cot[:, i * rows : (i + 1) * rows] = lax.dot_general(
            high_proj[...], dy_in[i][...], across, preferred_element_type=jnp.float32
        )


def last_kernel(name, sheet_in, dy, out_val, high_proj, sheet, proj_cot):
    width = dy.shape[1]
    tile = 512 if width % 512 == 0 else width
    total = 0.0
    for cut in range(0, width, tile):
        part = pl.ds(cut, tile)
        total += fold(dy[:, part].astype(jnp.float32) * out_val[:, part])
    sheet[...] = sheet_in[...]
    enter(sheet, name, total)
    proj_cot[...] = lax.dot_general(
        high_proj[...], dy[...], (((1,), (1,)), ((), ())), preferred_element_type=jnp.float32
    )


def on_core(kernel, args, out_shape, flops=0):
    inside = pl.BlockSpec(memory_space=pltpu.VMEM)
    return pl.pallas_call(
        kernel,
        out_shape=[jax.ShapeDtypeStruct(shape, jnp.float32) for shape in out_shape],
        in_specs=[inside] * len(args),
        out_specs=[inside] * len(out_shape),
        compiler_params=pltpu.CompilerParams(vmem_limit_bytes=16 * 1024 * 1024),
        cost_estimate=pl.CostEstimate(flops=flops, bytes_accessed=2**20, transcendentals=0),
    )(*args)


def outcome_kernel(jobs, returned, routes, *refs):
    low_in, proj_in = refs[: len(jobs)], refs[len(jobs) : 2 * len(jobs)]
    feat, route_grad = refs[-2:]
    rows = returned.shape[2]
    docs, rank = feat.shape[0], feat.shape[2]
    low_side, high_side = [], []
    for names, low, proj_cot in zip(jobs, low_in, proj_in):
        low_side.append(low[...])
        for i, name in enumerate(names):
            place = slice(i * rows, (i + 1) * rows)
            owner = block_owner(name, returned.shape[0] // 2)
            weight = returned[owner, 1:2, :]
            doc = returned[owner, 2:3, :].astype(jnp.int32)
            parts = [jnp.where(doc == d, weight, 0.0) * proj_cot[:, place] for d in range(docs)]
            high_side.append(jnp.concatenate(parts, axis=0).astype(jnp.bfloat16))
    total = lax.dot_general(
        jnp.concatenate(low_side, axis=1),
        jnp.concatenate(high_side, axis=1),
        (((1,), (1,)), ((), ())),
        preferred_element_type=jnp.float32,
    )
    for d in range(docs):
        feat[d] = total[:, d * rank : (d + 1) * rank]
    picked = jnp.zeros(route_grad.shape, jnp.float32)
    for e in range(returned.shape[0]):
        picked = jnp.where(routes[...] == e, returned[e, 0:1, :], picked)
    route_grad[...] = picked


def facts_kernel(routes, combine, doc_ids, out):
    groups, lines, rows = out.shape
    expert = lax.broadcasted_iota(jnp.int32, (groups, rows), 0)
    weight = jnp.zeros((groups, rows), jnp.float32)
    for k in range(routes.shape[0]):
        share = combine[k : k + 1, :].astype(jnp.float32)
        weight += jnp.where(routes[k : k + 1, :] == expert, share, 0.0)
    line = lax.broadcasted_iota(jnp.int32, (lines, rows), 0)
    doc = doc_ids[...].astype(jnp.float32)
    for e in range(groups):
        out[e] = jnp.where(line == 1, weight[e : e + 1, :], doc)


def stack_kernel(top, bottom, out):
    rows = top.shape[0]
    out[:rows, :] = top[...]
    out[rows:, :] = bottom[...]


def stack(top, bottom):
    inside = pl.BlockSpec(memory_space=pltpu.VMEM)
    return pl.pallas_call(
        stack_kernel,
        out_shape=jax.ShapeDtypeStruct((2 * top.shape[0], top.shape[1]), top.dtype),
        in_specs=[inside] * 2,
        out_specs=inside,
        compiler_params=pltpu.CompilerParams(vmem_limit_bytes=8 * 1024 * 1024),
    )(top, bottom)


def split_kernel(cuts, block, *parts):
    for (begin, count), part in zip(cuts, parts):
        part[...] = block[begin : begin + count, :]


def split(block, cuts):
    inside = pl.BlockSpec(memory_space=pltpu.VMEM)
    return pl.pallas_call(
        functools.partial(split_kernel, cuts),
        out_shape=[
            jax.ShapeDtypeStruct((count, block.shape[1]), block.dtype) for _, count in cuts
        ],
        in_specs=[inside],
        out_specs=[inside] * len(cuts),
        compiler_params=pltpu.CompilerParams(vmem_limit_bytes=8 * 1024 * 1024),
    )(block)


def by_ring(
    tokens, cotangent, routes, combine, doc_ids, w_gate, w_up, w_down, proj_hidden, proj_output
):
    tok_rows, chosen = routes.shape
    groups = lax.axis_size("exp")
    docs_count = max(2, tok_rows * groups // DOC_TOK)
    chips = groups // 2
    half = chips // 2
    ring = list(range(0, chips, 2)) + list(range(chips - 1, 0, -2))
    onward = []
    for place in range(chips):
        onward.append((2 * ring[place], 2 * ring[(place + 1) % chips]))
        onward.append((2 * ring[place] + 1, 2 * ring[place - 1] + 1))
    across = [(i, i ^ 1) for i in range(groups)]

    def hop(block):
        return lax.ppermute(block, "exp", onward)

    def swap(block):
        return lax.ppermute(block, "exp", across)

    arrivals = [(c, step) for step in range(1, half + 1) for c in ("ab" if step < half else "a")]
    jobs = [(("a", 0, False), ("a", 0, True))]
    for i, (c, step) in enumerate(arrivals):
        job = ((c, step, False),)
        if i > 0:
            job += (arrivals[i - 1] + (True,),)
        if i == 1:
            job += (arrivals[0] + (False,),)
        if i == len(arrivals) - 1:
            jobs += [(job[1], job[0]), ((c, step, True),)]
        elif i != 0:
            jobs.append(job)

    sheet = pl.pallas_call(
        facts_kernel,
        out_shape=jax.ShapeDtypeStruct((groups, 4, tok_rows), jnp.float32),
        in_specs=[pl.BlockSpec(memory_space=pltpu.VMEM)] * 3,
        out_specs=pl.BlockSpec(memory_space=pltpu.VMEM),
        compiler_params=pltpu.CompilerParams(vmem_limit_bytes=8 * 1024 * 1024),
    )(routes.T, combine.T, doc_ids[None, :])
    first = (hop(tokens), hop(cotangent))
    beside = stack(swap(tokens), swap(cotangent))

    inside = pl.BlockSpec(memory_space=pltpu.VMEM)
    given = (w_gate[0], w_up[0], w_down[0], proj_hidden[0].T, proj_output[0].T)
    weights = None
    lows, projs = [], []
    held = {("a", 0, True): beside}
    todo = list(jobs)

    def take():
        nonlocal sheet, weights
        names = todo.pop(0)
        blocks = [held[name] for name in names if name in held]
        if weights is None:
            sheet, low_side, proj_cot, *weights = work(
                names, sheet, blocks, given, apart=(tokens, cotangent), load=1
            )
        else:
            sheet, low_side, proj_cot = work(names, sheet, blocks, weights)
        lows.append(low_side)
        projs.append(proj_cot)

    chain = {"b": beside}
    for i, (c, step) in enumerate(arrivals[:-1]):
        block = hop(chain[c]) if i > 0 else first
        if i != 1:
            take()
            sheet, block = lax.optimization_barrier((sheet, block))
        if i == 0:
            block = stack(*block)
        chain[c] = held[(c, step, False)] = block
        if i < len(arrivals) - 2:
            held[(c, step, True)] = swap(block)
    cut = tok_rows // 2
    cuts = ((0, cut), (cut, cut), (tok_rows, tok_rows))
    *x, dy = split(chain["a"], cuts)
    dy, _ = lax.optimization_barrier((dy, chain["b"]))
    x, dy = [hop(part) for part in x], hop(dy)
    *x_before, dy_before = split(chain["b"], ((0, tok_rows), (tok_rows, tok_rows)))
    x_before, dy_before = [swap(part) for part in x_before], swap(dy_before)
    take()
    sheet, x = lax.optimization_barrier((sheet, x))
    hidden, low_first, low_last = front(
        x_before + x + [swap(part) for part in x], weights, tok_rows
    )
    hidden, dy = lax.optimization_barrier((hidden, dy))
    dy_beside = swap(dy)
    rank = proj_output.shape[2]
    sheet, proj_cot, out_val = on_core(
        functools.partial(out_kernel, todo.pop(0)),
        (sheet, dy_before, dy, hidden, weights[2], weights[4]),
        [sheet.shape, (rank, 2 * tok_rows), tokens.shape],
        flops=6 * tok_rows * hidden.shape[1] * tokens.shape[1],
    )
    lows.append(low_first)
    projs.append(proj_cot)
    ((name,),) = todo
    sheet, proj_cot = on_core(
        functools.partial(last_kernel, name),
        (sheet, dy_beside, out_val, weights[4]),
        [sheet.shape, (rank, tok_rows)],
    )
    lows.append(low_last)
    projs.append(proj_cot)
    returned = lax.all_to_all(sheet, "exp", split_axis=0, concat_axis=0, tiled=True)
    feature, route_grad = pl.pallas_call(
        functools.partial(outcome_kernel, jobs),
        out_shape=[
            jax.ShapeDtypeStruct((docs_count, rank, rank), jnp.float32),
            jax.ShapeDtypeStruct((chosen, tok_rows), jnp.float32),
        ],
        in_specs=[inside] * (2 + 2 * len(lows)),
        out_specs=[inside] * 2,
        compiler_params=pltpu.CompilerParams(vmem_limit_bytes=16 * 1024 * 1024),
    )(returned, routes.T, *lows, *projs)
    return feature[:, None], route_grad.T


def by_routing(
    tokens, cotangent, routes, combine, doc_ids, w_gate, w_up, w_down, proj_hidden, proj_output
):
    tok_rows, chosen = routes.shape
    local_count = w_gate.shape[0]
    groups = lax.axis_size("exp")
    experts = local_count * groups
    capacity = max(2, tok_rows * chosen * 5 // (4 * experts))
    docs_count = max(2, tok_rows * groups // DOC_TOK)
    entries = tok_rows * chosen
    width = tokens.shape[1]
    flat_routes = routes.reshape(-1)
    member = (flat_routes[:, None] == jnp.arange(experts, dtype=jnp.int32)[None, :]).astype(
        jnp.int32
    )
    slot_rank = jnp.sum((jnp.cumsum(member, axis=0) - 1) * member, axis=1)
    position = flat_routes * capacity + slot_rank
    source = (
        jnp.full((experts * capacity,), -1, jnp.int32)
        .at[position]
        .set(jnp.arange(entries, dtype=jnp.int32))
    )
    filled = source >= 0
    safe_source = jnp.maximum(source, 0)
    token_of = safe_source // chosen
    send_x = jnp.where(filled[:, None], tokens[token_of], 0)
    send_dy = jnp.where(filled[:, None], cotangent[token_of], 0)
    send_w = jnp.where(filled, combine.reshape(-1)[safe_source], 0)
    send_doc = jnp.where(filled, doc_ids[token_of], -1).astype(jnp.bfloat16)

    def exchange(array):
        array = array.reshape((groups, local_count, capacity) + array.shape[1:])
        return lax.all_to_all(array, "exp", split_axis=0, concat_axis=0, tiled=True)

    recv_x, recv_dy, recv_w, recv_doc = (
        exchange(send_x),
        exchange(send_dy),
        exchange(send_w),
        exchange(send_doc),
    )
    slots = groups * capacity
    grads, feats = [], []
    for e in range(local_count):
        hidden = swiglu(recv_x[:, e].reshape(slots, width), w_gate[e], w_up[e])
        grad, feature = finish(
            hidden,
            recv_dy[:, e].reshape(slots, width),
            recv_w[:, e].reshape(slots),
            recv_doc[:, e].reshape(slots),
            w_down[e],
            proj_hidden[e],
            proj_output[e],
            docs_count,
        )
        grads.append(grad.reshape(groups, capacity))
        feats.append(feature)
    slot_grad = jnp.stack(grads, axis=1)
    returned = lax.all_to_all(slot_grad, "exp", split_axis=0, concat_axis=0, tiled=True)
    route_grad = returned.reshape(-1)[position].reshape(tok_rows, chosen)
    return jnp.stack(feats, axis=1), route_grad


def on_device(tokens, cotangent, routes, combine, doc_ids, w_gate, *rest):
    tok_rows, chosen = routes.shape
    experts = w_gate.shape[0] * lax.axis_size("exp")
    dense = w_gate.shape[0] == 1 and 4 * chosen >= experts and experts >= 8 and experts % 4 == 0
    plan = by_ring if dense else by_routing
    return plan(tokens, cotangent, routes, combine, doc_ids, w_gate, *rest)


def solution(mesh):
    placed = (
        P(("grp", "exp"), None),
        P(("grp", "exp"), None),
        P(("grp", "exp"), None),
        P(("grp", "exp"), None),
        P(("grp", "exp")),
        P("exp", None, None),
        P("exp", None, None),
        P("exp", None, None),
        P("exp", None, None),
        P("exp", None, None),
    )
    return jax.shard_map(
        on_device,
        mesh=mesh,
        in_specs=placed,
        out_specs=(P("grp", "exp", None, None), P(("grp", "exp"), None)),
        check_vma=False,
    )
```

```python
import functools

import jax
import jax.numpy as jnp
from jax import lax
from jax.experimental import pallas as pl
from jax.experimental.pallas import tpu as pltpu
from jax.sharding import PartitionSpec as P

DOC_TOK = 512
LOAD_MIB = 40


def swiglu(rows, w_gate, w_up):
    gate_val = jnp.dot(rows, w_gate, preferred_element_type=jnp.float32)
    up_val = jnp.dot(rows, w_up, preferred_element_type=jnp.float32)
    return (jax.nn.silu(gate_val) * up_val).astype(jnp.bfloat16)


def finish(hidden, rows_dy, rows_w, rows_doc, w_down, proj_hidden, proj_output, docs_count):
    out_val = jnp.dot(hidden, w_down, preferred_element_type=jnp.float32)
    grad = jnp.sum(rows_dy.astype(jnp.float32) * out_val, axis=-1)
    low_side = jnp.dot(hidden, proj_hidden, preferred_element_type=jnp.float32).astype(
        jnp.bfloat16
    )
    proj_cot = jnp.dot(rows_dy, proj_output, preferred_element_type=jnp.float32)
    high_side = (rows_w.astype(jnp.float32)[:, None] * proj_cot).astype(jnp.bfloat16)
    doc_table = jnp.arange(docs_count, dtype=jnp.int32).astype(jnp.bfloat16)
    onehot = (rows_doc[:, None] == doc_table).astype(jnp.bfloat16)
    spread = onehot[:, :, None] * low_side[:, None, :]
    spread = spread.reshape(spread.shape[0], -1)
    feature = lax.dot_general(
        spread, high_side, (((0,), (0,)), ((), ())), preferred_element_type=jnp.float32
    )
    return grad, feature.reshape(docs_count, low_side.shape[1], high_side.shape[1])


def block_owner(name, chips):
    chain, step, handed = name
    me = lax.axis_index("exp")
    core, chip = lax.rem(me, 2), lax.div(me, 2)
    turn = chips // 2
    place = jnp.where(lax.rem(chip, 2) == 0, lax.div(chip, 2), chips - 1 - lax.div(chip, 2))
    way = 2 * core - 1
    place = place + (-way if handed else way) * step
    place = lax.rem(place + chips, chips)
    chip = jnp.where(place < turn, 2 * place, 2 * (chips - 1 - place) + 1)
    return 2 * chip + (core if (chain == "a") != handed else 1 - core)


def rows_kernel(names, load, *refs):
    blocks = len(names)
    apart = refs[1:3] if load else ()
    refs = refs[:1] + refs[3:] if load else refs
    whole = blocks - 1 if load else blocks
    sheet_in, block_in = refs[0], refs[1 : 1 + whole]
    given = refs[1 + whole : 6 + whole]
    sheet, low_side, proj_cot = refs[6 + whole : 9 + whole]
    x_all, dy_all, low_sum, grad_sum = refs[-5:-1] if load else refs[-4:]
    w_gate, w_up, w_down, low_proj, high_proj = refs[9 + whole : 14 + whole] if load else given
    rows = x_all.shape[0] // blocks
    across = (((1,), (1,)), ((), ()))
    units = w_gate.shape[1]
    tile = 256 if units % 256 == 0 else units
    tiles = units // tile
    lanes = grad_sum.shape[1]
    copies = []
    if load:
        rank = given[3].shape[0]
        for j in range(tiles):
            part = pl.ds(j * tile, tile)
            copies.append((given[0].at[:, part], w_gate.at[:, part]))
            copies.append((given[1].at[:, part], w_up.at[:, part]))
            copies.append((given[2].at[part, :], w_down.at[part, :]))
        for i in range(low_proj.shape[0] // rank):
            copies.append((given[3], low_proj.at[pl.ds(i * rank, rank), :]))
        copies.append((given[4], high_proj))
        copies.append((apart[0], x_all.at[:rows]))
        copies.append((apart[1], dy_all.at[:rows]))
        copies = [
            pltpu.make_async_copy(src, dst, refs[-1].at[i]) for i, (src, dst) in enumerate(copies)
        ]
        for copy in copies[3 * tiles :] + copies[: 3 * tiles]:
            copy.start()
    if blocks == 1:
        x_all, dy_all = block_in[0].at[:rows, :], block_in[0].at[rows:, :]
    for i, block in enumerate(block_in if blocks > 1 else ()):
        place = slice((blocks - whole + i) * rows, (blocks - whole + i + 1) * rows)
        x_all[place, :] = block[:rows, :]
        dy_all[place, :] = block[rows:, :]

    def one_tile(j):
        part = pl.ds(j * tile, tile)
        gate_val = jnp.dot(x_all[...], w_gate[:, part], preferred_element_type=jnp.float32)
        up_val = jnp.dot(x_all[...], w_up[:, part], preferred_element_type=jnp.float32)
        hidden = (jax.nn.silu(gate_val) * up_val).astype(jnp.bfloat16)
        back = lax.dot_general(
            dy_all[...], w_down[part, :], across, preferred_element_type=jnp.float32
        )
        terms = hidden.astype(jnp.float32) * back
        total = terms[:, :lanes]
        for cut in range(lanes, tile, lanes):
            total += terms[:, cut : cut + lanes]
        grad_sum[...] = total if j == 0 else grad_sum[...] + total
        low = lax.dot_general(
            low_proj[:, part], hidden, across, preferred_element_type=jnp.float32
        )
        low_sum[...] = low if j == 0 else low_sum[...] + low

    for copy in copies[3 * tiles :]:
        copy.wait()
    for j in range(tiles):
        for copy in copies[3 * j : 3 * j + 3] if load else []:
            copy.wait()
        one_tile(j)

    low_side[...] = low_sum[...].astype(low_side.dtype)
    proj_cot[...] = lax.dot_general(
        high_proj[...], dy_all[...], across, preferred_element_type=jnp.float32
    )
    sheet[...] = sheet_in[...]
    for i in range(blocks):
        total = jnp.sum(
            jnp.transpose(grad_sum[i * rows : (i + 1) * rows, :]), axis=0, keepdims=True
        )
        sheet[block_owner(names[i], sheet.shape[0] // 2), :, : total.shape[1]] = total


def work(names, sheet, block_in, weights, apart=(), load=0):
    width, units = weights[0].shape
    low_width, rank = weights[3].shape[0] * max(load, 1), weights[4].shape[0]
    blocks = len(names)
    rows = block_in[0].shape[0] // 2
    inside = pl.BlockSpec(memory_space=pltpu.VMEM)
    loaded = []
    if load:
        shapes = [w.shape for w in weights]
        shapes[3] = (low_width, units)
        loaded = [jax.ShapeDtypeStruct(shape, weights[0].dtype) for shape in shapes]
    tiles = units // 256 if units % 256 == 0 else 1
    call = pl.pallas_call(
        functools.partial(rows_kernel, names, load > 0),
        out_shape=[
            jax.ShapeDtypeStruct(sheet.shape, jnp.float32),
            jax.ShapeDtypeStruct((low_width, blocks * rows), jnp.bfloat16),
            jax.ShapeDtypeStruct((rank, blocks * rows), jnp.float32),
        ]
        + loaded,
        in_specs=[inside]
        + [pl.BlockSpec(memory_space=pl.ANY)] * len(apart)
        + [inside] * len(block_in)
        + [pl.BlockSpec(memory_space=pl.ANY) if load else inside] * len(weights),
        out_specs=[inside] * (3 + len(loaded)),
        scratch_shapes=[
            pltpu.VMEM((blocks * rows, width), jnp.bfloat16),
            pltpu.VMEM((blocks * rows, width), jnp.bfloat16),
            pltpu.VMEM((low_width, blocks * rows), jnp.float32),
            pltpu.VMEM((blocks * rows, 128), jnp.float32),
        ]
        + ([pltpu.SemaphoreType.DMA((3 * tiles + load + 3,))] if load else []),
        compiler_params=pltpu.CompilerParams(
            vmem_limit_bytes=(LOAD_MIB if load else 16) * 1024 * 1024
        ),
        cost_estimate=pl.CostEstimate(
            flops=6 * blocks * rows * width * units,
            bytes_accessed=4 * blocks * rows * width,
            transcendentals=blocks * rows * units,
        ),
    )
    return call(sheet, *apart, *block_in, *weights)


def front_kernel(*refs):
    blocks = len(refs) - 8
    x_in = refs[:blocks]
    w_gate, w_up, low_proj, hidden, low_first, low_last, x_all, low_sum = refs[blocks:]
    begin = 0
    for x in x_in:
        x_all[begin : begin + x.shape[0], :] = x[...]
        begin += x.shape[0]
    units = w_gate.shape[1]
    tile = 256 if units % 256 == 0 else units
    for cut in range(0, units, tile):
        part = pl.ds(cut, tile)
        gate_val = jnp.dot(x_all[...], w_gate[:, part], preferred_element_type=jnp.float32)
        up_val = jnp.dot(x_all[...], w_up[:, part], preferred_element_type=jnp.float32)
        piece = (jax.nn.silu(gate_val) * up_val).astype(jnp.bfloat16)
        hidden[:, part] = piece
        low = lax.dot_general(
            low_proj[:, part],
            piece,
            (((1,), (1,)), ((), ())),
            preferred_element_type=jnp.float32,
        )
        low_sum[...] = low if cut == 0 else low_sum[...] + low
    cut = low_first.shape[1]
    low_first[...] = low_sum[:, :cut].astype(low_first.dtype)
    low_last[...] = low_sum[:, cut:].astype(low_last.dtype)


def front(x_in, weights, last):
    w_gate, w_up, _, low_proj, _ = weights
    rows, width = sum(x.shape[0] for x in x_in), x_in[0].shape[1]
    units = w_gate.shape[1]
    inside = pl.BlockSpec(memory_space=pltpu.VMEM)
    return pl.pallas_call(
        front_kernel,
        out_shape=[
            jax.ShapeDtypeStruct((rows, units), jnp.bfloat16),
            jax.ShapeDtypeStruct((low_proj.shape[0], rows - last), jnp.bfloat16),
            jax.ShapeDtypeStruct((low_proj.shape[0], last), jnp.bfloat16),
        ],
        in_specs=[inside] * (len(x_in) + 3),
        out_specs=[inside] * 3,
        scratch_shapes=[
            pltpu.VMEM((rows, width), jnp.bfloat16),
            pltpu.VMEM((low_proj.shape[0], rows), jnp.float32),
        ],
        compiler_params=pltpu.CompilerParams(vmem_limit_bytes=16 * 1024 * 1024),
        cost_estimate=pl.CostEstimate(
            flops=4 * rows * width * units,
            bytes_accessed=2 * rows * width,
            transcendentals=rows * units,
        ),
    )(*x_in, w_gate, w_up, low_proj)


def fold(product):
    total = product[:, :128]
    for spot in range(128, product.shape[1], 128):
        total += product[:, spot : spot + 128]
    return total


def enter(sheet, name, total):
    line = jnp.sum(jnp.transpose(total), axis=0, keepdims=True)
    sheet[block_owner(name, sheet.shape[0] // 2), :, : line.shape[1]] = line


def out_kernel(names, *refs):
    blocks = len(names)
    sheet_in, dy_in = refs[0], refs[1 : 1 + blocks]
    hidden, w_down, high_proj, sheet, proj_cot, rest = refs[1 + blocks :]
    rows = dy_in[0].shape[0]
    across = (((1,), (1,)), ((), ()))
    width = w_down.shape[1]
    tile = 512 if width % 512 == 0 else width
    totals = [0.0] * blocks
    for cut in range(0, width, tile):
        part = pl.ds(cut, tile)
        out_val = jnp.dot(hidden[...], w_down[:, part], preferred_element_type=jnp.float32)
        for i in range(blocks):
            dy = dy_in[i][:, part].astype(jnp.float32)
            totals[i] += fold(dy * out_val[i * rows : (i + 1) * rows, :])
        rest[:, part] = out_val[blocks * rows :, :]
    sheet[...] = sheet_in[...]
    for i in range(blocks):
        enter(sheet, names[i], totals[i])
        proj_cot[:, i * rows : (i + 1) * rows] = lax.dot_general(
            high_proj[...], dy_in[i][...], across, preferred_element_type=jnp.float32
        )


def last_kernel(name, sheet_in, dy, out_val, high_proj, sheet, proj_cot):
    width = dy.shape[1]
    tile = 512 if width % 512 == 0 else width
    total = 0.0
    for cut in range(0, width, tile):
        part = pl.ds(cut, tile)
        total += fold(dy[:, part].astype(jnp.float32) * out_val[:, part])
    sheet[...] = sheet_in[...]
    enter(sheet, name, total)
    proj_cot[...] = lax.dot_general(
        high_proj[...], dy[...], (((1,), (1,)), ((), ())), preferred_element_type=jnp.float32
    )


def on_core(kernel, args, out_shape, flops=0):
    inside = pl.BlockSpec(memory_space=pltpu.VMEM)
    return pl.pallas_call(
        kernel,
        out_shape=[jax.ShapeDtypeStruct(shape, jnp.float32) for shape in out_shape],
        in_specs=[inside] * len(args),
        out_specs=[inside] * len(out_shape),
        compiler_params=pltpu.CompilerParams(vmem_limit_bytes=16 * 1024 * 1024),
        cost_estimate=pl.CostEstimate(flops=flops, bytes_accessed=2**20, transcendentals=0),
    )(*args)


def outcome_kernel(jobs, returned, routes, *refs):
    low_in, proj_in = refs[: len(jobs)], refs[len(jobs) : 2 * len(jobs)]
    feat, route_grad = refs[-2:]
    rows = returned.shape[2] // 3
    rank = proj_in[0].shape[0]
    docs = feat.shape[0] // rank
    spread, high_side = [], []
    for names, low_side, proj_cot in zip(jobs, low_in, proj_in):
        for i, name in enumerate(names):
            place = slice(i * rows, (i + 1) * rows)
            owner = block_owner(name, returned.shape[0] // 2)
            weight = returned[owner, :, rows : 2 * rows]
            doc = returned[owner, :, 2 * rows :].astype(jnp.int32)
            high_side.append((weight * proj_cot[:, place]).astype(jnp.bfloat16))
            low = low_side[:, place].astype(jnp.float32)
            parts = [jnp.where(doc == d, low, 0.0) for d in range(docs)]
            spread.append(jnp.concatenate(parts, axis=0).astype(jnp.bfloat16))
    feat[...] = lax.dot_general(
        jnp.concatenate(spread, axis=1),
        jnp.concatenate(high_side, axis=1),
        (((1,), (1,)), ((), ())),
        preferred_element_type=jnp.float32,
    )
    picked = jnp.zeros(route_grad.shape, jnp.float32)
    for e in range(returned.shape[0]):
        picked = jnp.where(routes[...] == e, returned[e, :, :rows], picked)
    route_grad[...] = picked


def facts_kernel(routes, combine, doc_ids, out):
    groups, rows = out.shape[0], routes.shape[1]
    expert = lax.broadcasted_iota(jnp.int32, (groups, rows), 0)
    weight = jnp.zeros((groups, rows), jnp.float32)
    for k in range(routes.shape[0]):
        share = combine[k : k + 1, :].astype(jnp.float32)
        weight += jnp.where(routes[k : k + 1, :] == expert, share, 0.0)
    doc = doc_ids[...].astype(jnp.float32)
    for e in range(groups):
        out[e] = jnp.concatenate([doc, weight[e : e + 1, :], doc], axis=1)


def stack_kernel(top, bottom, out):
    rows = top.shape[0]
    out[:rows, :] = top[...]
    out[rows:, :] = bottom[...]


def stack(top, bottom):
    inside = pl.BlockSpec(memory_space=pltpu.VMEM)
    return pl.pallas_call(
        stack_kernel,
        out_shape=jax.ShapeDtypeStruct((2 * top.shape[0], top.shape[1]), top.dtype),
        in_specs=[inside] * 2,
        out_specs=inside,
        compiler_params=pltpu.CompilerParams(vmem_limit_bytes=8 * 1024 * 1024),
    )(top, bottom)


def split_kernel(cuts, block, *parts):
    for (begin, count), part in zip(cuts, parts):
        part[...] = block[begin : begin + count, :]


def split(block, cuts):
    inside = pl.BlockSpec(memory_space=pltpu.VMEM)
    return pl.pallas_call(
        functools.partial(split_kernel, cuts),
        out_shape=[
            jax.ShapeDtypeStruct((count, block.shape[1]), block.dtype) for _, count in cuts
        ],
        in_specs=[inside],
        out_specs=[inside] * len(cuts),
        compiler_params=pltpu.CompilerParams(vmem_limit_bytes=8 * 1024 * 1024),
    )(block)


def by_ring(
    tokens, cotangent, routes, combine, doc_ids, w_gate, w_up, w_down, proj_hidden, proj_output
):
    tok_rows, chosen = routes.shape
    groups = lax.axis_size("exp")
    docs_count = max(2, tok_rows * groups // DOC_TOK)
    chips = groups // 2
    half = chips // 2
    ring = list(range(0, chips, 2)) + list(range(chips - 1, 0, -2))
    onward = []
    for place in range(chips):
        onward.append((2 * ring[place], 2 * ring[(place + 1) % chips]))
        onward.append((2 * ring[place] + 1, 2 * ring[place - 1] + 1))
    across = [(i, i ^ 1) for i in range(groups)]

    def hop(block):
        return lax.ppermute(block, "exp", onward)

    def swap(block):
        return lax.ppermute(block, "exp", across)

    arrivals = [(c, step) for step in range(1, half + 1) for c in ("ab" if step < half else "a")]
    jobs = [(("a", 0, False), ("a", 0, True))]
    for i, (c, step) in enumerate(arrivals):
        job = ((c, step, False),)
        if i > 0:
            job += (arrivals[i - 1] + (True,),)
        if i == 1:
            job += (arrivals[0] + (False,),)
        if i == len(arrivals) - 1:
            jobs += [(job[1], job[0]), ((c, step, True),)]
        elif i != 0:
            jobs.append(job)

    sheet = pl.pallas_call(
        facts_kernel,
        out_shape=jax.ShapeDtypeStruct((groups, 1, 3 * tok_rows), jnp.float32),
        in_specs=[pl.BlockSpec(memory_space=pltpu.VMEM)] * 3,
        out_specs=pl.BlockSpec(memory_space=pltpu.VMEM),
        compiler_params=pltpu.CompilerParams(vmem_limit_bytes=8 * 1024 * 1024),
    )(routes.T, combine.T, doc_ids[None, :])
    first = (hop(tokens), hop(cotangent))
    beside = stack(swap(tokens), swap(cotangent))

    inside = pl.BlockSpec(memory_space=pltpu.VMEM)
    given = (w_gate[0], w_up[0], w_down[0], proj_hidden[0].T, proj_output[0].T)
    weights = None
    lows, projs = [], []
    held = {("a", 0, True): beside}
    todo = list(jobs)

    def take():
        nonlocal sheet, weights
        names = todo.pop(0)
        blocks = [held[name] for name in names if name in held]
        if weights is None:
            sheet, low_side, proj_cot, *weights = work(
                names, sheet, blocks, given, apart=(tokens, cotangent), load=1
            )
        else:
            sheet, low_side, proj_cot = work(names, sheet, blocks, weights)
        lows.append(low_side)
        projs.append(proj_cot)

    chain = {"b": beside}
    for i, (c, step) in enumerate(arrivals[:-1]):
        block = hop(chain[c]) if i > 0 else first
        if i != 1:
            take()
            sheet, block = lax.optimization_barrier((sheet, block))
        if i == 0:
            block = stack(*block)
        chain[c] = held[(c, step, False)] = block
        if i < len(arrivals) - 2:
            held[(c, step, True)] = swap(block)
    cut = tok_rows // 2
    cuts = ((0, cut), (cut, cut), (tok_rows, tok_rows))
    *x, dy = split(chain["a"], cuts)
    dy, _ = lax.optimization_barrier((dy, chain["b"]))
    x, dy = [hop(part) for part in x], hop(dy)
    *x_before, dy_before = split(chain["b"], ((0, tok_rows), (tok_rows, tok_rows)))
    x_before, dy_before = [swap(part) for part in x_before], swap(dy_before)
    take()
    sheet, x = lax.optimization_barrier((sheet, x))
    hidden, low_first, low_last = front(
        x_before + x + [swap(part) for part in x], weights, tok_rows
    )
    hidden, dy = lax.optimization_barrier((hidden, dy))
    dy_beside = swap(dy)
    rank = proj_output.shape[2]
    sheet, proj_cot, out_val = on_core(
        functools.partial(out_kernel, todo.pop(0)),
        (sheet, dy_before, dy, hidden, weights[2], weights[4]),
        [sheet.shape, (rank, 2 * tok_rows), tokens.shape],
        flops=6 * tok_rows * hidden.shape[1] * tokens.shape[1],
    )
    lows.append(low_first)
    projs.append(proj_cot)
    ((name,),) = todo
    sheet, proj_cot = on_core(
        functools.partial(last_kernel, name),
        (sheet, dy_beside, out_val, weights[4]),
        [sheet.shape, (rank, tok_rows)],
    )
    lows.append(low_last)
    projs.append(proj_cot)
    returned = lax.all_to_all(sheet, "exp", split_axis=0, concat_axis=0, tiled=True)
    feature, route_grad = pl.pallas_call(
        functools.partial(outcome_kernel, jobs),
        out_shape=[
            jax.ShapeDtypeStruct((docs_count * rank, rank), jnp.float32),
            jax.ShapeDtypeStruct((chosen, tok_rows), jnp.float32),
        ],
        in_specs=[inside] * (2 + 2 * len(lows)),
        out_specs=[inside] * 2,
        compiler_params=pltpu.CompilerParams(vmem_limit_bytes=16 * 1024 * 1024),
    )(returned, routes.T, *lows, *projs)
    return feature.reshape(docs_count, 1, rank, rank), route_grad.T


def by_routing(
    tokens, cotangent, routes, combine, doc_ids, w_gate, w_up, w_down, proj_hidden, proj_output
):
    tok_rows, chosen = routes.shape
    local_count = w_gate.shape[0]
    groups = lax.axis_size("exp")
    experts = local_count * groups
    capacity = max(2, tok_rows * chosen * 5 // (4 * experts))
    docs_count = max(2, tok_rows * groups // DOC_TOK)
    entries = tok_rows * chosen
    width = tokens.shape[1]
    flat_routes = routes.reshape(-1)
    member = (flat_routes[:, None] == jnp.arange(experts, dtype=jnp.int32)[None, :]).astype(
        jnp.int32
    )
    slot_rank = jnp.sum((jnp.cumsum(member, axis=0) - 1) * member, axis=1)
    position = flat_routes * capacity + slot_rank
    source = (
        jnp.full((experts * capacity,), -1, jnp.int32)
        .at[position]
        .set(jnp.arange(entries, dtype=jnp.int32))
    )
    filled = source >= 0
    safe_source = jnp.maximum(source, 0)
    token_of = safe_source // chosen
    send_x = jnp.where(filled[:, None], tokens[token_of], 0)
    send_dy = jnp.where(filled[:, None], cotangent[token_of], 0)
    send_w = jnp.where(filled, combine.reshape(-1)[safe_source], 0)
    send_doc = jnp.where(filled, doc_ids[token_of], -1).astype(jnp.bfloat16)

    def exchange(array):
        array = array.reshape((groups, local_count, capacity) + array.shape[1:])
        return lax.all_to_all(array, "exp", split_axis=0, concat_axis=0, tiled=True)

    recv_x, recv_dy, recv_w, recv_doc = (
        exchange(send_x),
        exchange(send_dy),
        exchange(send_w),
        exchange(send_doc),
    )
    slots = groups * capacity
    grads, feats = [], []
    for e in range(local_count):
        hidden = swiglu(recv_x[:, e].reshape(slots, width), w_gate[e], w_up[e])
        grad, feature = finish(
            hidden,
            recv_dy[:, e].reshape(slots, width),
            recv_w[:, e].reshape(slots),
            recv_doc[:, e].reshape(slots),
            w_down[e],
            proj_hidden[e],
            proj_output[e],
            docs_count,
        )
        grads.append(grad.reshape(groups, capacity))
        feats.append(feature)
    slot_grad = jnp.stack(grads, axis=1)
    returned = lax.all_to_all(slot_grad, "exp", split_axis=0, concat_axis=0, tiled=True)
    route_grad = returned.reshape(-1)[position].reshape(tok_rows, chosen)
    return jnp.stack(feats, axis=1), route_grad


def on_device(tokens, cotangent, routes, combine, doc_ids, w_gate, *rest):
    tok_rows, chosen = routes.shape
    experts = w_gate.shape[0] * lax.axis_size("exp")
    dense = w_gate.shape[0] == 1 and 4 * chosen >= experts and experts >= 8 and experts % 4 == 0
    plan = by_ring if dense else by_routing
    return plan(tokens, cotangent, routes, combine, doc_ids, w_gate, *rest)


def solution(mesh):
    placed = (
        P(("grp", "exp"), None),
        P(("grp", "exp"), None),
        P(("grp", "exp"), None),
        P(("grp", "exp"), None),
        P(("grp", "exp")),
        P("exp", None, None),
        P("exp", None, None),
        P("exp", None, None),
        P("exp", None, None),
        P("exp", None, None),
    )
    return jax.shard_map(
        on_device,
        mesh=mesh,
        in_specs=placed,
        out_specs=(P("grp", "exp", None, None), P(("grp", "exp"), None)),
        check_vma=False,
    )
```

```python
import functools

import jax
import jax.numpy as jnp
from jax import lax
from jax.experimental import pallas as pl
from jax.experimental.pallas import tpu as pltpu
from jax.sharding import PartitionSpec as P

DOC_TOK = 512
LOAD_MIB = 40


def swiglu(rows, w_gate, w_up):
    gate_val = jnp.dot(rows, w_gate, preferred_element_type=jnp.float32)
    up_val = jnp.dot(rows, w_up, preferred_element_type=jnp.float32)
    return (jax.nn.silu(gate_val) * up_val).astype(jnp.bfloat16)


def finish(hidden, rows_dy, rows_w, rows_doc, w_down, proj_hidden, proj_output, docs_count):
    out_val = jnp.dot(hidden, w_down, preferred_element_type=jnp.float32)
    grad = jnp.sum(rows_dy.astype(jnp.float32) * out_val, axis=-1)
    low_side = jnp.dot(hidden, proj_hidden, preferred_element_type=jnp.float32).astype(
        jnp.bfloat16
    )
    proj_cot = jnp.dot(rows_dy, proj_output, preferred_element_type=jnp.float32)
    high_side = (rows_w.astype(jnp.float32)[:, None] * proj_cot).astype(jnp.bfloat16)
    doc_table = jnp.arange(docs_count, dtype=jnp.int32).astype(jnp.bfloat16)
    onehot = (rows_doc[:, None] == doc_table).astype(jnp.bfloat16)
    spread = onehot[:, :, None] * low_side[:, None, :]
    spread = spread.reshape(spread.shape[0], -1)
    feature = lax.dot_general(
        spread, high_side, (((0,), (0,)), ((), ())), preferred_element_type=jnp.float32
    )
    return grad, feature.reshape(docs_count, low_side.shape[1], high_side.shape[1])


def block_owner(name, chips):
    chain, step, handed = name
    me = lax.axis_index("exp")
    core, chip = lax.rem(me, 2), lax.div(me, 2)
    turn = chips // 2
    place = jnp.where(lax.rem(chip, 2) == 0, lax.div(chip, 2), chips - 1 - lax.div(chip, 2))
    way = 2 * core - 1
    place = place + (-way if handed else way) * step
    place = lax.rem(place + chips, chips)
    chip = jnp.where(place < turn, 2 * place, 2 * (chips - 1 - place) + 1)
    return 2 * chip + (core if (chain == "a") != handed else 1 - core)


def rows_kernel(names, load, *refs):
    blocks = len(names)
    apart = refs[1:3] if load else ()
    refs = refs[:1] + refs[3:] if load else refs
    whole = blocks - 1 if load else blocks
    sheet_in, block_in = refs[0], refs[1 : 1 + whole]
    given = refs[1 + whole : 6 + whole]
    sheet, low_side, proj_cot = refs[6 + whole : 9 + whole]
    x_all, dy_all, low_sum, grad_sum = refs[-5:-1] if load else refs[-4:]
    w_gate, w_up, w_down, low_proj, high_proj = refs[9 + whole : 14 + whole] if load else given
    rows = x_all.shape[0] // blocks
    across = (((1,), (1,)), ((), ()))
    units = w_gate.shape[1]
    tile = 256 if units % 256 == 0 else units
    tiles = units // tile
    lanes = grad_sum.shape[1]
    copies = []
    if load:
        rank = given[3].shape[0]
        for j in range(tiles):
            part = pl.ds(j * tile, tile)
            copies.append((given[0].at[:, part], w_gate.at[:, part]))
            copies.append((given[1].at[:, part], w_up.at[:, part]))
            copies.append((given[2].at[part, :], w_down.at[part, :]))
        for i in range(low_proj.shape[0] // rank):
            copies.append((given[3], low_proj.at[pl.ds(i * rank, rank), :]))
        copies.append((given[4], high_proj))
        copies.append((apart[0], x_all.at[:rows]))
        copies.append((apart[1], dy_all.at[:rows]))
        copies = [
            pltpu.make_async_copy(src, dst, refs[-1].at[i]) for i, (src, dst) in enumerate(copies)
        ]
        for copy in copies[3 * tiles :] + copies[: 3 * tiles]:
            copy.start()
    if blocks == 1:
        x_all, dy_all = block_in[0].at[:rows, :], block_in[0].at[rows:, :]
    for i, block in enumerate(block_in if blocks > 1 else ()):
        place = slice((blocks - whole + i) * rows, (blocks - whole + i + 1) * rows)
        x_all[place, :] = block[:rows, :]
        dy_all[place, :] = block[rows:, :]

    def one_tile(j):
        part = pl.ds(j * tile, tile)
        gate_val = jnp.dot(x_all[...], w_gate[:, part], preferred_element_type=jnp.float32)
        up_val = jnp.dot(x_all[...], w_up[:, part], preferred_element_type=jnp.float32)
        hidden = (jax.nn.silu(gate_val) * up_val).astype(jnp.bfloat16)
        back = lax.dot_general(
            dy_all[...], w_down[part, :], across, preferred_element_type=jnp.float32
        )
        terms = hidden.astype(jnp.float32) * back
        total = terms[:, :lanes]
        for cut in range(lanes, tile, lanes):
            total += terms[:, cut : cut + lanes]
        grad_sum[...] = total if j == 0 else grad_sum[...] + total
        low = lax.dot_general(
            low_proj[:, part], hidden, across, preferred_element_type=jnp.float32
        )
        low_sum[...] = low if j == 0 else low_sum[...] + low

    for copy in copies[3 * tiles :]:
        copy.wait()
    for j in range(tiles):
        for copy in copies[3 * j : 3 * j + 3] if load else []:
            copy.wait()
        one_tile(j)

    low_side[...] = low_sum[...].astype(low_side.dtype)
    proj_cot[...] = lax.dot_general(
        high_proj[...], dy_all[...], across, preferred_element_type=jnp.float32
    )
    sheet[...] = sheet_in[...]
    for i in range(blocks):
        total = jnp.sum(
            jnp.transpose(grad_sum[i * rows : (i + 1) * rows, :]), axis=0, keepdims=True
        )
        sheet[block_owner(names[i], sheet.shape[0] // 2), :, : total.shape[1]] = total


def work(names, sheet, block_in, weights, apart=(), load=0):
    width, units = weights[0].shape
    low_width, rank = weights[3].shape[0] * max(load, 1), weights[4].shape[0]
    blocks = len(names)
    rows = block_in[0].shape[0] // 2
    inside = pl.BlockSpec(memory_space=pltpu.VMEM)
    loaded = []
    if load:
        shapes = [w.shape for w in weights]
        shapes[3] = (low_width, units)
        loaded = [jax.ShapeDtypeStruct(shape, weights[0].dtype) for shape in shapes]
    tiles = units // 256 if units % 256 == 0 else 1
    call = pl.pallas_call(
        functools.partial(rows_kernel, names, load > 0),
        out_shape=[
            jax.ShapeDtypeStruct(sheet.shape, jnp.float32),
            jax.ShapeDtypeStruct((low_width, blocks * rows), jnp.bfloat16),
            jax.ShapeDtypeStruct((rank, blocks * rows), jnp.float32),
        ]
        + loaded,
        in_specs=[inside]
        + [pl.BlockSpec(memory_space=pl.ANY)] * len(apart)
        + [inside] * len(block_in)
        + [pl.BlockSpec(memory_space=pl.ANY) if load else inside] * len(weights),
        out_specs=[inside] * (3 + len(loaded)),
        scratch_shapes=[
            pltpu.VMEM((blocks * rows, width), jnp.bfloat16),
            pltpu.VMEM((blocks * rows, width), jnp.bfloat16),
            pltpu.VMEM((low_width, blocks * rows), jnp.float32),
            pltpu.VMEM((blocks * rows, 128), jnp.float32),
        ]
        + ([pltpu.SemaphoreType.DMA((3 * tiles + load + 3,))] if load else []),
        compiler_params=pltpu.CompilerParams(
            vmem_limit_bytes=(LOAD_MIB if load else 16) * 1024 * 1024
        ),
        cost_estimate=pl.CostEstimate(
            flops=6 * blocks * rows * width * units,
            bytes_accessed=4 * blocks * rows * width,
            transcendentals=blocks * rows * units,
        ),
    )
    return call(sheet, *apart, *block_in, *weights)


def front_kernel(begin, x_in, w_gate, w_up, low_proj, hidden, low_side, x_all, low_sum):
    rows = 0
    for x in x_in:
        x_all[rows : rows + x.shape[0], :] = x[...]
        rows += x.shape[0]
    units = w_gate.shape[1]
    tile = 256 if units % 256 == 0 else units
    for cut in range(0, units, tile):
        part = pl.ds(cut, tile)
        gate_val = jnp.dot(x_all[...], w_gate[:, part], preferred_element_type=jnp.float32)
        up_val = jnp.dot(x_all[...], w_up[:, part], preferred_element_type=jnp.float32)
        piece = (jax.nn.silu(gate_val) * up_val).astype(jnp.bfloat16)
        hidden[begin : begin + rows, part] = piece
        low = lax.dot_general(
            low_proj[:, part],
            piece,
            (((1,), (1,)), ((), ())),
            preferred_element_type=jnp.float32,
        )
        low_sum[...] = low if cut == 0 else low_sum[...] + low
    low_side[...] = low_sum[...].astype(low_side.dtype)


def front(x_in, weights, begin, room, held=()):
    w_gate, w_up, _, low_proj, _ = weights
    rows, width = sum(x.shape[0] for x in x_in), x_in[0].shape[1]
    units = w_gate.shape[1]
    inside = pl.BlockSpec(memory_space=pltpu.VMEM)
    count = len(x_in)

    def kernel(*refs):
        front_kernel(begin, refs[:count], *refs[count : count + 3], *refs[-4:])

    return pl.pallas_call(
        kernel,
        out_shape=[
            jax.ShapeDtypeStruct((room, units), jnp.bfloat16),
            jax.ShapeDtypeStruct((low_proj.shape[0], rows), jnp.bfloat16),
        ],
        in_specs=[inside] * (count + 3 + len(held)),
        out_specs=[inside] * 2,
        input_output_aliases={count + 3: 0} if held else {},
        scratch_shapes=[
            pltpu.VMEM((rows, width), jnp.bfloat16),
            pltpu.VMEM((low_proj.shape[0], rows), jnp.float32),
        ],
        compiler_params=pltpu.CompilerParams(vmem_limit_bytes=16 * 1024 * 1024),
        cost_estimate=pl.CostEstimate(flops=0, bytes_accessed=0, transcendentals=0),
    )(*x_in, w_gate, w_up, low_proj, *held)


def fold(product):
    total = product[:, :128]
    for spot in range(128, product.shape[1], 128):
        total += product[:, spot : spot + 128]
    return total


def enter(sheet, name, total):
    line = jnp.sum(jnp.transpose(total), axis=0, keepdims=True)
    sheet[block_owner(name, sheet.shape[0] // 2), :, : line.shape[1]] = line


def out_kernel(names, *refs):
    blocks = len(names)
    sheet_in, dy_in = refs[0], refs[1 : 1 + blocks]
    hidden, w_down, high_proj, sheet, proj_cot, rest = refs[1 + blocks :]
    rows = dy_in[0].shape[0]
    across = (((1,), (1,)), ((), ()))
    width = w_down.shape[1]
    tile = 512 if width % 512 == 0 else width
    totals = [0.0] * blocks
    for cut in range(0, width, tile):
        part = pl.ds(cut, tile)
        out_val = jnp.dot(hidden[...], w_down[:, part], preferred_element_type=jnp.float32)
        for i in range(blocks):
            dy = dy_in[i][:, part].astype(jnp.float32)
            totals[i] += fold(dy * out_val[i * rows : (i + 1) * rows, :])
        rest[:, part] = out_val[blocks * rows :, :]
    sheet[...] = sheet_in[...]
    for i in range(blocks):
        enter(sheet, names[i], totals[i])
        proj_cot[:, i * rows : (i + 1) * rows] = lax.dot_general(
            high_proj[...], dy_in[i][...], across, preferred_element_type=jnp.float32
        )


def last_kernel(name, sheet_in, dy, out_val, high_proj, sheet, proj_cot):
    width = dy.shape[1]
    tile = 512 if width % 512 == 0 else width
    total = 0.0
    for cut in range(0, width, tile):
        part = pl.ds(cut, tile)
        total += fold(dy[:, part].astype(jnp.float32) * out_val[:, part])
    sheet[...] = sheet_in[...]
    enter(sheet, name, total)
    proj_cot[...] = lax.dot_general(
        high_proj[...], dy[...], (((1,), (1,)), ((), ())), preferred_element_type=jnp.float32
    )


def on_core(kernel, args, out_shape, flops=0):
    inside = pl.BlockSpec(memory_space=pltpu.VMEM)
    return pl.pallas_call(
        kernel,
        out_shape=[jax.ShapeDtypeStruct(shape, jnp.float32) for shape in out_shape],
        in_specs=[inside] * len(args),
        out_specs=[inside] * len(out_shape),
        compiler_params=pltpu.CompilerParams(vmem_limit_bytes=16 * 1024 * 1024),
        cost_estimate=pl.CostEstimate(flops=flops, bytes_accessed=2**20, transcendentals=0),
    )(*args)


def outcome_kernel(jobs, returned, routes, *refs):
    low_in, proj_in = refs[: len(jobs)], refs[len(jobs) : 2 * len(jobs)]
    feat, route_grad = refs[-2:]
    rows = returned.shape[2] // 3
    rank = proj_in[0].shape[0]
    docs = feat.shape[0] // rank
    spread, high_side = [], []
    for names, low_side, proj_cot in zip(jobs, low_in, proj_in):
        for i, name in enumerate(names):
            place = slice(i * rows, (i + 1) * rows)
            owner = block_owner(name, returned.shape[0] // 2)
            weight = returned[owner, :, rows : 2 * rows]
            doc = returned[owner, :, 2 * rows :].astype(jnp.int32)
            high_side.append((weight * proj_cot[:, place]).astype(jnp.bfloat16))
            low = low_side[:, place].astype(jnp.float32)
            parts = [jnp.where(doc == d, low, 0.0) for d in range(docs)]
            spread.append(jnp.concatenate(parts, axis=0).astype(jnp.bfloat16))
    feat[...] = lax.dot_general(
        jnp.concatenate(spread, axis=1),
        jnp.concatenate(high_side, axis=1),
        (((1,), (1,)), ((), ())),
        preferred_element_type=jnp.float32,
    )
    picked = jnp.zeros(route_grad.shape, jnp.float32)
    for e in range(returned.shape[0]):
        picked = jnp.where(routes[...] == e, returned[e, :, :rows], picked)
    route_grad[...] = picked


def facts_kernel(routes, combine, doc_ids, out):
    groups, rows = out.shape[0], routes.shape[1]
    expert = lax.broadcasted_iota(jnp.int32, (groups, rows), 0)
    weight = jnp.zeros((groups, rows), jnp.float32)
    for k in range(routes.shape[0]):
        share = combine[k : k + 1, :].astype(jnp.float32)
        weight += jnp.where(routes[k : k + 1, :] == expert, share, 0.0)
    doc = doc_ids[...].astype(jnp.float32)
    for e in range(groups):
        out[e] = jnp.concatenate([doc, weight[e : e + 1, :], doc], axis=1)


def stack_kernel(top, bottom, out):
    rows = top.shape[0]
    out[:rows, :] = top[...]
    out[rows:, :] = bottom[...]


def stack(top, bottom):
    inside = pl.BlockSpec(memory_space=pltpu.VMEM)
    return pl.pallas_call(
        stack_kernel,
        out_shape=jax.ShapeDtypeStruct((2 * top.shape[0], top.shape[1]), top.dtype),
        in_specs=[inside] * 2,
        out_specs=inside,
        compiler_params=pltpu.CompilerParams(vmem_limit_bytes=8 * 1024 * 1024),
    )(top, bottom)


def split_kernel(cuts, block, *parts):
    for (begin, count), part in zip(cuts, parts):
        part[...] = block[begin : begin + count, :]


def split(block, cuts):
    inside = pl.BlockSpec(memory_space=pltpu.VMEM)
    return pl.pallas_call(
        functools.partial(split_kernel, cuts),
        out_shape=[
            jax.ShapeDtypeStruct((count, block.shape[1]), block.dtype) for _, count in cuts
        ],
        in_specs=[inside],
        out_specs=[inside] * len(cuts),
        compiler_params=pltpu.CompilerParams(vmem_limit_bytes=8 * 1024 * 1024),
    )(block)


def by_ring(
    tokens, cotangent, routes, combine, doc_ids, w_gate, w_up, w_down, proj_hidden, proj_output
):
    tok_rows, chosen = routes.shape
    groups = lax.axis_size("exp")
    docs_count = max(2, tok_rows * groups // DOC_TOK)
    chips = groups // 2
    half = chips // 2
    ring = list(range(0, chips, 2)) + list(range(chips - 1, 0, -2))
    onward = []
    for place in range(chips):
        onward.append((2 * ring[place], 2 * ring[(place + 1) % chips]))
        onward.append((2 * ring[place] + 1, 2 * ring[place - 1] + 1))
    across = [(i, i ^ 1) for i in range(groups)]

    def hop(block):
        return lax.ppermute(block, "exp", onward)

    def swap(block):
        return lax.ppermute(block, "exp", across)

    arrivals = [(c, step) for step in range(1, half + 1) for c in ("ab" if step < half else "a")]
    jobs = [(("a", 0, False), ("a", 0, True))]
    for i, (c, step) in enumerate(arrivals):
        job = ((c, step, False),)
        if i > 0:
            job += (arrivals[i - 1] + (True,),)
        if i == 1:
            job += (arrivals[0] + (False,),)
        if i == len(arrivals) - 1:
            jobs += [(job[1], job[0]), ((c, step, True),)]
        elif i != 0:
            jobs.append(job)

    sheet = pl.pallas_call(
        facts_kernel,
        out_shape=jax.ShapeDtypeStruct((groups, 1, 3 * tok_rows), jnp.float32),
        in_specs=[pl.BlockSpec(memory_space=pltpu.VMEM)] * 3,
        out_specs=pl.BlockSpec(memory_space=pltpu.VMEM),
        compiler_params=pltpu.CompilerParams(vmem_limit_bytes=8 * 1024 * 1024),
    )(routes.T, combine.T, doc_ids[None, :])
    first = (hop(tokens), hop(cotangent))
    beside = stack(swap(tokens), swap(cotangent))

    inside = pl.BlockSpec(memory_space=pltpu.VMEM)
    given = (w_gate[0], w_up[0], w_down[0], proj_hidden[0].T, proj_output[0].T)
    weights = None
    lows, projs = [], []
    held = {("a", 0, True): beside}
    todo = list(jobs)

    def take():
        nonlocal sheet, weights
        names = todo.pop(0)
        blocks = [held[name] for name in names if name in held]
        if weights is None:
            sheet, low_side, proj_cot, *weights = work(
                names, sheet, blocks, given, apart=(tokens, cotangent), load=1
            )
        else:
            sheet, low_side, proj_cot = work(names, sheet, blocks, weights)
        lows.append(low_side)
        projs.append(proj_cot)

    chain = {"b": beside}
    for i, (c, step) in enumerate(arrivals[:-1]):
        block = hop(chain[c]) if i > 0 else first
        if i != 1:
            take()
            sheet, block = lax.optimization_barrier((sheet, block))
        if i == 0:
            block = stack(*block)
        chain[c] = held[(c, step, False)] = block
        if i < len(arrivals) - 2:
            held[(c, step, True)] = swap(block)
    cut = tok_rows // 2
    cuts = ((0, cut), (cut, cut), (tok_rows, tok_rows))
    *x, dy = split(chain["a"], cuts)
    dy, _ = lax.optimization_barrier((dy, chain["b"]))
    x, dy = [hop(part) for part in x], hop(dy)
    *x_before, dy_before = split(chain["b"], ((0, tok_rows), (tok_rows, tok_rows)))
    x_before, dy_before = [swap(part) for part in x_before], swap(dy_before)
    take()
    sheet, x = lax.optimization_barrier((sheet, x))
    x_beside = [swap(part) for part in x]
    hidden, low_first = front(x_before + x, weights, 0, 3 * tok_rows)
    hidden, low_last = front(x_beside, weights, 2 * tok_rows, 3 * tok_rows, (hidden,))
    hidden, dy = lax.optimization_barrier((hidden, dy))
    dy_beside = swap(dy)
    rank = proj_output.shape[2]
    sheet, proj_cot, out_val = on_core(
        functools.partial(out_kernel, todo.pop(0)),
        (sheet, dy_before, dy, hidden, weights[2], weights[4]),
        [sheet.shape, (rank, 2 * tok_rows), tokens.shape],
        flops=6 * tok_rows * hidden.shape[1] * tokens.shape[1],
    )
    lows.append(low_first)
    projs.append(proj_cot)
    ((name,),) = todo
    sheet, proj_cot = on_core(
        functools.partial(last_kernel, name),
        (sheet, dy_beside, out_val, weights[4]),
        [sheet.shape, (rank, tok_rows)],
    )
    lows.append(low_last)
    projs.append(proj_cot)
    returned = lax.all_to_all(sheet, "exp", split_axis=0, concat_axis=0, tiled=True)
    feature, route_grad = pl.pallas_call(
        functools.partial(outcome_kernel, jobs),
        out_shape=[
            jax.ShapeDtypeStruct((docs_count * rank, rank), jnp.float32),
            jax.ShapeDtypeStruct((chosen, tok_rows), jnp.float32),
        ],
        in_specs=[inside] * (2 + 2 * len(lows)),
        out_specs=[inside] * 2,
        compiler_params=pltpu.CompilerParams(vmem_limit_bytes=16 * 1024 * 1024),
    )(returned, routes.T, *lows, *projs)
    return feature.reshape(docs_count, 1, rank, rank), route_grad.T


def by_routing(
    tokens, cotangent, routes, combine, doc_ids, w_gate, w_up, w_down, proj_hidden, proj_output
):
    tok_rows, chosen = routes.shape
    local_count = w_gate.shape[0]
    groups = lax.axis_size("exp")
    experts = local_count * groups
    capacity = max(2, tok_rows * chosen * 5 // (4 * experts))
    docs_count = max(2, tok_rows * groups // DOC_TOK)
    entries = tok_rows * chosen
    width = tokens.shape[1]
    flat_routes = routes.reshape(-1)
    member = (flat_routes[:, None] == jnp.arange(experts, dtype=jnp.int32)[None, :]).astype(
        jnp.int32
    )
    slot_rank = jnp.sum((jnp.cumsum(member, axis=0) - 1) * member, axis=1)
    position = flat_routes * capacity + slot_rank
    source = (
        jnp.full((experts * capacity,), -1, jnp.int32)
        .at[position]
        .set(jnp.arange(entries, dtype=jnp.int32))
    )
    filled = source >= 0
    safe_source = jnp.maximum(source, 0)
    token_of = safe_source // chosen
    send_x = jnp.where(filled[:, None], tokens[token_of], 0)
    send_dy = jnp.where(filled[:, None], cotangent[token_of], 0)
    send_w = jnp.where(filled, combine.reshape(-1)[safe_source], 0)
    send_doc = jnp.where(filled, doc_ids[token_of], -1).astype(jnp.bfloat16)

    def exchange(array):
        array = array.reshape((groups, local_count, capacity) + array.shape[1:])
        return lax.all_to_all(array, "exp", split_axis=0, concat_axis=0, tiled=True)

    recv_x, recv_dy, recv_w, recv_doc = (
        exchange(send_x),
        exchange(send_dy),
        exchange(send_w),
        exchange(send_doc),
    )
    slots = groups * capacity
    grads, feats = [], []
    for e in range(local_count):
        hidden = swiglu(recv_x[:, e].reshape(slots, width), w_gate[e], w_up[e])
        grad, feature = finish(
            hidden,
            recv_dy[:, e].reshape(slots, width),
            recv_w[:, e].reshape(slots),
            recv_doc[:, e].reshape(slots),
            w_down[e],
            proj_hidden[e],
            proj_output[e],
            docs_count,
        )
        grads.append(grad.reshape(groups, capacity))
        feats.append(feature)
    slot_grad = jnp.stack(grads, axis=1)
    returned = lax.all_to_all(slot_grad, "exp", split_axis=0, concat_axis=0, tiled=True)
    route_grad = returned.reshape(-1)[position].reshape(tok_rows, chosen)
    return jnp.stack(feats, axis=1), route_grad


def on_device(tokens, cotangent, routes, combine, doc_ids, w_gate, *rest):
    tok_rows, chosen = routes.shape
    experts = w_gate.shape[0] * lax.axis_size("exp")
    dense = w_gate.shape[0] == 1 and 4 * chosen >= experts and experts >= 8 and experts % 4 == 0
    plan = by_ring if dense else by_routing
    return plan(tokens, cotangent, routes, combine, doc_ids, w_gate, *rest)


def solution(mesh):
    placed = (
        P(("grp", "exp"), None),
        P(("grp", "exp"), None),
        P(("grp", "exp"), None),
        P(("grp", "exp"), None),
        P(("grp", "exp")),
        P("exp", None, None),
        P("exp", None, None),
        P("exp", None, None),
        P("exp", None, None),
        P("exp", None, None),
    )
    return jax.shard_map(
        on_device,
        mesh=mesh,
        in_specs=placed,
        out_specs=(P("grp", "exp", None, None), P(("grp", "exp"), None)),
        check_vma=False,
    )
```

```python
import functools

import jax
import jax.numpy as jnp
from jax import lax
from jax.experimental import pallas as pl
from jax.experimental.pallas import tpu as pltpu
from jax.sharding import PartitionSpec as P

DOC_TOK = 512
LOAD_MIB = 40


def swiglu(rows, w_gate, w_up):
    gate_val = jnp.dot(rows, w_gate, preferred_element_type=jnp.float32)
    up_val = jnp.dot(rows, w_up, preferred_element_type=jnp.float32)
    return (jax.nn.silu(gate_val) * up_val).astype(jnp.bfloat16)


def finish(hidden, rows_dy, rows_w, rows_doc, w_down, proj_hidden, proj_output, docs_count):
    out_val = jnp.dot(hidden, w_down, preferred_element_type=jnp.float32)
    grad = jnp.sum(rows_dy.astype(jnp.float32) * out_val, axis=-1)
    low_side = jnp.dot(hidden, proj_hidden, preferred_element_type=jnp.float32).astype(
        jnp.bfloat16
    )
    proj_cot = jnp.dot(rows_dy, proj_output, preferred_element_type=jnp.float32)
    high_side = (rows_w.astype(jnp.float32)[:, None] * proj_cot).astype(jnp.bfloat16)
    doc_table = jnp.arange(docs_count, dtype=jnp.int32).astype(jnp.bfloat16)
    onehot = (rows_doc[:, None] == doc_table).astype(jnp.bfloat16)
    spread = onehot[:, :, None] * low_side[:, None, :]
    spread = spread.reshape(spread.shape[0], -1)
    feature = lax.dot_general(
        spread, high_side, (((0,), (0,)), ((), ())), preferred_element_type=jnp.float32
    )
    return grad, feature.reshape(docs_count, low_side.shape[1], high_side.shape[1])


def block_owner(name, chips):
    chain, step, handed = name
    me = lax.axis_index("exp")
    core, chip = lax.rem(me, 2), lax.div(me, 2)
    turn = chips // 2
    place = jnp.where(lax.rem(chip, 2) == 0, lax.div(chip, 2), chips - 1 - lax.div(chip, 2))
    way = 2 * core - 1
    place = place + (-way if handed else way) * step
    place = lax.rem(place + chips, chips)
    chip = jnp.where(place < turn, 2 * place, 2 * (chips - 1 - place) + 1)
    return 2 * chip + (core if (chain == "a") != handed else 1 - core)


def rows_kernel(names, load, *refs):
    blocks = len(names)
    apart = refs[1:3] if load else ()
    refs = refs[:1] + refs[3:] if load else refs
    whole = blocks - 1 if load else blocks
    sheet_in, block_in = refs[0], refs[1 : 1 + whole]
    given = refs[1 + whole : 6 + whole]
    sheet, low_side, proj_cot = refs[6 + whole : 9 + whole]
    x_all, dy_all, low_sum, grad_sum = refs[-5:-1] if load else refs[-4:]
    w_gate, w_up, w_down, low_proj, high_proj = refs[9 + whole : 14 + whole] if load else given
    rows = x_all.shape[0] // blocks
    across = (((1,), (1,)), ((), ()))
    units = w_gate.shape[1]
    tile = 256 if units % 256 == 0 else units
    tiles = units // tile
    lanes = grad_sum.shape[1]
    copies = []
    if load:
        rank = given[3].shape[0]
        for j in range(tiles):
            part = pl.ds(j * tile, tile)
            copies.append((given[0].at[:, part], w_gate.at[:, part]))
            copies.append((given[1].at[:, part], w_up.at[:, part]))
            copies.append((given[2].at[part, :], w_down.at[part, :]))
        for i in range(low_proj.shape[0] // rank):
            copies.append((given[3], low_proj.at[pl.ds(i * rank, rank), :]))
        copies.append((given[4], high_proj))
        copies.append((apart[0], x_all.at[:rows]))
        copies.append((apart[1], dy_all.at[:rows]))
        copies = [
            pltpu.make_async_copy(src, dst, refs[-1].at[i]) for i, (src, dst) in enumerate(copies)
        ]
        for copy in copies[3 * tiles :] + copies[: 3 * tiles]:
            copy.start()
    if blocks == 1:
        x_all, dy_all = block_in[0].at[:rows, :], block_in[0].at[rows:, :]
    for i, block in enumerate(block_in if blocks > 1 else ()):
        place = slice((blocks - whole + i) * rows, (blocks - whole + i + 1) * rows)
        x_all[place, :] = block[:rows, :]
        dy_all[place, :] = block[rows:, :]

    def one_tile(j):
        part = pl.ds(j * tile, tile)
        gate_val = jnp.dot(x_all[...], w_gate[:, part], preferred_element_type=jnp.float32)
        up_val = jnp.dot(x_all[...], w_up[:, part], preferred_element_type=jnp.float32)
        hidden = (jax.nn.silu(gate_val) * up_val).astype(jnp.bfloat16)
        back = lax.dot_general(
            dy_all[...], w_down[part, :], across, preferred_element_type=jnp.float32
        )
        terms = hidden.astype(jnp.float32) * back
        total = terms[:, :lanes]
        for cut in range(lanes, tile, lanes):
            total += terms[:, cut : cut + lanes]
        grad_sum[...] = total if j == 0 else grad_sum[...] + total
        low = lax.dot_general(
            low_proj[:, part], hidden, across, preferred_element_type=jnp.float32
        )
        low_sum[...] = low if j == 0 else low_sum[...] + low

    for copy in copies[3 * tiles :]:
        copy.wait()
    for j in range(tiles):
        for copy in copies[3 * j : 3 * j + 3] if load else []:
            copy.wait()
        one_tile(j)

    low_side[...] = low_sum[...].astype(low_side.dtype)
    proj_cot[...] = lax.dot_general(
        high_proj[...], dy_all[...], across, preferred_element_type=jnp.float32
    )
    sheet[...] = sheet_in[...]
    for i in range(blocks):
        total = jnp.sum(
            jnp.transpose(grad_sum[i * rows : (i + 1) * rows, :]), axis=0, keepdims=True
        )
        sheet[block_owner(names[i], sheet.shape[0] // 2), :, : total.shape[1]] = total


def work(names, sheet, block_in, weights, apart=(), load=0):
    width, units = weights[0].shape
    low_width, rank = weights[3].shape[0] * max(load, 1), weights[4].shape[0]
    blocks = len(names)
    rows = block_in[0].shape[0] // 2
    inside = pl.BlockSpec(memory_space=pltpu.VMEM)
    loaded = []
    if load:
        shapes = [w.shape for w in weights]
        shapes[3] = (low_width, units)
        loaded = [jax.ShapeDtypeStruct(shape, weights[0].dtype) for shape in shapes]
    tiles = units // 256 if units % 256 == 0 else 1
    call = pl.pallas_call(
        functools.partial(rows_kernel, names, load > 0),
        out_shape=[
            jax.ShapeDtypeStruct(sheet.shape, jnp.float32),
            jax.ShapeDtypeStruct((low_width, blocks * rows), jnp.bfloat16),
            jax.ShapeDtypeStruct((rank, blocks * rows), jnp.float32),
        ]
        + loaded,
        in_specs=[inside]
        + [pl.BlockSpec(memory_space=pl.ANY)] * len(apart)
        + [inside] * len(block_in)
        + [pl.BlockSpec(memory_space=pl.ANY) if load else inside] * len(weights),
        out_specs=[inside] * (3 + len(loaded)),
        scratch_shapes=[
            pltpu.VMEM((blocks * rows, width), jnp.bfloat16),
            pltpu.VMEM((blocks * rows, width), jnp.bfloat16),
            pltpu.VMEM((low_width, blocks * rows), jnp.float32),
            pltpu.VMEM((blocks * rows, 128), jnp.float32),
        ]
        + ([pltpu.SemaphoreType.DMA((3 * tiles + load + 3,))] if load else []),
        compiler_params=pltpu.CompilerParams(
            vmem_limit_bytes=(LOAD_MIB if load else 16) * 1024 * 1024
        ),
        cost_estimate=pl.CostEstimate(
            flops=6 * blocks * rows * width * units,
            bytes_accessed=4 * blocks * rows * width,
            transcendentals=blocks * rows * units,
        ),
    )
    return call(sheet, *apart, *block_in, *weights)


def front_kernel(*refs):
    blocks = len(refs) - 8
    x_in = refs[:blocks]
    w_gate, w_up, low_proj, hidden, low_first, low_last, x_all, low_sum = refs[blocks:]
    begin = 0
    for x in x_in:
        x_all[begin : begin + x.shape[0], :] = x[...]
        begin += x.shape[0]
    units = w_gate.shape[1]
    tile = 256 if units % 256 == 0 else units
    for cut in range(0, units, tile):
        part = pl.ds(cut, tile)
        gate_val = jnp.dot(x_all[...], w_gate[:, part], preferred_element_type=jnp.float32)
        up_val = jnp.dot(x_all[...], w_up[:, part], preferred_element_type=jnp.float32)
        piece = (jax.nn.silu(gate_val) * up_val).astype(jnp.bfloat16)
        hidden[:, part] = piece
        low = lax.dot_general(
            low_proj[:, part],
            piece,
            (((1,), (1,)), ((), ())),
            preferred_element_type=jnp.float32,
        )
        low_sum[...] = low if cut == 0 else low_sum[...] + low
    cut = low_first.shape[1]
    low_first[...] = low_sum[:, :cut].astype(low_first.dtype)
    low_last[...] = low_sum[:, cut:].astype(low_last.dtype)


def front(x_in, weights, last):
    w_gate, w_up, _, low_proj, _ = weights
    rows, width = sum(x.shape[0] for x in x_in), x_in[0].shape[1]
    units = w_gate.shape[1]
    inside = pl.BlockSpec(memory_space=pltpu.VMEM)
    return pl.pallas_call(
        front_kernel,
        out_shape=[
            jax.ShapeDtypeStruct((rows, units), jnp.bfloat16),
            jax.ShapeDtypeStruct((low_proj.shape[0], rows - last), jnp.bfloat16),
            jax.ShapeDtypeStruct((low_proj.shape[0], last), jnp.bfloat16),
        ],
        in_specs=[inside] * (len(x_in) + 3),
        out_specs=[inside] * 3,
        scratch_shapes=[
            pltpu.VMEM((rows, width), jnp.bfloat16),
            pltpu.VMEM((low_proj.shape[0], rows), jnp.float32),
        ],
        compiler_params=pltpu.CompilerParams(vmem_limit_bytes=16 * 1024 * 1024),
        cost_estimate=pl.CostEstimate(
            flops=4 * rows * width * units,
            bytes_accessed=2 * rows * width,
            transcendentals=rows * units,
        ),
    )(*x_in, w_gate, w_up, low_proj)


def fold(product):
    total = product[:, :128]
    for spot in range(128, product.shape[1], 128):
        total += product[:, spot : spot + 128]
    return total


def enter(sheet, name, total):
    line = jnp.sum(jnp.transpose(total), axis=0, keepdims=True)
    sheet[block_owner(name, sheet.shape[0] // 2), :, : line.shape[1]] = line


def out_kernel(names, *refs):
    blocks = len(names)
    sheet_in, dy_in = refs[0], refs[1 : 1 + blocks]
    hidden, w_down, high_proj, sheet, proj_cot, rest = refs[1 + blocks :]
    rows = dy_in[0].shape[0]
    across = (((1,), (1,)), ((), ()))
    width = w_down.shape[1]
    tile = 256 if width % 256 == 0 else width
    totals = [0.0] * blocks
    for cut in range(0, width, tile):
        part = pl.ds(cut, tile)
        out_val = jnp.dot(hidden[...], w_down[:, part], preferred_element_type=jnp.float32)
        for i in range(blocks):
            dy = dy_in[i][:, part].astype(jnp.float32)
            totals[i] += fold(dy * out_val[i * rows : (i + 1) * rows, :])
        rest[:, part] = out_val[blocks * rows :, :]
    sheet[...] = sheet_in[...]
    for i in range(blocks):
        enter(sheet, names[i], totals[i])
        proj_cot[:, i * rows : (i + 1) * rows] = lax.dot_general(
            high_proj[...], dy_in[i][...], across, preferred_element_type=jnp.float32
        )


def last_kernel(name, sheet_in, dy, out_val, high_proj, sheet, proj_cot):
    width = dy.shape[1]
    tile = 512 if width % 512 == 0 else width
    total = 0.0
    for cut in range(0, width, tile):
        part = pl.ds(cut, tile)
        total += fold(dy[:, part].astype(jnp.float32) * out_val[:, part])
    sheet[...] = sheet_in[...]
    enter(sheet, name, total)
    proj_cot[...] = lax.dot_general(
        high_proj[...], dy[...], (((1,), (1,)), ((), ())), preferred_element_type=jnp.float32
    )


def on_core(kernel, args, out_shape, flops=0):
    inside = pl.BlockSpec(memory_space=pltpu.VMEM)
    return pl.pallas_call(
        kernel,
        out_shape=[jax.ShapeDtypeStruct(shape, jnp.float32) for shape in out_shape],
        in_specs=[inside] * len(args),
        out_specs=[inside] * len(out_shape),
        compiler_params=pltpu.CompilerParams(vmem_limit_bytes=16 * 1024 * 1024),
        cost_estimate=pl.CostEstimate(flops=flops, bytes_accessed=2**20, transcendentals=0),
    )(*args)


def outcome_kernel(jobs, returned, routes, *refs):
    low_in, proj_in = refs[: len(jobs)], refs[len(jobs) : 2 * len(jobs)]
    feat, route_grad = refs[-2:]
    rows = returned.shape[2] // 3
    rank = proj_in[0].shape[0]
    docs = feat.shape[0] // rank
    spread, high_side = [], []
    for names, low_side, proj_cot in zip(jobs, low_in, proj_in):
        for i, name in enumerate(names):
            place = slice(i * rows, (i + 1) * rows)
            owner = block_owner(name, returned.shape[0] // 2)
            weight = returned[owner, :, rows : 2 * rows]
            doc = returned[owner, :, 2 * rows :].astype(jnp.int32)
            high_side.append((weight * proj_cot[:, place]).astype(jnp.bfloat16))
            low = low_side[:, place].astype(jnp.float32)
            parts = [jnp.where(doc == d, low, 0.0) for d in range(docs)]
            spread.append(jnp.concatenate(parts, axis=0).astype(jnp.bfloat16))
    feat[...] = lax.dot_general(
        jnp.concatenate(spread, axis=1),
        jnp.concatenate(high_side, axis=1),
        (((1,), (1,)), ((), ())),
        preferred_element_type=jnp.float32,
    )
    picked = jnp.zeros(route_grad.shape, jnp.float32)
    for e in range(returned.shape[0]):
        picked = jnp.where(routes[...] == e, returned[e, :, :rows], picked)
    route_grad[...] = picked


def facts_kernel(routes, combine, doc_ids, out):
    groups, rows = out.shape[0], routes.shape[1]
    expert = lax.broadcasted_iota(jnp.int32, (groups, rows), 0)
    weight = jnp.zeros((groups, rows), jnp.float32)
    for k in range(routes.shape[0]):
        share = combine[k : k + 1, :].astype(jnp.float32)
        weight += jnp.where(routes[k : k + 1, :] == expert, share, 0.0)
    doc = doc_ids[...].astype(jnp.float32)
    for e in range(groups):
        out[e] = jnp.concatenate([doc, weight[e : e + 1, :], doc], axis=1)


def stack_kernel(top, bottom, out):
    rows = top.shape[0]
    out[:rows, :] = top[...]
    out[rows:, :] = bottom[...]


def stack(top, bottom):
    inside = pl.BlockSpec(memory_space=pltpu.VMEM)
    return pl.pallas_call(
        stack_kernel,
        out_shape=jax.ShapeDtypeStruct((2 * top.shape[0], top.shape[1]), top.dtype),
        in_specs=[inside] * 2,
        out_specs=inside,
        compiler_params=pltpu.CompilerParams(vmem_limit_bytes=8 * 1024 * 1024),
    )(top, bottom)


def split_kernel(cuts, block, *parts):
    for (begin, count), part in zip(cuts, parts):
        part[...] = block[begin : begin + count, :]


def split(block, cuts):
    inside = pl.BlockSpec(memory_space=pltpu.VMEM)
    return pl.pallas_call(
        functools.partial(split_kernel, cuts),
        out_shape=[
            jax.ShapeDtypeStruct((count, block.shape[1]), block.dtype) for _, count in cuts
        ],
        in_specs=[inside],
        out_specs=[inside] * len(cuts),
        compiler_params=pltpu.CompilerParams(vmem_limit_bytes=8 * 1024 * 1024),
    )(block)


def by_ring(
    tokens, cotangent, routes, combine, doc_ids, w_gate, w_up, w_down, proj_hidden, proj_output
):
    tok_rows, chosen = routes.shape
    groups = lax.axis_size("exp")
    docs_count = max(2, tok_rows * groups // DOC_TOK)
    chips = groups // 2
    half = chips // 2
    ring = list(range(0, chips, 2)) + list(range(chips - 1, 0, -2))
    onward = []
    for place in range(chips):
        onward.append((2 * ring[place], 2 * ring[(place + 1) % chips]))
        onward.append((2 * ring[place] + 1, 2 * ring[place - 1] + 1))
    across = [(i, i ^ 1) for i in range(groups)]

    def hop(block):
        return lax.ppermute(block, "exp", onward)

    def swap(block):
        return lax.ppermute(block, "exp", across)

    arrivals = [(c, step) for step in range(1, half + 1) for c in ("ab" if step < half else "a")]
    jobs = [(("a", 0, False), ("a", 0, True))]
    for i, (c, step) in enumerate(arrivals):
        job = ((c, step, False),)
        if i > 0:
            job += (arrivals[i - 1] + (True,),)
        if i == 1:
            job += (arrivals[0] + (False,),)
        if i == len(arrivals) - 1:
            jobs += [(job[1], job[0]), ((c, step, True),)]
        elif i != 0:
            jobs.append(job)

    sheet = pl.pallas_call(
        facts_kernel,
        out_shape=jax.ShapeDtypeStruct((groups, 1, 3 * tok_rows), jnp.float32),
        in_specs=[pl.BlockSpec(memory_space=pltpu.VMEM)] * 3,
        out_specs=pl.BlockSpec(memory_space=pltpu.VMEM),
        compiler_params=pltpu.CompilerParams(vmem_limit_bytes=8 * 1024 * 1024),
    )(routes.T, combine.T, doc_ids[None, :])
    first = (hop(tokens), hop(cotangent))
    beside = stack(swap(tokens), swap(cotangent))

    inside = pl.BlockSpec(memory_space=pltpu.VMEM)
    given = (w_gate[0], w_up[0], w_down[0], proj_hidden[0].T, proj_output[0].T)
    weights = None
    lows, projs = [], []
    held = {("a", 0, True): beside}
    todo = list(jobs)

    def take():
        nonlocal sheet, weights
        names = todo.pop(0)
        blocks = [held[name] for name in names if name in held]
        if weights is None:
            sheet, low_side, proj_cot, *weights = work(
                names, sheet, blocks, given, apart=(tokens, cotangent), load=1
            )
        else:
            sheet, low_side, proj_cot = work(names, sheet, blocks, weights)
        lows.append(low_side)
        projs.append(proj_cot)

    chain = {"b": beside}
    for i, (c, step) in enumerate(arrivals[:-1]):
        block = hop(chain[c]) if i > 0 else first
        if i != 1:
            take()
            sheet, block = lax.optimization_barrier((sheet, block))
        if i == 0:
            block = stack(*block)
        chain[c] = held[(c, step, False)] = block
        if i < len(arrivals) - 2:
            held[(c, step, True)] = swap(block)
    cut = tok_rows // 2
    cuts = ((0, cut), (cut, cut), (tok_rows, tok_rows))
    *x, dy = split(chain["a"], cuts)
    dy, _ = lax.optimization_barrier((dy, chain["b"]))
    x, dy = [hop(part) for part in x], hop(dy)
    *x_before, dy_before = split(chain["b"], ((0, tok_rows), (tok_rows, tok_rows)))
    x_before, dy_before = [swap(part) for part in x_before], swap(dy_before)
    take()
    sheet, x = lax.optimization_barrier((sheet, x))
    hidden, low_first, low_last = front(
        x_before + x + [swap(part) for part in x], weights, tok_rows
    )
    hidden, dy = lax.optimization_barrier((hidden, dy))
    dy_beside = swap(dy)
    rank = proj_output.shape[2]
    sheet, proj_cot, out_val = on_core(
        functools.partial(out_kernel, todo.pop(0)),
        (sheet, dy_before, dy, hidden, weights[2], weights[4]),
        [sheet.shape, (rank, 2 * tok_rows), tokens.shape],
        flops=6 * tok_rows * hidden.shape[1] * tokens.shape[1],
    )
    lows.append(low_first)
    projs.append(proj_cot)
    ((name,),) = todo
    sheet, proj_cot = on_core(
        functools.partial(last_kernel, name),
        (sheet, dy_beside, out_val, weights[4]),
        [sheet.shape, (rank, tok_rows)],
    )
    lows.append(low_last)
    projs.append(proj_cot)
    returned = lax.all_to_all(sheet, "exp", split_axis=0, concat_axis=0, tiled=True)
    feature, route_grad = pl.pallas_call(
        functools.partial(outcome_kernel, jobs),
        out_shape=[
            jax.ShapeDtypeStruct((docs_count * rank, rank), jnp.float32),
            jax.ShapeDtypeStruct((chosen, tok_rows), jnp.float32),
        ],
        in_specs=[inside] * (2 + 2 * len(lows)),
        out_specs=[inside] * 2,
        compiler_params=pltpu.CompilerParams(vmem_limit_bytes=16 * 1024 * 1024),
    )(returned, routes.T, *lows, *projs)
    return feature.reshape(docs_count, 1, rank, rank), route_grad.T


def by_routing(
    tokens, cotangent, routes, combine, doc_ids, w_gate, w_up, w_down, proj_hidden, proj_output
):
    tok_rows, chosen = routes.shape
    local_count = w_gate.shape[0]
    groups = lax.axis_size("exp")
    experts = local_count * groups
    capacity = max(2, tok_rows * chosen * 5 // (4 * experts))
    docs_count = max(2, tok_rows * groups // DOC_TOK)
    entries = tok_rows * chosen
    width = tokens.shape[1]
    flat_routes = routes.reshape(-1)
    member = (flat_routes[:, None] == jnp.arange(experts, dtype=jnp.int32)[None, :]).astype(
        jnp.int32
    )
    slot_rank = jnp.sum((jnp.cumsum(member, axis=0) - 1) * member, axis=1)
    position = flat_routes * capacity + slot_rank
    source = (
        jnp.full((experts * capacity,), -1, jnp.int32)
        .at[position]
        .set(jnp.arange(entries, dtype=jnp.int32))
    )
    filled = source >= 0
    safe_source = jnp.maximum(source, 0)
    token_of = safe_source // chosen
    send_x = jnp.where(filled[:, None], tokens[token_of], 0)
    send_dy = jnp.where(filled[:, None], cotangent[token_of], 0)
    send_w = jnp.where(filled, combine.reshape(-1)[safe_source], 0)
    send_doc = jnp.where(filled, doc_ids[token_of], -1).astype(jnp.bfloat16)

    def exchange(array):
        array = array.reshape((groups, local_count, capacity) + array.shape[1:])
        return lax.all_to_all(array, "exp", split_axis=0, concat_axis=0, tiled=True)

    recv_x, recv_dy, recv_w, recv_doc = (
        exchange(send_x),
        exchange(send_dy),
        exchange(send_w),
        exchange(send_doc),
    )
    slots = groups * capacity
    grads, feats = [], []
    for e in range(local_count):
        hidden = swiglu(recv_x[:, e].reshape(slots, width), w_gate[e], w_up[e])
        grad, feature = finish(
            hidden,
            recv_dy[:, e].reshape(slots, width),
            recv_w[:, e].reshape(slots),
            recv_doc[:, e].reshape(slots),
            w_down[e],
            proj_hidden[e],
            proj_output[e],
            docs_count,
        )
        grads.append(grad.reshape(groups, capacity))
        feats.append(feature)
    slot_grad = jnp.stack(grads, axis=1)
    returned = lax.all_to_all(slot_grad, "exp", split_axis=0, concat_axis=0, tiled=True)
    route_grad = returned.reshape(-1)[position].reshape(tok_rows, chosen)
    return jnp.stack(feats, axis=1), route_grad


def on_device(tokens, cotangent, routes, combine, doc_ids, w_gate, *rest):
    tok_rows, chosen = routes.shape
    experts = w_gate.shape[0] * lax.axis_size("exp")
    dense = w_gate.shape[0] == 1 and 4 * chosen >= experts and experts >= 8 and experts % 4 == 0
    plan = by_ring if dense else by_routing
    return plan(tokens, cotangent, routes, combine, doc_ids, w_gate, *rest)


def solution(mesh):
    placed = (
        P(("grp", "exp"), None),
        P(("grp", "exp"), None),
        P(("grp", "exp"), None),
        P(("grp", "exp"), None),
        P(("grp", "exp")),
        P("exp", None, None),
        P("exp", None, None),
        P("exp", None, None),
        P("exp", None, None),
        P("exp", None, None),
    )
    return jax.shard_map(
        on_device,
        mesh=mesh,
        in_specs=placed,
        out_specs=(P("grp", "exp", None, None), P(("grp", "exp"), None)),
        check_vma=False,
    )
```

```python
import functools

import jax
import jax.numpy as jnp
from jax import lax
from jax.experimental import pallas as pl
from jax.experimental.pallas import tpu as pltpu
from jax.sharding import PartitionSpec as P

DOC_TOK = 512
LOAD_MIB = 40


def swiglu(rows, w_gate, w_up):
    gate_val = jnp.dot(rows, w_gate, preferred_element_type=jnp.float32)
    up_val = jnp.dot(rows, w_up, preferred_element_type=jnp.float32)
    return (jax.nn.silu(gate_val) * up_val).astype(jnp.bfloat16)


def finish(hidden, rows_dy, rows_w, rows_doc, w_down, proj_hidden, proj_output, docs_count):
    out_val = jnp.dot(hidden, w_down, preferred_element_type=jnp.float32)
    grad = jnp.sum(rows_dy.astype(jnp.float32) * out_val, axis=-1)
    low_side = jnp.dot(hidden, proj_hidden, preferred_element_type=jnp.float32).astype(
        jnp.bfloat16
    )
    proj_cot = jnp.dot(rows_dy, proj_output, preferred_element_type=jnp.float32)
    high_side = (rows_w.astype(jnp.float32)[:, None] * proj_cot).astype(jnp.bfloat16)
    doc_table = jnp.arange(docs_count, dtype=jnp.int32).astype(jnp.bfloat16)
    onehot = (rows_doc[:, None] == doc_table).astype(jnp.bfloat16)
    spread = onehot[:, :, None] * low_side[:, None, :]
    spread = spread.reshape(spread.shape[0], -1)
    feature = lax.dot_general(
        spread, high_side, (((0,), (0,)), ((), ())), preferred_element_type=jnp.float32
    )
    return grad, feature.reshape(docs_count, low_side.shape[1], high_side.shape[1])


def block_owner(name, chips):
    chain, step, handed = name
    me = lax.axis_index("exp")
    core, chip = lax.rem(me, 2), lax.div(me, 2)
    turn = chips // 2
    place = jnp.where(lax.rem(chip, 2) == 0, lax.div(chip, 2), chips - 1 - lax.div(chip, 2))
    way = 2 * core - 1
    place = place + (-way if handed else way) * step
    place = lax.rem(place + chips, chips)
    chip = jnp.where(place < turn, 2 * place, 2 * (chips - 1 - place) + 1)
    return 2 * chip + (core if (chain == "a") != handed else 1 - core)


def rows_kernel(names, load, *refs):
    blocks = len(names)
    apart = refs[1:3] if load else ()
    refs = refs[:1] + refs[3:] if load else refs
    whole = blocks - 1 if load else blocks
    sheet_in, block_in = refs[0], refs[1 : 1 + whole]
    given = refs[1 + whole : 6 + whole]
    sheet, low_side, proj_cot = refs[6 + whole : 9 + whole]
    x_all, dy_all, low_sum, grad_sum = refs[-5:-1] if load else refs[-4:]
    w_gate, w_up, w_down, low_proj, high_proj = refs[9 + whole : 14 + whole] if load else given
    rows = x_all.shape[0] // blocks
    across = (((1,), (1,)), ((), ()))
    units = w_gate.shape[1]
    tile = 256 if units % 256 == 0 else units
    tiles = units // tile
    lanes = grad_sum.shape[1]
    copies = []
    if load:
        rank = given[3].shape[0]
        for j in range(tiles):
            part = pl.ds(j * tile, tile)
            copies.append((given[0].at[:, part], w_gate.at[:, part]))
            copies.append((given[1].at[:, part], w_up.at[:, part]))
            copies.append((given[2].at[part, :], w_down.at[part, :]))
        for i in range(low_proj.shape[0] // rank):
            copies.append((given[3], low_proj.at[pl.ds(i * rank, rank), :]))
        copies.append((given[4], high_proj))
        copies.append((apart[0], x_all.at[:rows]))
        copies.append((apart[1], dy_all.at[:rows]))
        copies = [
            pltpu.make_async_copy(src, dst, refs[-1].at[i]) for i, (src, dst) in enumerate(copies)
        ]
        for copy in copies[3 * tiles :] + copies[: 3 * tiles]:
            copy.start()
    if blocks == 1:
        x_all, dy_all = block_in[0].at[:rows, :], block_in[0].at[rows:, :]
    for i, block in enumerate(block_in if blocks > 1 else ()):
        place = slice((blocks - whole + i) * rows, (blocks - whole + i + 1) * rows)
        x_all[place, :] = block[:rows, :]
        dy_all[place, :] = block[rows:, :]

    def one_tile(j):
        part = pl.ds(j * tile, tile)
        gate_val = jnp.dot(x_all[...], w_gate[:, part], preferred_element_type=jnp.float32)
        up_val = jnp.dot(x_all[...], w_up[:, part], preferred_element_type=jnp.float32)
        hidden = (jax.nn.silu(gate_val) * up_val).astype(jnp.bfloat16)
        back = lax.dot_general(
            dy_all[...], w_down[part, :], across, preferred_element_type=jnp.float32
        )
        terms = hidden.astype(jnp.float32) * back
        total = terms[:, :lanes]
        for cut in range(lanes, tile, lanes):
            total += terms[:, cut : cut + lanes]
        grad_sum[...] = total if j == 0 else grad_sum[...] + total
        low = lax.dot_general(
            low_proj[:, part], hidden, across, preferred_element_type=jnp.float32
        )
        low_sum[...] = low if j == 0 else low_sum[...] + low

    for copy in copies[3 * tiles :]:
        copy.wait()
    for j in range(tiles):
        for copy in copies[3 * j : 3 * j + 3] if load else []:
            copy.wait()
        one_tile(j)

    low_side[...] = low_sum[...].astype(low_side.dtype)
    proj_cot[...] = lax.dot_general(
        high_proj[...], dy_all[...], across, preferred_element_type=jnp.float32
    )
    sheet[...] = sheet_in[...]
    for i in range(blocks):
        total = jnp.sum(
            jnp.transpose(grad_sum[i * rows : (i + 1) * rows, :]), axis=0, keepdims=True
        )
        sheet[block_owner(names[i], sheet.shape[0] // 2), :, : total.shape[1]] = total


def work(names, sheet, block_in, weights, apart=(), load=0):
    width, units = weights[0].shape
    low_width, rank = weights[3].shape[0] * max(load, 1), weights[4].shape[0]
    blocks = len(names)
    rows = block_in[0].shape[0] // 2
    inside = pl.BlockSpec(memory_space=pltpu.VMEM)
    loaded = []
    if load:
        shapes = [w.shape for w in weights]
        shapes[3] = (low_width, units)
        loaded = [jax.ShapeDtypeStruct(shape, weights[0].dtype) for shape in shapes]
    tiles = units // 256 if units % 256 == 0 else 1
    call = pl.pallas_call(
        functools.partial(rows_kernel, names, load > 0),
        out_shape=[
            jax.ShapeDtypeStruct(sheet.shape, jnp.float32),
            jax.ShapeDtypeStruct((low_width, blocks * rows), jnp.bfloat16),
            jax.ShapeDtypeStruct((rank, blocks * rows), jnp.float32),
        ]
        + loaded,
        in_specs=[inside]
        + [pl.BlockSpec(memory_space=pl.ANY)] * len(apart)
        + [inside] * len(block_in)
        + [pl.BlockSpec(memory_space=pl.ANY) if load else inside] * len(weights),
        out_specs=[inside] * (3 + len(loaded)),
        scratch_shapes=[
            pltpu.VMEM((blocks * rows, width), jnp.bfloat16),
            pltpu.VMEM((blocks * rows, width), jnp.bfloat16),
            pltpu.VMEM((low_width, blocks * rows), jnp.float32),
            pltpu.VMEM((blocks * rows, 128), jnp.float32),
        ]
        + ([pltpu.SemaphoreType.DMA((3 * tiles + load + 3,))] if load else []),
        compiler_params=pltpu.CompilerParams(
            vmem_limit_bytes=(LOAD_MIB if load else 16) * 1024 * 1024
        ),
        cost_estimate=pl.CostEstimate(
            flops=6 * blocks * rows * width * units,
            bytes_accessed=4 * blocks * rows * width,
            transcendentals=blocks * rows * units,
        ),
    )
    return call(sheet, *apart, *block_in, *weights)


def front_kernel(begin, x_in, w_gate, w_up, low_proj, hidden, low_side, x_all, low_sum):
    rows = 0
    for x in x_in:
        x_all[rows : rows + x.shape[0], :] = x[...]
        rows += x.shape[0]
    units = w_gate.shape[1]
    tile = 256 if units % 256 == 0 else units
    for cut in range(0, units, tile):
        part = pl.ds(cut, tile)
        gate_val = jnp.dot(x_all[...], w_gate[:, part], preferred_element_type=jnp.float32)
        up_val = jnp.dot(x_all[...], w_up[:, part], preferred_element_type=jnp.float32)
        piece = (jax.nn.silu(gate_val) * up_val).astype(jnp.bfloat16)
        hidden[begin : begin + rows, part] = piece
        low = lax.dot_general(
            low_proj[:, part],
            piece,
            (((1,), (1,)), ((), ())),
            preferred_element_type=jnp.float32,
        )
        low_sum[...] = low if cut == 0 else low_sum[...] + low
    low_side[...] = low_sum[...].astype(low_side.dtype)


def front(x_in, weights, begin, room, held=()):
    w_gate, w_up, _, low_proj, _ = weights
    rows, width = sum(x.shape[0] for x in x_in), x_in[0].shape[1]
    units = w_gate.shape[1]
    inside = pl.BlockSpec(memory_space=pltpu.VMEM)
    count = len(x_in)

    def kernel(*refs):
        front_kernel(begin, refs[:count], *refs[count : count + 3], *refs[-4:])

    return pl.pallas_call(
        kernel,
        out_shape=[
            jax.ShapeDtypeStruct((room, units), jnp.bfloat16),
            jax.ShapeDtypeStruct((low_proj.shape[0], rows), jnp.bfloat16),
        ],
        in_specs=[inside] * (count + 3 + len(held)),
        out_specs=[inside] * 2,
        input_output_aliases={count + 3: 0} if held else {},
        scratch_shapes=[
            pltpu.VMEM((rows, width), jnp.bfloat16),
            pltpu.VMEM((low_proj.shape[0], rows), jnp.float32),
        ],
        compiler_params=pltpu.CompilerParams(vmem_limit_bytes=16 * 1024 * 1024),
        cost_estimate=pl.CostEstimate(flops=0, bytes_accessed=0, transcendentals=0),
    )(*x_in, w_gate, w_up, low_proj, *held)


def fold(product):
    total = product[:, :128]
    for spot in range(128, product.shape[1], 128):
        total += product[:, spot : spot + 128]
    return total


def enter(sheet, name, total):
    line = jnp.sum(jnp.transpose(total), axis=0, keepdims=True)
    sheet[block_owner(name, sheet.shape[0] // 2), :, : line.shape[1]] = line


def out_kernel(names, *refs):
    blocks = len(names)
    sheet_in, dy_in = refs[0], refs[1 : 1 + blocks]
    hidden, w_down, high_proj, sheet, proj_cot, rest = refs[1 + blocks :]
    rows = dy_in[0].shape[0]
    across = (((1,), (1,)), ((), ()))
    width = w_down.shape[1]
    tile = 256 if width % 256 == 0 else width
    totals = [0.0] * blocks
    for cut in range(0, width, tile):
        part = pl.ds(cut, tile)
        out_val = jnp.dot(hidden[...], w_down[:, part], preferred_element_type=jnp.float32)
        for i in range(blocks):
            dy = dy_in[i][:, part].astype(jnp.float32)
            totals[i] += fold(dy * out_val[i * rows : (i + 1) * rows, :])
        rest[:, part] = out_val[blocks * rows :, :]
    sheet[...] = sheet_in[...]
    for i in range(blocks):
        enter(sheet, names[i], totals[i])
        proj_cot[:, i * rows : (i + 1) * rows] = lax.dot_general(
            high_proj[...], dy_in[i][...], across, preferred_element_type=jnp.float32
        )


def last_kernel(name, sheet_in, dy, out_val, high_proj, sheet, proj_cot):
    width = dy.shape[1]
    tile = 512 if width % 512 == 0 else width
    total = 0.0
    for cut in range(0, width, tile):
        part = pl.ds(cut, tile)
        total += fold(dy[:, part].astype(jnp.float32) * out_val[:, part])
    sheet[...] = sheet_in[...]
    enter(sheet, name, total)
    proj_cot[...] = lax.dot_general(
        high_proj[...], dy[...], (((1,), (1,)), ((), ())), preferred_element_type=jnp.float32
    )


def on_core(kernel, args, out_shape, flops=0):
    inside = pl.BlockSpec(memory_space=pltpu.VMEM)
    return pl.pallas_call(
        kernel,
        out_shape=[jax.ShapeDtypeStruct(shape, jnp.float32) for shape in out_shape],
        in_specs=[inside] * len(args),
        out_specs=[inside] * len(out_shape),
        compiler_params=pltpu.CompilerParams(vmem_limit_bytes=16 * 1024 * 1024),
        cost_estimate=pl.CostEstimate(flops=flops, bytes_accessed=2**20, transcendentals=0),
    )(*args)


def outcome_kernel(jobs, returned, routes, *refs):
    low_in, proj_in = refs[: len(jobs)], refs[len(jobs) : 2 * len(jobs)]
    feat, route_grad = refs[-2:]
    rows = returned.shape[2] // 3
    rank = proj_in[0].shape[0]
    docs = feat.shape[0] // rank
    spread, high_side = [], []
    for names, low_side, proj_cot in zip(jobs, low_in, proj_in):
        for i, name in enumerate(names):
            place = slice(i * rows, (i + 1) * rows)
            owner = block_owner(name, returned.shape[0] // 2)
            weight = returned[owner, :, rows : 2 * rows]
            doc = returned[owner, :, 2 * rows :].astype(jnp.int32)
            high_side.append((weight * proj_cot[:, place]).astype(jnp.bfloat16))
            low = low_side[:, place].astype(jnp.float32)
            parts = [jnp.where(doc == d, low, 0.0) for d in range(docs)]
            spread.append(jnp.concatenate(parts, axis=0).astype(jnp.bfloat16))
    feat[...] = lax.dot_general(
        jnp.concatenate(spread, axis=1),
        jnp.concatenate(high_side, axis=1),
        (((1,), (1,)), ((), ())),
        preferred_element_type=jnp.float32,
    )
    picked = jnp.zeros(route_grad.shape, jnp.float32)
    for e in range(returned.shape[0]):
        picked = jnp.where(routes[...] == e, returned[e, :, :rows], picked)
    route_grad[...] = picked


def facts_kernel(routes, combine, doc_ids, out):
    groups, rows = out.shape[0], routes.shape[1]
    expert = lax.broadcasted_iota(jnp.int32, (groups, rows), 0)
    weight = jnp.zeros((groups, rows), jnp.float32)
    for k in range(routes.shape[0]):
        share = combine[k : k + 1, :].astype(jnp.float32)
        weight += jnp.where(routes[k : k + 1, :] == expert, share, 0.0)
    doc = doc_ids[...].astype(jnp.float32)
    for e in range(groups):
        out[e] = jnp.concatenate([doc, weight[e : e + 1, :], doc], axis=1)


def stack_kernel(top, bottom, out):
    rows = top.shape[0]
    out[:rows, :] = top[...]
    out[rows:, :] = bottom[...]


def stack(top, bottom):
    inside = pl.BlockSpec(memory_space=pltpu.VMEM)
    return pl.pallas_call(
        stack_kernel,
        out_shape=jax.ShapeDtypeStruct((2 * top.shape[0], top.shape[1]), top.dtype),
        in_specs=[inside] * 2,
        out_specs=inside,
        compiler_params=pltpu.CompilerParams(vmem_limit_bytes=8 * 1024 * 1024),
    )(top, bottom)


def split_kernel(cuts, block, *parts):
    for (begin, count), part in zip(cuts, parts):
        part[...] = block[begin : begin + count, :]


def split(block, cuts):
    inside = pl.BlockSpec(memory_space=pltpu.VMEM)
    return pl.pallas_call(
        functools.partial(split_kernel, cuts),
        out_shape=[
            jax.ShapeDtypeStruct((count, block.shape[1]), block.dtype) for _, count in cuts
        ],
        in_specs=[inside],
        out_specs=[inside] * len(cuts),
        compiler_params=pltpu.CompilerParams(vmem_limit_bytes=8 * 1024 * 1024),
    )(block)


def by_ring(
    tokens, cotangent, routes, combine, doc_ids, w_gate, w_up, w_down, proj_hidden, proj_output
):
    tok_rows, chosen = routes.shape
    groups = lax.axis_size("exp")
    docs_count = max(2, tok_rows * groups // DOC_TOK)
    chips = groups // 2
    half = chips // 2
    ring = list(range(0, chips, 2)) + list(range(chips - 1, 0, -2))
    onward = []
    for place in range(chips):
        onward.append((2 * ring[place], 2 * ring[(place + 1) % chips]))
        onward.append((2 * ring[place] + 1, 2 * ring[place - 1] + 1))
    across = [(i, i ^ 1) for i in range(groups)]

    def hop(block):
        return lax.ppermute(block, "exp", onward)

    def swap(block):
        return lax.ppermute(block, "exp", across)

    arrivals = [(c, step) for step in range(1, half + 1) for c in ("ab" if step < half else "a")]
    jobs = [(("a", 0, False), ("a", 0, True))]
    for i, (c, step) in enumerate(arrivals):
        job = ((c, step, False),)
        if i > 0:
            job += (arrivals[i - 1] + (True,),)
        if i == 1:
            job += (arrivals[0] + (False,),)
        if i == len(arrivals) - 1:
            jobs += [(job[1], job[0]), ((c, step, True),)]
        elif i != 0:
            jobs.append(job)

    sheet = pl.pallas_call(
        facts_kernel,
        out_shape=jax.ShapeDtypeStruct((groups, 1, 3 * tok_rows), jnp.float32),
        in_specs=[pl.BlockSpec(memory_space=pltpu.VMEM)] * 3,
        out_specs=pl.BlockSpec(memory_space=pltpu.VMEM),
        compiler_params=pltpu.CompilerParams(vmem_limit_bytes=8 * 1024 * 1024),
    )(routes.T, combine.T, doc_ids[None, :])
    first = (hop(tokens), hop(cotangent))
    beside = stack(swap(tokens), swap(cotangent))

    inside = pl.BlockSpec(memory_space=pltpu.VMEM)
    given = (w_gate[0], w_up[0], w_down[0], proj_hidden[0].T, proj_output[0].T)
    weights = None
    lows, projs = [], []
    held = {("a", 0, True): beside}
    todo = list(jobs)

    def take():
        nonlocal sheet, weights
        names = todo.pop(0)
        blocks = [held[name] for name in names if name in held]
        if weights is None:
            sheet, low_side, proj_cot, *weights = work(
                names, sheet, blocks, given, apart=(tokens, cotangent), load=1
            )
        else:
            sheet, low_side, proj_cot = work(names, sheet, blocks, weights)
        lows.append(low_side)
        projs.append(proj_cot)

    chain = {"b": beside}
    for i, (c, step) in enumerate(arrivals[:-1]):
        block = hop(chain[c]) if i > 0 else first
        if i != 1:
            take()
            sheet, block = lax.optimization_barrier((sheet, block))
        if i == 0:
            block = stack(*block)
        chain[c] = held[(c, step, False)] = block
        if i < len(arrivals) - 2:
            held[(c, step, True)] = swap(block)
    cut = tok_rows // 2
    cuts = ((0, cut), (cut, cut), (tok_rows, tok_rows))
    *x, dy = split(chain["a"], cuts)
    dy, _ = lax.optimization_barrier((dy, chain["b"]))
    x, dy = [hop(part) for part in x], hop(dy)
    *x_before, dy_before = split(chain["b"], ((0, tok_rows), (tok_rows, tok_rows)))
    x_before, dy_before = [swap(part) for part in x_before], swap(dy_before)
    take()
    sheet, x = lax.optimization_barrier((sheet, x))
    x_beside = [swap(part) for part in x]
    hidden, low_first = front(x_before + x, weights, 0, 3 * tok_rows)
    hidden, low_last = front(x_beside, weights, 2 * tok_rows, 3 * tok_rows, (hidden,))
    hidden, dy = lax.optimization_barrier((hidden, dy))
    dy_beside = swap(dy)
    rank = proj_output.shape[2]
    sheet, proj_cot, out_val = on_core(
        functools.partial(out_kernel, todo.pop(0)),
        (sheet, dy_before, dy, hidden, weights[2], weights[4]),
        [sheet.shape, (rank, 2 * tok_rows), tokens.shape],
        flops=6 * tok_rows * hidden.shape[1] * tokens.shape[1],
    )
    lows.append(low_first)
    projs.append(proj_cot)
    ((name,),) = todo
    sheet, proj_cot = on_core(
        functools.partial(last_kernel, name),
        (sheet, dy_beside, out_val, weights[4]),
        [sheet.shape, (rank, tok_rows)],
    )
    lows.append(low_last)
    projs.append(proj_cot)
    returned = lax.all_to_all(sheet, "exp", split_axis=0, concat_axis=0, tiled=True)
    feature, route_grad = pl.pallas_call(
        functools.partial(outcome_kernel, jobs),
        out_shape=[
            jax.ShapeDtypeStruct((docs_count * rank, rank), jnp.float32),
            jax.ShapeDtypeStruct((chosen, tok_rows), jnp.float32),
        ],
        in_specs=[inside] * (2 + 2 * len(lows)),
        out_specs=[inside] * 2,
        compiler_params=pltpu.CompilerParams(vmem_limit_bytes=16 * 1024 * 1024),
    )(returned, routes.T, *lows, *projs)
    return feature.reshape(docs_count, 1, rank, rank), route_grad.T


def by_routing(
    tokens, cotangent, routes, combine, doc_ids, w_gate, w_up, w_down, proj_hidden, proj_output
):
    tok_rows, chosen = routes.shape
    local_count = w_gate.shape[0]
    groups = lax.axis_size("exp")
    experts = local_count * groups
    capacity = max(2, tok_rows * chosen * 5 // (4 * experts))
    docs_count = max(2, tok_rows * groups // DOC_TOK)
    entries = tok_rows * chosen
    width = tokens.shape[1]
    flat_routes = routes.reshape(-1)
    member = (flat_routes[:, None] == jnp.arange(experts, dtype=jnp.int32)[None, :]).astype(
        jnp.int32
    )
    slot_rank = jnp.sum((jnp.cumsum(member, axis=0) - 1) * member, axis=1)
    position = flat_routes * capacity + slot_rank
    source = (
        jnp.full((experts * capacity,), -1, jnp.int32)
        .at[position]
        .set(jnp.arange(entries, dtype=jnp.int32))
    )
    filled = source >= 0
    safe_source = jnp.maximum(source, 0)
    token_of = safe_source // chosen
    send_x = jnp.where(filled[:, None], tokens[token_of], 0)
    send_dy = jnp.where(filled[:, None], cotangent[token_of], 0)
    send_w = jnp.where(filled, combine.reshape(-1)[safe_source], 0)
    send_doc = jnp.where(filled, doc_ids[token_of], -1).astype(jnp.bfloat16)

    def exchange(array):
        array = array.reshape((groups, local_count, capacity) + array.shape[1:])
        return lax.all_to_all(array, "exp", split_axis=0, concat_axis=0, tiled=True)

    recv_x, recv_dy, recv_w, recv_doc = (
        exchange(send_x),
        exchange(send_dy),
        exchange(send_w),
        exchange(send_doc),
    )
    slots = groups * capacity
    grads, feats = [], []
    for e in range(local_count):
        hidden = swiglu(recv_x[:, e].reshape(slots, width), w_gate[e], w_up[e])
        grad, feature = finish(
            hidden,
            recv_dy[:, e].reshape(slots, width),
            recv_w[:, e].reshape(slots),
            recv_doc[:, e].reshape(slots),
            w_down[e],
            proj_hidden[e],
            proj_output[e],
            docs_count,
        )
        grads.append(grad.reshape(groups, capacity))
        feats.append(feature)
    slot_grad = jnp.stack(grads, axis=1)
    returned = lax.all_to_all(slot_grad, "exp", split_axis=0, concat_axis=0, tiled=True)
    route_grad = returned.reshape(-1)[position].reshape(tok_rows, chosen)
    return jnp.stack(feats, axis=1), route_grad


def on_device(tokens, cotangent, routes, combine, doc_ids, w_gate, *rest):
    tok_rows, chosen = routes.shape
    experts = w_gate.shape[0] * lax.axis_size("exp")
    dense = w_gate.shape[0] == 1 and 4 * chosen >= experts and experts >= 8 and experts % 4 == 0
    plan = by_ring if dense else by_routing
    return plan(tokens, cotangent, routes, combine, doc_ids, w_gate, *rest)


def solution(mesh):
    placed = (
        P(("grp", "exp"), None),
        P(("grp", "exp"), None),
        P(("grp", "exp"), None),
        P(("grp", "exp"), None),
        P(("grp", "exp")),
        P("exp", None, None),
        P("exp", None, None),
        P("exp", None, None),
        P("exp", None, None),
        P("exp", None, None),
    )
    return jax.shard_map(
        on_device,
        mesh=mesh,
        in_specs=placed,
        out_specs=(P("grp", "exp", None, None), P(("grp", "exp"), None)),
        check_vma=False,
    )
```

```python
import functools

import jax
import jax.numpy as jnp
from jax import lax
from jax.experimental import pallas as pl
from jax.experimental.pallas import tpu as pltpu
from jax.sharding import PartitionSpec as P

DOC_TOK = 512
LOAD_MIB = 40


def swiglu(rows, w_gate, w_up):
    gate_val = jnp.dot(rows, w_gate, preferred_element_type=jnp.float32)
    up_val = jnp.dot(rows, w_up, preferred_element_type=jnp.float32)
    return (jax.nn.silu(gate_val) * up_val).astype(jnp.bfloat16)


def finish(hidden, rows_dy, rows_w, rows_doc, w_down, proj_hidden, proj_output, docs_count):
    out_val = jnp.dot(hidden, w_down, preferred_element_type=jnp.float32)
    grad = jnp.sum(rows_dy.astype(jnp.float32) * out_val, axis=-1)
    low_side = jnp.dot(hidden, proj_hidden, preferred_element_type=jnp.float32).astype(
        jnp.bfloat16
    )
    proj_cot = jnp.dot(rows_dy, proj_output, preferred_element_type=jnp.float32)
    high_side = (rows_w.astype(jnp.float32)[:, None] * proj_cot).astype(jnp.bfloat16)
    doc_table = jnp.arange(docs_count, dtype=jnp.int32).astype(jnp.bfloat16)
    onehot = (rows_doc[:, None] == doc_table).astype(jnp.bfloat16)
    spread = onehot[:, :, None] * low_side[:, None, :]
    spread = spread.reshape(spread.shape[0], -1)
    feature = lax.dot_general(
        spread, high_side, (((0,), (0,)), ((), ())), preferred_element_type=jnp.float32
    )
    return grad, feature.reshape(docs_count, low_side.shape[1], high_side.shape[1])


def block_owner(name, chips):
    chain, step, handed = name
    me = lax.axis_index("exp")
    core, chip = lax.rem(me, 2), lax.div(me, 2)
    turn = chips // 2
    place = jnp.where(lax.rem(chip, 2) == 0, lax.div(chip, 2), chips - 1 - lax.div(chip, 2))
    way = 2 * core - 1
    place = place + (-way if handed else way) * step
    place = lax.rem(place + chips, chips)
    chip = jnp.where(place < turn, 2 * place, 2 * (chips - 1 - place) + 1)
    return 2 * chip + (core if (chain == "a") != handed else 1 - core)


def rows_kernel(names, load, *refs):
    blocks = len(names)
    apart = refs[1:3] if load else ()
    refs = refs[:1] + refs[3:] if load else refs
    whole = blocks - 1 if load else blocks
    sheet_in, block_in = refs[0], refs[1 : 1 + whole]
    given = refs[1 + whole : 6 + whole]
    sheet, low_side, proj_cot = refs[6 + whole : 9 + whole]
    x_all, dy_all, low_sum, grad_sum = refs[-5:-1] if load else refs[-4:]
    w_gate, w_up, w_down, low_proj, high_proj = refs[9 + whole : 14 + whole] if load else given
    rows = x_all.shape[0] // blocks
    across = (((1,), (1,)), ((), ()))
    units = w_gate.shape[1]
    tile = 256 if units % 256 == 0 else units
    tiles = units // tile
    lanes = grad_sum.shape[1]
    copies = []
    if load:
        rank = given[3].shape[0]
        for j in range(tiles):
            part = pl.ds(j * tile, tile)
            copies.append((given[0].at[:, part], w_gate.at[:, part]))
            copies.append((given[1].at[:, part], w_up.at[:, part]))
            copies.append((given[2].at[part, :], w_down.at[part, :]))
        for i in range(low_proj.shape[0] // rank):
            copies.append((given[3], low_proj.at[pl.ds(i * rank, rank), :]))
        copies.append((given[4], high_proj))
        copies.append((apart[0], x_all.at[:rows]))
        copies.append((apart[1], dy_all.at[:rows]))
        copies = [
            pltpu.make_async_copy(src, dst, refs[-1].at[i]) for i, (src, dst) in enumerate(copies)
        ]
        for copy in copies[3 * tiles :] + copies[: 3 * tiles]:
            copy.start()
    if blocks == 1:
        x_all, dy_all = block_in[0].at[:rows, :], block_in[0].at[rows:, :]
    for i, block in enumerate(block_in if blocks > 1 else ()):
        place = slice((blocks - whole + i) * rows, (blocks - whole + i + 1) * rows)
        x_all[place, :] = block[:rows, :]
        dy_all[place, :] = block[rows:, :]

    def one_tile(j):
        part = pl.ds(j * tile, tile)
        gate_val = jnp.dot(x_all[...], w_gate[:, part], preferred_element_type=jnp.float32)
        up_val = jnp.dot(x_all[...], w_up[:, part], preferred_element_type=jnp.float32)
        hidden = (jax.nn.silu(gate_val) * up_val).astype(jnp.bfloat16)
        back = lax.dot_general(
            dy_all[...], w_down[part, :], across, preferred_element_type=jnp.float32
        )
        terms = hidden.astype(jnp.float32) * back
        total = terms[:, :lanes]
        for cut in range(lanes, tile, lanes):
            total += terms[:, cut : cut + lanes]
        grad_sum[...] = total if j == 0 else grad_sum[...] + total
        low = lax.dot_general(
            low_proj[:, part], hidden, across, preferred_element_type=jnp.float32
        )
        low_sum[...] = low if j == 0 else low_sum[...] + low

    for copy in copies[3 * tiles :]:
        copy.wait()
    for j in range(tiles):
        for copy in copies[3 * j : 3 * j + 3] if load else []:
            copy.wait()
        one_tile(j)

    low_side[...] = low_sum[...].astype(low_side.dtype)
    proj_cot[...] = lax.dot_general(
        high_proj[...], dy_all[...], across, preferred_element_type=jnp.float32
    )
    sheet[...] = sheet_in[...]
    for i in range(blocks):
        total = jnp.sum(
            jnp.transpose(grad_sum[i * rows : (i + 1) * rows, :]), axis=0, keepdims=True
        )
        sheet[block_owner(names[i], sheet.shape[0] // 2), :, : total.shape[1]] = total


def work(names, sheet, block_in, weights, apart=(), load=0):
    width, units = weights[0].shape
    low_width, rank = weights[3].shape[0] * max(load, 1), weights[4].shape[0]
    blocks = len(names)
    rows = block_in[0].shape[0] // 2
    inside = pl.BlockSpec(memory_space=pltpu.VMEM)
    loaded = []
    if load:
        shapes = [w.shape for w in weights]
        shapes[3] = (low_width, units)
        loaded = [jax.ShapeDtypeStruct(shape, weights[0].dtype) for shape in shapes]
    tiles = units // 256 if units % 256 == 0 else 1
    call = pl.pallas_call(
        functools.partial(rows_kernel, names, load > 0),
        out_shape=[
            jax.ShapeDtypeStruct(sheet.shape, jnp.float32),
            jax.ShapeDtypeStruct((low_width, blocks * rows), jnp.bfloat16),
            jax.ShapeDtypeStruct((rank, blocks * rows), jnp.float32),
        ]
        + loaded,
        in_specs=[inside]
        + [pl.BlockSpec(memory_space=pl.ANY)] * len(apart)
        + [inside] * len(block_in)
        + [pl.BlockSpec(memory_space=pl.ANY) if load else inside] * len(weights),
        out_specs=[inside] * (3 + len(loaded)),
        scratch_shapes=[
            pltpu.VMEM((blocks * rows, width), jnp.bfloat16),
            pltpu.VMEM((blocks * rows, width), jnp.bfloat16),
            pltpu.VMEM((low_width, blocks * rows), jnp.float32),
            pltpu.VMEM((blocks * rows, 128), jnp.float32),
        ]
        + ([pltpu.SemaphoreType.DMA((3 * tiles + load + 3,))] if load else []),
        compiler_params=pltpu.CompilerParams(
            vmem_limit_bytes=(LOAD_MIB if load else 16) * 1024 * 1024
        ),
        cost_estimate=pl.CostEstimate(
            flops=6 * blocks * rows * width * units,
            bytes_accessed=4 * blocks * rows * width,
            transcendentals=blocks * rows * units,
        ),
    )
    return call(sheet, *apart, *block_in, *weights)


def front_kernel(begin, x_in, w_gate, w_up, low_proj, hidden, low_side, x_all, low_sum):
    rows = 0
    for x in x_in:
        x_all[rows : rows + x.shape[0], :] = x[...]
        rows += x.shape[0]
    units = w_gate.shape[1]
    tile = 256 if units % 256 == 0 else units
    for cut in range(0, units, tile):
        part = pl.ds(cut, tile)
        gate_val = jnp.dot(x_all[...], w_gate[:, part], preferred_element_type=jnp.float32)
        up_val = jnp.dot(x_all[...], w_up[:, part], preferred_element_type=jnp.float32)
        piece = (jax.nn.silu(gate_val) * up_val).astype(jnp.bfloat16)
        hidden[begin : begin + rows, part] = piece
        low = lax.dot_general(
            low_proj[:, part],
            piece,
            (((1,), (1,)), ((), ())),
            preferred_element_type=jnp.float32,
        )
        low_sum[...] = low if cut == 0 else low_sum[...] + low
    low_side[...] = low_sum[...].astype(low_side.dtype)


def front(x_in, weights, begin, room, held=()):
    w_gate, w_up, _, low_proj, _ = weights
    rows, width = sum(x.shape[0] for x in x_in), x_in[0].shape[1]
    units = w_gate.shape[1]
    inside = pl.BlockSpec(memory_space=pltpu.VMEM)
    count = len(x_in)

    def kernel(*refs):
        front_kernel(begin, refs[:count], *refs[count : count + 3], *refs[-4:])

    return pl.pallas_call(
        kernel,
        out_shape=[
            jax.ShapeDtypeStruct((room, units), jnp.bfloat16),
            jax.ShapeDtypeStruct((low_proj.shape[0], rows), jnp.bfloat16),
        ],
        in_specs=[inside] * (count + 3 + len(held)),
        out_specs=[inside] * 2,
        input_output_aliases={count + 3: 0} if held else {},
        scratch_shapes=[
            pltpu.VMEM((rows, width), jnp.bfloat16),
            pltpu.VMEM((low_proj.shape[0], rows), jnp.float32),
        ],
        compiler_params=pltpu.CompilerParams(vmem_limit_bytes=16 * 1024 * 1024),
        cost_estimate=pl.CostEstimate(flops=0, bytes_accessed=0, transcendentals=0),
    )(*x_in, w_gate, w_up, low_proj, *held)


def fold(product):
    total = product[:, :128]
    for spot in range(128, product.shape[1], 128):
        total += product[:, spot : spot + 128]
    return total


def enter(sheet, name, total):
    line = jnp.sum(jnp.transpose(total), axis=0, keepdims=True)
    sheet[block_owner(name, sheet.shape[0] // 2), :, : line.shape[1]] = line


def out_kernel(names, *refs):
    blocks = len(names)
    sheet_in, dy_in = refs[0], refs[1 : 1 + blocks]
    hidden, w_down, high_proj, sheet, proj_cot, rest = refs[1 + blocks :]
    rows = dy_in[0].shape[0]
    across = (((1,), (1,)), ((), ()))
    width = w_down.shape[1]
    tile = 256 if width % 256 == 0 else width
    totals = [0.0] * blocks
    for cut in range(0, width, tile):
        part = pl.ds(cut, tile)
        out_val = jnp.dot(hidden[...], w_down[:, part], preferred_element_type=jnp.float32)
        for i in range(blocks):
            dy = dy_in[i][:, part].astype(jnp.float32)
            totals[i] += fold(dy * out_val[i * rows : (i + 1) * rows, :])
        rest[:, part] = out_val[blocks * rows :, :]
    for i in range(blocks):
        enter(sheet, names[i], totals[i])
        proj_cot[:, i * rows : (i + 1) * rows] = lax.dot_general(
            high_proj[...], dy_in[i][...], across, preferred_element_type=jnp.float32
        )


def last_kernel(name, sheet_in, dy, out_val, high_proj, sheet, proj_cot):
    width = dy.shape[1]
    tile = 512 if width % 512 == 0 else width
    total = 0.0
    for cut in range(0, width, tile):
        part = pl.ds(cut, tile)
        total += fold(dy[:, part].astype(jnp.float32) * out_val[:, part])
    enter(sheet, name, total)
    proj_cot[...] = lax.dot_general(
        high_proj[...], dy[...], (((1,), (1,)), ((), ())), preferred_element_type=jnp.float32
    )


def on_core(kernel, args, out_shape, flops=0):
    inside = pl.BlockSpec(memory_space=pltpu.VMEM)
    return pl.pallas_call(
        kernel,
        out_shape=[jax.ShapeDtypeStruct(shape, jnp.float32) for shape in out_shape],
        in_specs=[inside] * len(args),
        out_specs=[inside] * len(out_shape),
        input_output_aliases={0: 0},
        compiler_params=pltpu.CompilerParams(vmem_limit_bytes=16 * 1024 * 1024),
        cost_estimate=pl.CostEstimate(flops=flops, bytes_accessed=2**20, transcendentals=0),
    )(*args)


def outcome_kernel(jobs, returned, routes, *refs):
    low_in, proj_in = refs[: len(jobs)], refs[len(jobs) : 2 * len(jobs)]
    feat, route_grad = refs[-2:]
    rows = returned.shape[2] // 3
    rank = proj_in[0].shape[0]
    docs = feat.shape[0] // rank
    spread, high_side = [], []
    for names, low_side, proj_cot in zip(jobs, low_in, proj_in):
        for i, name in enumerate(names):
            place = slice(i * rows, (i + 1) * rows)
            owner = block_owner(name, returned.shape[0] // 2)
            weight = returned[owner, :, rows : 2 * rows]
            doc = returned[owner, :, 2 * rows :].astype(jnp.int32)
            high_side.append((weight * proj_cot[:, place]).astype(jnp.bfloat16))
            low = low_side[:, place].astype(jnp.float32)
            parts = [jnp.where(doc == d, low, 0.0) for d in range(docs)]
            spread.append(jnp.concatenate(parts, axis=0).astype(jnp.bfloat16))
    feat[...] = lax.dot_general(
        jnp.concatenate(spread, axis=1),
        jnp.concatenate(high_side, axis=1),
        (((1,), (1,)), ((), ())),
        preferred_element_type=jnp.float32,
    )
    picked = jnp.zeros(route_grad.shape, jnp.float32)
    for e in range(returned.shape[0]):
        picked = jnp.where(routes[...] == e, returned[e, :, :rows], picked)
    route_grad[...] = picked


def facts_kernel(routes, combine, doc_ids, out):
    groups, rows = out.shape[0], routes.shape[1]
    expert = lax.broadcasted_iota(jnp.int32, (groups, rows), 0)
    weight = jnp.zeros((groups, rows), jnp.float32)
    for k in range(routes.shape[0]):
        share = combine[k : k + 1, :].astype(jnp.float32)
        weight += jnp.where(routes[k : k + 1, :] == expert, share, 0.0)
    doc = doc_ids[...].astype(jnp.float32)
    for e in range(groups):
        out[e] = jnp.concatenate([doc, weight[e : e + 1, :], doc], axis=1)


def stack_kernel(top, bottom, out):
    rows = top.shape[0]
    out[:rows, :] = top[...]
    out[rows:, :] = bottom[...]


def stack(top, bottom):
    inside = pl.BlockSpec(memory_space=pltpu.VMEM)
    return pl.pallas_call(
        stack_kernel,
        out_shape=jax.ShapeDtypeStruct((2 * top.shape[0], top.shape[1]), top.dtype),
        in_specs=[inside] * 2,
        out_specs=inside,
        compiler_params=pltpu.CompilerParams(vmem_limit_bytes=8 * 1024 * 1024),
    )(top, bottom)


def split_kernel(cuts, block, *parts):
    for (begin, count), part in zip(cuts, parts):
        part[...] = block[begin : begin + count, :]


def split(block, cuts):
    inside = pl.BlockSpec(memory_space=pltpu.VMEM)
    return pl.pallas_call(
        functools.partial(split_kernel, cuts),
        out_shape=[
            jax.ShapeDtypeStruct((count, block.shape[1]), block.dtype) for _, count in cuts
        ],
        in_specs=[inside],
        out_specs=[inside] * len(cuts),
        compiler_params=pltpu.CompilerParams(vmem_limit_bytes=8 * 1024 * 1024),
    )(block)


def by_ring(
    tokens, cotangent, routes, combine, doc_ids, w_gate, w_up, w_down, proj_hidden, proj_output
):
    tok_rows, chosen = routes.shape
    groups = lax.axis_size("exp")
    docs_count = max(2, tok_rows * groups // DOC_TOK)
    chips = groups // 2
    half = chips // 2
    ring = list(range(0, chips, 2)) + list(range(chips - 1, 0, -2))
    onward = []
    for place in range(chips):
        onward.append((2 * ring[place], 2 * ring[(place + 1) % chips]))
        onward.append((2 * ring[place] + 1, 2 * ring[place - 1] + 1))
    across = [(i, i ^ 1) for i in range(groups)]

    def hop(block):
        return lax.ppermute(block, "exp", onward)

    def swap(block):
        return lax.ppermute(block, "exp", across)

    arrivals = [(c, step) for step in range(1, half + 1) for c in ("ab" if step < half else "a")]
    jobs = [(("a", 0, False), ("a", 0, True))]
    for i, (c, step) in enumerate(arrivals):
        job = ((c, step, False),)
        if i > 0:
            job += (arrivals[i - 1] + (True,),)
        if i == 1:
            job += (arrivals[0] + (False,),)
        if i == len(arrivals) - 1:
            jobs += [(job[1], job[0]), ((c, step, True),)]
        elif i != 0:
            jobs.append(job)

    sheet = pl.pallas_call(
        facts_kernel,
        out_shape=jax.ShapeDtypeStruct((groups, 1, 3 * tok_rows), jnp.float32),
        in_specs=[pl.BlockSpec(memory_space=pltpu.VMEM)] * 3,
        out_specs=pl.BlockSpec(memory_space=pltpu.VMEM),
        compiler_params=pltpu.CompilerParams(vmem_limit_bytes=8 * 1024 * 1024),
    )(routes.T, combine.T, doc_ids[None, :])
    first = (hop(tokens), hop(cotangent))
    beside = stack(swap(tokens), swap(cotangent))

    inside = pl.BlockSpec(memory_space=pltpu.VMEM)
    given = (w_gate[0], w_up[0], w_down[0], proj_hidden[0].T, proj_output[0].T)
    weights = None
    lows, projs = [], []
    held = {("a", 0, True): beside}
    todo = list(jobs)

    def take():
        nonlocal sheet, weights
        names = todo.pop(0)
        blocks = [held[name] for name in names if name in held]
        if weights is None:
            sheet, low_side, proj_cot, *weights = work(
                names, sheet, blocks, given, apart=(tokens, cotangent), load=1
            )
        else:
            sheet, low_side, proj_cot = work(names, sheet, blocks, weights)
        lows.append(low_side)
        projs.append(proj_cot)

    chain = {"b": beside}
    for i, (c, step) in enumerate(arrivals[:-1]):
        block = hop(chain[c]) if i > 0 else first
        if i != 1:
            take()
            sheet, block = lax.optimization_barrier((sheet, block))
        if i == 0:
            block = stack(*block)
        chain[c] = held[(c, step, False)] = block
        if i < len(arrivals) - 2:
            held[(c, step, True)] = swap(block)
    cut = tok_rows // 2
    cuts = ((0, cut), (cut, cut), (tok_rows, tok_rows))
    *x, dy = split(chain["a"], cuts)
    dy, _ = lax.optimization_barrier((dy, chain["b"]))
    x, dy = [hop(part) for part in x], hop(dy)
    *x_before, dy_before = split(chain["b"], ((0, tok_rows), (tok_rows, tok_rows)))
    x_before, dy_before = [swap(part) for part in x_before], swap(dy_before)
    take()
    sheet, x = lax.optimization_barrier((sheet, x))
    x_beside = [swap(part) for part in x]
    hidden, low_first = front(x_before + x, weights, 0, 3 * tok_rows)
    hidden, low_last = front(x_beside, weights, 2 * tok_rows, 3 * tok_rows, (hidden,))
    hidden, dy = lax.optimization_barrier((hidden, dy))
    dy_beside = swap(dy)
    rank = proj_output.shape[2]
    sheet, proj_cot, out_val = on_core(
        functools.partial(out_kernel, todo.pop(0)),
        (sheet, dy_before, dy, hidden, weights[2], weights[4]),
        [sheet.shape, (rank, 2 * tok_rows), tokens.shape],
        flops=6 * tok_rows * hidden.shape[1] * tokens.shape[1],
    )
    lows.append(low_first)
    projs.append(proj_cot)
    ((name,),) = todo
    sheet, proj_cot = on_core(
        functools.partial(last_kernel, name),
        (sheet, dy_beside, out_val, weights[4]),
        [sheet.shape, (rank, tok_rows)],
    )
    lows.append(low_last)
    projs.append(proj_cot)
    returned = lax.all_to_all(sheet, "exp", split_axis=0, concat_axis=0, tiled=True)
    feature, route_grad = pl.pallas_call(
        functools.partial(outcome_kernel, jobs),
        out_shape=[
            jax.ShapeDtypeStruct((docs_count * rank, rank), jnp.float32),
            jax.ShapeDtypeStruct((chosen, tok_rows), jnp.float32),
        ],
        in_specs=[inside] * (2 + 2 * len(lows)),
        out_specs=[inside] * 2,
        compiler_params=pltpu.CompilerParams(vmem_limit_bytes=16 * 1024 * 1024),
    )(returned, routes.T, *lows, *projs)
    return feature.reshape(docs_count, 1, rank, rank), route_grad.T


def by_routing(
    tokens, cotangent, routes, combine, doc_ids, w_gate, w_up, w_down, proj_hidden, proj_output
):
    tok_rows, chosen = routes.shape
    local_count = w_gate.shape[0]
    groups = lax.axis_size("exp")
    experts = local_count * groups
    capacity = max(2, tok_rows * chosen * 5 // (4 * experts))
    docs_count = max(2, tok_rows * groups // DOC_TOK)
    entries = tok_rows * chosen
    width = tokens.shape[1]
    flat_routes = routes.reshape(-1)
    member = (flat_routes[:, None] == jnp.arange(experts, dtype=jnp.int32)[None, :]).astype(
        jnp.int32
    )
    slot_rank = jnp.sum((jnp.cumsum(member, axis=0) - 1) * member, axis=1)
    position = flat_routes * capacity + slot_rank
    source = (
        jnp.full((experts * capacity,), -1, jnp.int32)
        .at[position]
        .set(jnp.arange(entries, dtype=jnp.int32))
    )
    filled = source >= 0
    safe_source = jnp.maximum(source, 0)
    token_of = safe_source // chosen
    send_x = jnp.where(filled[:, None], tokens[token_of], 0)
    send_dy = jnp.where(filled[:, None], cotangent[token_of], 0)
    send_w = jnp.where(filled, combine.reshape(-1)[safe_source], 0)
    send_doc = jnp.where(filled, doc_ids[token_of], -1).astype(jnp.bfloat16)

    def exchange(array):
        array = array.reshape((groups, local_count, capacity) + array.shape[1:])
        return lax.all_to_all(array, "exp", split_axis=0, concat_axis=0, tiled=True)

    recv_x, recv_dy, recv_w, recv_doc = (
        exchange(send_x),
        exchange(send_dy),
        exchange(send_w),
        exchange(send_doc),
    )
    slots = groups * capacity
    grads, feats = [], []
    for e in range(local_count):
        hidden = swiglu(recv_x[:, e].reshape(slots, width), w_gate[e], w_up[e])
        grad, feature = finish(
            hidden,
            recv_dy[:, e].reshape(slots, width),
            recv_w[:, e].reshape(slots),
            recv_doc[:, e].reshape(slots),
            w_down[e],
            proj_hidden[e],
            proj_output[e],
            docs_count,
        )
        grads.append(grad.reshape(groups, capacity))
        feats.append(feature)
    slot_grad = jnp.stack(grads, axis=1)
    returned = lax.all_to_all(slot_grad, "exp", split_axis=0, concat_axis=0, tiled=True)
    route_grad = returned.reshape(-1)[position].reshape(tok_rows, chosen)
    return jnp.stack(feats, axis=1), route_grad


def on_device(tokens, cotangent, routes, combine, doc_ids, w_gate, *rest):
    tok_rows, chosen = routes.shape
    experts = w_gate.shape[0] * lax.axis_size("exp")
    dense = w_gate.shape[0] == 1 and 4 * chosen >= experts and experts >= 8 and experts % 4 == 0
    plan = by_ring if dense else by_routing
    return plan(tokens, cotangent, routes, combine, doc_ids, w_gate, *rest)


def solution(mesh):
    placed = (
        P(("grp", "exp"), None),
        P(("grp", "exp"), None),
        P(("grp", "exp"), None),
        P(("grp", "exp"), None),
        P(("grp", "exp")),
        P("exp", None, None),
        P("exp", None, None),
        P("exp", None, None),
        P("exp", None, None),
        P("exp", None, None),
    )
    return jax.shard_map(
        on_device,
        mesh=mesh,
        in_specs=placed,
        out_specs=(P("grp", "exp", None, None), P(("grp", "exp"), None)),
        check_vma=False,
    )
```
